32 devices in a mesh: blk: 4 (over y, x), grp: 8 (over z, core).
Axes of the slice: x: 2, y: 2, z: 4, core: 2. Of those that a mesh axis runs over, the one named last changes fastest.
Arguments:
- picture_vectors: bfloat16 [4096, 1152], P(('blk', 'grp')), may hold values from -1.1953125 to 1.1953125
- caption_vectors: bfloat16 [4096, 1152], P(('blk', 'grp')), may hold values from -1.1953125 to 1.1953125
- matching_caption: int32 [4096], P(('blk', 'grp')), may hold values from 0 to 4095, each once
- sharpness_parameter: float32 [1], replicated, may hold values from 1 to 4
- additive_intercept: float32 [1], replicated, may hold values from -6 to -2
Outputs:
- picture_derivative: float32 [4096, 1152], P(('blk', 'grp'))
- text_grad: float32 [4096, 1152], P(('blk', 'grp'))
The draws below stay inside these ranges and needn't reach their ends.
Inputs may be any that keep to these rules, and one draw needn't show every extreme that they name: matching_caption is a permutation: each text is the positive of exactly one image.
All inputs are finite; a program needn't handle non-finite values.
Results may differ from the reference program's by a relative error of at most 0.0011.
Values may be sent and summed in bfloat16 or wider, within the bound.
No kernel may reach another device: no remote copies, remote signals or barrier semaphores. Data moves between devices by JAX's collectives and lax.ppermute only.
A program may use at most 64 MiB of HBM per device.

```python
import math
import jax
import jax.numpy as jnp
from jax import lax

D = 1152
BATCH = 4096


def block_levels(rng, shape, cuts, smallest, top_value):
    gain = 1.0
    for axis_at, parts in cuts:
        steps = jax.random.uniform(jax.random.fold_in(jax.random.fold_in(rng, 6), axis_at), (parts,), jnp.float32, smallest / len(cuts), top_value / len(cuts))
        gain = gain * jnp.repeat(jnp.exp(steps), shape[axis_at] // parts).reshape((-1,) + (1,) * (len(shape) - 1 - axis_at))
    return gain


def bell_draw(key, dims, scale, bound, cuts=(), held_as=jnp.bfloat16):
    drawn = jax.random.normal(key, dims, jnp.float32) * scale
    if len(cuts) > 0:
        drawn = block_levels(key, dims, cuts, -0.22, 0.18) * drawn
    return jnp.clip(drawn, min=-bound, max=bound).astype(held_as)


def setup_inputs(seed: int = 0) -> dict:
    splits = jax.random.split(jax.random.key(seed), 6)
    return {
        "picture_vectors": bell_draw(splits[0], (BATCH, D), 0.2, 1.1953125, ((0, 32),)),
        "caption_vectors": bell_draw(splits[1], (BATCH, D), 0.2, 1.1953125, ((0, 32),)),
        "matching_caption": jax.random.permutation(splits[2], BATCH).astype(jnp.int32),
        "sharpness_parameter": jnp.clip(jnp.exp(jax.random.uniform(splits[3], (1,), jnp.float32, math.log(1.0), math.log(4.0))), 1.0, 4.0),
        "additive_intercept": jnp.clip(jax.random.uniform(splits[4], (1,), jnp.float32, -6.0, -2.0), -6.0, -2.0),
    }


def piece_derivative(pinned_sample, guest_captions, matching_pair, sharpness_factor, moved_intercept):
    similarity_matrix = jnp.dot(pinned_sample, guest_captions.T, preferred_element_type=jnp.float32)
    pair_coefficients = (jax.nn.sigmoid(sharpness_factor * similarity_matrix + moved_intercept) - matching_pair).astype(jnp.bfloat16)
    return sharpness_factor * jnp.dot(pair_coefficients, guest_captions, preferred_element_type=jnp.float32)


def reference(picture_vectors, caption_vectors, matching_caption, sharpness_parameter, additive_intercept):
    sharpness_factor = sharpness_parameter[0]
    moved_intercept = additive_intercept[0]
    row_block = BATCH // 8
    all_ids = jnp.arange(BATCH, dtype=jnp.int32)

    def image_rows(start):
        pinned_sample = lax.dynamic_slice_in_dim(picture_vectors, start, row_block, 0)
        own_pairs = lax.dynamic_slice_in_dim(matching_caption, start, row_block, 0)
        matching_pair = (own_pairs[:, None] == all_ids[None, :]).astype(jnp.float32)
        return piece_derivative(pinned_sample, caption_vectors, matching_pair, sharpness_factor, moved_intercept)

    def text_rows(start):
        pinned_sample = lax.dynamic_slice_in_dim(caption_vectors, start, row_block, 0)
        own_ids = start + jnp.arange(row_block, dtype=jnp.int32)
        matching_pair = (own_ids[:, None] == matching_caption[None, :]).astype(jnp.float32)
        return piece_derivative(pinned_sample, picture_vectors, matching_pair, sharpness_factor, moved_intercept)

    starts = jnp.arange(8, dtype=jnp.int32) * row_block
    picture_derivative = lax.map(image_rows, starts).reshape(BATCH, -1)
    text_grad = lax.map(text_rows, starts).reshape(BATCH, -1)
    return picture_derivative, text_grad
```

```python
import math

import jax
import jax.numpy as jnp
from jax import lax
from jax.experimental import pallas as pl
from jax.experimental.pallas import tpu as pltpu
from jax.sharding import PartitionSpec as P

LOG2E = 1.4426950408889634
CODE_TOP = 32000.0
CODE_STEPS = 32.0
CODE_ROWS = 16
TILE = 256


def scale_code(top):
    return jnp.ceil(jnp.log(jnp.maximum(top, 1e-30)) * (CODE_STEPS * LOG2E))


def encoded(value):
    code = scale_code(jnp.max(jnp.abs(value), axis=0, keepdims=True))
    gain = CODE_TOP * jnp.exp(code * (-1.0 / (CODE_STEPS * LOG2E)))
    whole = jnp.round(value * gain).astype(jnp.int32).astype(jnp.int16)
    scales = jnp.broadcast_to(code.astype(jnp.int32), (CODE_ROWS, value.shape[1]))
    return whole, scales.astype(jnp.int16)


def decoded(ref, rows, columns):
    code = ref[pl.ds(rows, CODE_ROWS), columns].astype(jnp.int32).astype(jnp.float32)[:1]
    gain = jnp.exp(code * (1.0 / (CODE_STEPS * LOG2E))) * (1.0 / CODE_TOP)
    return ref[pl.ds(0, rows), columns].astype(jnp.int32).astype(jnp.float32) * gain


def gradient_kernel(row_count, column_count, kept, *refs):
    scalars, row_keys, column_keys = refs[:3]
    x_parts = refs[3 : 3 + row_count]
    y_parts = refs[3 + row_count : 3 + row_count + column_count]
    outs = refs[3 + row_count + column_count : 3 + 2 * row_count + column_count]
    x_all, y_all, weights, x_sems, y_sems = refs[3 + 2 * row_count + column_count :]
    size, width = x_parts[0].shape
    x_copies = [
        pltpu.make_async_copy(p, x_all.at[pl.ds(i * size, size)], x_sems.at[i])
        for i, p in enumerate(x_parts)
    ]
    y_copies = [
        pltpu.make_async_copy(p, y_all.at[pl.ds(i * size, size)], y_sems.at[i])
        for i, p in enumerate(y_parts)
    ]
    for c in x_copies + y_copies:
        c.start()
    slope = scalars[0] * LOG2E
    shift = scalars[1] * LOG2E
    for c in x_copies:
        c.wait()
    per_tile = TILE // size
    keys = [
        jnp.tile(jnp.broadcast_to(row_keys[i : i + 1, :], (size, size)).T, (1, per_tile))
        for i in range(row_count)
    ]
    for n in range(column_count // per_tile):
        for c in y_copies[n * per_tile : (n + 1) * per_tile]:
            c.wait()
        other = jnp.concatenate(
            [column_keys[n * per_tile + k : n * per_tile + k + 1, :] for k in range(per_tile)], axis=1
        )
        scores = lax.dot_general(
            x_all[...],
            y_all[pl.ds(n * TILE, TILE), :],
            (((1,), (1,)), ((), ())),
            preferred_element_type=jnp.float32,
        )
        for i in range(row_count):
            z = scores[i * size : (i + 1) * size] * slope + shift
            sig = 1.0 / (1.0 + jnp.exp2(-z))
            w = jnp.where(keys[i] == other, sig - 1.0, sig)
            weights[pl.ds(i * size, size), pl.ds(n * TILE, TILE)] = w.astype(jnp.bfloat16)
    start = 0
    while start < width:
        span = min(TILE, width - start)
        columns = pl.ds(start, span)
        sums = jnp.dot(weights[...], y_all[:, columns], preferred_element_type=jnp.float32)
        for i in range(row_count):
            block = sums[i * size : (i + 1) * size]
            if i < kept:
                outs[i][:, columns] = block
            else:
                whole, scales = encoded(block)
                outs[i][pl.ds(0, size), columns] = whole
                outs[i][pl.ds(size, CODE_ROWS), columns] = scales
        start += span


def gradient_parts(scalars, row_keys, column_keys, x_parts, y_parts, kept):
    size, width = x_parts[0].shape
    rows, columns = len(x_parts), len(y_parts)
    whole = jax.ShapeDtypeStruct((size, width), jnp.float32)
    coded = jax.ShapeDtypeStruct((size + CODE_ROWS, width), jnp.int16)
    smem = pl.BlockSpec(memory_space=pltpu.SMEM)
    vmem = pl.BlockSpec(memory_space=pltpu.VMEM)
    anywhere = pl.BlockSpec(memory_space=pl.ANY)
    return pl.pallas_call(
        lambda *refs: gradient_kernel(rows, columns, kept, *refs),
        out_shape=[whole if i < kept else coded for i in range(rows)],
        in_specs=[smem, vmem, vmem] + [anywhere] * (rows + columns),
        out_specs=[vmem] * rows,
        scratch_shapes=[
            pltpu.VMEM((rows * size, width), jnp.bfloat16),
            pltpu.VMEM((columns * size, width), jnp.bfloat16),
            pltpu.VMEM((rows * size, columns * size), jnp.bfloat16),
            pltpu.SemaphoreType.DMA((rows,)),
            pltpu.SemaphoreType.DMA((columns,)),
        ],
        compiler_params=pltpu.CompilerParams(vmem_limit_bytes=48 * 2**20),
        cost_estimate=pl.CostEstimate(
            flops=4 * rows * columns * size * size * width,
            bytes_accessed=(rows + columns) * size * width * 2 + rows * size * width * 4,
            transcendentals=rows * columns * size * size,
        ),
        name="gradient_parts",
    )(scalars, row_keys, column_keys, *x_parts, *y_parts)


def combined(scalars, kept, received, final):
    size, width = kept.shape

    def kernel(scalars, kept, *refs):
        out = refs[-1]
        for start in range(0, width, 128):
            columns = pl.ds(start, 128)
            total = kept[:, columns]
            for r in refs[:-1]:
                total = total + decoded(r, size, columns)
            if final:
                out[:, columns] = total * scalars[0]
            else:
                whole, scales = encoded(total)
                out[pl.ds(0, size), columns] = whole
                out[pl.ds(size, CODE_ROWS), columns] = scales

    smem = pl.BlockSpec(memory_space=pltpu.SMEM)
    vmem = pl.BlockSpec(memory_space=pltpu.VMEM)
    shape = (size, width) if final else (size + CODE_ROWS, width)
    return pl.pallas_call(
        kernel,
        out_shape=jax.ShapeDtypeStruct(shape, jnp.float32 if final else jnp.int16),
        in_specs=[smem] + [vmem] * (1 + len(received)),
        out_specs=vmem,
        cost_estimate=pl.CostEstimate(
            flops=8 * size * width, bytes_accessed=12 * size * width, transcendentals=0
        ),
        name="output_sum" if final else "passed_sum",
    )(scalars, kept, *received)


def swapped(block, step):
    axis, bit = step
    return lax.ppermute(block, axis, [(i, i ^ bit) for i in range(lax.axis_size(axis))])


def gathered(block, steps):
    blocks = [block]
    for step in steps:
        blocks = blocks + [swapped(b, step) for b in blocks]
    return blocks


def scattered_sum(scalars, parts, steps):
    received = [[] for _ in parts]
    for s in reversed(range(len(steps))):
        half = 1 << s
        for m in reversed(range(half)):
            top = parts[half + m]
            if s + 1 < len(steps):
                top = combined(scalars, top, received[half + m], False)
            received[m].append(swapped(top, steps[s]))
    return combined(scalars, parts[0], received[0], True)


def bit_steps(axis):
    return [(axis, 1 << k) for k in range(int(math.log2(lax.axis_size(axis))))]


def owner_keys(steps, size):
    owners = [(lax.axis_index("blk"), lax.axis_index("grp"))]
    for axis, bit in steps:
        owners = owners + [(b ^ bit, g) if axis == "blk" else (b, g ^ bit) for b, g in owners]
    grp_count = lax.axis_size("grp")
    firsts = jnp.stack([(b * grp_count + g) * size for b, g in owners])
    return firsts[:, None] + jnp.arange(size, dtype=jnp.int32)[None, :]


def per_device(
    picture_vectors, caption_vectors, matching_caption, sharpness_parameter, additive_intercept
):
    size = picture_vectors.shape[0]
    scalars = jnp.concatenate([sharpness_parameter, additive_intercept])
    core, *grp_steps = bit_steps("grp")
    blk_steps = bit_steps("blk")
    every = grp_steps + blk_steps
    image_steps, text_steps = every[0::2], every[1::2]

    images = gathered(picture_vectors, image_steps)
    texts = gathered(caption_vectors, text_steps)
    labels = matching_caption[None, :]
    for step in image_steps + [core]:
        labels = jnp.concatenate([labels, swapped(labels, step)])
    all_images = images + [swapped(b, core) for b in images]
    all_texts = texts + [swapped(b, core) for b in texts]
    ids = owner_keys(text_steps + [core], size)

    image_parts = gradient_parts(
        scalars, labels[: len(images)], ids, images, all_texts, len(images) // 2
    )
    text_parts = gradient_parts(
        scalars, ids[: len(texts)], labels, texts, all_images, len(texts) // 2
    )
    picture_derivative = scattered_sum(scalars, image_parts, image_steps)
    text_grad = scattered_sum(scalars, text_parts, text_steps)
    return (picture_derivative, text_grad)


def solution(mesh):
    placed = (P(("blk", "grp"), None), P(("blk", "grp"), None), P(("blk", "grp")), P(), P())
    return jax.shard_map(
        per_device,
        mesh=mesh,
        in_specs=placed,
        out_specs=(P(("blk", "grp"), None), P(("blk", "grp"), None)),
        check_vma=False,
    )
```

```python
import math

import jax
import jax.numpy as jnp
from jax import lax
from jax.experimental import pallas as pl
from jax.experimental.pallas import tpu as pltpu
from jax.sharding import PartitionSpec as P

LOG2E = 1.4426950408889634
CODE_TOP = 32000.0
CODE_STEPS = 32.0
CODE_ROWS = 16
TILE = 256


def scale_code(top):
    return jnp.ceil(jnp.log(jnp.maximum(top, 1e-30)) * (CODE_STEPS * LOG2E))


def encoded(value):
    code = scale_code(jnp.max(jnp.abs(value), axis=0, keepdims=True))
    gain = CODE_TOP * jnp.exp(code * (-1.0 / (CODE_STEPS * LOG2E)))
    whole = jnp.round(value * gain).astype(jnp.int32).astype(jnp.int16)
    scales = jnp.broadcast_to(code.astype(jnp.int32), (CODE_ROWS, value.shape[1]))
    return whole, scales.astype(jnp.int16)


def decoded(ref, rows, columns):
    code = ref[pl.ds(rows, CODE_ROWS), columns].astype(jnp.int32).astype(jnp.float32)[:1]
    gain = jnp.exp(code * (1.0 / (CODE_STEPS * LOG2E))) * (1.0 / CODE_TOP)
    return ref[pl.ds(0, rows), columns].astype(jnp.int32).astype(jnp.float32) * gain


def key_column(keys, index):
    size = keys.shape[1]
    return jnp.broadcast_to(keys[index : index + 1, :], (size, size)).T


def add_products(refs, rows, columns, before, emit):
    scalars, row_keys, column_keys, x_parts, y_parts, weights = refs
    size, width = x_parts[0].shape
    slope = scalars[0] * LOG2E
    shift = scalars[1] * LOG2E
    x_all = jnp.concatenate([x_parts[r][...] for r in rows], axis=0)
    per_tile = TILE // size
    keys = [jnp.tile(key_column(row_keys, r), (1, per_tile)) for r in rows]
    for n in range(0, len(columns), per_tile):
        tile = columns[n : n + per_tile]
        y_tile = jnp.concatenate([y_parts[c][...] for c in tile], axis=0)
        other = jnp.concatenate([column_keys[c : c + 1, :] for c in tile], axis=1)
        scores = lax.dot_general(
            x_all, y_tile, (((1,), (1,)), ((), ())), preferred_element_type=jnp.float32
        )
        for i in range(len(rows)):
            z = scores[i * size : (i + 1) * size] * slope + shift
            sig = 1.0 / (1.0 + jnp.exp2(-z))
            w = jnp.where(keys[i] == other, sig - 1.0, sig)
            weights[pl.ds(i * size, size), pl.ds(n * size, TILE)] = w.astype(jnp.bfloat16)
    for start in range(0, width, TILE):
        span = min(TILE, width - start)
        part = pl.ds(start, span)
        y_part = jnp.concatenate([y_parts[c][:, part] for c in columns], axis=0)
        sums = jnp.dot(
            weights[pl.ds(0, len(rows) * size), pl.ds(0, len(columns) * size)],
            y_part,
            preferred_element_type=jnp.float32,
        )
        for i, r in enumerate(rows):
            block = sums[i * size : (i + 1) * size]
            emit(r, part, block if before is None else before[r][:, part] + block)


def gradient_call(kernel, name, scalars, keys, x_parts, y_parts, before, out_shape, pairs):
    size, width = x_parts[0].shape
    rows, columns, sums = len(x_parts), len(y_parts), len(before)

    def body(*refs):
        x_refs, refs_left = refs[3 : 3 + rows], refs[3 + rows :]
        y_refs, refs_left = refs_left[:columns], refs_left[columns:]
        sum_refs, outs = refs_left[:sums], refs_left[sums:-1]
        kernel((*refs[:3], x_refs, y_refs, refs[-1]), sum_refs, outs)

    smem = pl.BlockSpec(memory_space=pltpu.SMEM)
    vmem = pl.BlockSpec(memory_space=pltpu.VMEM)
    held = sum(math.prod(o.shape) * o.dtype.itemsize for o in out_shape)
    held += sum(math.prod(o.shape) * o.dtype.itemsize for o in [*x_parts, *y_parts, *before])
    held += rows * columns * size * size * 2
    return pl.pallas_call(
        body,
        out_shape=out_shape,
        in_specs=[smem] + [vmem] * (2 + rows + columns + sums),
        out_specs=[vmem] * len(out_shape),
        scratch_shapes=[pltpu.VMEM((rows * size, columns * size), jnp.bfloat16)],
        compiler_params=pltpu.CompilerParams(vmem_limit_bytes=held + 8 * 2**20),
        cost_estimate=pl.CostEstimate(
            flops=pairs * size,
            bytes_accessed=pairs * size,
            transcendentals=0,
        ),
        name=name,
    )(scalars, *keys, *x_parts, *y_parts, *before)


def early_sums(scalars, keys, x_parts, y_parts):
    size, width = x_parts[0].shape
    rows, columns = list(range(len(x_parts))), list(range(len(y_parts)))

    def kernel(refs, _, outs):
        def emit(r, part, block):
            outs[r][:, part] = block

        add_products(refs, rows, columns, None, emit)

    shapes = [jax.ShapeDtypeStruct((size, width), jnp.float32)] * len(rows)
    return gradient_call(
        kernel, "early_sums", scalars, keys, x_parts, y_parts, [], shapes, len(rows) * len(columns)
    )


def late_sums(scalars, keys, x_parts, y_parts, early_rows, late_columns, before, kept):
    size, width = x_parts[0].shape
    late_rows = [r for r in range(len(x_parts)) if r not in early_rows]
    slot = {r: i for i, r in enumerate(early_rows)}

    def kernel(refs, sums, outs):
        def emit(r, part, block):
            if r < kept:
                outs[r][:, part] = block
            else:
                whole, scales = encoded(block)
                outs[r][pl.ds(0, size), part] = whole
                outs[r][pl.ds(size, CODE_ROWS), part] = scales

        add_products(refs, late_rows, list(range(len(y_parts))), None, emit)
        add_products(refs, early_rows, late_columns, {r: sums[slot[r]] for r in early_rows}, emit)

    whole = jax.ShapeDtypeStruct((size, width), jnp.float32)
    coded = jax.ShapeDtypeStruct((size + CODE_ROWS, width), jnp.int16)
    shapes = [whole if r < kept else coded for r in range(len(x_parts))]
    pairs = len(late_rows) * len(y_parts) + len(early_rows) * len(late_columns)
    return gradient_call(
        kernel, "late_sums", scalars, keys, x_parts, y_parts, before, shapes, pairs
    )


def picked(keys, chosen):
    return jnp.stack([keys[i] for i in chosen])


def combined(scalars, kept, received, final):
    size, width = kept.shape

    def kernel(scalars, kept, *refs):
        out = refs[-1]
        for start in range(0, width, 128):
            columns = pl.ds(start, 128)
            total = kept[:, columns]
            for r in refs[:-1]:
                total = total + decoded(r, size, columns)
            if final:
                out[:, columns] = total * scalars[0]
            else:
                whole, scales = encoded(total)
                out[pl.ds(0, size), columns] = whole
                out[pl.ds(size, CODE_ROWS), columns] = scales

    smem = pl.BlockSpec(memory_space=pltpu.SMEM)
    vmem = pl.BlockSpec(memory_space=pltpu.VMEM)
    shape = (size, width) if final else (size + CODE_ROWS, width)
    return pl.pallas_call(
        kernel,
        out_shape=jax.ShapeDtypeStruct(shape, jnp.float32 if final else jnp.int16),
        in_specs=[smem] + [vmem] * (1 + len(received)),
        out_specs=vmem,
        compiler_params=pltpu.CompilerParams(vmem_limit_bytes=8 * 2**20),
        cost_estimate=pl.CostEstimate(
            flops=8 * size * width, bytes_accessed=12 * size * width, transcendentals=0
        ),
        name="output_sum" if final else "passed_sum",
    )(scalars, kept, *received)


def swapped(block, step):
    axis, bit = step
    return lax.ppermute(block, axis, [(i, i ^ bit) for i in range(lax.axis_size(axis))])


def gathered(block, steps):
    blocks = [block]
    for step in steps:
        blocks = blocks + [swapped(b, step) for b in blocks]
    return blocks


def scattered_sum(scalars, parts, steps):
    received = [[] for _ in parts]
    for s in reversed(range(len(steps))):
        half = 1 << s
        for m in reversed(range(half)):
            top = parts[half + m]
            if s + 1 < len(steps):
                top = combined(scalars, top, received[half + m], False)
            received[m].append(swapped(top, steps[s]))
    return combined(scalars, parts[0], received[0], True)


def bit_steps(axis):
    return [(axis, 1 << k) for k in range(int(math.log2(lax.axis_size(axis))))]


def owner_keys(steps, size):
    owners = [(lax.axis_index("blk"), lax.axis_index("grp"))]
    for axis, bit in steps:
        owners = owners + [(b ^ bit, g) if axis == "blk" else (b, g ^ bit) for b, g in owners]
    grp_count = lax.axis_size("grp")
    firsts = jnp.stack([(b * grp_count + g) * size for b, g in owners])
    return firsts[:, None] + jnp.arange(size, dtype=jnp.int32)[None, :]


def per_device(
    picture_vectors, caption_vectors, matching_caption, sharpness_parameter, additive_intercept
):
    size = picture_vectors.shape[0]
    scalars = jnp.concatenate([sharpness_parameter, additive_intercept])
    core, *grp_steps = bit_steps("grp")
    blk_steps = bit_steps("blk")
    every = grp_steps + blk_steps
    image_steps, text_steps = every[0::2], every[1::2]

    images = gathered(picture_vectors, image_steps)
    texts = gathered(caption_vectors, text_steps)
    labels = matching_caption[None, :]
    for step in image_steps + [core]:
        labels = jnp.concatenate([labels, swapped(labels, step)])
    ids = owner_keys(text_steps + [core], size)

    def split(count):
        early = [m for m in range(count) if m <= count // 2]
        return early, [m for m in range(count) if m not in early]

    image_count, text_count = len(images), len(texts)
    early_images, late_images = split(image_count)
    early_texts, late_texts = split(text_count)
    other_images = {m: swapped(images[m], core) for m in early_images}
    other_texts = {m: swapped(texts[m], core) for m in early_texts}

    def columns(chosen, count):
        return chosen + [count + m for m in chosen]

    text_before = early_sums(
        scalars,
        (picked(ids, early_texts), picked(labels, columns(early_images, image_count))),
        [texts[m] for m in early_texts],
        [images[m] for m in early_images] + [other_images[m] for m in early_images],
    )
    image_before = early_sums(
        scalars,
        (picked(labels, early_images), picked(ids, columns(early_texts, text_count))),
        [images[m] for m in early_images],
        [texts[m] for m in early_texts] + [other_texts[m] for m in early_texts],
    )
    images, texts, text_before, image_before = lax.optimization_barrier(
        (images, texts, text_before, image_before)
    )
    other_images |= {m: swapped(images[m], core) for m in late_images}
    other_texts |= {m: swapped(texts[m], core) for m in late_texts}
    text_parts = late_sums(
        scalars,
        (ids[:text_count], labels),
        texts,
        images + [other_images[m] for m in range(image_count)],
        early_texts,
        columns(late_images, image_count),
        text_before,
        text_count // 2,
    )
    text_parts, image_scalars = lax.optimization_barrier((text_parts, scalars))
    image_parts = late_sums(
        image_scalars,
        (labels[:image_count], ids),
        images,
        texts + [other_texts[m] for m in range(text_count)],
        early_images,
        columns(late_texts, text_count),
        image_before,
        image_count // 2,
    )
    picture_derivative = scattered_sum(scalars, image_parts, image_steps)
    text_grad = scattered_sum(scalars, text_parts, text_steps)
    return (picture_derivative, text_grad)


def solution(mesh):
    placed = (P(("blk", "grp"), None), P(("blk", "grp"), None), P(("blk", "grp")), P(), P())
    return jax.shard_map(
        per_device,
        mesh=mesh,
        in_specs=placed,
        out_specs=(P(("blk", "grp"), None), P(("blk", "grp"), None)),
        check_vma=False,
    )
```

```python
import math

import jax
import jax.numpy as jnp
from jax import lax
from jax.experimental import pallas as pl
from jax.experimental.pallas import tpu as pltpu
from jax.sharding import PartitionSpec as P

LOG2E = 1.4426950408889634
CODE_TOP = 32000.0
CODE_STEPS = 32.0
CODE_ROWS = 8
LABEL_ROWS = 8
LABEL_BASE = 128
TILE = 256


def scale_code(top):
    return jnp.ceil(jnp.log(jnp.maximum(top, 1e-30)) * (CODE_STEPS * LOG2E))


def encoded(value):
    code = scale_code(jnp.max(jnp.abs(value), axis=0, keepdims=True))
    gain = CODE_TOP * jnp.exp(code * (-1.0 / (CODE_STEPS * LOG2E)))
    whole = jnp.round(value * gain).astype(jnp.int32).astype(jnp.int16)
    scales = jnp.broadcast_to(code.astype(jnp.int32), (CODE_ROWS, value.shape[1]))
    return whole, scales.astype(jnp.int16)


def decoded(ref, rows, columns):
    code = ref[pl.ds(rows, CODE_ROWS), columns].astype(jnp.int32).astype(jnp.float32)[:1]
    gain = jnp.exp(code * (1.0 / (CODE_STEPS * LOG2E))) * (1.0 / CODE_TOP)
    return ref[pl.ds(0, rows), columns].astype(jnp.int32).astype(jnp.float32) * gain


def keys_of(block, size, first):
    if block.shape[0] == size:
        ids = lax.broadcasted_iota(jnp.int32, (1, size), 1) + first
        return ids.astype(jnp.float32)
    parts = block[pl.ds(size, LABEL_ROWS), pl.ds(0, size)].astype(jnp.float32)
    return parts[0:1] * LABEL_BASE + parts[1:2]


def labelled(images, labels):
    size, width = images.shape
    parts = jnp.stack([labels // LABEL_BASE, labels % LABEL_BASE]).astype(jnp.bfloat16)
    parts = jnp.pad(parts, ((0, LABEL_ROWS - 2), (0, width - size)))
    return jnp.concatenate([images, parts])


def add_products(refs, rows, columns, before, emit):
    scalars, row_firsts, column_firsts, x_parts, y_parts, weights = refs
    width = x_parts[0].shape[1]
    size = min(x_parts[0].shape[0], y_parts[0].shape[0])
    slope = scalars[0] * LOG2E
    shift = scalars[1] * LOG2E
    x_all = jnp.concatenate([x_parts[r][pl.ds(0, size), :] for r in rows], axis=0)
    per_tile = TILE // size
    keys = [
        jnp.tile(
            jnp.broadcast_to(keys_of(x_parts[r], size, row_firsts[r]), (size, size)).T,
            (1, per_tile),
        )
        for r in rows
    ]
    for n in range(0, len(columns), per_tile):
        tile = columns[n : n + per_tile]
        y_tile = jnp.concatenate([y_parts[c][pl.ds(0, size), :] for c in tile], axis=0)
        other = jnp.concatenate(
            [keys_of(y_parts[c], size, column_firsts[c]) for c in tile], axis=1
        )
        scores = lax.dot_general(
            x_all, y_tile, (((1,), (1,)), ((), ())), preferred_element_type=jnp.float32
        )
        for i in range(len(rows)):
            z = scores[i * size : (i + 1) * size] * slope + shift
            sig = 1.0 / (1.0 + jnp.exp2(-z))
            w = jnp.where(keys[i] == other, sig - 1.0, sig)
            weights[pl.ds(i * size, size), pl.ds(n * size, TILE)] = w.astype(jnp.bfloat16)
    for start in range(0, width, TILE):
        span = min(TILE, width - start)
        part = pl.ds(start, span)
        y_part = jnp.concatenate([y_parts[c][pl.ds(0, size), part] for c in columns], axis=0)
        sums = jnp.dot(
            weights[pl.ds(0, len(rows) * size), pl.ds(0, len(columns) * size)],
            y_part,
            preferred_element_type=jnp.float32,
        )
        for i, r in enumerate(rows):
            block = sums[i * size : (i + 1) * size]
            emit(r, part, block if before is None else before[r][:, part] + block)


def gradient_call(kernel, name, scalars, firsts, x_parts, y_parts, before, out_shape, pairs):
    size = min(x_parts[0].shape[0], y_parts[0].shape[0])
    rows, columns, sums = len(x_parts), len(y_parts), len(before)

    def body(*refs):
        x_refs, refs_left = refs[3 : 3 + rows], refs[3 + rows :]
        y_refs, refs_left = refs_left[:columns], refs_left[columns:]
        sum_refs, outs = refs_left[:sums], refs_left[sums:-1]
        kernel((*refs[:3], x_refs, y_refs, refs[-1]), sum_refs, outs)

    smem = pl.BlockSpec(memory_space=pltpu.SMEM)
    vmem = pl.BlockSpec(memory_space=pltpu.VMEM)
    held = sum(math.prod(o.shape) * o.dtype.itemsize for o in out_shape)
    held += sum(math.prod(o.shape) * o.dtype.itemsize for o in [*x_parts, *y_parts, *before])
    held += rows * columns * size * size * 2
    return pl.pallas_call(
        body,
        out_shape=out_shape,
        in_specs=[smem] * 3 + [vmem] * (rows + columns + sums),
        out_specs=[vmem] * len(out_shape),
        scratch_shapes=[pltpu.VMEM((rows * size, columns * size), jnp.bfloat16)],
        compiler_params=pltpu.CompilerParams(vmem_limit_bytes=held + 8 * 2**20),
        cost_estimate=pl.CostEstimate(
            flops=pairs * size,
            bytes_accessed=pairs * size,
            transcendentals=0,
        ),
        name=name,
    )(scalars, *firsts, *x_parts, *y_parts, *before)


def early_sums(scalars, firsts, x_parts, y_parts):
    size, width = min(x_parts[0].shape[0], y_parts[0].shape[0]), x_parts[0].shape[1]
    rows, columns = list(range(len(x_parts))), list(range(len(y_parts)))

    def kernel(refs, _, outs):
        def emit(r, part, block):
            outs[r][:, part] = block

        add_products(refs, rows, columns, None, emit)

    shapes = [jax.ShapeDtypeStruct((size, width), jnp.float32)] * len(rows)
    return gradient_call(
        kernel, "early_sums", scalars, firsts, x_parts, y_parts, [], shapes, len(rows) * len(columns)
    )


def late_sums(scalars, firsts, x_parts, y_parts, early_rows, late_columns, before, kept):
    size, width = min(x_parts[0].shape[0], y_parts[0].shape[0]), x_parts[0].shape[1]
    late_rows = [r for r in range(len(x_parts)) if r not in early_rows]
    slot = {r: i for i, r in enumerate(early_rows)}

    def kernel(refs, sums, outs):
        def emit(r, part, block):
            if r < kept:
                outs[r][:, part] = block
            else:
                whole, scales = encoded(block)
                outs[r][pl.ds(0, size), part] = whole
                outs[r][pl.ds(size, CODE_ROWS), part] = scales

        add_products(refs, late_rows, list(range(len(y_parts))), None, emit)
        add_products(refs, early_rows, late_columns, {r: sums[slot[r]] for r in early_rows}, emit)

    whole = jax.ShapeDtypeStruct((size, width), jnp.float32)
    coded = jax.ShapeDtypeStruct((size + CODE_ROWS, width), jnp.int16)
    shapes = [whole if r < kept else coded for r in range(len(x_parts))]
    pairs = len(late_rows) * len(y_parts) + len(early_rows) * len(late_columns)
    return gradient_call(
        kernel, "late_sums", scalars, firsts, x_parts, y_parts, before, shapes, pairs
    )


def picked(firsts, chosen):
    return jnp.stack([firsts[i] for i in chosen])


def combined(scalars, kept, received, final):
    size, width = kept.shape

    def kernel(scalars, kept, *refs):
        out = refs[-1]
        for start in range(0, width, 128):
            columns = pl.ds(start, 128)
            total = kept[:, columns]
            for r in refs[:-1]:
                total = total + decoded(r, size, columns)
            if final:
                out[:, columns] = total * scalars[0]
            else:
                whole, scales = encoded(total)
                out[pl.ds(0, size), columns] = whole
                out[pl.ds(size, CODE_ROWS), columns] = scales

    smem = pl.BlockSpec(memory_space=pltpu.SMEM)
    vmem = pl.BlockSpec(memory_space=pltpu.VMEM)
    shape = (size, width) if final else (size + CODE_ROWS, width)
    return pl.pallas_call(
        kernel,
        out_shape=jax.ShapeDtypeStruct(shape, jnp.float32 if final else jnp.int16),
        in_specs=[smem] + [vmem] * (1 + len(received)),
        out_specs=vmem,
        compiler_params=pltpu.CompilerParams(vmem_limit_bytes=8 * 2**20),
        cost_estimate=pl.CostEstimate(
            flops=8 * size * width, bytes_accessed=12 * size * width, transcendentals=0
        ),
        name="output_sum" if final else "passed_sum",
    )(scalars, kept, *received)


def swapped(block, step):
    axis, bit = step
    return lax.ppermute(block, axis, [(i, i ^ bit) for i in range(lax.axis_size(axis))])


def gathered(block, steps):
    blocks = [block]
    for step in steps:
        blocks = blocks + [swapped(b, step) for b in blocks]
    return blocks


def scattered_sum(scalars, parts, steps):
    received = [[] for _ in parts]
    for s in reversed(range(len(steps))):
        half = 1 << s
        for m in reversed(range(half)):
            top = parts[half + m]
            if s + 1 < len(steps):
                top = combined(scalars, top, received[half + m], False)
            received[m].append(swapped(top, steps[s]))
    return combined(scalars, parts[0], received[0], True)


def bit_steps(axis):
    return [(axis, 1 << k) for k in range(int(math.log2(lax.axis_size(axis))))]


def first_rows(steps, size):
    owners = [(lax.axis_index("blk"), lax.axis_index("grp"))]
    for axis, bit in steps:
        owners = owners + [(b ^ bit, g) if axis == "blk" else (b, g ^ bit) for b, g in owners]
    grp_count = lax.axis_size("grp")
    return [(b * grp_count + g) * size for b, g in owners]


def per_device(
    picture_vectors, caption_vectors, matching_caption, sharpness_parameter, additive_intercept
):
    size = picture_vectors.shape[0]
    scalars = jnp.concatenate([sharpness_parameter, additive_intercept])
    core, *grp_steps = bit_steps("grp")
    blk_steps = bit_steps("blk")
    every = grp_steps + blk_steps
    image_steps, text_steps = every[0::2], every[1::2]

    images = gathered(labelled(picture_vectors, matching_caption), image_steps)
    texts = gathered(caption_vectors, text_steps)
    image_firsts = first_rows(image_steps + [core], size)
    text_firsts = first_rows(text_steps + [core], size)

    def split(count):
        early = [m for m in range(count) if m <= count // 2]
        return early, [m for m in range(count) if m not in early]

    image_count, text_count = len(images), len(texts)
    early_images, late_images = split(image_count)
    early_texts, late_texts = split(text_count)
    other_images = {m: swapped(images[m], core) for m in early_images}
    other_texts = {m: swapped(texts[m], core) for m in early_texts}

    def columns(chosen, count):
        return chosen + [count + m for m in chosen]

    text_before = early_sums(
        scalars,
        (picked(text_firsts, early_texts), picked(image_firsts, columns(early_images, image_count))),
        [texts[m] for m in early_texts],
        [images[m] for m in early_images] + [other_images[m] for m in early_images],
    )
    image_before = early_sums(
        scalars,
        (picked(image_firsts, early_images), picked(text_firsts, columns(early_texts, text_count))),
        [images[m] for m in early_images],
        [texts[m] for m in early_texts] + [other_texts[m] for m in early_texts],
    )
    images, texts, text_before, image_before = lax.optimization_barrier(
        (images, texts, text_before, image_before)
    )
    other_images |= {m: swapped(images[m], core) for m in late_images}
    other_texts |= {m: swapped(texts[m], core) for m in late_texts}
    text_parts = late_sums(
        scalars,
        (jnp.stack(text_firsts[:text_count]), jnp.stack(image_firsts)),
        texts,
        images + [other_images[m] for m in range(image_count)],
        early_texts,
        columns(late_images, image_count),
        text_before,
        text_count // 2,
    )
    text_parts, image_scalars = lax.optimization_barrier((text_parts, scalars))
    image_parts = late_sums(
        image_scalars,
        (jnp.stack(image_firsts[:image_count]), jnp.stack(text_firsts)),
        images,
        texts + [other_texts[m] for m in range(text_count)],
        early_images,
        columns(late_texts, text_count),
        image_before,
        image_count // 2,
    )
    picture_derivative = scattered_sum(scalars, image_parts, image_steps)
    text_grad = scattered_sum(scalars, text_parts, text_steps)
    return (picture_derivative, text_grad)


def solution(mesh):
    placed = (P(("blk", "grp"), None), P(("blk", "grp"), None), P(("blk", "grp")), P(), P())
    return jax.shard_map(
        per_device,
        mesh=mesh,
        in_specs=placed,
        out_specs=(P(("blk", "grp"), None), P(("blk", "grp"), None)),
        check_vma=False,
    )
```

```python
import math

import jax
import jax.numpy as jnp
from jax import lax
from jax.experimental import pallas as pl
from jax.experimental.pallas import tpu as pltpu
from jax.sharding import PartitionSpec as P

LOG2E = 1.4426950408889634
CODE_TOP = 32000.0
CODE_STEPS = 32.0
CODE_ROWS = 8
LABEL_ROWS = 8
LABEL_BASE = 128
TILE = 256


def scale_code(top):
    return jnp.ceil(jnp.log(jnp.maximum(top, 1e-30)) * (CODE_STEPS * LOG2E))


def encoded(value):
    code = scale_code(jnp.max(jnp.abs(value), axis=0, keepdims=True))
    gain = CODE_TOP * jnp.exp(code * (-1.0 / (CODE_STEPS * LOG2E)))
    whole = jnp.round(value * gain).astype(jnp.int32).astype(jnp.int16)
    scales = jnp.broadcast_to(code.astype(jnp.int32), (CODE_ROWS, value.shape[1]))
    return whole, scales.astype(jnp.int16)


def decoded(ref, rows, columns):
    code = ref[pl.ds(rows, CODE_ROWS), columns].astype(jnp.int32).astype(jnp.float32)[:1]
    gain = jnp.exp(code * (1.0 / (CODE_STEPS * LOG2E))) * (1.0 / CODE_TOP)
    return ref[pl.ds(0, rows), columns].astype(jnp.int32).astype(jnp.float32) * gain


def keys_of(block, size, mask):
    if block.shape[0] == size:
        ids = lax.broadcasted_iota(jnp.int32, (1, size), 1) + first_row(mask, size)
        return ids.astype(jnp.float32)
    parts = block[pl.ds(size, LABEL_ROWS), pl.ds(0, size)].astype(jnp.float32)
    return parts[0:1] * LABEL_BASE + parts[1:2]


def labelled(images, labels):
    size, width = images.shape

    def kernel(images, labels, out):
        out[pl.ds(0, size), :] = images[...]
        out[pl.ds(size, LABEL_ROWS), :] = jnp.zeros((LABEL_ROWS, width), jnp.bfloat16)
        row = labels[...]
        low = lax.rem(row, LABEL_BASE)
        high = lax.div(row, LABEL_BASE)
        at = lax.broadcasted_iota(jnp.int32, (LABEL_ROWS, size), 0)
        parts = jnp.where(at == 0, high, jnp.where(at == 1, low, 0))
        out[pl.ds(size, LABEL_ROWS), pl.ds(0, size)] = parts.astype(jnp.float32).astype(jnp.bfloat16)

    vmem = pl.BlockSpec(memory_space=pltpu.VMEM)
    return pl.pallas_call(
        kernel,
        out_shape=jax.ShapeDtypeStruct((size + LABEL_ROWS, width), jnp.bfloat16),
        in_specs=[vmem, vmem],
        out_specs=vmem,
        compiler_params=pltpu.CompilerParams(vmem_limit_bytes=4 * 2**20),
        cost_estimate=pl.CostEstimate(flops=size, bytes_accessed=size, transcendentals=0),
        name="labelled_rows",
    )(images, labels[None, :])


def first_row(mask, size):
    owner = (lax.axis_index("blk") ^ mask[0]) * lax.axis_size("grp") + (lax.axis_index("grp") ^ mask[1])
    return owner * size


def add_products(refs, rows, columns, before, emit):
    scalars, row_masks, column_masks, x_parts, y_parts, weights = refs
    width = x_parts[0].shape[1]
    size = min(x_parts[0].shape[0], y_parts[0].shape[0])
    slope = scalars[0][0] * LOG2E
    shift = scalars[1][0] * LOG2E
    x_all = jnp.concatenate([x_parts[r][pl.ds(0, size), :] for r in rows], axis=0)
    per_tile = TILE // size
    keys = [
        jnp.tile(
            jnp.broadcast_to(keys_of(x_parts[r], size, row_masks[r]), (size, size)).T,
            (1, per_tile),
        )
        for r in rows
    ]
    for n in range(0, len(columns), per_tile):
        tile = columns[n : n + per_tile]
        y_tile = jnp.concatenate([y_parts[c][pl.ds(0, size), :] for c in tile], axis=0)
        other = jnp.concatenate(
            [keys_of(y_parts[c], size, column_masks[c]) for c in tile], axis=1
        )
        scores = lax.dot_general(
            x_all, y_tile, (((1,), (1,)), ((), ())), preferred_element_type=jnp.float32
        )
        for i in range(len(rows)):
            z = scores[i * size : (i + 1) * size] * slope + shift
            sig = 1.0 / (1.0 + jnp.exp2(-z))
            w = jnp.where(keys[i] == other, sig - 1.0, sig)
            weights[pl.ds(i * size, size), pl.ds(n * size, TILE)] = w.astype(jnp.bfloat16)
    for start in range(0, width, TILE):
        span = min(TILE, width - start)
        part = pl.ds(start, span)
        y_part = jnp.concatenate([y_parts[c][pl.ds(0, size), part] for c in columns], axis=0)
        sums = jnp.dot(
            weights[pl.ds(0, len(rows) * size), pl.ds(0, len(columns) * size)],
            y_part,
            preferred_element_type=jnp.float32,
        )
        for i, r in enumerate(rows):
            block = sums[i * size : (i + 1) * size]
            emit(r, part, block if before is None else before[r][:, part] + block)


def gradient_call(
    kernel, name, scalars, masks, x_parts, y_parts, before, out_shape, pairs, after=()
):
    size = min(x_parts[0].shape[0], y_parts[0].shape[0])
    rows, columns, sums = len(x_parts), len(y_parts), len(before)

    def body(*refs):
        x_refs, refs_left = refs[2 : 2 + rows], refs[2 + rows :]
        y_refs, refs_left = refs_left[:columns], refs_left[columns:]
        sum_refs, outs = refs_left[:sums], refs_left[sums + len(after) : -1]
        kernel((refs[:2], *masks, x_refs, y_refs, refs[-1]), sum_refs, outs)

    smem = pl.BlockSpec(memory_space=pltpu.SMEM)
    vmem = pl.BlockSpec(memory_space=pltpu.VMEM)
    held = sum(math.prod(o.shape) * o.dtype.itemsize for o in out_shape)
    held += sum(math.prod(o.shape) * o.dtype.itemsize for o in [*x_parts, *y_parts, *before])
    held += rows * columns * size * size * 2
    return pl.pallas_call(
        body,
        out_shape=out_shape,
        in_specs=[smem] * 2
        + [vmem] * (rows + columns + sums)
        + [pl.BlockSpec(memory_space=pl.ANY)] * len(after),
        out_specs=[vmem] * len(out_shape),
        scratch_shapes=[pltpu.VMEM((rows * size, columns * size), jnp.bfloat16)],
        compiler_params=pltpu.CompilerParams(vmem_limit_bytes=held + 8 * 2**20),
        cost_estimate=pl.CostEstimate(
            flops=pairs * size,
            bytes_accessed=pairs * size,
            transcendentals=0,
        ),
        name=name,
    )(*scalars, *x_parts, *y_parts, *before, *after)


def early_sums(scalars, masks, x_parts, y_parts):
    size, width = min(x_parts[0].shape[0], y_parts[0].shape[0]), x_parts[0].shape[1]
    rows, columns = list(range(len(x_parts))), list(range(len(y_parts)))

    def kernel(refs, _, outs):
        def emit(r, part, block):
            outs[r][:, part] = block

        add_products(refs, rows, columns, None, emit)

    shapes = [jax.ShapeDtypeStruct((size, width), jnp.float32)] * len(rows)
    return gradient_call(
        kernel, "early_sums", scalars, masks, x_parts, y_parts, [], shapes, len(rows) * len(columns)
    )


def late_sums(
    scalars, masks, x_parts, y_parts, early_rows, late_columns, before, kept, after=()
):
    size, width = min(x_parts[0].shape[0], y_parts[0].shape[0]), x_parts[0].shape[1]
    late_rows = [r for r in range(len(x_parts)) if r not in early_rows]
    slot = {r: i for i, r in enumerate(early_rows)}

    def kernel(refs, sums, outs):
        def emit(r, part, block):
            if r < kept:
                outs[r][:, part] = block
            else:
                whole, scales = encoded(block)
                outs[r][pl.ds(0, size), part] = whole
                outs[r][pl.ds(size, CODE_ROWS), part] = scales

        add_products(refs, late_rows, list(range(len(y_parts))), None, emit)
        add_products(refs, early_rows, late_columns, {r: sums[slot[r]] for r in early_rows}, emit)

    whole = jax.ShapeDtypeStruct((size, width), jnp.float32)
    coded = jax.ShapeDtypeStruct((size + CODE_ROWS, width), jnp.int16)
    shapes = [whole if r < kept else coded for r in range(len(x_parts))]
    pairs = len(late_rows) * len(y_parts) + len(early_rows) * len(late_columns)
    return gradient_call(
        kernel, "late_sums", scalars, masks, x_parts, y_parts, before, shapes, pairs, after
    )


def combined(scalars, kept, received, final):
    size, width = kept.shape

    def kernel(sharpness, kept, *refs):
        out = refs[-1]
        for start in range(0, width, 128):
            columns = pl.ds(start, 128)
            total = kept[:, columns]
            for r in refs[:-1]:
                total = total + decoded(r, size, columns)
            if final:
                out[:, columns] = total * sharpness[0]
            else:
                whole, scales = encoded(total)
                out[pl.ds(0, size), columns] = whole
                out[pl.ds(size, CODE_ROWS), columns] = scales

    smem = pl.BlockSpec(memory_space=pltpu.SMEM)
    vmem = pl.BlockSpec(memory_space=pltpu.VMEM)
    shape = (size, width) if final else (size + CODE_ROWS, width)
    return pl.pallas_call(
        kernel,
        out_shape=jax.ShapeDtypeStruct(shape, jnp.float32 if final else jnp.int16),
        in_specs=[smem] + [vmem] * (1 + len(received)),
        out_specs=vmem,
        compiler_params=pltpu.CompilerParams(vmem_limit_bytes=8 * 2**20),
        cost_estimate=pl.CostEstimate(
            flops=8 * size * width, bytes_accessed=12 * size * width, transcendentals=0
        ),
        name="output_sum" if final else "passed_sum",
    )(scalars[0], kept, *received)


def swapped(block, step):
    axis, bit = step
    return lax.ppermute(block, axis, [(i, i ^ bit) for i in range(lax.axis_size(axis))])


def gathered(block, steps):
    blocks = [block]
    for step in steps:
        blocks = blocks + [swapped(b, step) for b in blocks]
    return blocks


def scattered_sum(scalars, parts, steps):
    received = [[] for _ in parts]
    for s in reversed(range(len(steps))):
        half = 1 << s
        for m in reversed(range(half)):
            top = parts[half + m]
            if s + 1 < len(steps):
                top = combined(scalars, top, received[half + m], False)
            received[m].append(swapped(top, steps[s]))
    return combined(scalars, parts[0], received[0], True)


def bit_steps(axis):
    return [(axis, 1 << k) for k in range(int(math.log2(lax.axis_size(axis))))]


def owner_masks(steps):
    masks = [(0, 0)]
    for axis, bit in steps:
        masks = masks + [(b ^ bit, g) if axis == "blk" else (b, g ^ bit) for b, g in masks]
    return masks


def per_device(
    picture_vectors, caption_vectors, matching_caption, sharpness_parameter, additive_intercept
):
    scalars = (sharpness_parameter, additive_intercept)
    core, *grp_steps = bit_steps("grp")
    blk_steps = bit_steps("blk")
    every = grp_steps + blk_steps
    image_steps, text_steps = every[0::2], every[1::2]

    images = gathered(labelled(picture_vectors, matching_caption), image_steps)
    texts = gathered(caption_vectors, text_steps)
    image_masks = owner_masks(image_steps + [core])
    text_masks = owner_masks(text_steps + [core])

    def split(count):
        early = [m for m in range(count) if m <= count // 2]
        return early, [m for m in range(count) if m not in early]

    image_count, text_count = len(images), len(texts)
    early_images, late_images = split(image_count)
    early_texts, late_texts = split(text_count)
    other_images = {m: swapped(images[m], core) for m in early_images}
    other_texts = {m: swapped(texts[m], core) for m in early_texts}

    def picked(masks, chosen):
        return [masks[i] for i in chosen]

    def columns(chosen, count):
        return chosen + [count + m for m in chosen]

    text_before = early_sums(
        scalars,
        (picked(text_masks, early_texts), picked(image_masks, columns(early_images, image_count))),
        [texts[m] for m in early_texts],
        [images[m] for m in early_images] + [other_images[m] for m in early_images],
    )
    image_before = early_sums(
        scalars,
        (picked(image_masks, early_images), picked(text_masks, columns(early_texts, text_count))),
        [images[m] for m in early_images],
        [texts[m] for m in early_texts] + [other_texts[m] for m in early_texts],
    )
    images, texts, text_before, image_before = lax.optimization_barrier(
        (images, texts, text_before, image_before)
    )
    other_images |= {m: swapped(images[m], core) for m in late_images}
    other_texts |= {m: swapped(texts[m], core) for m in late_texts}
    text_parts = late_sums(
        scalars,
        (text_masks, image_masks),
        texts,
        images + [other_images[m] for m in range(image_count)],
        early_texts,
        columns(late_images, image_count),
        text_before,
        text_count // 2,
    )
    image_parts = late_sums(
        scalars,
        (image_masks, text_masks),
        images,
        texts + [other_texts[m] for m in range(text_count)],
        early_images,
        columns(late_texts, text_count),
        image_before,
        image_count // 2,
        text_parts[-1:],
    )
    picture_derivative = scattered_sum(scalars, image_parts, image_steps)
    text_grad = scattered_sum(scalars, text_parts, text_steps)
    return (picture_derivative, text_grad)


def solution(mesh):
    placed = (P(("blk", "grp"), None), P(("blk", "grp"), None), P(("blk", "grp")), P(), P())
    return jax.shard_map(
        per_device,
        mesh=mesh,
        in_specs=placed,
        out_specs=(P(("blk", "grp"), None), P(("blk", "grp"), None)),
        check_vma=False,
    )
```

```python
import math

import jax
import jax.numpy as jnp
from jax import lax
from jax.experimental import pallas as pl
from jax.experimental.pallas import tpu as pltpu
from jax.sharding import PartitionSpec as P

LOG2E = 1.4426950408889634
CODE_TOP = 32000.0
CODE_STEPS = 32.0
EXTRA_ROWS = 8
LABEL_BASE = 128
TILE = 256
LANES = 128
SMEM = pl.BlockSpec(memory_space=pltpu.SMEM)
VMEM = pl.BlockSpec(memory_space=pltpu.VMEM)
ANY = pl.BlockSpec(memory_space=pl.ANY)


def whole(array):
    return ((array, 0, 0),)


def part_widths(width):
    first = min(3 * TILE, width - LANES)
    return (first, width - first)


def column_tiles(width):
    tiles, begin = [], 0
    for p, w in enumerate(part_widths(width)):
        tiles += [(p, k, begin + k, min(TILE, w - k)) for k in range(0, w, TILE)]
        begin += w
    return tiles


def piece(block, rows, tile):
    p, inner, start, span = tile
    ref, row, column = block[0 if len(block) == 1 else p]
    first = start if len(block) == 1 else inner
    return ref.at[pl.ds(row + rows[0], rows[1]), pl.ds(column + first, span)]


class Operands:
    def __init__(self):
        self.pairs = []

    def add(self, array, spec):
        for i, (a, s) in enumerate(self.pairs):
            if a is array and s is spec:
                return i
        self.pairs.append((array, spec))
        return len(self.pairs) - 1

    def block(self, block):
        at = [(self.add(a, VMEM), row, column) for a, row, column in block]
        return lambda refs: tuple((refs[i], row, column) for i, row, column in at)


def scale_code(top):
    return jnp.ceil(jnp.log(jnp.maximum(top, 1e-30)) * (CODE_STEPS * LOG2E))


def encode(value, block, tile):
    size, span = value.shape
    code = scale_code(jnp.max(jnp.abs(value), axis=0, keepdims=True))
    gain = CODE_TOP * jnp.exp(code * (-1.0 / (CODE_STEPS * LOG2E)))
    piece(block, (0, size), tile)[...] = (
        jnp.round(value * gain).astype(jnp.int32).astype(jnp.int16)
    )
    scales = jnp.broadcast_to(code.astype(jnp.int32), (EXTRA_ROWS, span)).astype(jnp.int16)
    piece(block, (size, EXTRA_ROWS), tile)[...] = scales


def decoded(block, size, tile):
    code = piece(block, (size, EXTRA_ROWS), tile)[...].astype(jnp.int32).astype(jnp.float32)
    gain = jnp.exp(code[:1] * (1.0 / (CODE_STEPS * LOG2E))) * (1.0 / CODE_TOP)
    return piece(block, (0, size), tile)[...].astype(jnp.int32).astype(jnp.float32) * gain


def call(kernel, name, operands, out_shape, scratch, room, cost, after=(), held_back=()):
    arrays = [a for a, _ in operands]
    held = sum(math.prod(a.shape) * a.dtype.itemsize for a in [*arrays, *out_shape])

    def body(*refs):
        results = refs[len(arrays) + len(after) + len(held_back) :]
        kernel(refs[: len(arrays)], results[: len(out_shape)] + results[len(out_shape) + len(held_back) :])

    return pl.pallas_call(
        body,
        out_shape=[*out_shape, *(jax.ShapeDtypeStruct(a.shape, a.dtype) for a in held_back)],
        in_specs=[s for _, s in operands] + [ANY] * (len(after) + len(held_back)),
        out_specs=[VMEM] * len(out_shape) + [ANY] * len(held_back),
        input_output_aliases={
            len(arrays) + len(after) + i: len(out_shape) + i for i in range(len(held_back))
        },
        scratch_shapes=scratch,
        compiler_params=pltpu.CompilerParams(vmem_limit_bytes=held + room),
        cost_estimate=pl.CostEstimate(flops=cost, bytes_accessed=cost, transcendentals=0),
        name=name,
    )(*arrays, *after, *held_back)


def labelled(images, labels):
    size, width = images.shape

    def kernel(ins, outs):
        (out,) = outs
        row = ins[1][...]
        low, high = lax.rem(row, LABEL_BASE), lax.div(row, LABEL_BASE)
        at = lax.broadcasted_iota(jnp.int32, (EXTRA_ROWS, size), 0)
        parts = jnp.where(at == 0, high, jnp.where(at == 1, low, 0)).astype(jnp.float32)
        out[pl.ds(0, size), :] = ins[0][...]
        out[pl.ds(size, EXTRA_ROWS), :] = jnp.zeros((EXTRA_ROWS, width), jnp.bfloat16)
        out[pl.ds(size, EXTRA_ROWS), pl.ds(0, size)] = parts.astype(jnp.bfloat16)

    shape = jax.ShapeDtypeStruct((size + EXTRA_ROWS, width), jnp.bfloat16)
    operands = [(images, VMEM), (labels[None, :], VMEM)]
    return call(kernel, "labelled", operands, [shape], [], 2**21, size)[0]


def bundled(texts, images):
    size, width = texts[0][0].shape[0], texts[0][0].shape[1]
    operands = Operands()
    views = [operands.block(texts), operands.block(images)]

    def kernel(ins, outs):
        for view, first, count in zip(views, (0, size), (size, size + EXTRA_ROWS)):
            ((ref, row, column),) = view(ins)
            outs[0][pl.ds(first, count), :] = ref[pl.ds(row, count), pl.ds(column, width)]

    shape = jax.ShapeDtypeStruct((2 * size + EXTRA_ROWS, width), jnp.bfloat16)
    (both,) = call(kernel, "bundled", operands.pairs, [shape], [], 2**21, size)
    return both


def first_row(mask, size):
    owner = (lax.axis_index("blk") ^ mask[0]) * lax.axis_size("grp") + (lax.axis_index("grp") ^ mask[1])
    return owner * size


def keys_of(block, size, mask, is_image):
    if not is_image:
        ids = lax.broadcasted_iota(jnp.int32, (1, size), 1) + first_row(mask, size)
        return ids.astype(jnp.float32)
    parts = piece(block, (size, EXTRA_ROWS), (0, 0, 0, size))[...].astype(jnp.float32)
    return parts[0:1] * LABEL_BASE + parts[1:2]


def gradient_sums(name, size, scalars, x_blocks, y_blocks, masks, x_images, jobs, before, emits, after=()):
    width = x_blocks[0][0][0].shape[1]
    x_masks, y_masks = masks
    per_tile = TILE // size
    widths = part_widths(width)
    shapes, where = [], {}

    def result(extra, w, dtype):
        shapes.append(jax.ShapeDtypeStruct((size + extra, w), dtype))
        return len(shapes) - 1

    for r, kind in enumerate(emits):
        if kind == "float":
            where[r] = [(result(0, width, jnp.float32), 0, 0)]
        else:
            cut = widths if kind == "parts" else (width,)
            where[r] = [(result(EXTRA_ROWS, w, jnp.int16), 0, 0) for w in cut]
    operands = Operands()
    slope_at, shift_at = [operands.add(s, SMEM) for s in scalars]
    x_views = [operands.block(b) for b in x_blocks]
    y_views = [operands.block(b) for b in y_blocks]
    before_at = {r: operands.add(b, VMEM) for r, b in before.items()}

    def kernel(ins, refs):
        outs, weights = refs[:-1], refs[-1]
        slope, shift = ins[slope_at][0] * LOG2E, ins[shift_at][0] * LOG2E
        x_refs, y_refs = [v(ins) for v in x_views], [v(ins) for v in y_views]

        def stacked(chosen):
            return jnp.concatenate(
                [ref[pl.ds(row, size), pl.ds(column, width)] for ((ref, row, column),) in chosen],
                axis=0,
            )

        for rows, columns in jobs:
            x_all = stacked([x_refs[r] for r in rows])
            keys = [
                jnp.broadcast_to(keys_of(x_refs[r], size, x_masks[r], x_images), (size, size)).T
                for r in rows
            ]
            for n in range(0, len(columns), per_tile):
                chosen = columns[n : n + per_tile]
                other = jnp.concatenate(
                    [keys_of(y_refs[c], size, y_masks[c], not x_images) for c in chosen], axis=1
                )
                scores = lax.dot_general(
                    x_all,
                    stacked([y_refs[c] for c in chosen]),
                    (((1,), (1,)), ((), ())),
                    preferred_element_type=jnp.float32,
                )
                for i in range(len(rows)):
                    z = scores[i * size : (i + 1) * size] * slope + shift
                    sig = 1.0 / (1.0 + jnp.exp2(-z))
                    w = jnp.where(jnp.tile(keys[i], (1, per_tile)) == other, sig - 1.0, sig)
                    weights[pl.ds(i * size, size), pl.ds(n * size, TILE)] = w.astype(jnp.bfloat16)
            for tile in column_tiles(width):
                sums = jnp.dot(
                    weights[pl.ds(0, len(rows) * size), pl.ds(0, len(columns) * size)],
                    jnp.concatenate([piece(y_refs[c], (0, size), tile)[...] for c in columns], axis=0),
                    preferred_element_type=jnp.float32,
                )
                for i, r in enumerate(rows):
                    block = sums[i * size : (i + 1) * size]
                    if r in before_at:
                        block = block + piece(whole(ins[before_at[r]]), (0, size), tile)[...]
                    out = tuple((outs[o], row, column) for o, row, column in where[r])
                    if emits[r] == "float":
                        piece(out, (0, size), tile)[...] = block
                    else:
                        encode(block, out, tile)

    pairs = sum(len(rows) * len(columns) for rows, columns in jobs)
    scratch = [pltpu.VMEM((len(x_blocks) * size, len(y_blocks) * size), jnp.bfloat16)]
    room = len(x_blocks) * len(y_blocks) * size * size * 2 + 8 * 2**20
    results = call(kernel, name, operands.pairs, shapes, scratch, room, pairs * size, after)
    return [tuple(results[o] for o, _, _ in where[r]) for r in range(len(emits))]


def passed_sum(kept, received, part, held_back=()):
    size, width = kept.shape
    operands = Operands()
    kept_at = operands.add(kept, VMEM)
    views = [operands.block(b if part is None or len(b) == 1 else (b[part],) * 2) for b in received]

    def kernel(ins, outs):
        for tile in column_tiles(width):
            p, inner, _, span = tile
            if part is None or p == part:
                total = piece(whole(ins[kept_at]), (0, size), tile)[...]
                for view in views:
                    total = total + decoded(view(ins), size, tile)
                encode(total, whole(outs[0]), tile if part is None else (0, 0, inner, span))

    cut = width if part is None else part_widths(width)[part]
    shape = jax.ShapeDtypeStruct((size + EXTRA_ROWS, cut), jnp.int16)
    return call(kernel, "passed_sum", operands.pairs, [shape], [], 2**21, size, (), held_back)


def output_sum(sharpness, kept, received):
    size, width = kept.shape
    operands = Operands()
    sharpness_at = operands.add(sharpness, SMEM)
    kept_at = operands.add(kept, VMEM)
    views = [operands.block(b) for b in received]

    def kernel(ins, outs):
        for tile in column_tiles(width):
            total = piece(whole(ins[kept_at]), (0, size), tile)[...]
            for view in views:
                total = total + decoded(view(ins), size, tile)
            piece(whole(outs[0]), (0, size), tile)[...] = total * ins[sharpness_at][0]

    shape = jax.ShapeDtypeStruct((size, width), jnp.float32)
    return call(kernel, "output_sum", operands.pairs, [shape], [], 2**21, size)[0]


def swapped(array, step):
    axis, bit = step
    return lax.ppermute(array, axis, [(i, i ^ bit) for i in range(lax.axis_size(axis))])


def gathered(own, steps):
    arrays = [own]
    for step in steps:
        arrays = arrays + [swapped(a, step) for a in arrays]
    return [whole(a) for a in arrays]


def other_core(texts, images, core):
    both = swapped(bundled(texts, images), core)
    return ((both, 0, 0),), ((both, texts[0][0].shape[0], 0),)


def scattered_sum(sharpness, kept, coded, steps):
    def sent(block, step):
        return [(swapped(p, step), 0, 0) for p in block]

    last = steps[-1]
    if len(coded[-1]) == 1:
        received = [[sent(c, last)] for c in coded]
        begun = None
    else:
        received = [[None]] + [[sent(c[:1], last)] for c in coded[1:]]
        n = len(kept) - 1
        begun, *rest = passed_sum(
            kept[n], received[n], 0, [c[-1] for c in coded[1:]] + [coded[0][0]]
        )
        for r, c in zip(received[1:] + received[:1], rest):
            if r is received[0]:
                r[0] = sent([c], last)
            else:
                r[0] = r[0] + sent([c], last)
    for s in reversed(range(len(steps) - 1)):
        for m in reversed(range(1 << s)):
            n = m | 1 << s
            parts = range(2) if len(received[n][0]) == 2 else [None]
            passed = []
            for p in parts:
                if begun is not None:
                    passed.append(begun)
                    begun = None
                else:
                    passed += passed_sum(kept[n], received[n], p)
            received[m].append(sent(passed, steps[s]))
    return output_sum(sharpness, kept[0], received[0])


def bit_steps(axis):
    return [(axis, 1 << k) for k in range(int(math.log2(lax.axis_size(axis))))]


def owner_masks(steps):
    masks = [(0, 0)]
    for axis, bit in steps:
        masks = masks + [(b ^ bit, g) if axis == "blk" else (b, g ^ bit) for b, g in masks]
    return masks


def per_device(
    picture_vectors, caption_vectors, matching_caption, sharpness_parameter, additive_intercept
):
    scalars = (sharpness_parameter, additive_intercept)
    size = picture_vectors.shape[0]
    core, *grp_steps = bit_steps("grp")
    every = grp_steps + bit_steps("blk")
    steps = [every[0::2], every[1::2]]
    assert len(steps[0]) == len(steps[1]) >= 2
    masks = [owner_masks(s + [core]) for s in steps]
    count = 1 << len(steps[0])
    half = count // 2
    early, late = list(range(half + 1)), list(range(half + 1, count))
    own = [labelled(picture_vectors, matching_caption), caption_vectors]
    blocks = [gathered(o, s) for o, s in zip(own, steps)]
    others = [{}, {}]
    for m in early:
        others[1][m], others[0][m] = other_core(blocks[1][m], blocks[0][m], core)

    def sums(name, kind, rows, columns, jobs, before, emits, after=()):
        other = 1 - kind
        x_blocks = [blocks[kind][m] for m in rows]
        y_blocks = [blocks[other][m] for m in columns] + [others[other][m] for m in columns]
        x_masks = [masks[kind][m] for m in rows]
        y_masks = [masks[other][m + shift] for shift in (0, count) for m in columns]
        return gradient_sums(
            name,
            size,
            scalars,
            x_blocks,
            y_blocks,
            (x_masks, y_masks),
            kind == 0,
            jobs,
            before,
            emits,
            after,
        )

    before = []
    for k in range(2):
        jobs = [(early, list(range(2 * len(early))))]
        results = sums("early_sums", k, early, early, jobs, {}, ["float"] * len(early))
        before.append([s for (s,) in results])
    arrays = [[b[m][0][0] for m in late] for b in blocks]
    arrays, before = lax.optimization_barrier((arrays, before))
    for k in range(2):
        for m, a in zip(late, arrays[k]):
            blocks[k][m] = whole(a)
            others[k][m] = whole(swapped(a, core))
    every = list(range(count))
    jobs = [(late, every + [count + m for m in every]), (early, late + [count + m for m in late])]
    coded, kept, after = [None, None], [None, None], ()
    for k, cut in ((1, "whole"), (0, "whole")):
        emits = ["float"] * half + ["whole"] + [cut] * len(late)
        results = sums(
            "late_sums", k, every, every, jobs, dict(zip(early, before[k])), emits, after
        )
        kept[k] = [s for (s,) in results[:half]]
        coded[k] = results[half:]
        after = coded[k][0]
    return tuple(scattered_sum(scalars[0], kept[k], coded[k], steps[k]) for k in range(2))


def solution(mesh):
    placed = (P(("blk", "grp"), None), P(("blk", "grp"), None), P(("blk", "grp")), P(), P())
    return jax.shard_map(
        per_device,
        mesh=mesh,
        in_specs=placed,
        out_specs=(P(("blk", "grp"), None), P(("blk", "grp"), None)),
        check_vma=False,
    )
```

```python
import math

import jax
import jax.numpy as jnp
from jax import lax
from jax.experimental import pallas as pl
from jax.experimental.pallas import tpu as pltpu
from jax.sharding import PartitionSpec as P

LOG2E = 1.4426950408889634
CODE_TOP = 32000.0
CODE_STEPS = 32.0
EXTRA_ROWS = 8
LABEL_BASE = 128
TILE = 256
LANES = 128
VMEM_BYTES = 2**26
SMEM = pl.BlockSpec(memory_space=pltpu.SMEM)
VMEM = pl.BlockSpec(memory_space=pltpu.VMEM)
ANY = pl.BlockSpec(memory_space=pl.ANY)
HBM = pl.BlockSpec(memory_space=pltpu.HBM)


def whole(array):
    return ((array, 0, 0),)


def part_widths(width):
    first = min(3 * TILE, width - LANES)
    return (first, width - first)


def column_tiles(width):
    tiles, begin = [], 0
    for p, w in enumerate(part_widths(width)):
        tiles += [(p, k, begin + k, min(TILE, w - k)) for k in range(0, w, TILE)]
        begin += w
    return tiles


def piece(block, rows, tile):
    p, inner, start, span = tile
    ref, row, column = block[0 if len(block) == 1 else p]
    first = start if len(block) == 1 else inner
    return ref.at[pl.ds(row + rows[0], rows[1]), pl.ds(column + first, span)]


class Operands:
    def __init__(self):
        self.pairs = []

    def add(self, array, spec):
        for i, (a, s) in enumerate(self.pairs):
            if a is array and s is spec:
                return i
        self.pairs.append((array, spec))
        return len(self.pairs) - 1

    def block(self, block):
        at = [(self.add(a, VMEM), row, column) for a, row, column in block]
        return lambda refs: tuple((refs[i], row, column) for i, row, column in at)


def scale_code(top):
    return jnp.ceil(jnp.log(jnp.maximum(top, 1e-30)) * (CODE_STEPS * LOG2E))


def encode(value, block, tile):
    size, span = value.shape
    code = scale_code(jnp.max(jnp.abs(value), axis=0, keepdims=True))
    gain = CODE_TOP * jnp.exp(code * (-1.0 / (CODE_STEPS * LOG2E)))
    piece(block, (0, size), tile)[...] = (
        jnp.round(value * gain).astype(jnp.int32).astype(jnp.int16)
    )
    scales = jnp.broadcast_to(code.astype(jnp.int32), (EXTRA_ROWS, span)).astype(jnp.int16)
    piece(block, (size, EXTRA_ROWS), tile)[...] = scales


def decoded(block, size, tile):
    code = piece(block, (size, EXTRA_ROWS), tile)[...].astype(jnp.int32).astype(jnp.float32)
    gain = jnp.exp(code[:1] * (1.0 / (CODE_STEPS * LOG2E))) * (1.0 / CODE_TOP)
    return piece(block, (0, size), tile)[...].astype(jnp.int32).astype(jnp.float32) * gain


def call(kernel, name, operands, out_shape, scratch, room, cost, after=(), held_back=(), limit=None):
    arrays = [a for a, _ in operands]
    held = sum(math.prod(a.shape) * a.dtype.itemsize for a in [*arrays, *out_shape])

    def body(*refs):
        results = refs[len(arrays) + len(after) + len(held_back) :]
        kernel(refs[: len(arrays)], results[: len(out_shape)] + results[len(out_shape) + len(held_back) :])

    return pl.pallas_call(
        body,
        out_shape=[*out_shape, *(jax.ShapeDtypeStruct(a.shape, a.dtype) for a in held_back)],
        in_specs=[s for _, s in operands] + [ANY] * (len(after) + len(held_back)),
        out_specs=[VMEM] * len(out_shape) + [ANY] * len(held_back),
        input_output_aliases={
            len(arrays) + len(after) + i: len(out_shape) + i for i in range(len(held_back))
        },
        scratch_shapes=scratch,
        compiler_params=pltpu.CompilerParams(vmem_limit_bytes=limit or held + room),
        cost_estimate=pl.CostEstimate(flops=cost, bytes_accessed=cost, transcendentals=0),
        name=name,
    )(*arrays, *after, *held_back)


def staged(images, texts, labels):
    size, width = images.shape

    def kernel(ins, refs):
        *outs, row, sems = refs
        copies = [pltpu.make_async_copy(ins[2], row, sems.at[4])]
        for k, (source, out, first) in enumerate(((1, 0, 0), (0, 1, 0), (1, 2, 0), (0, 2, size))):
            target = outs[out].at[pl.ds(first, size)]
            copies.append(pltpu.make_async_copy(ins[source], target, sems.at[k]))
        for c in copies:
            c.start()
        copies[0].wait()
        low, high = lax.rem(row[...], LABEL_BASE), lax.div(row[...], LABEL_BASE)
        at = lax.broadcasted_iota(jnp.int32, (EXTRA_ROWS, size), 0)
        parts = jnp.where(at == 0, high, jnp.where(at == 1, low, 0)).astype(jnp.float32)
        for out, first in ((outs[1], size), (outs[2], 2 * size)):
            rows = pl.ds(first, EXTRA_ROWS)
            out[rows, :] = jnp.zeros((EXTRA_ROWS, width), jnp.bfloat16)
            out[rows, pl.ds(0, size)] = parts.astype(jnp.bfloat16)
        for c in copies[1:]:
            c.wait()

    shapes = [
        jax.ShapeDtypeStruct((n, width), jnp.bfloat16)
        for n in (size, size + EXTRA_ROWS, 2 * size + EXTRA_ROWS)
    ]
    scratch = [pltpu.VMEM((1, size), jnp.int32), pltpu.SemaphoreType.DMA((5,))]
    operands = [(images, HBM), (texts, HBM), (labels[None, :], HBM)]
    room = VMEM_BYTES - sum(2 * math.prod(o.shape) for o in shapes) - 2**17
    return call(kernel, "staged", operands, shapes, scratch, room, size, limit=room)


def bundled(texts, images):
    size, width = texts[0][0].shape[0], texts[0][0].shape[1]
    operands = Operands()
    views = [operands.block(texts), operands.block(images)]

    def kernel(ins, outs):
        for view, first, count in zip(views, (0, size), (size, size + EXTRA_ROWS)):
            ((ref, row, column),) = view(ins)
            outs[0][pl.ds(first, count), :] = ref[pl.ds(row, count), pl.ds(column, width)]

    shape = jax.ShapeDtypeStruct((2 * size + EXTRA_ROWS, width), jnp.bfloat16)
    (both,) = call(kernel, "bundled", operands.pairs, [shape], [], 2**21, size)
    return both


def first_row(mask, size):
    owner = (lax.axis_index("blk") ^ mask[0]) * lax.axis_size("grp") + (lax.axis_index("grp") ^ mask[1])
    return owner * size


def keys_of(block, size, mask, is_image):
    if not is_image:
        ids = lax.broadcasted_iota(jnp.int32, (1, size), 1) + first_row(mask, size)
        return ids.astype(jnp.float32)
    parts = piece(block, (size, EXTRA_ROWS), (0, 0, 0, size))[...].astype(jnp.float32)
    return parts[0:1] * LABEL_BASE + parts[1:2]


def gradient_sums(name, size, scalars, x_blocks, y_blocks, masks, x_images, jobs, before, emits, sequence, after=()):
    width = x_blocks[0][0][0].shape[1]
    x_masks, y_masks = masks
    per_tile = TILE // size
    widths = part_widths(width)
    shapes, where = [], {}

    def result(extra, w, dtype):
        shapes.append(jax.ShapeDtypeStruct((size + extra, w), dtype))
        return len(shapes) - 1

    for r, kind in enumerate(emits):
        if kind == "float":
            where[r] = [(result(0, width, jnp.float32), 0, 0)]
        else:
            cut = widths if kind == "parts" else (width,)
            where[r] = [(result(EXTRA_ROWS, w, jnp.int16), 0, 0) for w in cut]
    operands = Operands()
    slope_at, shift_at = [operands.add(s, SMEM) for s in scalars]
    for b in sequence:
        operands.block(b)
    x_views = [operands.block(b) for b in x_blocks]
    y_views = [operands.block(b) for b in y_blocks]
    before_at = {r: operands.add(b, VMEM) for r, b in before.items()}

    def kernel(ins, refs):
        outs, weights = refs[:-1], refs[-1]
        slope, shift = ins[slope_at][0] * LOG2E, ins[shift_at][0] * LOG2E
        x_refs, y_refs = [v(ins) for v in x_views], [v(ins) for v in y_views]

        def stacked(chosen):
            return jnp.concatenate(
                [ref[pl.ds(row, size), pl.ds(column, width)] for ((ref, row, column),) in chosen],
                axis=0,
            )

        for rows, columns in jobs:
            x_all = stacked([x_refs[r] for r in rows])
            keys = [
                jnp.broadcast_to(keys_of(x_refs[r], size, x_masks[r], x_images), (size, size)).T
                for r in rows
            ]
            for n in range(0, len(columns), per_tile):
                chosen = columns[n : n + per_tile]
                other = jnp.concatenate(
                    [keys_of(y_refs[c], size, y_masks[c], not x_images) for c in chosen], axis=1
                )
                scores = lax.dot_general(
                    x_all,
                    stacked([y_refs[c] for c in chosen]),
                    (((1,), (1,)), ((), ())),
                    preferred_element_type=jnp.float32,
                )
                for i in range(len(rows)):
                    z = scores[i * size : (i + 1) * size] * slope + shift
                    sig = 1.0 / (1.0 + jnp.exp2(-z))
                    w = jnp.where(jnp.tile(keys[i], (1, per_tile)) == other, sig - 1.0, sig)
                    weights[pl.ds(i * size, size), pl.ds(n * size, TILE)] = w.astype(jnp.bfloat16)
            for tile in column_tiles(width):
                sums = jnp.dot(
                    weights[pl.ds(0, len(rows) * size), pl.ds(0, len(columns) * size)],
                    jnp.concatenate([piece(y_refs[c], (0, size), tile)[...] for c in columns], axis=0),
                    preferred_element_type=jnp.float32,
                )
                for i, r in enumerate(rows):
                    block = sums[i * size : (i + 1) * size]
                    if r in before_at:
                        block = block + piece(whole(ins[before_at[r]]), (0, size), tile)[...]
                    out = tuple((outs[o], row, column) for o, row, column in where[r])
                    if emits[r] == "float":
                        piece(out, (0, size), tile)[...] = block
                    else:
                        encode(block, out, tile)

    pairs = sum(len(rows) * len(columns) for rows, columns in jobs)
    scratch = [pltpu.VMEM((len(x_blocks) * size, len(y_blocks) * size), jnp.bfloat16)]
    room = len(x_blocks) * len(y_blocks) * size * size * 2 + 8 * 2**20
    results = call(kernel, name, operands.pairs, shapes, scratch, room, pairs * size, after)
    return [tuple(results[o] for o, _, _ in where[r]) for r in range(len(emits))]


def passed_sum(kept, received, part, held_back=()):
    size, width = kept.shape
    operands = Operands()
    kept_at = operands.add(kept, VMEM)
    views = [operands.block(b if part is None or len(b) == 1 else (b[part],) * 2) for b in received]

    def kernel(ins, outs):
        for tile in column_tiles(width):
            p, inner, _, span = tile
            if part is None or p == part:
                total = piece(whole(ins[kept_at]), (0, size), tile)[...]
                for view in views:
                    total = total + decoded(view(ins), size, tile)
                encode(total, whole(outs[0]), tile if part is None else (0, 0, inner, span))

    cut = width if part is None else part_widths(width)[part]
    shape = jax.ShapeDtypeStruct((size + EXTRA_ROWS, cut), jnp.int16)
    return call(kernel, "passed_sum", operands.pairs, [shape], [], 2**21, size, (), held_back)


def output_sum(sharpness, kept, received):
    size, width = kept.shape
    operands = Operands()
    sharpness_at = operands.add(sharpness, SMEM)
    kept_at = operands.add(kept, VMEM)
    views = [operands.block(b) for b in received]

    def kernel(ins, outs):
        for tile in column_tiles(width):
            total = piece(whole(ins[kept_at]), (0, size), tile)[...]
            for view in views:
                total = total + decoded(view(ins), size, tile)
            piece(whole(outs[0]), (0, size), tile)[...] = total * ins[sharpness_at][0]

    shape = jax.ShapeDtypeStruct((size, width), jnp.float32)
    return call(kernel, "output_sum", operands.pairs, [shape], [], 2**21, size)[0]


def swapped(array, step):
    axis, bit = step
    return lax.ppermute(array, axis, [(i, i ^ bit) for i in range(lax.axis_size(axis))])


def scattered_sum(sharpness, kept, coded, steps):
    def sent(block, step):
        return [(swapped(p, step), 0, 0) for p in block]

    last = steps[-1]
    if len(coded[-1]) == 1:
        received = [[sent(c, last)] for c in coded]
        begun = None
    else:
        received = [[None]] + [[sent(c[:1], last)] for c in coded[1:]]
        n = len(kept) - 1
        begun, *rest = passed_sum(
            kept[n], received[n], 0, [c[-1] for c in coded[1:]] + [coded[0][0]]
        )
        for r, c in zip(received[1:] + received[:1], rest):
            if r is received[0]:
                r[0] = sent([c], last)
            else:
                r[0] = r[0] + sent([c], last)
    for s in reversed(range(len(steps) - 1)):
        for m in reversed(range(1 << s)):
            n = m | 1 << s
            parts = range(2) if len(received[n][0]) == 2 else [None]
            passed = []
            for p in parts:
                if begun is not None:
                    passed.append(begun)
                    begun = None
                else:
                    passed += passed_sum(kept[n], received[n], p)
            received[m].append(sent(passed, steps[s]))
    return output_sum(sharpness, kept[0], received[0])


def bit_steps(axis):
    return [(axis, 1 << k) for k in range(int(math.log2(lax.axis_size(axis))))]


def owner_masks(steps):
    masks = [(0, 0)]
    for axis, bit in steps:
        masks = masks + [(b ^ bit, g) if axis == "blk" else (b, g ^ bit) for b, g in masks]
    return masks


def per_device(
    picture_vectors, caption_vectors, matching_caption, sharpness_parameter, additive_intercept
):
    scalars = (sharpness_parameter, additive_intercept)
    size = picture_vectors.shape[0]
    core, *grp_steps = bit_steps("grp")
    every = grp_steps + bit_steps("blk")
    steps = [every[0::2], every[1::2]]
    assert len(steps[0]) == len(steps[1]) >= 2
    masks = [owner_masks(s + [core]) for s in steps]
    count = 1 << len(steps[0])
    half = count // 2
    early, late = list(range(half + 1)), list(range(half + 1, count))
    own_texts, own_images, own_both = staged(picture_vectors, caption_vectors, matching_caption)
    arrays = [{0: own_images}, {0: own_texts}]
    for i in range(len(steps[0])):
        for k in (1, 0):
            arrays[k][1 << i] = swapped(arrays[k][0], steps[k][i])
    others = [{}, {}]

    def swap_cores(m, both):
        both = swapped(both, core)
        others[1][m], others[0][m] = whole(both), ((both, size, 0),)

    swap_cores(0, own_both)
    for i in range(1, len(steps[0])):
        for m in range(1, 1 << i):
            for k in (1, 0):
                arrays[k][m | 1 << i] = swapped(arrays[k][m], steps[k][i])
    blocks = [[whole(a[m]) for m in range(count)] for a in arrays]
    for m in early[1:]:
        swap_cores(m, bundled(blocks[1][m], blocks[0][m]))

    def sums(name, kind, rows, columns, jobs, before, emits, after=()):
        other = 1 - kind
        x_blocks = [blocks[kind][m] for m in rows]
        y_blocks = [blocks[other][m] for m in columns] + [others[other][m] for m in columns]
        x_masks = [masks[kind][m] for m in rows]
        y_masks = [masks[other][m + shift] for shift in (0, count) for m in columns]
        return gradient_sums(
            name,
            size,
            scalars,
            x_blocks,
            y_blocks,
            (x_masks, y_masks),
            kind == 0,
            jobs,
            before,
            emits,
            [blocks[k][m] for m in rows[1:] + rows[:1] for k in (1, 0)],
            after,
        )

    before = []
    for k in range(2):
        jobs = [(early, list(range(2 * len(early))))]
        results = sums("early_sums", k, early, early, jobs, {}, ["float"] * len(early))
        before.append([s for (s,) in results])
    arrays = [[b[m][0][0] for m in late] for b in blocks[::-1]]
    arrays, before = lax.optimization_barrier((arrays, before))
    for k in (1, 0):
        for m, a in zip(late, arrays[1 - k]):
            blocks[k][m] = whole(a)
            others[k][m] = whole(swapped(a, core))
    every = list(range(count))
    jobs = [(late, every + [count + m for m in every]), (early, late + [count + m for m in late])]
    coded, kept, after = [None, None], [None, None], ()
    for k, cut in ((1, "whole"), (0, "whole")):
        emits = ["float"] * half + ["whole"] + [cut] * len(late)
        results = sums(
            "late_sums", k, every, every, jobs, dict(zip(early, before[k])), emits, after
        )
        kept[k] = [s for (s,) in results[:half]]
        coded[k] = results[half:]
        after = coded[k][0]
    return tuple(scattered_sum(scalars[0], kept[k], coded[k], steps[k]) for k in range(2))


def solution(mesh):
    placed = (P(("blk", "grp"), None), P(("blk", "grp"), None), P(("blk", "grp")), P(), P())
    return jax.shard_map(
        per_device,
        mesh=mesh,
        in_specs=placed,
        out_specs=(P(("blk", "grp"), None), P(("blk", "grp"), None)),
        check_vma=False,
    )
```

```python
import math

import jax
import jax.numpy as jnp
from jax import lax
from jax.experimental import pallas as pl
from jax.experimental.pallas import tpu as pltpu
from jax.sharding import PartitionSpec as P

LOG2E = 1.4426950408889634
CODE_TOP = 32000.0
CODE_STEPS = 32.0
EXTRA_ROWS = 8
LABEL_BASE = 128
TILE = 256
LANES = 128
BUNDLE_COST = 6 * 10**8
SMEM = pl.BlockSpec(memory_space=pltpu.SMEM)
VMEM = pl.BlockSpec(memory_space=pltpu.VMEM)
ANY = pl.BlockSpec(memory_space=pl.ANY)


def whole(array):
    return ((array, 0, 0),)


def part_widths(width):
    first = min(3 * TILE, width - LANES)
    return (first, width - first)


def column_tiles(width):
    tiles, begin = [], 0
    for p, w in enumerate(part_widths(width)):
        tiles += [(p, k, begin + k, min(TILE, w - k)) for k in range(0, w, TILE)]
        begin += w
    return tiles


def piece(block, rows, tile):
    p, inner, start, span = tile
    ref, row, column = block[0 if len(block) == 1 else p]
    first = start if len(block) == 1 else inner
    return ref.at[pl.ds(row + rows[0], rows[1]), pl.ds(column + first, span)]


class Operands:
    def __init__(self):
        self.pairs = []

    def add(self, array, spec):
        for i, (a, s) in enumerate(self.pairs):
            if a is array and s is spec:
                return i
        self.pairs.append((array, spec))
        return len(self.pairs) - 1

    def block(self, block):
        at = [(self.add(a, VMEM), row, column) for a, row, column in block]
        return lambda refs: tuple((refs[i], row, column) for i, row, column in at)


def scale_code(top):
    return jnp.ceil(jnp.log(jnp.maximum(top, 1e-30)) * (CODE_STEPS * LOG2E))


def encode(value, block, tile):
    size, span = value.shape
    code = scale_code(jnp.max(jnp.abs(value), axis=0, keepdims=True))
    gain = CODE_TOP * jnp.exp(code * (-1.0 / (CODE_STEPS * LOG2E)))
    piece(block, (0, size), tile)[...] = (
        jnp.round(value * gain).astype(jnp.int32).astype(jnp.int16)
    )
    scales = jnp.broadcast_to(code.astype(jnp.int32), (EXTRA_ROWS, span)).astype(jnp.int16)
    piece(block, (size, EXTRA_ROWS), tile)[...] = scales


def decoded(block, size, tile):
    code = piece(block, (size, EXTRA_ROWS), tile)[...].astype(jnp.int32).astype(jnp.float32)
    gain = jnp.exp(code[:1] * (1.0 / (CODE_STEPS * LOG2E))) * (1.0 / CODE_TOP)
    return piece(block, (0, size), tile)[...].astype(jnp.int32).astype(jnp.float32) * gain


def call(kernel, name, operands, out_shape, scratch, room, cost, after=(), held_back=()):
    arrays = [a for a, _ in operands]
    held = sum(math.prod(a.shape) * a.dtype.itemsize for a in [*arrays, *out_shape])

    def body(*refs):
        results = refs[len(arrays) + len(after) + len(held_back) :]
        kernel(refs[: len(arrays)], results[: len(out_shape)] + results[len(out_shape) + len(held_back) :])

    return pl.pallas_call(
        body,
        out_shape=[*out_shape, *(jax.ShapeDtypeStruct(a.shape, a.dtype) for a in held_back)],
        in_specs=[s for _, s in operands] + [ANY] * (len(after) + len(held_back)),
        out_specs=[VMEM] * len(out_shape) + [ANY] * len(held_back),
        input_output_aliases={
            len(arrays) + len(after) + i: len(out_shape) + i for i in range(len(held_back))
        },
        scratch_shapes=scratch,
        compiler_params=pltpu.CompilerParams(vmem_limit_bytes=held + room),
        cost_estimate=pl.CostEstimate(flops=cost, bytes_accessed=cost, transcendentals=0),
        name=name,
    )(*arrays, *after, *held_back)


def labelled(images, labels, after=()):
    size, width = images.shape

    def kernel(ins, outs):
        outs[0][pl.ds(0, size), :] = ins[0][...]
        outs[0][pl.ds(size, EXTRA_ROWS), :] = jnp.zeros((EXTRA_ROWS, width), jnp.bfloat16)
        row = ins[1][...]
        low, high = lax.rem(row, LABEL_BASE), lax.div(row, LABEL_BASE)
        at = lax.broadcasted_iota(jnp.int32, (EXTRA_ROWS, size), 0)
        parts = jnp.where(at == 0, high, jnp.where(at == 1, low, 0)).astype(jnp.float32)
        outs[0][pl.ds(size, EXTRA_ROWS), pl.ds(0, size)] = parts.astype(jnp.bfloat16)

    shape = jax.ShapeDtypeStruct((size + EXTRA_ROWS, width), jnp.bfloat16)
    operands = [(images, VMEM), (labels, VMEM)]
    return call(kernel, "labelled", operands, [shape], [], 2**21, size, after)[0]


def bundled(texts, images, cost, after=()):
    arrays = (texts, images)
    width = arrays[0].shape[1]

    def kernel(ins, outs):
        first = 0
        for ref in ins:
            outs[0][pl.ds(first, ref.shape[0]), :] = ref[...]
            first += ref.shape[0]

    shape = jax.ShapeDtypeStruct((sum(a.shape[0] for a in arrays), width), jnp.bfloat16)
    operands = [(a, VMEM) for a in arrays]
    return call(kernel, "bundled", operands, [shape], [], 2**21, cost, after)[0]


def first_row(mask, size):
    owner = (lax.axis_index("blk") ^ mask[0]) * lax.axis_size("grp") + (lax.axis_index("grp") ^ mask[1])
    return owner * size


def keys_of(block, size, mask, is_image):
    if not is_image:
        ids = lax.broadcasted_iota(jnp.int32, (1, size), 1) + first_row(mask, size)
        return ids.astype(jnp.float32)
    parts = piece(block, (size, EXTRA_ROWS), (0, 0, 0, size))[...].astype(jnp.float32)
    return parts[0:1] * LABEL_BASE + parts[1:2]


def gradient_sums(name, size, scalars, x_blocks, y_blocks, masks, x_images, jobs, before, emits, sequence, after=()):
    width = x_blocks[0][0][0].shape[1]
    x_masks, y_masks = masks
    per_tile = TILE // size
    widths = part_widths(width)
    shapes, where = [], {}

    def result(extra, w, dtype):
        shapes.append(jax.ShapeDtypeStruct((size + extra, w), dtype))
        return len(shapes) - 1

    for r, kind in enumerate(emits):
        if kind == "float":
            where[r] = [(result(0, width, jnp.float32), 0, 0)]
        else:
            cut = widths if kind == "parts" else (width,)
            where[r] = [(result(EXTRA_ROWS, w, jnp.int16), 0, 0) for w in cut]
    operands = Operands()
    slope_at, shift_at = [operands.add(s, SMEM) for s in scalars]
    for b in sequence:
        operands.block(b)
    x_views = [operands.block(b) for b in x_blocks]
    y_views = [operands.block(b) for b in y_blocks]
    before_at = {r: operands.add(b, VMEM) for r, b in before.items()}

    def kernel(ins, refs):
        outs, weights = refs[:-1], refs[-1]
        slope, shift = ins[slope_at][0] * LOG2E, ins[shift_at][0] * LOG2E
        x_refs, y_refs = [v(ins) for v in x_views], [v(ins) for v in y_views]

        def stacked(chosen):
            return jnp.concatenate(
                [ref[pl.ds(row, size), pl.ds(column, width)] for ((ref, row, column),) in chosen],
                axis=0,
            )

        for rows, columns in jobs:
            x_all = stacked([x_refs[r] for r in rows])
            keys = [
                jnp.broadcast_to(keys_of(x_refs[r], size, x_masks[r], x_images), (size, size)).T
                for r in rows
            ]
            for n in range(0, len(columns), per_tile):
                chosen = columns[n : n + per_tile]
                other = jnp.concatenate(
                    [keys_of(y_refs[c], size, y_masks[c], not x_images) for c in chosen], axis=1
                )
                scores = lax.dot_general(
                    x_all,
                    stacked([y_refs[c] for c in chosen]),
                    (((1,), (1,)), ((), ())),
                    preferred_element_type=jnp.float32,
                )
                for i in range(len(rows)):
                    z = scores[i * size : (i + 1) * size] * slope + shift
                    sig = 1.0 / (1.0 + jnp.exp2(-z))
                    w = jnp.where(jnp.tile(keys[i], (1, len(chosen))) == other, sig - 1.0, sig)
                    there = pl.ds(n * size, len(chosen) * size)
                    weights[pl.ds(i * size, size), there] = w.astype(jnp.bfloat16)
            for tile in column_tiles(width):
                sums = jnp.dot(
                    weights[pl.ds(0, len(rows) * size), pl.ds(0, len(columns) * size)],
                    jnp.concatenate([piece(y_refs[c], (0, size), tile)[...] for c in columns], axis=0),
                    preferred_element_type=jnp.float32,
                )
                for i, r in enumerate(rows):
                    block = sums[i * size : (i + 1) * size]
                    if r in before_at:
                        block = block + piece(whole(ins[before_at[r]]), (0, size), tile)[...]
                    out = tuple((outs[o], row, column) for o, row, column in where[r])
                    if emits[r] == "float":
                        piece(out, (0, size), tile)[...] = block
                    else:
                        encode(block, out, tile)

    pairs = sum(len(rows) * len(columns) for rows, columns in jobs)
    scratch = [pltpu.VMEM((len(x_blocks) * size, len(y_blocks) * size), jnp.bfloat16)]
    room = len(x_blocks) * len(y_blocks) * size * size * 2 + 8 * 2**20
    results = call(kernel, name, operands.pairs, shapes, scratch, room, pairs * size, after)
    return [tuple(results[o] for o, _, _ in where[r]) for r in range(len(emits))]


def passed_sum(kept, received, part, held_back=()):
    size, width = kept.shape
    operands = Operands()
    kept_at = operands.add(kept, VMEM)
    views = [operands.block(b if part is None or len(b) == 1 else (b[part],) * 2) for b in received]

    def kernel(ins, outs):
        for tile in column_tiles(width):
            p, inner, _, span = tile
            if part is None or p == part:
                total = piece(whole(ins[kept_at]), (0, size), tile)[...]
                for view in views:
                    total = total + decoded(view(ins), size, tile)
                encode(total, whole(outs[0]), tile if part is None else (0, 0, inner, span))

    cut = width if part is None else part_widths(width)[part]
    shape = jax.ShapeDtypeStruct((size + EXTRA_ROWS, cut), jnp.int16)
    return call(kernel, "passed_sum", operands.pairs, [shape], [], 2**21, size, (), held_back)


def output_sum(sharpness, kept, received):
    size, width = kept.shape
    operands = Operands()
    sharpness_at = operands.add(sharpness, SMEM)
    kept_at = operands.add(kept, VMEM)
    views = [operands.block(b) for b in received]

    def kernel(ins, outs):
        for tile in column_tiles(width):
            total = piece(whole(ins[kept_at]), (0, size), tile)[...]
            for view in views:
                total = total + decoded(view(ins), size, tile)
            piece(whole(outs[0]), (0, size), tile)[...] = total * ins[sharpness_at][0]

    shape = jax.ShapeDtypeStruct((size, width), jnp.float32)
    return call(kernel, "output_sum", operands.pairs, [shape], [], 2**21, size)[0]


def swapped(array, step):
    axis, bit = step
    return lax.ppermute(array, axis, [(i, i ^ bit) for i in range(lax.axis_size(axis))])


def scattered_sum(sharpness, kept, coded, steps):
    def sent(block, step):
        return [(swapped(p, step), 0, 0) for p in block]

    last = steps[-1]
    if len(coded[-1]) == 1:
        received = [[sent(c, last)] for c in coded]
        begun = None
    else:
        received = [[None]] + [[sent(c[:1], last)] for c in coded[1:]]
        n = len(kept) - 1
        begun, *rest = passed_sum(
            kept[n], received[n], 0, [c[-1] for c in coded[1:]] + [coded[0][0]]
        )
        for r, c in zip(received[1:] + received[:1], rest):
            if r is received[0]:
                r[0] = sent([c], last)
            else:
                r[0] = r[0] + sent([c], last)
    for s in reversed(range(len(steps) - 1)):
        for m in reversed(range(1 << s)):
            n = m | 1 << s
            parts = range(2) if len(received[n][0]) == 2 else [None]
            passed = []
            for p in parts:
                if begun is not None:
                    passed.append(begun)
                    begun = None
                else:
                    passed += passed_sum(kept[n], received[n], p)
            received[m].append(sent(passed, steps[s]))
    return output_sum(sharpness, kept[0], received[0])


def bit_steps(axis):
    return [(axis, 1 << k) for k in range(int(math.log2(lax.axis_size(axis))))]


def owner_masks(steps):
    masks = [(0, 0)]
    for axis, bit in steps:
        masks = masks + [(b ^ bit, g) if axis == "blk" else (b, g ^ bit) for b, g in masks]
    return masks


def per_device(
    picture_vectors, caption_vectors, matching_caption, sharpness_parameter, additive_intercept
):
    scalars = (sharpness_parameter, additive_intercept)
    size = picture_vectors.shape[0]
    core, *grp_steps = bit_steps("grp")
    every = grp_steps + bit_steps("blk")
    steps = [every[0::2], every[1::2]]
    assert len(steps[0]) == len(steps[1]) >= 2
    masks = [owner_masks(s + [core]) for s in steps]
    count = 1 << len(steps[0])
    half = count // 2
    early, late = list(range(half + 1)), list(range(half + 1, count))
    labels = matching_caption[None, :]
    first_texts = swapped(caption_vectors, steps[1][0])
    first_images = [swapped(a, steps[0][0]) for a in (picture_vectors, labels)]
    arrays = [{0: labelled(picture_vectors, labels), 1: labelled(*first_images, [first_texts])}, {0: caption_vectors, 1: first_texts}]
    for i in range(1, len(steps[0])):
        for k in (1, 0):
            for m in range(1 << i):
                arrays[k][m | 1 << i] = swapped(arrays[k][m], steps[k][i])
    blocks = [[whole(a[m]) for m in range(count)] for a in arrays]
    others = [{}, {}]
    for m in early:
        if m == 0:
            cost, after = size, [arrays[1][half]]
        else:
            cost, after = (BUNDLE_COST if m == 1 else size), []
        both = swapped(bundled(arrays[1][m], arrays[0][m], cost, after), core)
        others[1][m], others[0][m] = whole(both), ((both, size, 0),)

    def sums(name, kind, rows, columns, cores, jobs, before, emits, after=()):
        other = 1 - kind
        x_blocks = [blocks[kind][m] for m in rows]
        y_blocks = [(blocks, others)[c][other][m] for c in cores for m in columns]
        x_masks = [masks[kind][m] for m in rows]
        y_masks = [masks[other][m + c * count] for c in cores for m in columns]
        return gradient_sums(
            name,
            size,
            scalars,
            x_blocks,
            y_blocks,
            (x_masks, y_masks),
            kind == 0,
            jobs,
            before,
            emits,
            [blocks[k][m] for m in rows[1:] + rows[:1] for k in (1, 0)],
            after,
        )

    before = [{}, {}]
    for c in range(2):
        for k in range(2):
            jobs = [(early, early)]
            results = sums("early_sums", k, early, early, [c], jobs, before[k], ["float"] * len(early))
            before[k] = {m: s for m, (s,) in zip(early, results)}
    arrays = [[b[m][0][0] for m in late] for b in blocks[::-1]]
    arrays, before = lax.optimization_barrier((arrays, before))
    for k in (1, 0):
        for m, a in zip(late, arrays[1 - k]):
            blocks[k][m] = whole(a)
            others[k][m] = whole(swapped(a, core))
    every = list(range(count))
    jobs = [(late, every + [count + m for m in every]), (early, late + [count + m for m in late])]
    coded, kept, after = [None, None], [None, None], ()
    for k, cut in ((1, "whole"), (0, "whole")):
        emits = ["float"] * half + ["whole"] + [cut] * len(late)
        results = sums(
            "late_sums", k, every, every, (0, 1), jobs, before[k], emits, after
        )
        kept[k] = [s for (s,) in results[:half]]
        coded[k] = results[half:]
        after = coded[k][0]
    return tuple(scattered_sum(scalars[0], kept[k], coded[k], steps[k]) for k in range(2))


def solution(mesh):
    placed = (P(("blk", "grp"), None), P(("blk", "grp"), None), P(("blk", "grp")), P(), P())
    return jax.shard_map(
        per_device,
        mesh=mesh,
        in_specs=placed,
        out_specs=(P(("blk", "grp"), None), P(("blk", "grp"), None)),
        check_vma=False,
    )
```

```python
import math

import jax
import jax.numpy as jnp
from jax import lax
from jax.experimental import pallas as pl
from jax.experimental.pallas import tpu as pltpu
from jax.sharding import PartitionSpec as P

LOG2E = 1.4426950408889634
CODE_TOP = 32000.0
CODE_STEPS = 32.0
EXTRA_ROWS = 8
LABEL_BASE = 128
TILE = 256
LANES = 128
BUNDLE_COST = 6 * 10**8
SMEM = pl.BlockSpec(memory_space=pltpu.SMEM)
VMEM = pl.BlockSpec(memory_space=pltpu.VMEM)
ANY = pl.BlockSpec(memory_space=pl.ANY)


def whole(array):
    return ((array, 0, 0),)


def part_widths(width):
    first = min(3 * TILE, width - LANES)
    return (first, width - first)


def column_tiles(width):
    tiles, begin = [], 0
    for p, w in enumerate(part_widths(width)):
        tiles += [(p, k, begin + k, min(TILE, w - k)) for k in range(0, w, TILE)]
        begin += w
    return tiles


def piece(block, rows, tile):
    p, inner, start, span = tile
    ref, row, column = block[0 if len(block) == 1 else p]
    first = start if len(block) == 1 else inner
    return ref.at[pl.ds(row + rows[0], rows[1]), pl.ds(column + first, span)]


class Operands:
    def __init__(self):
        self.pairs = []

    def add(self, array, spec):
        for i, (a, s) in enumerate(self.pairs):
            if a is array and s is spec:
                return i
        self.pairs.append((array, spec))
        return len(self.pairs) - 1

    def block(self, block):
        at = [(self.add(a, VMEM), row, column) for a, row, column in block]
        return lambda refs: tuple((refs[i], row, column) for i, row, column in at)


def scale_code(top):
    return jnp.ceil(jnp.log(jnp.maximum(top, 1e-30)) * (CODE_STEPS * LOG2E))


def encode(value, block, tile):
    size, span = value.shape
    code = scale_code(jnp.max(jnp.abs(value), axis=0, keepdims=True))
    gain = CODE_TOP * jnp.exp(code * (-1.0 / (CODE_STEPS * LOG2E)))
    piece(block, (0, size), tile)[...] = (
        jnp.round(value * gain).astype(jnp.int32).astype(jnp.int16)
    )
    scales = jnp.broadcast_to(code.astype(jnp.int32), (EXTRA_ROWS, span)).astype(jnp.int16)
    piece(block, (size, EXTRA_ROWS), tile)[...] = scales


def decoded(block, size, tile):
    code = piece(block, (size, EXTRA_ROWS), tile)[...].astype(jnp.int32).astype(jnp.float32)
    gain = jnp.exp(code[:1] * (1.0 / (CODE_STEPS * LOG2E))) * (1.0 / CODE_TOP)
    return piece(block, (0, size), tile)[...].astype(jnp.int32).astype(jnp.float32) * gain


def call(kernel, name, operands, out_shape, scratch, room, cost, after=(), held_back=()):
    arrays = [a for a, _ in operands]
    held = sum(math.prod(a.shape) * a.dtype.itemsize for a in [*arrays, *out_shape])

    def body(*refs):
        results = refs[len(arrays) + len(after) + len(held_back) :]
        kernel(refs[: len(arrays)], results[: len(out_shape)] + results[len(out_shape) + len(held_back) :])

    return pl.pallas_call(
        body,
        out_shape=[*out_shape, *(jax.ShapeDtypeStruct(a.shape, a.dtype) for a in held_back)],
        in_specs=[s for _, s in operands] + [ANY] * (len(after) + len(held_back)),
        out_specs=[VMEM] * len(out_shape) + [ANY] * len(held_back),
        input_output_aliases={
            len(arrays) + len(after) + i: len(out_shape) + i for i in range(len(held_back))
        },
        scratch_shapes=scratch,
        compiler_params=pltpu.CompilerParams(vmem_limit_bytes=held + room),
        cost_estimate=pl.CostEstimate(flops=cost, bytes_accessed=cost, transcendentals=0),
        name=name,
    )(*arrays, *after, *held_back)


def labelled(images, labels, after=()):
    size, width = images.shape

    def kernel(ins, outs):
        outs[0][pl.ds(0, size), :] = ins[0][...]
        outs[0][pl.ds(size, EXTRA_ROWS), :] = jnp.zeros((EXTRA_ROWS, width), jnp.bfloat16)
        row = ins[1][...]
        low, high = lax.rem(row, LABEL_BASE), lax.div(row, LABEL_BASE)
        at = lax.broadcasted_iota(jnp.int32, (EXTRA_ROWS, size), 0)
        parts = jnp.where(at == 0, high, jnp.where(at == 1, low, 0)).astype(jnp.float32)
        outs[0][pl.ds(size, EXTRA_ROWS), pl.ds(0, size)] = parts.astype(jnp.bfloat16)

    shape = jax.ShapeDtypeStruct((size + EXTRA_ROWS, width), jnp.bfloat16)
    operands = [(images, VMEM), (labels, VMEM)]
    return call(kernel, "labelled", operands, [shape], [], 2**21, size, after)[0]


def bundled(arrays, cost):
    width = arrays[0].shape[1]

    def kernel(ins, outs):
        first = 0
        for ref in ins:
            outs[0][pl.ds(first, ref.shape[0]), :] = ref[...]
            first += ref.shape[0]

    shape = jax.ShapeDtypeStruct((sum(a.shape[0] for a in arrays), width), jnp.bfloat16)
    operands = [(a, VMEM) for a in arrays]
    return call(kernel, "bundled", operands, [shape], [], 2**21, cost)[0]


def first_row(mask, size):
    owner = (lax.axis_index("blk") ^ mask[0]) * lax.axis_size("grp") + (lax.axis_index("grp") ^ mask[1])
    return owner * size


def keys_of(block, size, mask, is_image):
    if not is_image:
        ids = lax.broadcasted_iota(jnp.int32, (1, size), 1) + first_row(mask, size)
        return ids.astype(jnp.float32)
    parts = piece(block, (size, EXTRA_ROWS), (0, 0, 0, size))[...].astype(jnp.float32)
    return parts[0:1] * LABEL_BASE + parts[1:2]


def gradient_sums(name, size, scalars, x_blocks, y_blocks, masks, x_images, jobs, before, emits, sequence, after=()):
    width = x_blocks[0][0][0].shape[1]
    x_masks, y_masks = masks
    per_tile = TILE // size
    widths = part_widths(width)
    shapes, where = [], {}

    def result(extra, w, dtype):
        shapes.append(jax.ShapeDtypeStruct((size + extra, w), dtype))
        return len(shapes) - 1

    for r, kind in enumerate(emits):
        if kind == "float":
            where[r] = [(result(0, width, jnp.float32), 0, 0)]
        else:
            cut = widths if kind == "parts" else (width,)
            where[r] = [(result(EXTRA_ROWS, w, jnp.int16), 0, 0) for w in cut]
    operands = Operands()
    slope_at, shift_at = [operands.add(s, SMEM) for s in scalars]
    for b in sequence:
        operands.block(b)
    x_views = [operands.block(b) for b in x_blocks]
    y_views = [operands.block(b) for b in y_blocks]
    before_at = {r: operands.add(b, VMEM) for r, b in before.items()}

    def kernel(ins, refs):
        outs, weights = refs[:-1], refs[-1]
        slope, shift = ins[slope_at][0] * LOG2E, ins[shift_at][0] * LOG2E
        x_refs, y_refs = [v(ins) for v in x_views], [v(ins) for v in y_views]

        def stacked(chosen):
            return jnp.concatenate(
                [ref[pl.ds(row, size), pl.ds(column, width)] for ((ref, row, column),) in chosen],
                axis=0,
            )

        for rows, columns in jobs:
            x_all = stacked([x_refs[r] for r in rows])
            keys = [
                jnp.broadcast_to(keys_of(x_refs[r], size, x_masks[r], x_images), (size, size)).T
                for r in rows
            ]
            for n in range(0, len(columns), per_tile):
                chosen = columns[n : n + per_tile]
                other = jnp.concatenate(
                    [keys_of(y_refs[c], size, y_masks[c], not x_images) for c in chosen], axis=1
                )
                scores = lax.dot_general(
                    x_all,
                    stacked([y_refs[c] for c in chosen]),
                    (((1,), (1,)), ((), ())),
                    preferred_element_type=jnp.float32,
                )
                for i in range(len(rows)):
                    z = scores[i * size : (i + 1) * size] * slope + shift
                    sig = 1.0 / (1.0 + jnp.exp2(-z))
                    w = jnp.where(jnp.tile(keys[i], (1, len(chosen))) == other, sig - 1.0, sig)
                    there = pl.ds(n * size, len(chosen) * size)
                    weights[pl.ds(i * size, size), there] = w.astype(jnp.bfloat16)
            for tile in column_tiles(width):
                sums = jnp.dot(
                    weights[pl.ds(0, len(rows) * size), pl.ds(0, len(columns) * size)],
                    jnp.concatenate([piece(y_refs[c], (0, size), tile)[...] for c in columns], axis=0),
                    preferred_element_type=jnp.float32,
                )
                for i, r in enumerate(rows):
                    block = sums[i * size : (i + 1) * size]
                    if r in before_at:
                        block = block + piece(whole(ins[before_at[r]]), (0, size), tile)[...]
                    out = tuple((outs[o], row, column) for o, row, column in where[r])
                    if emits[r] == "float":
                        piece(out, (0, size), tile)[...] = block
                    else:
                        encode(block, out, tile)

    pairs = sum(len(rows) * len(columns) for rows, columns in jobs)
    scratch = [pltpu.VMEM((len(x_blocks) * size, len(y_blocks) * size), jnp.bfloat16)]
    room = len(x_blocks) * len(y_blocks) * size * size * 2 + 8 * 2**20
    results = call(kernel, name, operands.pairs, shapes, scratch, room, pairs * size, after)
    return [tuple(results[o] for o, _, _ in where[r]) for r in range(len(emits))]


def passed_sum(kept, received, part, held_back=()):
    size, width = kept.shape
    operands = Operands()
    kept_at = operands.add(kept, VMEM)
    views = [operands.block(b if part is None or len(b) == 1 else (b[part],) * 2) for b in received]

    def kernel(ins, outs):
        for tile in column_tiles(width):
            p, inner, _, span = tile
            if part is None or p == part:
                total = piece(whole(ins[kept_at]), (0, size), tile)[...]
                for view in views:
                    total = total + decoded(view(ins), size, tile)
                encode(total, whole(outs[0]), tile if part is None else (0, 0, inner, span))

    cut = width if part is None else part_widths(width)[part]
    shape = jax.ShapeDtypeStruct((size + EXTRA_ROWS, cut), jnp.int16)
    return call(kernel, "passed_sum", operands.pairs, [shape], [], 2**21, size, (), held_back)


def output_sums(sharpness, sums):
    size, width = sums[0][0].shape
    operands = Operands()
    sharpness_at = operands.add(sharpness, SMEM)
    views = [(operands.add(kept, VMEM), [operands.block(b) for b in blocks]) for kept, blocks in sums]

    def kernel(ins, outs):
        for out, (kept_at, received) in zip(outs, views):
            for tile in column_tiles(width):
                total = piece(whole(ins[kept_at]), (0, size), tile)[...]
                for view in received:
                    total = total + decoded(view(ins), size, tile)
                piece(whole(out), (0, size), tile)[...] = total * ins[sharpness_at][0]

    shapes = [jax.ShapeDtypeStruct((size, width), jnp.float32)] * len(sums)
    return call(kernel, "output_sums", operands.pairs, shapes, [], 2**21, size)


def swapped(array, step):
    axis, bit = step
    return lax.ppermute(array, axis, [(i, i ^ bit) for i in range(lax.axis_size(axis))])


def scattered(kept, coded, steps):
    def sent(block, step):
        return [(swapped(p, step), 0, 0) for p in block]

    last = steps[-1]
    if len(coded[-1]) == 1:
        received = [[sent(c, last)] for c in coded]
        begun = None
    else:
        received = [[None]] + [[sent(c[:1], last)] for c in coded[1:]]
        n = len(kept) - 1
        begun, *rest = passed_sum(
            kept[n], received[n], 0, [c[-1] for c in coded[1:]] + [coded[0][0]]
        )
        for r, c in zip(received[1:] + received[:1], rest):
            if r is received[0]:
                r[0] = sent([c], last)
            else:
                r[0] = r[0] + sent([c], last)
    for s in reversed(range(len(steps) - 1)):
        for m in reversed(range(1 << s)):
            n = m | 1 << s
            parts = range(2) if len(received[n][0]) == 2 else [None]
            passed = []
            for p in parts:
                if begun is not None:
                    passed.append(begun)
                    begun = None
                else:
                    passed += passed_sum(kept[n], received[n], p)
            received[m].append(sent(passed, steps[s]))
    return kept[0], received[0]


def bit_steps(axis):
    return [(axis, 1 << k) for k in range(int(math.log2(lax.axis_size(axis))))]


def owner_masks(steps):
    masks = [(0, 0)]
    for axis, bit in steps:
        masks = masks + [(b ^ bit, g) if axis == "blk" else (b, g ^ bit) for b, g in masks]
    return masks


def per_device(
    picture_vectors, caption_vectors, matching_caption, sharpness_parameter, additive_intercept
):
    scalars = (sharpness_parameter, additive_intercept)
    size = picture_vectors.shape[0]
    core, *grp_steps = bit_steps("grp")
    every = grp_steps + bit_steps("blk")
    steps = [every[0::2], every[1::2]]
    assert len(steps[0]) == len(steps[1]) >= 2
    masks = [owner_masks(s + [core]) for s in steps]
    count = 1 << len(steps[0])
    half = count // 2
    early, late = list(range(half + 1)), list(range(half + 1, count))
    labels = matching_caption[None, :]
    first_texts = swapped(caption_vectors, steps[1][0])
    first_images = [swapped(a, steps[0][0]) for a in (picture_vectors, labels)]
    arrays = [{0: labelled(picture_vectors, labels), 1: labelled(*first_images, [first_texts])}, {0: caption_vectors, 1: first_texts}]
    for i in range(1, len(steps[0])):
        for k in (1, 0):
            for m in range(1 << i):
                arrays[k][m | 1 << i] = swapped(arrays[k][m], steps[k][i])
    blocks = [[whole(a[m]) for m in range(count)] for a in arrays]
    others = [{}, {}]
    both = bundled([arrays[1][1], arrays[0][1]], BUNDLE_COST)
    rest = [m for m in early if m != 1]
    both = swapped(bundled([both] + [arrays[k][m] for m in rest for k in (1, 0)], size), core)
    for i, m in enumerate([1] + rest):
        row = i * (2 * size + EXTRA_ROWS)
        others[1][m], others[0][m] = ((both, row, 0),), ((both, row + size, 0),)

    def sums(name, kind, rows, columns, cores, jobs, before, emits, after=()):
        other = 1 - kind
        x_blocks = [blocks[kind][m] for m in rows]
        y_blocks = [(blocks, others)[c][other][m] for c in cores for m in columns]
        x_masks = [masks[kind][m] for m in rows]
        y_masks = [masks[other][m + c * count] for c in cores for m in columns]
        return gradient_sums(
            name,
            size,
            scalars,
            x_blocks,
            y_blocks,
            (x_masks, y_masks),
            kind == 0,
            jobs,
            before,
            emits,
            [blocks[k][m] for m in rows[1:] + rows[:1] for k in (1, 0)],
            after,
        )

    before = []
    for k in range(2):
        jobs = [(early, list(range(2 * len(early))))]
        results = sums("early_sums", k, early, early, (0, 1), jobs, {}, ["float"] * len(early))
        before.append({m: s for m, (s,) in zip(early, results)})
    arrays = [[b[m][0][0] for m in late] for b in blocks[::-1]]
    arrays, before = lax.optimization_barrier((arrays, before))
    for k in (1, 0):
        for m, a in zip(late, arrays[1 - k]):
            blocks[k][m] = whole(a)
            others[k][m] = whole(swapped(a, core))
    every = list(range(count))
    jobs = [(late, every + [count + m for m in every]), (early, late + [count + m for m in late])]
    coded, kept, after = [None, None], [None, None], ()
    for k, cut in ((1, "whole"), (0, "whole")):
        emits = ["float"] * half + ["whole"] + [cut] * len(late)
        results = sums(
            "late_sums", k, every, every, (0, 1), jobs, before[k], emits, after
        )
        kept[k] = [s for (s,) in results[:half]]
        coded[k] = results[half:]
        after = coded[k][0]
    return tuple(output_sums(scalars[0], [scattered(kept[k], coded[k], steps[k]) for k in range(2)]))


def solution(mesh):
    placed = (P(("blk", "grp"), None), P(("blk", "grp"), None), P(("blk", "grp")), P(), P())
    return jax.shard_map(
        per_device,
        mesh=mesh,
        in_specs=placed,
        out_specs=(P(("blk", "grp"), None), P(("blk", "grp"), None)),
        check_vma=False,
    )
```

```python
import math

import jax
import jax.numpy as jnp
from jax import lax
from jax.experimental import pallas as pl
from jax.experimental.pallas import tpu as pltpu
from jax.sharding import PartitionSpec as P

LOG2E = 1.4426950408889634
CODE_TOP = 32000.0
CODE_STEPS = 32.0
EXTRA_ROWS = 8
LABEL_BASE = 128
TILE = 256
LANES = 128
BUNDLE_COST = 6 * 10**8
SMEM = pl.BlockSpec(memory_space=pltpu.SMEM)
VMEM = pl.BlockSpec(memory_space=pltpu.VMEM)
ANY = pl.BlockSpec(memory_space=pl.ANY)


def whole(array):
    return ((array, 0, 0),)


def part_widths(width):
    first = min(3 * TILE, width - LANES)
    return (first, width - first)


def column_tiles(width):
    tiles, begin = [], 0
    for p, w in enumerate(part_widths(width)):
        tiles += [(p, k, begin + k, min(TILE, w - k)) for k in range(0, w, TILE)]
        begin += w
    return tiles


def piece(block, rows, tile):
    p, inner, start, span = tile
    ref, row, column = block[0 if len(block) == 1 else p]
    first = start if len(block) == 1 else inner
    return ref.at[pl.ds(row + rows[0], rows[1]), pl.ds(column + first, span)]


class Operands:
    def __init__(self):
        self.pairs = []

    def add(self, array, spec):
        for i, (a, s) in enumerate(self.pairs):
            if a is array and s is spec:
                return i
        self.pairs.append((array, spec))
        return len(self.pairs) - 1

    def block(self, block):
        at = [(self.add(a, VMEM), row, column) for a, row, column in block]
        return lambda refs: tuple((refs[i], row, column) for i, row, column in at)


def scale_code(top):
    return jnp.ceil(jnp.log(jnp.maximum(top, 1e-30)) * (CODE_STEPS * LOG2E))


def encode(value, block, tile):
    size, span = value.shape
    code = scale_code(jnp.max(jnp.abs(value), axis=0, keepdims=True))
    gain = CODE_TOP * jnp.exp(code * (-1.0 / (CODE_STEPS * LOG2E)))
    piece(block, (0, size), tile)[...] = (
        jnp.round(value * gain).astype(jnp.int32).astype(jnp.int16)
    )
    scales = jnp.broadcast_to(code.astype(jnp.int32), (EXTRA_ROWS, span)).astype(jnp.int16)
    piece(block, (size, EXTRA_ROWS), tile)[...] = scales


def decoded(block, size, tile):
    code = piece(block, (size, EXTRA_ROWS), tile)[...].astype(jnp.int32).astype(jnp.float32)
    gain = jnp.exp(code[:1] * (1.0 / (CODE_STEPS * LOG2E))) * (1.0 / CODE_TOP)
    return piece(block, (0, size), tile)[...].astype(jnp.int32).astype(jnp.float32) * gain


def call(kernel, name, operands, out_shape, scratch, room, cost, after=(), held_back=()):
    arrays = [a for a, _ in operands]
    held = sum(math.prod(a.shape) * a.dtype.itemsize for a in [*arrays, *out_shape])

    def body(*refs):
        results = refs[len(arrays) + len(after) + len(held_back) :]
        kernel(refs[: len(arrays)], results[: len(out_shape)] + results[len(out_shape) + len(held_back) :])

    return pl.pallas_call(
        body,
        out_shape=[*out_shape, *(jax.ShapeDtypeStruct(a.shape, a.dtype) for a in held_back)],
        in_specs=[s for _, s in operands] + [ANY] * (len(after) + len(held_back)),
        out_specs=[VMEM] * len(out_shape) + [ANY] * len(held_back),
        input_output_aliases={
            len(arrays) + len(after) + i: len(out_shape) + i for i in range(len(held_back))
        },
        scratch_shapes=scratch,
        compiler_params=pltpu.CompilerParams(vmem_limit_bytes=held + room),
        cost_estimate=pl.CostEstimate(flops=cost, bytes_accessed=cost, transcendentals=0),
        name=name,
    )(*arrays, *after, *held_back)


def labelled(images, labels, after=()):
    size, width = images.shape

    def kernel(ins, outs):
        outs[0][pl.ds(0, size), :] = ins[0][...]
        outs[0][pl.ds(size, EXTRA_ROWS), :] = jnp.zeros((EXTRA_ROWS, width), jnp.bfloat16)
        row = ins[1][...]
        low, high = lax.rem(row, LABEL_BASE), lax.div(row, LABEL_BASE)
        at = lax.broadcasted_iota(jnp.int32, (EXTRA_ROWS, size), 0)
        parts = jnp.where(at == 0, high, jnp.where(at == 1, low, 0)).astype(jnp.float32)
        outs[0][pl.ds(size, EXTRA_ROWS), pl.ds(0, size)] = parts.astype(jnp.bfloat16)

    shape = jax.ShapeDtypeStruct((size + EXTRA_ROWS, width), jnp.bfloat16)
    operands = [(images, VMEM), (labels, VMEM)]
    return call(kernel, "labelled", operands, [shape], [], 2**21, size, after)[0]


def bundled(arrays, cost):
    width = arrays[0].shape[1]

    def kernel(ins, outs):
        first = 0
        for ref in ins:
            outs[0][pl.ds(first, ref.shape[0]), :] = ref[...]
            first += ref.shape[0]

    shape = jax.ShapeDtypeStruct((sum(a.shape[0] for a in arrays), width), jnp.bfloat16)
    operands = [(a, VMEM) for a in arrays]
    return call(kernel, "bundled", operands, [shape], [], 2**21, cost)[0]


def first_row(mask, size):
    owner = (lax.axis_index("blk") ^ mask[0]) * lax.axis_size("grp") + (lax.axis_index("grp") ^ mask[1])
    return owner * size


def keys_of(block, size, mask, is_image):
    if not is_image:
        ids = lax.broadcasted_iota(jnp.int32, (1, size), 1) + first_row(mask, size)
        return ids.astype(jnp.float32)
    parts = piece(block, (size, EXTRA_ROWS), (0, 0, 0, size))[...].astype(jnp.float32)
    return parts[0:1] * LABEL_BASE + parts[1:2]


def gradient_sums(name, size, scalars, x_blocks, y_blocks, masks, x_images, jobs, before, emits, sequence, after=()):
    width = x_blocks[0][0][0].shape[1]
    x_masks, y_masks = masks
    per_tile = TILE // size
    widths = part_widths(width)
    shapes, where = [], {}

    def result(extra, w, dtype):
        shapes.append(jax.ShapeDtypeStruct((size + extra, w), dtype))
        return len(shapes) - 1

    for r, kind in enumerate(emits):
        if kind == "float":
            where[r] = [(result(0, width, jnp.float32), 0, 0)]
        else:
            cut = widths if kind == "parts" else (width,)
            where[r] = [(result(EXTRA_ROWS, w, jnp.int16), 0, 0) for w in cut]
    operands = Operands()
    slope_at, shift_at = [operands.add(s, SMEM) for s in scalars]
    for b in sequence:
        operands.block(b)
    x_views = [operands.block(b) for b in x_blocks]
    y_views = [operands.block(b) for b in y_blocks]
    before_at = {r: operands.add(b, VMEM) for r, b in before.items()}

    def kernel(ins, refs):
        outs, weights = refs[:-1], refs[-1]
        slope, shift = ins[slope_at][0] * LOG2E, ins[shift_at][0] * LOG2E
        x_refs, y_refs = [v(ins) for v in x_views], [v(ins) for v in y_views]

        def stacked(chosen):
            return jnp.concatenate(
                [ref[pl.ds(row, size), pl.ds(column, width)] for ((ref, row, column),) in chosen],
                axis=0,
            )

        for rows, columns in jobs:
            x_all = stacked([x_refs[r] for r in rows])
            keys = [
                jnp.broadcast_to(keys_of(x_refs[r], size, x_masks[r], x_images), (size, size)).T
                for r in rows
            ]
            for n in range(0, len(columns), per_tile):
                chosen = columns[n : n + per_tile]
                other = jnp.concatenate(
                    [keys_of(y_refs[c], size, y_masks[c], not x_images) for c in chosen], axis=1
                )
                scores = lax.dot_general(
                    x_all,
                    stacked([y_refs[c] for c in chosen]),
                    (((1,), (1,)), ((), ())),
                    preferred_element_type=jnp.float32,
                )
                for i in range(len(rows)):
                    z = scores[i * size : (i + 1) * size] * slope + shift
                    sig = 1.0 / (1.0 + jnp.exp2(-z))
                    w = jnp.where(jnp.tile(keys[i], (1, len(chosen))) == other, sig - 1.0, sig)
                    there = pl.ds(n * size, len(chosen) * size)
                    weights[pl.ds(i * size, size), there] = w.astype(jnp.bfloat16)
            for tile in column_tiles(width):
                sums = jnp.dot(
                    weights[pl.ds(0, len(rows) * size), pl.ds(0, len(columns) * size)],
                    jnp.concatenate([piece(y_refs[c], (0, size), tile)[...] for c in columns], axis=0),
                    preferred_element_type=jnp.float32,
                )
                for i, r in enumerate(rows):
                    block = sums[i * size : (i + 1) * size]
                    if r in before_at:
                        block = block + piece(whole(ins[before_at[r]]), (0, size), tile)[...]
                    out = tuple((outs[o], row, column) for o, row, column in where[r])
                    if emits[r] == "float":
                        piece(out, (0, size), tile)[...] = block
                    else:
                        encode(block, out, tile)

    pairs = sum(len(rows) * len(columns) for rows, columns in jobs)
    scratch = [pltpu.VMEM((len(x_blocks) * size, len(y_blocks) * size), jnp.bfloat16)]
    room = len(x_blocks) * len(y_blocks) * size * size * 2 + 8 * 2**20
    results = call(kernel, name, operands.pairs, shapes, scratch, room, pairs * size, after)
    return [tuple(results[o] for o, _, _ in where[r]) for r in range(len(emits))]


def passed_sum(kept, received, part, held_back=()):
    size, width = kept.shape
    operands = Operands()
    kept_at = operands.add(kept, VMEM)
    views = [operands.block(b if part is None or len(b) == 1 else (b[part],) * 2) for b in received]

    def kernel(ins, outs):
        for tile in column_tiles(width):
            p, inner, _, span = tile
            if part is None or p == part:
                total = piece(whole(ins[kept_at]), (0, size), tile)[...]
                for view in views:
                    total = total + decoded(view(ins), size, tile)
                encode(total, whole(outs[0]), tile if part is None else (0, 0, inner, span))

    cut = width if part is None else part_widths(width)[part]
    shape = jax.ShapeDtypeStruct((size + EXTRA_ROWS, cut), jnp.int16)
    return call(kernel, "passed_sum", operands.pairs, [shape], [], 2**21, size, (), held_back)


def output_sums(sharpness, sums):
    size, width = sums[0][0].shape
    operands = Operands()
    sharpness_at = operands.add(sharpness, SMEM)
    views = [(operands.add(kept, VMEM), [operands.block(b) for b in blocks]) for kept, blocks in sums]

    def kernel(ins, outs):
        for out, (kept_at, received) in zip(outs, views):
            for tile in column_tiles(width):
                total = piece(whole(ins[kept_at]), (0, size), tile)[...]
                for view in received:
                    total = total + decoded(view(ins), size, tile)
                piece(whole(out), (0, size), tile)[...] = total * ins[sharpness_at][0]

    shapes = [jax.ShapeDtypeStruct((size, width), jnp.float32)] * len(sums)
    return call(kernel, "output_sums", operands.pairs, shapes, [], 2**21, size)


def swapped(array, step):
    axis, bit = step
    return lax.ppermute(array, axis, [(i, i ^ bit) for i in range(lax.axis_size(axis))])


def scattered(kept, coded, steps):
    def sent(block, step):
        return [(swapped(p, step), 0, 0) for p in block]

    half, waiting = len(kept), coded[0]
    received = [[]] + [[sent(c, steps[-1])] for c in coded[1:]]
    for s in reversed(range(len(steps) - 1)):
        for m in reversed(range(1 << s)):
            n = m | 1 << s
            block = passed_sum(kept[n], received[n], None, waiting)
            if n == half - 1:
                block, *waiting = block
                received[0].append(sent(waiting, steps[-1]))
                waiting, block = (), [block]
            received[m].append(sent(block, steps[s]))
    return kept[0], received[0][::-1]


def bit_steps(axis):
    return [(axis, 1 << k) for k in range(int(math.log2(lax.axis_size(axis))))]


def owner_masks(steps):
    masks = [(0, 0)]
    for axis, bit in steps:
        masks = masks + [(b ^ bit, g) if axis == "blk" else (b, g ^ bit) for b, g in masks]
    return masks


def per_device(
    picture_vectors, caption_vectors, matching_caption, sharpness_parameter, additive_intercept
):
    scalars = (sharpness_parameter, additive_intercept)
    size = picture_vectors.shape[0]
    core, *grp_steps = bit_steps("grp")
    every = grp_steps + bit_steps("blk")
    steps = [every[0::2], every[1::2]]
    assert len(steps[0]) == len(steps[1]) >= 2
    masks = [owner_masks(s + [core]) for s in steps]
    count = 1 << len(steps[0])
    half = count // 2
    early, late = list(range(half + 1)), list(range(half + 1, count))
    labels = matching_caption[None, :]
    first_texts = swapped(caption_vectors, steps[1][0])
    first_images = [swapped(a, steps[0][0]) for a in (picture_vectors, labels)]
    arrays = [{0: labelled(picture_vectors, labels), 1: labelled(*first_images, [first_texts])}, {0: caption_vectors, 1: first_texts}]
    for i in range(1, len(steps[0])):
        for k in (1, 0):
            for m in range(1 << i):
                arrays[k][m | 1 << i] = swapped(arrays[k][m], steps[k][i])
    blocks = [[whole(a[m]) for m in range(count)] for a in arrays]
    others = [{}, {}]
    both = bundled([arrays[1][1], arrays[0][1]], BUNDLE_COST)
    rest = [m for m in early if m != 1]
    both = swapped(bundled([both] + [arrays[k][m] for m in rest for k in (1, 0)], size), core)
    for i, m in enumerate([1] + rest):
        row = i * (2 * size + EXTRA_ROWS)
        others[1][m], others[0][m] = ((both, row, 0),), ((both, row + size, 0),)

    def sums(name, kind, rows, columns, cores, jobs, before, emits, after=()):
        other = 1 - kind
        x_blocks = [blocks[kind][m] for m in rows]
        y_blocks = [(blocks, others)[c][other][m] for c in cores for m in columns]
        x_masks = [masks[kind][m] for m in rows]
        y_masks = [masks[other][m + c * count] for c in cores for m in columns]
        return gradient_sums(
            name,
            size,
            scalars,
            x_blocks,
            y_blocks,
            (x_masks, y_masks),
            kind == 0,
            jobs,
            before,
            emits,
            [blocks[k][m] for m in rows[1:] + rows[:1] for k in (1, 0)],
            after,
        )

    before = []
    for k in range(2):
        jobs = [(early, list(range(2 * len(early))))]
        results = sums("early_sums", k, early, early, (0, 1), jobs, {}, ["float"] * len(early))
        before.append({m: s for m, (s,) in zip(early, results)})
    arrays = [[b[m][0][0] for m in late] for b in blocks[::-1]]
    arrays, before = lax.optimization_barrier((arrays, before))
    for k in (1, 0):
        for m, a in zip(late, arrays[1 - k]):
            blocks[k][m] = whole(a)
            others[k][m] = whole(swapped(a, core))
    every = list(range(count))
    jobs = [(late, every + [count + m for m in every]), (early, late + [count + m for m in late])]
    coded, kept, after = [None, None], [None, None], ()
    for k, cut in ((1, "whole"), (0, "whole")):
        emits = ["float"] * half + ["whole"] + [cut] * len(late)
        results = sums(
            "late_sums", k, every, every, (0, 1), jobs, before[k], emits, after
        )
        kept[k] = [s for (s,) in results[:half]]
        coded[k] = results[half:]
        after = coded[k][0]
    return tuple(output_sums(scalars[0], [scattered(kept[k], coded[k], steps[k]) for k in range(2)]))


def solution(mesh):
    placed = (P(("blk", "grp"), None), P(("blk", "grp"), None), P(("blk", "grp")), P(), P())
    return jax.shard_map(
        per_device,
        mesh=mesh,
        in_specs=placed,
        out_specs=(P(("blk", "grp"), None), P(("blk", "grp"), None)),
        check_vma=False,
    )
```

```python
import math

import jax
import jax.numpy as jnp
from jax import lax
from jax.experimental import pallas as pl
from jax.experimental.pallas import tpu as pltpu
from jax.sharding import PartitionSpec as P

LOG2E = 1.4426950408889634
CODE_TOP = 32000.0
CODE_STEPS = 32.0
EXTRA_ROWS = 8
LABEL_BASE = 128
TILE = 256
LANES = 128
BUNDLE_COST = 6 * 10**8
SMEM = pl.BlockSpec(memory_space=pltpu.SMEM)
VMEM = pl.BlockSpec(memory_space=pltpu.VMEM)
ANY = pl.BlockSpec(memory_space=pl.ANY)


def whole(array):
    return ((array, 0, 0),)


def part_widths(width):
    first = min(3 * TILE, width - LANES)
    return (first, width - first)


def column_tiles(width):
    tiles, begin = [], 0
    for p, w in enumerate(part_widths(width)):
        tiles += [(p, k, begin + k, min(TILE, w - k)) for k in range(0, w, TILE)]
        begin += w
    return tiles


def piece(block, rows, tile):
    p, inner, start, span = tile
    ref, row, column = block[0 if len(block) == 1 else p]
    first = start if len(block) == 1 else inner
    return ref.at[pl.ds(row + rows[0], rows[1]), pl.ds(column + first, span)]


class Operands:
    def __init__(self):
        self.pairs = []

    def add(self, array, spec):
        for i, (a, s) in enumerate(self.pairs):
            if a is array and s is spec:
                return i
        self.pairs.append((array, spec))
        return len(self.pairs) - 1

    def block(self, block):
        at = [(self.add(a, VMEM), row, column) for a, row, column in block]
        return lambda refs: tuple((refs[i], row, column) for i, row, column in at)


def scale_code(top):
    return jnp.ceil(jnp.log(jnp.maximum(top, 1e-30)) * (CODE_STEPS * LOG2E))


def encode(value, block, tile):
    size, span = value.shape
    code = scale_code(jnp.max(jnp.abs(value), axis=0, keepdims=True))
    gain = CODE_TOP * jnp.exp(code * (-1.0 / (CODE_STEPS * LOG2E)))
    piece(block, (0, size), tile)[...] = (
        jnp.round(value * gain).astype(jnp.int32).astype(jnp.int16)
    )
    scales = jnp.broadcast_to(code.astype(jnp.int32), (EXTRA_ROWS, span)).astype(jnp.int16)
    piece(block, (size, EXTRA_ROWS), tile)[...] = scales


def decoded(block, size, tile):
    code = piece(block, (size, EXTRA_ROWS), tile)[...].astype(jnp.int32).astype(jnp.float32)
    gain = jnp.exp(code[:1] * (1.0 / (CODE_STEPS * LOG2E))) * (1.0 / CODE_TOP)
    return piece(block, (0, size), tile)[...].astype(jnp.int32).astype(jnp.float32) * gain


def call(kernel, name, operands, out_shape, scratch, room, cost, after=(), held_back=()):
    arrays = [a for a, _ in operands]
    held = sum(math.prod(a.shape) * a.dtype.itemsize for a in [*arrays, *out_shape])

    def body(*refs):
        results = refs[len(arrays) + len(after) + len(held_back) :]
        kernel(refs[: len(arrays)], results[: len(out_shape)] + results[len(out_shape) + len(held_back) :])

    return pl.pallas_call(
        body,
        out_shape=[*out_shape, *(jax.ShapeDtypeStruct(a.shape, a.dtype) for a in held_back)],
        in_specs=[s for _, s in operands] + [ANY] * (len(after) + len(held_back)),
        out_specs=[VMEM] * len(out_shape) + [ANY] * len(held_back),
        input_output_aliases={
            len(arrays) + len(after) + i: len(out_shape) + i for i in range(len(held_back))
        },
        scratch_shapes=scratch,
        compiler_params=pltpu.CompilerParams(vmem_limit_bytes=held + room),
        cost_estimate=pl.CostEstimate(flops=cost, bytes_accessed=cost, transcendentals=0),
        name=name,
    )(*arrays, *after, *held_back)


def labelled(images, labels, after=()):
    size, width = images.shape

    def kernel(ins, outs):
        outs[0][pl.ds(0, size), :] = ins[0][...]
        outs[0][pl.ds(size, EXTRA_ROWS), :] = jnp.zeros((EXTRA_ROWS, width), jnp.bfloat16)
        row = ins[1][...]
        low, high = lax.rem(row, LABEL_BASE), lax.div(row, LABEL_BASE)
        at = lax.broadcasted_iota(jnp.int32, (EXTRA_ROWS, size), 0)
        parts = jnp.where(at == 0, high, jnp.where(at == 1, low, 0)).astype(jnp.float32)
        outs[0][pl.ds(size, EXTRA_ROWS), pl.ds(0, size)] = parts.astype(jnp.bfloat16)

    shape = jax.ShapeDtypeStruct((size + EXTRA_ROWS, width), jnp.bfloat16)
    operands = [(images, VMEM), (labels, VMEM)]
    return call(kernel, "labelled", operands, [shape], [], 2**21, size, after)[0]


def bundled(arrays, cost):
    width = arrays[0].shape[1]

    def kernel(ins, outs):
        first = 0
        for ref in ins:
            outs[0][pl.ds(first, ref.shape[0]), :] = ref[...]
            first += ref.shape[0]

    shape = jax.ShapeDtypeStruct((sum(a.shape[0] for a in arrays), width), jnp.bfloat16)
    operands = [(a, VMEM) for a in arrays]
    return call(kernel, "bundled", operands, [shape], [], 2**21, cost)[0]


def first_row(mask, size):
    owner = (lax.axis_index("blk") ^ mask[0]) * lax.axis_size("grp") + (lax.axis_index("grp") ^ mask[1])
    return owner * size


def keys_of(block, size, mask, is_image):
    if not is_image:
        ids = lax.broadcasted_iota(jnp.int32, (1, size), 1) + first_row(mask, size)
        return ids.astype(jnp.float32)
    parts = piece(block, (size, EXTRA_ROWS), (0, 0, 0, size))[...].astype(jnp.float32)
    return parts[0:1] * LABEL_BASE + parts[1:2]


def gradient_sums(name, size, scalars, x_blocks, y_blocks, masks, x_images, jobs, before, emits, sequence, after=()):
    width = x_blocks[0][0][0].shape[1]
    x_masks, y_masks = masks
    per_tile = TILE // size
    widths = part_widths(width)
    shapes, where = [], {}

    def result(extra, w, dtype):
        shapes.append(jax.ShapeDtypeStruct((size + extra, w), dtype))
        return len(shapes) - 1

    for r, kind in enumerate(emits):
        if kind == "float":
            where[r] = [(result(0, width, jnp.float32), 0, 0)]
        else:
            cut = widths if kind == "parts" else (width,)
            where[r] = [(result(EXTRA_ROWS, w, jnp.int16), 0, 0) for w in cut]
    operands = Operands()
    slope_at, shift_at = [operands.add(s, SMEM) for s in scalars]
    for b in sequence:
        operands.block(b)
    x_views = [operands.block(b) for b in x_blocks]
    y_views = [operands.block(b) for b in y_blocks]
    before_at = {r: operands.add(b, VMEM) for r, b in before.items()}

    def kernel(ins, refs):
        outs, weights = refs[:-1], refs[-1]
        slope, shift = ins[slope_at][0] * LOG2E, ins[shift_at][0] * LOG2E
        x_refs, y_refs = [v(ins) for v in x_views], [v(ins) for v in y_views]

        def stacked(chosen):
            return jnp.concatenate(
                [ref[pl.ds(row, size), pl.ds(column, width)] for ((ref, row, column),) in chosen],
                axis=0,
            )

        for rows, columns in jobs:
            x_all = stacked([x_refs[r] for r in rows])
            keys = [
                jnp.broadcast_to(keys_of(x_refs[r], size, x_masks[r], x_images), (size, size)).T
                for r in rows
            ]
            for n in range(0, len(columns), per_tile):
                chosen = columns[n : n + per_tile]
                other = jnp.concatenate(
                    [keys_of(y_refs[c], size, y_masks[c], not x_images) for c in chosen], axis=1
                )
                scores = lax.dot_general(
                    x_all,
                    stacked([y_refs[c] for c in chosen]),
                    (((1,), (1,)), ((), ())),
                    preferred_element_type=jnp.float32,
                )
                for i in range(len(rows)):
                    z = scores[i * size : (i + 1) * size] * slope + shift
                    sig = 1.0 / (1.0 + jnp.exp2(-z))
                    w = jnp.where(jnp.tile(keys[i], (1, len(chosen))) == other, sig - 1.0, sig)
                    there = pl.ds(n * size, len(chosen) * size)
                    weights[pl.ds(i * size, size), there] = w.astype(jnp.bfloat16)
            for tile in column_tiles(width):
                sums = jnp.dot(
                    weights[pl.ds(0, len(rows) * size), pl.ds(0, len(columns) * size)],
                    jnp.concatenate([piece(y_refs[c], (0, size), tile)[...] for c in columns], axis=0),
                    preferred_element_type=jnp.float32,
                )
                for i, r in enumerate(rows):
                    block = sums[i * size : (i + 1) * size]
                    if r in before_at:
                        block = block + piece(whole(ins[before_at[r]]), (0, size), tile)[...]
                    out = tuple((outs[o], row, column) for o, row, column in where[r])
                    if emits[r] == "float":
                        piece(out, (0, size), tile)[...] = block
                    else:
                        encode(block, out, tile)

    pairs = sum(len(rows) * len(columns) for rows, columns in jobs)
    scratch = [pltpu.VMEM((len(x_blocks) * size, len(y_blocks) * size), jnp.bfloat16)]
    room = len(x_blocks) * len(y_blocks) * size * size * 2 + 8 * 2**20
    results = call(kernel, name, operands.pairs, shapes, scratch, room, pairs * size, after)
    return [tuple(results[o] for o, _, _ in where[r]) for r in range(len(emits))]


def passed_sum(kept, received, part, held_back=(), after=()):
    size, width = kept.shape
    operands = Operands()
    kept_at = operands.add(kept, VMEM)
    views = [operands.block(b if part is None or len(b) == 1 else (b[part],) * 2) for b in received]

    def kernel(ins, outs):
        for tile in column_tiles(width):
            p, inner, _, span = tile
            if part is None or p == part:
                total = piece(whole(ins[kept_at]), (0, size), tile)[...]
                for view in views:
                    total = total + decoded(view(ins), size, tile)
                encode(total, whole(outs[0]), tile if part is None else (0, 0, inner, span))

    cut = width if part is None else part_widths(width)[part]
    shape = jax.ShapeDtypeStruct((size + EXTRA_ROWS, cut), jnp.int16)
    return call(kernel, "passed_sum", operands.pairs, [shape], [], 2**21, size, after, held_back)


def output_sums(sharpness, sums):
    size, width = sums[0][0].shape
    operands = Operands()
    sharpness_at = operands.add(sharpness, SMEM)
    views = [(operands.add(kept, VMEM), [operands.block(b) for b in blocks]) for kept, blocks in sums]

    def kernel(ins, outs):
        for out, (kept_at, received) in zip(outs, views):
            for tile in column_tiles(width):
                total = piece(whole(ins[kept_at]), (0, size), tile)[...]
                for view in received:
                    total = total + decoded(view(ins), size, tile)
                piece(whole(out), (0, size), tile)[...] = total * ins[sharpness_at][0]

    shapes = [jax.ShapeDtypeStruct((size, width), jnp.float32)] * len(sums)
    return call(kernel, "output_sums", operands.pairs, shapes, [], 2**21, size)


def swapped(array, step):
    axis, bit = step
    return lax.ppermute(array, axis, [(i, i ^ bit) for i in range(lax.axis_size(axis))])


def scattered(kept, coded, steps, after):
    def sent(block, step):
        return [(swapped(p, step), 0, 0) for p in block]

    half, waiting = len(kept), coded[0]
    received = [[]] + [[sent(c, steps[-1])] for c in coded[1:]]
    for s in reversed(range(len(steps) - 1)):
        for m in reversed(range(1 << s)):
            n = m | 1 << s
            block = passed_sum(kept[n], received[n], None, waiting, after)
            after = block[:1]
            if n == half - 1:
                block, *waiting = block
                received[0].append(sent(waiting, steps[-1]))
                waiting, block = (), [block]
            received[m].append(sent(block, steps[s]))
    return (kept[0], received[0][::-1]), after


def in_order(arrays):
    return call(lambda *refs: None, "held", [], [], [], 2**21, 1, (), arrays)


def bit_steps(axis):
    return [(axis, 1 << k) for k in range(int(math.log2(lax.axis_size(axis))))]


def owner_masks(steps):
    masks = [(0, 0)]
    for axis, bit in steps:
        masks = masks + [(b ^ bit, g) if axis == "blk" else (b, g ^ bit) for b, g in masks]
    return masks


def per_device(
    picture_vectors, caption_vectors, matching_caption, sharpness_parameter, additive_intercept
):
    scalars = (sharpness_parameter, additive_intercept)
    size = picture_vectors.shape[0]
    core, *grp_steps = bit_steps("grp")
    every = grp_steps + bit_steps("blk")
    steps = [every[0::2], every[1::2]]
    assert len(steps[0]) == len(steps[1]) >= 2
    masks = [owner_masks(s + [core]) for s in steps]
    count = 1 << len(steps[0])
    half = count // 2
    early, late = list(range(half + 1)), list(range(half + 1, count))
    labels = matching_caption[None, :]
    (first_texts,) = in_order([swapped(caption_vectors, steps[1][0])])
    first_images = [swapped(a, steps[0][0]) for a in (picture_vectors, labels)]
    arrays = [{0: labelled(picture_vectors, labels), 1: labelled(*first_images, [first_texts])}, {0: caption_vectors, 1: first_texts}]
    for i in range(1, len(steps[0])):
        for k in (1, 0):
            for m in range(1 << i):
                arrays[k][m | 1 << i] = swapped(arrays[k][m], steps[k][i])
    blocks = [[whole(a[m]) for m in range(count)] for a in arrays]
    others = [{}, {}]
    both = bundled([arrays[1][1], arrays[0][1]], BUNDLE_COST)
    rest = [m for m in early if m != 1]
    both = swapped(bundled([both] + [arrays[k][m] for m in rest for k in (1, 0)], size), core)
    for i, m in enumerate([1] + rest):
        row = i * (2 * size + EXTRA_ROWS)
        others[1][m], others[0][m] = ((both, row, 0),), ((both, row + size, 0),)

    def sums(name, kind, rows, columns, cores, jobs, before, emits, after=()):
        other = 1 - kind
        x_blocks = [blocks[kind][m] for m in rows]
        y_blocks = [(blocks, others)[c][other][m] for c in cores for m in columns]
        x_masks = [masks[kind][m] for m in rows]
        y_masks = [masks[other][m + c * count] for c in cores for m in columns]
        return gradient_sums(
            name,
            size,
            scalars,
            x_blocks,
            y_blocks,
            (x_masks, y_masks),
            kind == 0,
            jobs,
            before,
            emits,
            [blocks[k][m] for m in rows[1:] + rows[:1] for k in (1, 0)],
            after,
        )

    before = []
    for k in range(2):
        jobs = [(early, list(range(2 * len(early))))]
        results = sums("early_sums", k, early, early, (0, 1), jobs, {}, ["float"] * len(early))
        before.append({m: s for m, (s,) in zip(early, results)})
    arrays = [[b[m][0][0] for m in late] for b in blocks[::-1]]
    arrays, before = lax.optimization_barrier((arrays, before))
    for k in (1, 0):
        for m, a in zip(late, arrays[1 - k]):
            blocks[k][m] = whole(a)
            others[k][m] = whole(swapped(a, core))
    every, after = list(range(count)), ()
    coded, kept = [[None] * half, [None] * half], [None, None]
    for k in (1, 0):
        jobs, emits = [(list(range(len(late))), list(range(2 * count)))], ["whole"] * len(late)
        coded[k][1:] = sums("late_rows", k, late, every, (0, 1), jobs, {}, emits, after)
        after = coded[k][1]
    for k in (1, 0):
        jobs, emits = [(early, list(range(2 * len(late))))], ["float"] * half + ["whole"]
        *whole_sums, coded[k][0] = sums("late_columns", k, early, late, (0, 1), jobs, before[k], emits, after)
        kept[k], after = [s for (s,) in whole_sums], coded[k][0]
    texts, after = scattered(kept[1], coded[1], steps[1], ())
    images, _ = scattered(kept[0], coded[0], steps[0], after)
    kept_texts, blocks_in = texts
    blocks_in = [whole(a) for a in in_order([a for ((a, _, _),) in blocks_in[::-1]])]
    return tuple(output_sums(scalars[0], [images, (kept_texts, blocks_in)]))


def solution(mesh):
    placed = (P(("blk", "grp"), None), P(("blk", "grp"), None), P(("blk", "grp")), P(), P())
    return jax.shard_map(
        per_device,
        mesh=mesh,
        in_specs=placed,
        out_specs=(P(("blk", "grp"), None), P(("blk", "grp"), None)),
        check_vma=False,
    )
```

```python
import math

import jax
import jax.numpy as jnp
from jax import lax
from jax.experimental import pallas as pl
from jax.experimental.pallas import tpu as pltpu
from jax.sharding import PartitionSpec as P

LOG2E = 1.4426950408889634
CODE_TOP = 32000.0
CODE_STEPS = 32.0
EXTRA_ROWS = 8
LABEL_BASE = 128
TILE = 256
LANES = 128
BUNDLE_COST = 6 * 10**8
SMEM = pl.BlockSpec(memory_space=pltpu.SMEM)
VMEM = pl.BlockSpec(memory_space=pltpu.VMEM)
ANY = pl.BlockSpec(memory_space=pl.ANY)


def whole(array):
    return ((array, 0, 0),)


def part_widths(width):
    first = (width // LANES + 1) // 2 * LANES
    return (first, width - first)


def column_tiles(width):
    tiles, begin = [], 0
    for p, w in enumerate(part_widths(width)):
        tiles += [(p, k, begin + k, min(TILE, w - k)) for k in range(0, w, TILE)]
        begin += w
    return tiles


def piece(block, rows, tile):
    p, inner, start, span = tile
    ref, row, column = block[0 if len(block) == 1 else p]
    first = start if len(block) == 1 else inner
    return ref.at[pl.ds(row + rows[0], rows[1]), pl.ds(column + first, span)]


class Operands:
    def __init__(self):
        self.pairs = []

    def add(self, array, spec):
        for i, (a, s) in enumerate(self.pairs):
            if a is array and s is spec:
                return i
        self.pairs.append((array, spec))
        return len(self.pairs) - 1

    def block(self, block):
        at = [(self.add(a, VMEM), row, column) for a, row, column in block]
        return lambda refs: tuple((refs[i], row, column) for i, row, column in at)


def scale_code(top):
    return jnp.ceil(jnp.log(jnp.maximum(top, 1e-30)) * (CODE_STEPS * LOG2E))


def encode(value, block, tile):
    size, span = value.shape
    code = scale_code(jnp.max(jnp.abs(value), axis=0, keepdims=True))
    gain = CODE_TOP * jnp.exp(code * (-1.0 / (CODE_STEPS * LOG2E)))
    piece(block, (0, size), tile)[...] = (
        jnp.round(value * gain).astype(jnp.int32).astype(jnp.int16)
    )
    scales = jnp.broadcast_to(code.astype(jnp.int32), (EXTRA_ROWS, span)).astype(jnp.int16)
    piece(block, (size, EXTRA_ROWS), tile)[...] = scales


def decoded(block, size, tile):
    code = piece(block, (size, EXTRA_ROWS), tile)[...].astype(jnp.int32).astype(jnp.float32)
    gain = jnp.exp(code[:1] * (1.0 / (CODE_STEPS * LOG2E))) * (1.0 / CODE_TOP)
    return piece(block, (0, size), tile)[...].astype(jnp.int32).astype(jnp.float32) * gain


def call(kernel, name, operands, out_shape, scratch, room, cost, after=(), held_back=()):
    arrays = [a for a, _ in operands]
    held = sum(math.prod(a.shape) * a.dtype.itemsize for a in [*arrays, *out_shape])

    def body(*refs):
        results = refs[len(arrays) + len(after) + len(held_back) :]
        kernel(refs[: len(arrays)], results[: len(out_shape)] + results[len(out_shape) + len(held_back) :])

    return pl.pallas_call(
        body,
        out_shape=[*out_shape, *(jax.ShapeDtypeStruct(a.shape, a.dtype) for a in held_back)],
        in_specs=[s for _, s in operands] + [ANY] * (len(after) + len(held_back)),
        out_specs=[VMEM] * len(out_shape) + [ANY] * len(held_back),
        input_output_aliases={
            len(arrays) + len(after) + i: len(out_shape) + i for i in range(len(held_back))
        },
        scratch_shapes=scratch,
        compiler_params=pltpu.CompilerParams(vmem_limit_bytes=held + room),
        cost_estimate=pl.CostEstimate(flops=cost, bytes_accessed=cost, transcendentals=0),
        name=name,
    )(*arrays, *after, *held_back)


def labelled(images, labels, after=()):
    size, width = images.shape

    def kernel(ins, outs):
        outs[0][pl.ds(0, size), :] = ins[0][...]
        outs[0][pl.ds(size, EXTRA_ROWS), :] = jnp.zeros((EXTRA_ROWS, width), jnp.bfloat16)
        row = ins[1][...]
        low, high = lax.rem(row, LABEL_BASE), lax.div(row, LABEL_BASE)
        at = lax.broadcasted_iota(jnp.int32, (EXTRA_ROWS, size), 0)
        parts = jnp.where(at == 0, high, jnp.where(at == 1, low, 0)).astype(jnp.float32)
        outs[0][pl.ds(size, EXTRA_ROWS), pl.ds(0, size)] = parts.astype(jnp.bfloat16)

    shape = jax.ShapeDtypeStruct((size + EXTRA_ROWS, width), jnp.bfloat16)
    operands = [(images, VMEM), (labels, VMEM)]
    return call(kernel, "labelled", operands, [shape], [], 2**21, size, after)[0]


def bundled(arrays, cost):
    width = arrays[0].shape[1]

    def kernel(ins, outs):
        first = 0
        for ref in ins:
            outs[0][pl.ds(first, ref.shape[0]), :] = ref[...]
            first += ref.shape[0]

    shape = jax.ShapeDtypeStruct((sum(a.shape[0] for a in arrays), width), jnp.bfloat16)
    operands = [(a, VMEM) for a in arrays]
    return call(kernel, "bundled", operands, [shape], [], 2**21, cost)[0]


def first_row(mask, size):
    owner = (lax.axis_index("blk") ^ mask[0]) * lax.axis_size("grp") + (lax.axis_index("grp") ^ mask[1])
    return owner * size


def keys_of(block, size, mask, is_image):
    if not is_image:
        ids = lax.broadcasted_iota(jnp.int32, (1, size), 1) + first_row(mask, size)
        return ids.astype(jnp.float32)
    parts = piece(block, (size, EXTRA_ROWS), (0, 0, 0, size))[...].astype(jnp.float32)
    return parts[0:1] * LABEL_BASE + parts[1:2]


def gradient_sums(name, size, scalars, x_blocks, y_blocks, masks, x_images, jobs, before, emits, sequence, after=()):
    width = x_blocks[0][0][0].shape[1]
    x_masks, y_masks = masks
    per_tile = TILE // size
    widths = part_widths(width)
    shapes, where = [], {}

    def result(extra, w, dtype):
        shapes.append(jax.ShapeDtypeStruct((size + extra, w), dtype))
        return len(shapes) - 1

    for r, kind in enumerate(emits):
        if kind == "float":
            where[r] = [(result(0, width, jnp.float32), 0, 0)]
        else:
            cut = widths if kind == "parts" else (width,)
            where[r] = [(result(EXTRA_ROWS, w, jnp.int16), 0, 0) for w in cut]
    operands = Operands()
    slope_at, shift_at = [operands.add(s, SMEM) for s in scalars]
    for b in sequence:
        operands.block(b)
    x_views = [operands.block(b) for b in x_blocks]
    y_views = [operands.block(b) for b in y_blocks]
    before_at = {r: operands.add(b, VMEM) for r, b in before.items()}

    def kernel(ins, refs):
        outs, weights = refs[:-1], refs[-1]
        slope, shift = ins[slope_at][0] * LOG2E, ins[shift_at][0] * LOG2E
        x_refs, y_refs = [v(ins) for v in x_views], [v(ins) for v in y_views]

        def stacked(chosen):
            return jnp.concatenate(
                [ref[pl.ds(row, size), pl.ds(column, width)] for ((ref, row, column),) in chosen],
                axis=0,
            )

        for rows, columns in jobs:
            x_all = stacked([x_refs[r] for r in rows])
            keys = [
                jnp.broadcast_to(keys_of(x_refs[r], size, x_masks[r], x_images), (size, size)).T
                for r in rows
            ]
            for n in range(0, len(columns), per_tile):
                chosen = columns[n : n + per_tile]
                other = jnp.concatenate(
                    [keys_of(y_refs[c], size, y_masks[c], not x_images) for c in chosen], axis=1
                )
                scores = lax.dot_general(
                    x_all,
                    stacked([y_refs[c] for c in chosen]),
                    (((1,), (1,)), ((), ())),
                    preferred_element_type=jnp.float32,
                )
                for i in range(len(rows)):
                    z = scores[i * size : (i + 1) * size] * slope + shift
                    sig = 1.0 / (1.0 + jnp.exp2(-z))
                    w = jnp.where(jnp.tile(keys[i], (1, len(chosen))) == other, sig - 1.0, sig)
                    there = pl.ds(n * size, len(chosen) * size)
                    weights[pl.ds(i * size, size), there] = w.astype(jnp.bfloat16)
            for tile in column_tiles(width):
                sums = jnp.dot(
                    weights[pl.ds(0, len(rows) * size), pl.ds(0, len(columns) * size)],
                    jnp.concatenate([piece(y_refs[c], (0, size), tile)[...] for c in columns], axis=0),
                    preferred_element_type=jnp.float32,
                )
                for i, r in enumerate(rows):
                    block = sums[i * size : (i + 1) * size]
                    if r in before_at:
                        block = block + piece(whole(ins[before_at[r]]), (0, size), tile)[...]
                    out = tuple((outs[o], row, column) for o, row, column in where[r])
                    if emits[r] == "float":
                        piece(out, (0, size), tile)[...] = block
                    else:
                        encode(block, out, tile)

    pairs = sum(len(rows) * len(columns) for rows, columns in jobs)
    scratch = [pltpu.VMEM((len(x_blocks) * size, len(y_blocks) * size), jnp.bfloat16)]
    room = len(x_blocks) * len(y_blocks) * size * size * 2 + 8 * 2**20
    results = call(kernel, name, operands.pairs, shapes, scratch, room, pairs * size, after)
    return [tuple(results[o] for o, _, _ in where[r]) for r in range(len(emits))]


def passed_sum(kept, received, part, held_back=(), after=()):
    size, width = kept.shape
    operands = Operands()
    kept_at = operands.add(kept, VMEM)
    views = [operands.block(b if part is None or len(b) == 1 else (b[part],) * 2) for b in received]

    def kernel(ins, outs):
        for tile in column_tiles(width):
            p, inner, _, span = tile
            if part is None or p == part:
                total = piece(whole(ins[kept_at]), (0, size), tile)[...]
                for view in views:
                    total = total + decoded(view(ins), size, tile)
                encode(total, whole(outs[0]), tile if part is None else (0, 0, inner, span))

    cut = width if part is None else part_widths(width)[part]
    shape = jax.ShapeDtypeStruct((size + EXTRA_ROWS, cut), jnp.int16)
    return call(kernel, "passed_sum", operands.pairs, [shape], [], 2**21, size, after, held_back)


def output_sums(sharpness, sums):
    size, width = sums[0][0].shape
    operands = Operands()
    sharpness_at = operands.add(sharpness, SMEM)
    views = [(operands.add(kept, VMEM), [operands.block(b) for b in blocks]) for kept, blocks in sums]

    def kernel(ins, outs):
        for out, (kept_at, received) in zip(outs, views):
            for tile in column_tiles(width):
                total = piece(whole(ins[kept_at]), (0, size), tile)[...]
                for view in received:
                    total = total + decoded(view(ins), size, tile)
                piece(whole(out), (0, size), tile)[...] = total * ins[sharpness_at][0]

    shapes = [jax.ShapeDtypeStruct((size, width), jnp.float32)] * len(sums)
    return call(kernel, "output_sums", operands.pairs, shapes, [], 2**21, size)


def swapped(array, step):
    axis, bit = step
    return lax.ppermute(array, axis, [(i, i ^ bit) for i in range(lax.axis_size(axis))])


def scattered(kept, coded, steps, after):
    def sent(array, step):
        return (swapped(array, step), 0, 0)

    half = len(kept)
    received = [[]] + [[(sent(c[0], steps[-1]),)] for c in coded[1:]]
    waiting, last = [c[1] for c in coded[1:]], [coded[0][0]]
    for s in reversed(range(len(steps) - 1)):
        for m in reversed(range(1 << s)):
            n = m | 1 << s
            first, *begun = passed_sum(kept[n], received[n], 0, waiting)
            for r, c in zip(received[1:], begun):
                r[0] = r[0] + (sent(c, steps[-1]),)
            first = sent(first, steps[s])
            second, *ended = passed_sum(kept[n], received[n], 1, last, [first[0], *after])
            received[0] += [(sent(c, steps[-1]),) for c in ended]
            received[m].append((first, sent(second, steps[s])))
            waiting, last, after = (), (), [second]
    return kept[0], received[0], after


def in_order(arrays):
    return call(lambda *refs: None, "held", [], [], [], 2**21, 1, (), arrays)


def bit_steps(axis):
    return [(axis, 1 << k) for k in range(int(math.log2(lax.axis_size(axis))))]


def owner_masks(steps):
    masks = [(0, 0)]
    for axis, bit in steps:
        masks = masks + [(b ^ bit, g) if axis == "blk" else (b, g ^ bit) for b, g in masks]
    return masks


def per_device(
    picture_vectors, caption_vectors, matching_caption, sharpness_parameter, additive_intercept
):
    scalars = (sharpness_parameter, additive_intercept)
    size = picture_vectors.shape[0]
    core, *grp_steps = bit_steps("grp")
    every = grp_steps + bit_steps("blk")
    steps = [every[0::2], every[1::2]]
    assert len(steps[0]) == len(steps[1]) >= 2
    masks = [owner_masks(s + [core]) for s in steps]
    count = 1 << len(steps[0])
    half = count // 2
    early, late = list(range(half + 1)), list(range(half + 1, count))
    labels = matching_caption[None, :]
    (first_texts,) = in_order([swapped(caption_vectors, steps[1][0])])
    first_images = [swapped(a, steps[0][0]) for a in (picture_vectors, labels)]
    arrays = [{0: labelled(picture_vectors, labels), 1: labelled(*first_images, [first_texts])}, {0: caption_vectors, 1: first_texts}]
    for i in range(1, len(steps[0])):
        for k in (1, 0):
            for m in range(1 << i):
                arrays[k][m | 1 << i] = swapped(arrays[k][m], steps[k][i])
    blocks = [[whole(a[m]) for m in range(count)] for a in arrays]
    others = [{}, {}]
    both = bundled([arrays[1][1], arrays[0][1]], BUNDLE_COST)
    rest = [m for m in early if m != 1]
    both = swapped(bundled([both] + [arrays[k][m] for m in rest for k in (1, 0)], size), core)
    for i, m in enumerate([1] + rest):
        row = i * (2 * size + EXTRA_ROWS)
        others[1][m], others[0][m] = ((both, row, 0),), ((both, row + size, 0),)

    def sums(name, kind, rows, columns, cores, jobs, before, emits, after=()):
        other = 1 - kind
        x_blocks = [blocks[kind][m] for m in rows]
        y_blocks = [(blocks, others)[c][other][m] for c in cores for m in columns]
        x_masks = [masks[kind][m] for m in rows]
        y_masks = [masks[other][m + c * count] for c in cores for m in columns]
        return gradient_sums(
            name,
            size,
            scalars,
            x_blocks,
            y_blocks,
            (x_masks, y_masks),
            kind == 0,
            jobs,
            before,
            emits,
            [blocks[k][m] for m in rows[1:] + rows[:1] for k in (1, 0)],
            after,
        )

    before = []
    for k in range(2):
        jobs = [(early, list(range(2 * len(early))))]
        results = sums("early_sums", k, early, early, (0, 1), jobs, {}, ["float"] * len(early))
        before.append({m: s for m, (s,) in zip(early, results)})
    arrays = [[b[m][0][0] for m in late] for b in blocks[::-1]]
    arrays, before = lax.optimization_barrier((arrays, before))
    for k in (1, 0):
        for m, a in zip(late, arrays[1 - k]):
            blocks[k][m] = whole(a)
            others[k][m] = whole(swapped(a, core))
    every, after = list(range(count)), ()
    coded, kept = [[None] * half, [None] * half], [None, None]
    for k in (1, 0):
        jobs, emits = [(list(range(len(late))), list(range(2 * count)))], ["parts"] * len(late)
        coded[k][1:] = sums("late_rows", k, late, every, (0, 1), jobs, {}, emits, after)
        after = coded[k][1]
    for k in (1, 0):
        jobs, emits = [(early, list(range(2 * len(late))))], ["float"] * half + ["whole"]
        *whole_sums, coded[k][0] = sums("late_columns", k, early, late, (0, 1), jobs, before[k], emits, after)
        kept[k], after = [s for (s,) in whole_sums], coded[k][0]
    kept_texts, text_blocks, after = scattered(kept[1], coded[1], steps[1], ())
    kept_images, image_blocks, _ = scattered(kept[0], coded[0], steps[0], after)
    parts = iter(in_order([part[0] for b in text_blocks for part in b]))
    text_blocks = [tuple((next(parts), 0, 0) for _ in b) for b in text_blocks]
    return tuple(output_sums(scalars[0], [(kept_images, image_blocks), (kept_texts, text_blocks)]))


def solution(mesh):
    placed = (P(("blk", "grp"), None), P(("blk", "grp"), None), P(("blk", "grp")), P(), P())
    return jax.shard_map(
        per_device,
        mesh=mesh,
        in_specs=placed,
        out_specs=(P(("blk", "grp"), None), P(("blk", "grp"), None)),
        check_vma=False,
    )
```

```python
import math

import jax
import jax.numpy as jnp
from jax import lax
from jax.experimental import pallas as pl
from jax.experimental.pallas import tpu as pltpu
from jax.sharding import PartitionSpec as P

LOG2E = 1.4426950408889634
CODE_TOP = 32000.0
CODE_STEPS = 32.0
EXTRA_ROWS = 8
LABEL_BASE = 128
TILE = 256
LANES = 128
BUNDLE_COST = 6 * 10**8
SMEM = pl.BlockSpec(memory_space=pltpu.SMEM)
VMEM = pl.BlockSpec(memory_space=pltpu.VMEM)
ANY = pl.BlockSpec(memory_space=pl.ANY)


def whole(array):
    return ((array, 0, 0),)


def part_widths(width):
    first = min(3 * TILE, width - LANES)
    return (first, width - first)


def column_tiles(width):
    tiles, begin = [], 0
    for p, w in enumerate(part_widths(width)):
        tiles += [(p, k, begin + k, min(TILE, w - k)) for k in range(0, w, TILE)]
        begin += w
    return tiles


def piece(block, rows, tile):
    p, inner, start, span = tile
    ref, row, column = block[0 if len(block) == 1 else p]
    first = start if len(block) == 1 else inner
    return ref.at[pl.ds(row + rows[0], rows[1]), pl.ds(column + first, span)]


class Operands:
    def __init__(self):
        self.pairs = []

    def add(self, array, spec):
        for i, (a, s) in enumerate(self.pairs):
            if a is array and s is spec:
                return i
        self.pairs.append((array, spec))
        return len(self.pairs) - 1

    def block(self, block):
        at = [(self.add(a, VMEM), row, column) for a, row, column in block]
        return lambda refs: tuple((refs[i], row, column) for i, row, column in at)


def scale_code(top):
    return jnp.ceil(jnp.log(jnp.maximum(top, 1e-30)) * (CODE_STEPS * LOG2E))


def encode(value, block, tile):
    size, span = value.shape
    code = scale_code(jnp.max(jnp.abs(value), axis=0, keepdims=True))
    gain = CODE_TOP * jnp.exp(code * (-1.0 / (CODE_STEPS * LOG2E)))
    piece(block, (0, size), tile)[...] = (
        jnp.round(value * gain).astype(jnp.int32).astype(jnp.int16)
    )
    scales = jnp.broadcast_to(code.astype(jnp.int32), (EXTRA_ROWS, span)).astype(jnp.int16)
    piece(block, (size, EXTRA_ROWS), tile)[...] = scales


def decoded(block, size, tile):
    code = piece(block, (size, EXTRA_ROWS), tile)[...].astype(jnp.int32).astype(jnp.float32)
    gain = jnp.exp(code[:1] * (1.0 / (CODE_STEPS * LOG2E))) * (1.0 / CODE_TOP)
    return piece(block, (0, size), tile)[...].astype(jnp.int32).astype(jnp.float32) * gain


def call(kernel, name, operands, out_shape, scratch, room, cost, after=(), held_back=()):
    arrays = [a for a, _ in operands]
    held = sum(math.prod(a.shape) * a.dtype.itemsize for a in [*arrays, *out_shape])

    def body(*refs):
        results = refs[len(arrays) + len(after) + len(held_back) :]
        kernel(refs[: len(arrays)], results[: len(out_shape)] + results[len(out_shape) + len(held_back) :])

    return pl.pallas_call(
        body,
        out_shape=[*out_shape, *(jax.ShapeDtypeStruct(a.shape, a.dtype) for a in held_back)],
        in_specs=[s for _, s in operands] + [ANY] * (len(after) + len(held_back)),
        out_specs=[VMEM] * len(out_shape) + [ANY] * len(held_back),
        input_output_aliases={
            len(arrays) + len(after) + i: len(out_shape) + i for i in range(len(held_back))
        },
        scratch_shapes=scratch,
        compiler_params=pltpu.CompilerParams(vmem_limit_bytes=held + room),
        cost_estimate=pl.CostEstimate(flops=cost, bytes_accessed=cost, transcendentals=0),
        name=name,
    )(*arrays, *after, *held_back)


def labelled(images, labels, after=()):
    size, width = images.shape

    def kernel(ins, outs):
        outs[0][pl.ds(0, size), :] = ins[0][...]
        outs[0][pl.ds(size, EXTRA_ROWS), :] = jnp.zeros((EXTRA_ROWS, width), jnp.bfloat16)
        row = ins[1][...]
        low, high = lax.rem(row, LABEL_BASE), lax.div(row, LABEL_BASE)
        at = lax.broadcasted_iota(jnp.int32, (EXTRA_ROWS, size), 0)
        parts = jnp.where(at == 0, high, jnp.where(at == 1, low, 0)).astype(jnp.float32)
        outs[0][pl.ds(size, EXTRA_ROWS), pl.ds(0, size)] = parts.astype(jnp.bfloat16)

    shape = jax.ShapeDtypeStruct((size + EXTRA_ROWS, width), jnp.bfloat16)
    operands = [(images, VMEM), (labels, VMEM)]
    return call(kernel, "labelled", operands, [shape], [], 2**21, size, after)[0]


def bundled(arrays, cost):
    width = arrays[0].shape[1]

    def kernel(ins, outs):
        first = 0
        for ref in ins:
            outs[0][pl.ds(first, ref.shape[0]), :] = ref[...]
            first += ref.shape[0]

    shape = jax.ShapeDtypeStruct((sum(a.shape[0] for a in arrays), width), jnp.bfloat16)
    operands = [(a, VMEM) for a in arrays]
    return call(kernel, "bundled", operands, [shape], [], 2**21, cost)[0]


def first_row(mask, size):
    owner = (lax.axis_index("blk") ^ mask[0]) * lax.axis_size("grp") + (lax.axis_index("grp") ^ mask[1])
    return owner * size


def keys_of(block, size, mask, is_image):
    if not is_image:
        ids = lax.broadcasted_iota(jnp.int32, (1, size), 1) + first_row(mask, size)
        return ids.astype(jnp.float32)
    parts = piece(block, (size, EXTRA_ROWS), (0, 0, 0, size))[...].astype(jnp.float32)
    return parts[0:1] * LABEL_BASE + parts[1:2]


def gradient_sums(name, size, scalars, x_blocks, y_blocks, masks, x_images, jobs, before, emits, sequence, after=()):
    width = x_blocks[0][0][0].shape[1]
    x_masks, y_masks = masks
    per_tile = TILE // size
    widths = part_widths(width)
    shapes, where = [], {}

    def result(extra, w, dtype):
        shapes.append(jax.ShapeDtypeStruct((size + extra, w), dtype))
        return len(shapes) - 1

    for r, kind in enumerate(emits):
        if kind == "float":
            where[r] = [(result(0, width, jnp.float32), 0, 0)]
        else:
            cut = widths if kind == "parts" else (width,)
            where[r] = [(result(EXTRA_ROWS, w, jnp.int16), 0, 0) for w in cut]
    operands = Operands()
    slope_at, shift_at = [operands.add(s, SMEM) for s in scalars]
    for b in sequence:
        operands.block(b)
    x_views = [operands.block(b) for b in x_blocks]
    y_views = [operands.block(b) for b in y_blocks]
    before_at = {r: operands.add(b, VMEM) for r, b in before.items()}

    def kernel(ins, refs):
        outs, weights = refs[:-1], refs[-1]
        slope, shift = ins[slope_at][0] * LOG2E, ins[shift_at][0] * LOG2E
        x_refs, y_refs = [v(ins) for v in x_views], [v(ins) for v in y_views]

        def stacked(chosen):
            return jnp.concatenate(
                [ref[pl.ds(row, size), pl.ds(column, width)] for ((ref, row, column),) in chosen],
                axis=0,
            )

        for rows, columns in jobs:
            x_all = stacked([x_refs[r] for r in rows])
            keys = [
                jnp.broadcast_to(keys_of(x_refs[r], size, x_masks[r], x_images), (size, size)).T
                for r in rows
            ]
            for n in range(0, len(columns), per_tile):
                chosen = columns[n : n + per_tile]
                other = jnp.concatenate(
                    [keys_of(y_refs[c], size, y_masks[c], not x_images) for c in chosen], axis=1
                )
                scores = lax.dot_general(
                    x_all,
                    stacked([y_refs[c] for c in chosen]),
                    (((1,), (1,)), ((), ())),
                    preferred_element_type=jnp.float32,
                )
                for i in range(len(rows)):
                    z = scores[i * size : (i + 1) * size] * slope + shift
                    sig = 1.0 / (1.0 + jnp.exp2(-z))
                    w = jnp.where(jnp.tile(keys[i], (1, len(chosen))) == other, sig - 1.0, sig)
                    there = pl.ds(n * size, len(chosen) * size)
                    weights[pl.ds(i * size, size), there] = w.astype(jnp.bfloat16)
            for tile in column_tiles(width):
                sums = jnp.dot(
                    weights[pl.ds(0, len(rows) * size), pl.ds(0, len(columns) * size)],
                    jnp.concatenate([piece(y_refs[c], (0, size), tile)[...] for c in columns], axis=0),
                    preferred_element_type=jnp.float32,
                )
                for i, r in enumerate(rows):
                    block = sums[i * size : (i + 1) * size]
                    if r in before_at:
                        block = block + piece(whole(ins[before_at[r]]), (0, size), tile)[...]
                    out = tuple((outs[o], row, column) for o, row, column in where[r])
                    if emits[r] == "float":
                        piece(out, (0, size), tile)[...] = block
                    else:
                        encode(block, out, tile)

    pairs = sum(len(rows) * len(columns) for rows, columns in jobs)
    scratch = [pltpu.VMEM((len(x_blocks) * size, len(y_blocks) * size), jnp.bfloat16)]
    room = len(x_blocks) * len(y_blocks) * size * size * 2 + 8 * 2**20
    results = call(kernel, name, operands.pairs, shapes, scratch, room, pairs * size, after)
    return [tuple(results[o] for o, _, _ in where[r]) for r in range(len(emits))]


def passed_sum(kept, received, part, held_back=(), after=()):
    size, width = kept.shape
    operands = Operands()
    kept_at = operands.add(kept, VMEM)
    views = [operands.block(b if part is None or len(b) == 1 else (b[part],) * 2) for b in received]

    def kernel(ins, outs):
        for tile in column_tiles(width):
            p, inner, _, span = tile
            if part is None or p == part:
                total = piece(whole(ins[kept_at]), (0, size), tile)[...]
                for view in views:
                    total = total + decoded(view(ins), size, tile)
                encode(total, whole(outs[0]), tile if part is None else (0, 0, inner, span))

    cut = width if part is None else part_widths(width)[part]
    shape = jax.ShapeDtypeStruct((size + EXTRA_ROWS, cut), jnp.int16)
    return call(kernel, "passed_sum", operands.pairs, [shape], [], 2**21, size, after, held_back)


def output_sums(sharpness, sums):
    size, width = sums[0][0].shape
    operands = Operands()
    sharpness_at = operands.add(sharpness, SMEM)
    views = [(operands.add(kept, VMEM), [operands.block(b) for b in blocks]) for kept, blocks in sums]

    def kernel(ins, outs):
        for out, (kept_at, received) in zip(outs, views):
            for tile in column_tiles(width):
                total = piece(whole(ins[kept_at]), (0, size), tile)[...]
                for view in received:
                    total = total + decoded(view(ins), size, tile)
                piece(whole(out), (0, size), tile)[...] = total * ins[sharpness_at][0]

    shapes = [jax.ShapeDtypeStruct((size, width), jnp.float32)] * len(sums)
    return call(kernel, "output_sums", operands.pairs, shapes, [], 2**21, size)


def swapped(array, step):
    axis, bit = step
    return lax.ppermute(array, axis, [(i, i ^ bit) for i in range(lax.axis_size(axis))])


def scattered(kept, coded, steps, after):
    def sent(block, step):
        return [(swapped(p, step), 0, 0) for p in block]

    half, waiting = len(kept), coded[0]
    received = [[]] + [[sent(c, steps[-1])] for c in coded[1:]]
    for s in reversed(range(len(steps) - 1)):
        for m in reversed(range(1 << s)):
            n = m | 1 << s
            block = passed_sum(kept[n], received[n], None, waiting, after)
            after = block[:1]
            if n == half - 1:
                block, *waiting = block
                received[0].append(sent(waiting, steps[-1]))
                waiting, block = (), [block]
            received[m].append(sent(block, steps[s]))
    return (kept[0], received[0][::-1]), after


def in_order(arrays, after=()):
    return call(lambda *refs: None, "held", [], [], [], 2**21, 1, after, arrays)


def bit_steps(axis):
    return [(axis, 1 << k) for k in range(int(math.log2(lax.axis_size(axis))))]


def owner_masks(steps):
    masks = [(0, 0)]
    for axis, bit in steps:
        masks = masks + [(b ^ bit, g) if axis == "blk" else (b, g ^ bit) for b, g in masks]
    return masks


def per_device(
    picture_vectors, caption_vectors, matching_caption, sharpness_parameter, additive_intercept
):
    scalars = (sharpness_parameter, additive_intercept)
    size = picture_vectors.shape[0]
    core, *grp_steps = bit_steps("grp")
    every = grp_steps + bit_steps("blk")
    steps = [every[0::2], every[1::2]]
    assert len(steps[0]) == len(steps[1]) >= 2
    masks = [owner_masks(s + [core]) for s in steps]
    count = 1 << len(steps[0])
    half = count // 2
    early, late = list(range(half + 1)), list(range(half + 1, count))
    labels = matching_caption[None, :]
    (first_texts,) = in_order([swapped(caption_vectors, steps[1][0])])
    first_images = [swapped(a, steps[0][0]) for a in (picture_vectors, labels)]
    arrays = [{0: labelled(picture_vectors, labels), 1: labelled(*first_images, [first_texts])}, {0: caption_vectors, 1: first_texts}]
    for i in range(1, len(steps[0])):
        for k in (1, 0):
            for m in range(1 << i):
                arrays[k][m | 1 << i] = swapped(arrays[k][m], steps[k][i])
    blocks = [[whole(a[m]) for m in range(count)] for a in arrays]
    others = [{}, {}]
    both = bundled([arrays[1][1], arrays[0][1]], BUNDLE_COST)
    rest = [m for m in early if m != 1]
    both = swapped(bundled([both] + [arrays[k][m] for m in rest for k in (1, 0)], size), core)
    for i, m in enumerate([1] + rest):
        row = i * (2 * size + EXTRA_ROWS)
        others[1][m], others[0][m] = ((both, row, 0),), ((both, row + size, 0),)

    def sums(name, kind, rows, columns, jobs, before, emits, after=()):
        other = 1 - kind
        x_blocks = [blocks[kind][m] for m in rows]
        y_blocks = [(blocks, others)[c][other][m] for c, m in columns]
        x_masks = [masks[kind][m] for m in rows]
        y_masks = [masks[other][m + c * count] for c, m in columns]
        return gradient_sums(
            name,
            size,
            scalars,
            x_blocks,
            y_blocks,
            (x_masks, y_masks),
            kind == 0,
            jobs,
            before,
            emits,
            [blocks[k][m] for m in rows[1:] + rows[:1] for k in (1, 0)],
            after,
        )

    def both_cores(chosen):
        return [(c, m) for c in range(2) for m in chosen]

    def every_pair(rows, columns):
        return [(list(range(len(rows))), list(range(len(columns))))]

    before = []
    for k in range(2):
        columns = both_cores(early)
        jobs, emits = every_pair(early, columns), ["float"] * len(early)
        results = sums("early_sums", k, early, columns, jobs, {}, emits)
        before.append({m: s for m, (s,) in zip(early, results)})
    arrays = [[b[m][0][0] for m in late] for b in blocks[::-1]]
    arrays, before = lax.optimization_barrier((arrays, before))
    for k in (1, 0):
        for m, a in zip(late, arrays[1 - k]):
            blocks[k][m] = whole(a)
            others[k][m] = whole(swapped(a, core))
    after, begun = (), [{}, {}]
    coded, kept = [[None] * half, [None] * half], [None, None]
    for k in (1, 0):
        columns = [(0, m) for m in range(count)] + [(1, m) for m in early]
        jobs, emits = every_pair(late, columns), ["float"] * len(late)
        results = sums("late_rows_begun", k, late, columns, jobs, {}, emits, after)
        begun[k] = {i: s for i, (s,) in enumerate(results)}
        after = results[-1]
    for k in (1, 0):
        columns = [(1, m) for m in late]
        jobs, emits = every_pair(late, columns), ["whole"] * len(late)
        coded[k][1:] = sums("late_rows", k, late, columns, jobs, begun[k], emits, after)
        after = coded[k][1]
    for k in (1, 0):
        columns = both_cores(late)
        jobs, emits = every_pair(early, columns), ["float"] * half + ["whole"]
        *whole_sums, coded[k][0] = sums("late_columns", k, early, columns, jobs, before[k], emits, after)
        kept[k], after = [s for (s,) in whole_sums], coded[k][0]
    texts, after = scattered(kept[1], coded[1], steps[1], ())
    images, _ = scattered(kept[0], coded[0], steps[0], after)
    (kept_texts, text_blocks), (kept_images, image_blocks) = texts, images
    text_parts = in_order([b[0][0] for b in text_blocks[:-1]])
    image_parts = in_order([b[0][0] for b in image_blocks[:-1]], text_parts)
    text_blocks = [whole(a) for a in text_parts] + text_blocks[-1:]
    image_blocks = [whole(a) for a in image_parts] + image_blocks[-1:]
    return tuple(output_sums(scalars[0], [(kept_images, image_blocks), (kept_texts, text_blocks)]))


def solution(mesh):
    placed = (P(("blk", "grp"), None), P(("blk", "grp"), None), P(("blk", "grp")), P(), P())
    return jax.shard_map(
        per_device,
        mesh=mesh,
        in_specs=placed,
        out_specs=(P(("blk", "grp"), None), P(("blk", "grp"), None)),
        check_vma=False,
    )
```

```python
import math

import jax
import jax.numpy as jnp
from jax import lax
from jax.experimental import pallas as pl
from jax.experimental.pallas import tpu as pltpu
from jax.sharding import PartitionSpec as P

LOG2E = 1.4426950408889634
CODE_TOP = 32000.0
CODE_STEPS = 32.0
EXTRA_ROWS = 8
LABEL_BASE = 128
TILE = 256
LANES = 128
BUNDLE_COST = 6 * 10**8
SMEM = pl.BlockSpec(memory_space=pltpu.SMEM)
VMEM = pl.BlockSpec(memory_space=pltpu.VMEM)
ANY = pl.BlockSpec(memory_space=pl.ANY)


def whole(array):
    return ((array, 0, 0),)


def part_widths(width):
    first = min(3 * TILE, width - LANES)
    return (first, width - first)


def column_tiles(width):
    tiles, begin = [], 0
    for p, w in enumerate(part_widths(width)):
        tiles += [(p, k, begin + k, min(TILE, w - k)) for k in range(0, w, TILE)]
        begin += w
    return tiles


def piece(block, rows, tile):
    p, inner, start, span = tile
    ref, row, column = block[0 if len(block) == 1 else p]
    first = start if len(block) == 1 else inner
    return ref.at[pl.ds(row + rows[0], rows[1]), pl.ds(column + first, span)]


class Operands:
    def __init__(self):
        self.pairs = []

    def add(self, array, spec):
        for i, (a, s) in enumerate(self.pairs):
            if a is array and s is spec:
                return i
        self.pairs.append((array, spec))
        return len(self.pairs) - 1

    def block(self, block):
        at = [(self.add(a, VMEM), row, column) for a, row, column in block]
        return lambda refs: tuple((refs[i], row, column) for i, row, column in at)


def scale_code(top):
    return jnp.ceil(jnp.log(jnp.maximum(top, 1e-30)) * (CODE_STEPS * LOG2E))


def encode(value, block, tile):
    size, span = value.shape
    code = scale_code(jnp.max(jnp.abs(value), axis=0, keepdims=True))
    gain = CODE_TOP * jnp.exp(code * (-1.0 / (CODE_STEPS * LOG2E)))
    piece(block, (0, size), tile)[...] = (
        jnp.round(value * gain).astype(jnp.int32).astype(jnp.int16)
    )
    scales = jnp.broadcast_to(code.astype(jnp.int32), (EXTRA_ROWS, span)).astype(jnp.int16)
    piece(block, (size, EXTRA_ROWS), tile)[...] = scales


def decoded(block, size, tile):
    code = piece(block, (size, EXTRA_ROWS), tile)[...].astype(jnp.int32).astype(jnp.float32)
    gain = jnp.exp(code[:1] * (1.0 / (CODE_STEPS * LOG2E))) * (1.0 / CODE_TOP)
    return piece(block, (0, size), tile)[...].astype(jnp.int32).astype(jnp.float32) * gain


def call(kernel, name, operands, out_shape, scratch, room, cost, after=(), held_back=()):
    arrays = [a for a, _ in operands]
    held = sum(math.prod(a.shape) * a.dtype.itemsize for a in [*arrays, *out_shape])

    def body(*refs):
        results = refs[len(arrays) + len(after) + len(held_back) :]
        kernel(refs[: len(arrays)], results[: len(out_shape)] + results[len(out_shape) + len(held_back) :])

    return pl.pallas_call(
        body,
        out_shape=[*out_shape, *(jax.ShapeDtypeStruct(a.shape, a.dtype) for a in held_back)],
        in_specs=[s for _, s in operands] + [ANY] * (len(after) + len(held_back)),
        out_specs=[VMEM] * len(out_shape) + [ANY] * len(held_back),
        input_output_aliases={
            len(arrays) + len(after) + i: len(out_shape) + i for i in range(len(held_back))
        },
        scratch_shapes=scratch,
        compiler_params=pltpu.CompilerParams(vmem_limit_bytes=held + room),
        cost_estimate=pl.CostEstimate(flops=cost, bytes_accessed=cost, transcendentals=0),
        name=name,
    )(*arrays, *after, *held_back)


def labelled(images, labels, after=()):
    size, width = images.shape

    def kernel(ins, outs):
        outs[0][pl.ds(0, size), :] = ins[0][...]
        outs[0][pl.ds(size, EXTRA_ROWS), :] = jnp.zeros((EXTRA_ROWS, width), jnp.bfloat16)
        row = ins[1][...]
        low, high = lax.rem(row, LABEL_BASE), lax.div(row, LABEL_BASE)
        at = lax.broadcasted_iota(jnp.int32, (EXTRA_ROWS, size), 0)
        parts = jnp.where(at == 0, high, jnp.where(at == 1, low, 0)).astype(jnp.float32)
        outs[0][pl.ds(size, EXTRA_ROWS), pl.ds(0, size)] = parts.astype(jnp.bfloat16)

    shape = jax.ShapeDtypeStruct((size + EXTRA_ROWS, width), jnp.bfloat16)
    operands = [(images, VMEM), (labels, VMEM)]
    return call(kernel, "labelled", operands, [shape], [], 2**21, size, after)[0]


def bundled(arrays, cost):
    width = arrays[0].shape[1]

    def kernel(ins, outs):
        first = 0
        for ref in ins:
            outs[0][pl.ds(first, ref.shape[0]), :] = ref[...]
            first += ref.shape[0]

    shape = jax.ShapeDtypeStruct((sum(a.shape[0] for a in arrays), width), jnp.bfloat16)
    operands = [(a, VMEM) for a in arrays]
    return call(kernel, "bundled", operands, [shape], [], 2**21, cost)[0]


def first_row(mask, size):
    owner = (lax.axis_index("blk") ^ mask[0]) * lax.axis_size("grp") + (lax.axis_index("grp") ^ mask[1])
    return owner * size


def keys_of(block, size, mask, is_image):
    if not is_image:
        ids = lax.broadcasted_iota(jnp.int32, (1, size), 1) + first_row(mask, size)
        return ids.astype(jnp.float32)
    parts = piece(block, (size, EXTRA_ROWS), (0, 0, 0, size))[...].astype(jnp.float32)
    return parts[0:1] * LABEL_BASE + parts[1:2]


def gradient_sums(name, size, scalars, x_blocks, y_blocks, masks, x_images, jobs, before, emits, sequence, after=()):
    width = x_blocks[0][0][0].shape[1]
    x_masks, y_masks = masks
    per_tile = TILE // size
    widths = part_widths(width)
    shapes, where = [], {}

    def result(extra, w, dtype):
        shapes.append(jax.ShapeDtypeStruct((size + extra, w), dtype))
        return len(shapes) - 1

    for r, kind in enumerate(emits):
        if kind == "float":
            where[r] = [(result(0, width, jnp.float32), 0, 0)]
        else:
            cut = widths if kind == "parts" else (width,)
            where[r] = [(result(EXTRA_ROWS, w, jnp.int16), 0, 0) for w in cut]
    operands = Operands()
    slope_at, shift_at = [operands.add(s, SMEM) for s in scalars]
    for b in sequence:
        operands.block(b)
    x_views = [operands.block(b) for b in x_blocks]
    y_views = [operands.block(b) for b in y_blocks]
    before_at = {r: operands.add(b, VMEM) for r, b in before.items()}

    def kernel(ins, refs):
        outs, weights = refs[:-1], refs[-1]
        slope, shift = ins[slope_at][0] * LOG2E, ins[shift_at][0] * LOG2E
        x_refs, y_refs = [v(ins) for v in x_views], [v(ins) for v in y_views]

        def stacked(chosen):
            return jnp.concatenate(
                [ref[pl.ds(row, size), pl.ds(column, width)] for ((ref, row, column),) in chosen],
                axis=0,
            )

        for rows, columns in jobs:
            x_all = stacked([x_refs[r] for r in rows])
            keys = [
                jnp.broadcast_to(keys_of(x_refs[r], size, x_masks[r], x_images), (size, size)).T
                for r in rows
            ]
            for n in range(0, len(columns), per_tile):
                chosen = columns[n : n + per_tile]
                other = jnp.concatenate(
                    [keys_of(y_refs[c], size, y_masks[c], not x_images) for c in chosen], axis=1
                )
                scores = lax.dot_general(
                    x_all,
                    stacked([y_refs[c] for c in chosen]),
                    (((1,), (1,)), ((), ())),
                    preferred_element_type=jnp.float32,
                )
                for i in range(len(rows)):
                    z = scores[i * size : (i + 1) * size] * slope + shift
                    sig = 1.0 / (1.0 + jnp.exp2(-z))
                    w = jnp.where(jnp.tile(keys[i], (1, len(chosen))) == other, sig - 1.0, sig)
                    there = pl.ds(n * size, len(chosen) * size)
                    weights[pl.ds(i * size, size), there] = w.astype(jnp.bfloat16)
            for tile in column_tiles(width):
                sums = jnp.dot(
                    weights[pl.ds(0, len(rows) * size), pl.ds(0, len(columns) * size)],
                    jnp.concatenate([piece(y_refs[c], (0, size), tile)[...] for c in columns], axis=0),
                    preferred_element_type=jnp.float32,
                )
                for i, r in enumerate(rows):
                    block = sums[i * size : (i + 1) * size]
                    if r in before_at:
                        block = block + piece(whole(ins[before_at[r]]), (0, size), tile)[...]
                    out = tuple((outs[o], row, column) for o, row, column in where[r])
                    if emits[r] == "float":
                        piece(out, (0, size), tile)[...] = block
                    else:
                        encode(block, out, tile)

    pairs = sum(len(rows) * len(columns) for rows, columns in jobs)
    scratch = [pltpu.VMEM((len(x_blocks) * size, len(y_blocks) * size), jnp.bfloat16)]
    room = len(x_blocks) * len(y_blocks) * size * size * 2 + 8 * 2**20
    results = call(kernel, name, operands.pairs, shapes, scratch, room, pairs * size, after)
    return [tuple(results[o] for o, _, _ in where[r]) for r in range(len(emits))]


def passed_sum(kept, received, part, held_back=(), after=()):
    size, width = kept.shape
    operands = Operands()
    kept_at = operands.add(kept, VMEM)
    views = [operands.block(b if part is None or len(b) == 1 else (b[part],) * 2) for b in received]

    def kernel(ins, outs):
        for tile in column_tiles(width):
            p, inner, _, span = tile
            if part is None or p == part:
                total = piece(whole(ins[kept_at]), (0, size), tile)[...]
                for view in views:
                    total = total + decoded(view(ins), size, tile)
                encode(total, whole(outs[0]), tile if part is None else (0, 0, inner, span))

    cut = width if part is None else part_widths(width)[part]
    shape = jax.ShapeDtypeStruct((size + EXTRA_ROWS, cut), jnp.int16)
    return call(kernel, "passed_sum", operands.pairs, [shape], [], 2**21, size, after, held_back)


def output_sums(sharpness, sums):
    size, width = sums[0][0].shape
    operands = Operands()
    sharpness_at = operands.add(sharpness, SMEM)
    views = [(operands.add(kept, VMEM), [operands.block(b) for b in blocks]) for kept, blocks in sums]

    def kernel(ins, outs):
        for out, (kept_at, received) in zip(outs, views):
            for tile in column_tiles(width):
                total = piece(whole(ins[kept_at]), (0, size), tile)[...]
                for view in received:
                    total = total + decoded(view(ins), size, tile)
                piece(whole(out), (0, size), tile)[...] = total * ins[sharpness_at][0]

    shapes = [jax.ShapeDtypeStruct((size, width), jnp.float32)] * len(sums)
    return call(kernel, "output_sums", operands.pairs, shapes, [], 2**21, size)


def swapped(array, step):
    axis, bit = step
    return lax.ppermute(array, axis, [(i, i ^ bit) for i in range(lax.axis_size(axis))])


def scattered(kept, coded, steps, after):
    def sent(block, step):
        return [(swapped(p, step), 0, 0) for p in block]

    half, waiting = len(kept), coded[0]
    received = [[]] + [[sent(c, steps[-1])] for c in coded[1:]]
    for s in reversed(range(len(steps) - 1)):
        for m in reversed(range(1 << s)):
            n = m | 1 << s
            block = passed_sum(kept[n], received[n], None, waiting, after)
            after = block[:1]
            if n == half - 1:
                block, *waiting = block
                received[0].append(sent(waiting, steps[-1]))
                waiting, block = (), [block]
            received[m].append(sent(block, steps[s]))
    return (kept[0], received[0][::-1]), after


def in_order(arrays, after=()):
    return call(lambda *refs: None, "held", [], [], [], 2**21, 1, after, arrays)


def bit_steps(axis):
    return [(axis, 1 << k) for k in range(int(math.log2(lax.axis_size(axis))))]


def owner_masks(steps):
    masks = [(0, 0)]
    for axis, bit in steps:
        masks = masks + [(b ^ bit, g) if axis == "blk" else (b, g ^ bit) for b, g in masks]
    return masks


def per_device(
    picture_vectors, caption_vectors, matching_caption, sharpness_parameter, additive_intercept
):
    scalars = (sharpness_parameter, additive_intercept)
    size = picture_vectors.shape[0]
    core, *grp_steps = bit_steps("grp")
    every = grp_steps + bit_steps("blk")
    steps = [every[0::2], every[1::2]]
    assert len(steps[0]) == len(steps[1]) >= 2
    masks = [owner_masks(s + [core]) for s in steps]
    count = 1 << len(steps[0])
    half = count // 2
    early, late = list(range(half + 1)), list(range(half + 1, count))
    labels = matching_caption[None, :]
    (first_texts,) = in_order([swapped(caption_vectors, steps[1][0])])
    first_images = [swapped(a, steps[0][0]) for a in (picture_vectors, labels)]
    arrays = [{0: labelled(picture_vectors, labels), 1: labelled(*first_images, [first_texts])}, {0: caption_vectors, 1: first_texts}]
    for i in range(1, len(steps[0])):
        for k in (1, 0):
            for m in range(1 << i):
                arrays[k][m | 1 << i] = swapped(arrays[k][m], steps[k][i])
    blocks = [[whole(a[m]) for m in range(count)] for a in arrays]
    others = [{}, {}]
    both = bundled([arrays[1][1], arrays[0][1]], BUNDLE_COST)
    rest = [m for m in early if m != 1]
    both = swapped(bundled([both] + [arrays[k][m] for m in rest for k in (1, 0)], size), core)
    for i, m in enumerate([1] + rest):
        row = i * (2 * size + EXTRA_ROWS)
        others[1][m], others[0][m] = ((both, row, 0),), ((both, row + size, 0),)

    def sums(name, kind, rows, columns, jobs, before, emits, after=()):
        other = 1 - kind
        x_blocks = [blocks[kind][m] for m in rows]
        y_blocks = [(blocks, others)[c][other][m] for c, m in columns]
        x_masks = [masks[kind][m] for m in rows]
        y_masks = [masks[other][m + c * count] for c, m in columns]
        return gradient_sums(
            name,
            size,
            scalars,
            x_blocks,
            y_blocks,
            (x_masks, y_masks),
            kind == 0,
            jobs,
            before,
            emits,
            [blocks[k][m] for m in rows[1:] + rows[:1] for k in (1, 0)],
            after,
        )

    def both_cores(chosen):
        return [(c, m) for c in range(2) for m in chosen]

    def every_pair(rows, columns):
        return [(list(range(len(rows))), list(range(len(columns))))]

    before = []
    for k in range(2):
        columns = both_cores(early)
        jobs, emits = every_pair(early, columns), ["float"] * len(early)
        results = sums("early_sums", k, early, columns, jobs, {}, emits)
        before.append({m: s for m, (s,) in zip(early, results)})
    arrays = [[b[m][0][0] for m in late] for b in blocks[::-1]]
    arrays, before = lax.optimization_barrier((arrays, before))
    for k in (1, 0):
        for m, a in zip(late, arrays[1 - k]):
            blocks[k][m] = whole(a)
            others[k][m] = whole(swapped(a, core))
    after = ()
    coded, kept = [[None] * half, [None] * half], [None, None]
    for k in (1, 0):
        columns = [(0, m) for m in range(count)] + [(1, m) for m in early]
        jobs, emits = every_pair(late, columns), ["float"] * len(late)
        results = sums("late_rows_begun", k, late, columns, jobs, {}, emits, after)
        begun = {i: s for i, (s,) in enumerate(results)}
        columns = [(1, m) for m in late]
        jobs, emits = every_pair(late, columns), ["whole"] * len(late)
        coded[k][1:] = sums("late_rows", k, late, columns, jobs, begun, emits)
        after = coded[k][1]
    for k in (1, 0):
        columns = both_cores(late)
        jobs, emits = every_pair(early, columns), ["float"] * half + ["whole"]
        *whole_sums, coded[k][0] = sums("late_columns", k, early, columns, jobs, before[k], emits, after)
        kept[k], after = [s for (s,) in whole_sums], coded[k][0]
    texts, after = scattered(kept[1], coded[1], steps[1], ())
    images, _ = scattered(kept[0], coded[0], steps[0], after)
    (kept_texts, text_blocks), (kept_images, image_blocks) = texts, images
    text_parts = in_order([b[0][0] for b in text_blocks[:-1]])
    image_parts = in_order([b[0][0] for b in image_blocks[:-1]], text_parts)
    text_blocks = [whole(a) for a in text_parts] + text_blocks[-1:]
    image_blocks = [whole(a) for a in image_parts] + image_blocks[-1:]
    return tuple(output_sums(scalars[0], [(kept_images, image_blocks), (kept_texts, text_blocks)]))


def solution(mesh):
    placed = (P(("blk", "grp"), None), P(("blk", "grp"), None), P(("blk", "grp")), P(), P())
    return jax.shard_map(
        per_device,
        mesh=mesh,
        in_specs=placed,
        out_specs=(P(("blk", "grp"), None), P(("blk", "grp"), None)),
        check_vma=False,
    )
```

```python
import math

import jax
import jax.numpy as jnp
from jax import lax
from jax.experimental import pallas as pl
from jax.experimental.pallas import tpu as pltpu
from jax.sharding import PartitionSpec as P

LOG2E = 1.4426950408889634
CODE_TOP = 32000.0
CODE_STEPS = 32.0
EXTRA_ROWS = 8
LABEL_BASE = 128
TILE = 256
LANES = 128
BUNDLE_COST = 6 * 10**8
HELD_COST = 85 * 10**7
SMEM = pl.BlockSpec(memory_space=pltpu.SMEM)
VMEM = pl.BlockSpec(memory_space=pltpu.VMEM)
ANY = pl.BlockSpec(memory_space=pl.ANY)


def whole(array):
    return ((array, 0, 0),)


def part_widths(width):
    first = (width // LANES + 1) // 2 * LANES
    return (first, width - first)


def column_tiles(width):
    tiles, begin = [], 0
    for p, w in enumerate(part_widths(width)):
        tiles += [(p, k, begin + k, min(TILE, w - k)) for k in range(0, w, TILE)]
        begin += w
    return tiles


def piece(block, rows, tile):
    p, inner, start, span = tile
    ref, row, column = block[0 if len(block) == 1 else p]
    first = start if len(block) == 1 else inner
    return ref.at[pl.ds(row + rows[0], rows[1]), pl.ds(column + first, span)]


class Operands:
    def __init__(self):
        self.pairs = []

    def add(self, array, spec):
        for i, (a, s) in enumerate(self.pairs):
            if a is array and s is spec:
                return i
        self.pairs.append((array, spec))
        return len(self.pairs) - 1

    def block(self, block):
        at = [(self.add(a, VMEM), row, column) for a, row, column in block]
        return lambda refs: tuple((refs[i], row, column) for i, row, column in at)


def scale_code(top):
    return jnp.ceil(jnp.log(jnp.maximum(top, 1e-30)) * (CODE_STEPS * LOG2E))


def encode(value, block, tile):
    size, span = value.shape
    code = scale_code(jnp.max(jnp.abs(value), axis=0, keepdims=True))
    gain = CODE_TOP * jnp.exp(code * (-1.0 / (CODE_STEPS * LOG2E)))
    piece(block, (0, size), tile)[...] = (
        jnp.round(value * gain).astype(jnp.int32).astype(jnp.int16)
    )
    scales = jnp.broadcast_to(code.astype(jnp.int32), (EXTRA_ROWS, span)).astype(jnp.int16)
    piece(block, (size, EXTRA_ROWS), tile)[...] = scales


def decoded(block, size, tile):
    code = piece(block, (size, EXTRA_ROWS), tile)[...].astype(jnp.int32).astype(jnp.float32)
    gain = jnp.exp(code[:1] * (1.0 / (CODE_STEPS * LOG2E))) * (1.0 / CODE_TOP)
    return piece(block, (0, size), tile)[...].astype(jnp.int32).astype(jnp.float32) * gain


def call(kernel, name, operands, out_shape, scratch, room, cost, after=(), held_back=()):
    arrays = [a for a, _ in operands]
    held = sum(math.prod(a.shape) * a.dtype.itemsize for a in [*arrays, *out_shape])

    def body(*refs):
        results = refs[len(arrays) + len(after) + len(held_back) :]
        kernel(refs[: len(arrays)], results[: len(out_shape)] + results[len(out_shape) + len(held_back) :])

    return pl.pallas_call(
        body,
        out_shape=[*out_shape, *(jax.ShapeDtypeStruct(a.shape, a.dtype) for a in held_back)],
        in_specs=[s for _, s in operands] + [ANY] * (len(after) + len(held_back)),
        out_specs=[VMEM] * len(out_shape) + [ANY] * len(held_back),
        input_output_aliases={
            len(arrays) + len(after) + i: len(out_shape) + i for i in range(len(held_back))
        },
        scratch_shapes=scratch,
        compiler_params=pltpu.CompilerParams(vmem_limit_bytes=held + room),
        cost_estimate=pl.CostEstimate(flops=cost, bytes_accessed=cost, transcendentals=0),
        name=name,
    )(*arrays, *after, *held_back)


def labelled(images, labels, after=()):
    size, width = images.shape

    def kernel(ins, outs):
        outs[0][pl.ds(0, size), :] = ins[0][...]
        outs[0][pl.ds(size, EXTRA_ROWS), :] = jnp.zeros((EXTRA_ROWS, width), jnp.bfloat16)
        row = ins[1][...]
        low, high = lax.rem(row, LABEL_BASE), lax.div(row, LABEL_BASE)
        at = lax.broadcasted_iota(jnp.int32, (EXTRA_ROWS, size), 0)
        parts = jnp.where(at == 0, high, jnp.where(at == 1, low, 0)).astype(jnp.float32)
        outs[0][pl.ds(size, EXTRA_ROWS), pl.ds(0, size)] = parts.astype(jnp.bfloat16)

    shape = jax.ShapeDtypeStruct((size + EXTRA_ROWS, width), jnp.bfloat16)
    operands = [(images, VMEM), (labels, VMEM)]
    return call(kernel, "labelled", operands, [shape], [], 2**21, size, after)[0]


def bundled(arrays, cost):
    width = arrays[0].shape[1]

    def kernel(ins, outs):
        first = 0
        for ref in ins:
            outs[0][pl.ds(first, ref.shape[0]), :] = ref[...]
            first += ref.shape[0]

    shape = jax.ShapeDtypeStruct((sum(a.shape[0] for a in arrays), width), jnp.bfloat16)
    operands = [(a, VMEM) for a in arrays]
    return call(kernel, "bundled", operands, [shape], [], 2**21, cost)[0]


def first_row(mask, size):
    owner = (lax.axis_index("blk") ^ mask[0]) * lax.axis_size("grp") + (lax.axis_index("grp") ^ mask[1])
    return owner * size


def keys_of(block, size, mask, is_image):
    if not is_image:
        ids = lax.broadcasted_iota(jnp.int32, (1, size), 1) + first_row(mask, size)
        return ids.astype(jnp.float32)
    parts = piece(block, (size, EXTRA_ROWS), (0, 0, 0, size))[...].astype(jnp.float32)
    return parts[0:1] * LABEL_BASE + parts[1:2]


def gradient_sums(name, size, scalars, x_blocks, y_blocks, masks, x_images, jobs, before, emits, sequence, after=()):
    width = x_blocks[0][0][0].shape[1]
    x_masks, y_masks = masks
    per_tile = TILE // size
    widths = part_widths(width)
    shapes, where = [], {}

    def result(extra, w, dtype):
        shapes.append(jax.ShapeDtypeStruct((size + extra, w), dtype))
        return len(shapes) - 1

    for r, kind in enumerate(emits):
        if kind == "float":
            where[r] = [(result(0, width, jnp.float32), 0, 0)]
        else:
            cut = widths if kind == "parts" else (width,)
            where[r] = [(result(EXTRA_ROWS, w, jnp.int16), 0, 0) for w in cut]
    operands = Operands()
    slope_at, shift_at = [operands.add(s, SMEM) for s in scalars]
    for b in sequence:
        operands.block(b)
    x_views = [operands.block(b) for b in x_blocks]
    y_views = [operands.block(b) for b in y_blocks]
    before_at = {r: operands.add(b, VMEM) for r, b in before.items()}

    def kernel(ins, refs):
        outs, weights = refs[:-1], refs[-1]
        slope, shift = ins[slope_at][0] * LOG2E, ins[shift_at][0] * LOG2E
        x_refs, y_refs = [v(ins) for v in x_views], [v(ins) for v in y_views]

        def stacked(chosen):
            return jnp.concatenate(
                [ref[pl.ds(row, size), pl.ds(column, width)] for ((ref, row, column),) in chosen],
                axis=0,
            )

        for rows, columns in jobs:
            x_all = stacked([x_refs[r] for r in rows])
            keys = [
                jnp.broadcast_to(keys_of(x_refs[r], size, x_masks[r], x_images), (size, size)).T
                for r in rows
            ]
            for n in range(0, len(columns), per_tile):
                chosen = columns[n : n + per_tile]
                other = jnp.concatenate(
                    [keys_of(y_refs[c], size, y_masks[c], not x_images) for c in chosen], axis=1
                )
                scores = lax.dot_general(
                    x_all,
                    stacked([y_refs[c] for c in chosen]),
                    (((1,), (1,)), ((), ())),
                    preferred_element_type=jnp.float32,
                )
                for i in range(len(rows)):
                    z = scores[i * size : (i + 1) * size] * slope + shift
                    sig = 1.0 / (1.0 + jnp.exp2(-z))
                    w = jnp.where(jnp.tile(keys[i], (1, len(chosen))) == other, sig - 1.0, sig)
                    there = pl.ds(n * size, len(chosen) * size)
                    weights[pl.ds(i * size, size), there] = w.astype(jnp.bfloat16)
            for tile in column_tiles(width):
                sums = jnp.dot(
                    weights[pl.ds(0, len(rows) * size), pl.ds(0, len(columns) * size)],
                    jnp.concatenate([piece(y_refs[c], (0, size), tile)[...] for c in columns], axis=0),
                    preferred_element_type=jnp.float32,
                )
                for i, r in enumerate(rows):
                    block = sums[i * size : (i + 1) * size]
                    if r in before_at:
                        block = block + piece(whole(ins[before_at[r]]), (0, size), tile)[...]
                    out = tuple((outs[o], row, column) for o, row, column in where[r])
                    if emits[r] == "float":
                        piece(out, (0, size), tile)[...] = block
                    else:
                        encode(block, out, tile)

    pairs = sum(len(rows) * len(columns) for rows, columns in jobs)
    scratch = [pltpu.VMEM((len(x_blocks) * size, len(y_blocks) * size), jnp.bfloat16)]
    room = len(x_blocks) * len(y_blocks) * size * size * 2 + 8 * 2**20
    results = call(kernel, name, operands.pairs, shapes, scratch, room, pairs * size, after)
    return [tuple(results[o] for o, _, _ in where[r]) for r in range(len(emits))]


def passed_sum(kept, received, part, held_back=(), after=()):
    size, width = kept.shape
    operands = Operands()
    kept_at = operands.add(kept, VMEM)
    views = [operands.block(b if part is None or len(b) == 1 else (b[part],) * 2) for b in received]

    def kernel(ins, outs):
        for tile in column_tiles(width):
            p, inner, _, span = tile
            if part is None or p == part:
                total = piece(whole(ins[kept_at]), (0, size), tile)[...]
                for view in views:
                    total = total + decoded(view(ins), size, tile)
                encode(total, whole(outs[0]), tile if part is None else (0, 0, inner, span))

    cut = width if part is None else part_widths(width)[part]
    shape = jax.ShapeDtypeStruct((size + EXTRA_ROWS, cut), jnp.int16)
    return call(kernel, "passed_sum", operands.pairs, [shape], [], 2**21, size, after, held_back)


def output_sums(sharpness, sums):
    size, width = sums[0][0].shape
    operands = Operands()
    sharpness_at = operands.add(sharpness, SMEM)
    views = [(operands.add(kept, VMEM), [operands.block(b) for b in blocks]) for kept, blocks in sums]

    def kernel(ins, outs):
        for out, (kept_at, received) in zip(outs, views):
            for tile in column_tiles(width):
                total = piece(whole(ins[kept_at]), (0, size), tile)[...]
                for view in received:
                    total = total + decoded(view(ins), size, tile)
                piece(whole(out), (0, size), tile)[...] = total * ins[sharpness_at][0]

    shapes = [jax.ShapeDtypeStruct((size, width), jnp.float32)] * len(sums)
    return call(kernel, "output_sums", operands.pairs, shapes, [], 2**21, size)


def swapped(array, step):
    axis, bit = step
    return lax.ppermute(array, axis, [(i, i ^ bit) for i in range(lax.axis_size(axis))])


def scattered(kept, coded, steps, after):
    def sent(array, step):
        return (swapped(array, step), 0, 0)

    half = len(kept)
    received = [[]] + [[(sent(c[0], steps[-1]),)] for c in coded[1:]]
    waiting, last = [c[1] for c in coded[1:]], [coded[0][0]]
    for s in reversed(range(len(steps) - 1)):
        for m in reversed(range(1 << s)):
            n = m | 1 << s
            first, *begun = passed_sum(kept[n], received[n], 0, waiting + last)
            for r, c in zip(received[1:], begun):
                r[0] = r[0] + (sent(c, steps[-1]),)
            received[0] += [(sent(c, steps[-1]),) for c in begun[len(waiting) :]]
            first = sent(first, steps[s])
            (second,) = passed_sum(kept[n], received[n], 1, (), [first[0], *after])
            received[m].append((first, sent(second, steps[s])))
            waiting, last, after = [], [], [second]
    return kept[0], received[0], after


def in_order(arrays, after=(), cost=HELD_COST):
    return call(lambda *refs: None, "held", [], [], [], 2**21, cost, after, arrays)


def bit_steps(axis):
    return [(axis, 1 << k) for k in range(int(math.log2(lax.axis_size(axis))))]


def owner_masks(steps):
    masks = [(0, 0)]
    for axis, bit in steps:
        masks = masks + [(b ^ bit, g) if axis == "blk" else (b, g ^ bit) for b, g in masks]
    return masks


def per_device(
    picture_vectors, caption_vectors, matching_caption, sharpness_parameter, additive_intercept
):
    scalars = (sharpness_parameter, additive_intercept)
    size = picture_vectors.shape[0]
    core, *grp_steps = bit_steps("grp")
    every = grp_steps + bit_steps("blk")
    steps = [every[0::2], every[1::2]]
    assert len(steps[0]) == len(steps[1]) >= 2
    masks = [owner_masks(s + [core]) for s in steps]
    count = 1 << len(steps[0])
    half = count // 2
    early, late = list(range(half + 1)), list(range(half + 1, count))
    labels = matching_caption[None, :]
    (first_texts,) = in_order([swapped(caption_vectors, steps[1][0])], (), 1)
    first_images = [swapped(a, steps[0][0]) for a in (picture_vectors, labels)]
    arrays = [{0: labelled(picture_vectors, labels), 1: labelled(*first_images, [first_texts])}, {0: caption_vectors, 1: first_texts}]
    for i in range(1, len(steps[0])):
        for k in (1, 0):
            for m in range(1 << i):
                arrays[k][m | 1 << i] = swapped(arrays[k][m], steps[k][i])
    blocks = [[whole(a[m]) for m in range(count)] for a in arrays]
    others = [{}, {}]
    both = bundled([arrays[1][1], arrays[0][1]], BUNDLE_COST)
    rest = [m for m in early if m != 1]
    both = swapped(bundled([both] + [arrays[k][m] for m in rest for k in (1, 0)], size), core)
    for i, m in enumerate([1] + rest):
        row = i * (2 * size + EXTRA_ROWS)
        others[1][m], others[0][m] = ((both, row, 0),), ((both, row + size, 0),)

    def sums(name, kind, rows, columns, jobs, before, emits, after=()):
        other = 1 - kind
        x_blocks = [blocks[kind][m] for m in rows]
        y_blocks = [(blocks, others)[c][other][m] for c, m in columns]
        x_masks = [masks[kind][m] for m in rows]
        y_masks = [masks[other][m + c * count] for c, m in columns]
        return gradient_sums(
            name,
            size,
            scalars,
            x_blocks,
            y_blocks,
            (x_masks, y_masks),
            kind == 0,
            jobs,
            before,
            emits,
            [blocks[k][m] for m in rows[1:] + rows[:1] for k in (1, 0)],
            after,
        )

    def both_cores(chosen):
        return [(c, m) for c in range(2) for m in chosen]

    def every_pair(rows, columns):
        return [(list(range(len(rows))), list(range(len(columns))))]

    before = []
    for k in range(2):
        columns = both_cores(early)
        jobs, emits = every_pair(early, columns), ["float"] * len(early)
        results = sums("early_sums", k, early, columns, jobs, {}, emits)
        before.append({m: s for m, (s,) in zip(early, results)})
    arrays = [[b[m][0][0] for m in late] for b in blocks[::-1]]
    arrays, before = lax.optimization_barrier((arrays, before))
    for k in (1, 0):
        for m, a in zip(late, arrays[1 - k]):
            blocks[k][m] = whole(a)
            others[k][m] = whole(swapped(a, core))
    after = ()
    coded, kept = [[None] * half, [None] * half], [None, None]
    for k in (1, 0):
        columns = [(0, m) for m in range(count)] + [(1, m) for m in early]
        jobs, emits = every_pair(late, columns), ["float"] * len(late)
        results = sums("late_rows_begun", k, late, columns, jobs, {}, emits, after)
        begun = {i: s for i, (s,) in enumerate(results)}
        columns = [(1, m) for m in late]
        jobs, emits = every_pair(late, columns), ["parts"] * len(late)
        coded[k][1:] = sums("late_rows", k, late, columns, jobs, begun, emits)
        after = coded[k][1]
    for k in (1, 0):
        columns = both_cores(late)
        jobs, emits = every_pair(early, columns), ["float"] * half + ["whole"]
        *whole_sums, coded[k][0] = sums("late_columns", k, early, columns, jobs, before[k], emits, after)
        kept[k], after = [s for (s,) in whole_sums], coded[k][0]
    kept_texts, text_blocks, after = scattered(kept[1], coded[1], steps[1], ())
    kept_images, image_blocks, _ = scattered(kept[0], coded[0], steps[0], after)
    ends = ()
    for blocks_in in (text_blocks, image_blocks):
        ends = in_order([part[0] for b in blocks_in if len(b) > 1 for part in b], ends)
        parts = iter(ends)
        blocks_in[:] = [tuple((next(parts), 0, 0) for _ in b) if len(b) > 1 else b for b in blocks_in]
    return tuple(output_sums(scalars[0], [(kept_images, image_blocks), (kept_texts, text_blocks)]))


def solution(mesh):
    placed = (P(("blk", "grp"), None), P(("blk", "grp"), None), P(("blk", "grp")), P(), P())
    return jax.shard_map(
        per_device,
        mesh=mesh,
        in_specs=placed,
        out_specs=(P(("blk", "grp"), None), P(("blk", "grp"), None)),
        check_vma=False,
    )
```

```python
import math

import jax
import jax.numpy as jnp
from jax import lax
from jax.experimental import pallas as pl
from jax.experimental.pallas import tpu as pltpu
from jax.sharding import PartitionSpec as P

LOG2E = 1.4426950408889634
CODE_TOP = 32000.0
CODE_STEPS = 32.0
EXTRA_ROWS = 8
LABEL_BASE = 128
TILE = 256
LANES = 128
BUNDLE_COST = 6 * 10**8
HELD_COST = 3 * 10**8
SMEM = pl.BlockSpec(memory_space=pltpu.SMEM)
VMEM = pl.BlockSpec(memory_space=pltpu.VMEM)
ANY = pl.BlockSpec(memory_space=pl.ANY)


def whole(array):
    return ((array, 0, 0),)


def part_widths(width):
    first = width // (2 * LANES) * LANES
    return (first, width - first)


def column_tiles(width):
    tiles, begin = [], 0
    for p, w in enumerate(part_widths(width)):
        tiles += [(p, k, begin + k, min(TILE, w - k)) for k in range(0, w, TILE)]
        begin += w
    return tiles


def piece(block, rows, tile):
    p, inner, start, span = tile
    ref, row, column = block[0 if len(block) == 1 else p]
    first = start if len(block) == 1 else inner
    return ref.at[pl.ds(row + rows[0], rows[1]), pl.ds(column + first, span)]


class Operands:
    def __init__(self):
        self.pairs = []

    def add(self, array, spec):
        for i, (a, s) in enumerate(self.pairs):
            if a is array and s is spec:
                return i
        self.pairs.append((array, spec))
        return len(self.pairs) - 1

    def block(self, block):
        at = [(self.add(a, VMEM), row, column) for a, row, column in block]
        return lambda refs: tuple((refs[i], row, column) for i, row, column in at)


def scale_code(top):
    return jnp.ceil(jnp.log(jnp.maximum(top, 1e-30)) * (CODE_STEPS * LOG2E))


def encode(value, block, tile):
    size, span = value.shape
    code = scale_code(jnp.max(jnp.abs(value), axis=0, keepdims=True))
    gain = CODE_TOP * jnp.exp(code * (-1.0 / (CODE_STEPS * LOG2E)))
    piece(block, (0, size), tile)[...] = (
        jnp.round(value * gain).astype(jnp.int32).astype(jnp.int16)
    )
    scales = jnp.broadcast_to(code.astype(jnp.int32), (EXTRA_ROWS, span)).astype(jnp.int16)
    piece(block, (size, EXTRA_ROWS), tile)[...] = scales


def decoded(block, size, tile):
    code = piece(block, (size, EXTRA_ROWS), tile)[...].astype(jnp.int32).astype(jnp.float32)
    gain = jnp.exp(code[:1] * (1.0 / (CODE_STEPS * LOG2E))) * (1.0 / CODE_TOP)
    return piece(block, (0, size), tile)[...].astype(jnp.int32).astype(jnp.float32) * gain


def call(kernel, name, operands, out_shape, scratch, room, cost, after=(), held_back=()):
    arrays = [a for a, _ in operands]
    held = sum(math.prod(a.shape) * a.dtype.itemsize for a in [*arrays, *out_shape])

    def body(*refs):
        results = refs[len(arrays) + len(after) + len(held_back) :]
        kernel(refs[: len(arrays)], results[: len(out_shape)] + results[len(out_shape) + len(held_back) :])

    return pl.pallas_call(
        body,
        out_shape=[*out_shape, *(jax.ShapeDtypeStruct(a.shape, a.dtype) for a in held_back)],
        in_specs=[s for _, s in operands] + [ANY] * (len(after) + len(held_back)),
        out_specs=[VMEM] * len(out_shape) + [ANY] * len(held_back),
        input_output_aliases={
            len(arrays) + len(after) + i: len(out_shape) + i for i in range(len(held_back))
        },
        scratch_shapes=scratch,
        compiler_params=pltpu.CompilerParams(vmem_limit_bytes=held + room),
        cost_estimate=pl.CostEstimate(flops=cost, bytes_accessed=cost, transcendentals=0),
        name=name,
    )(*arrays, *after, *held_back)


def labelled(images, labels, after=()):
    size, width = images.shape

    def kernel(ins, outs):
        outs[0][pl.ds(0, size), :] = ins[0][...]
        outs[0][pl.ds(size, EXTRA_ROWS), :] = jnp.zeros((EXTRA_ROWS, width), jnp.bfloat16)
        row = ins[1][...]
        low, high = lax.rem(row, LABEL_BASE), lax.div(row, LABEL_BASE)
        at = lax.broadcasted_iota(jnp.int32, (EXTRA_ROWS, size), 0)
        parts = jnp.where(at == 0, high, jnp.where(at == 1, low, 0)).astype(jnp.float32)
        outs[0][pl.ds(size, EXTRA_ROWS), pl.ds(0, size)] = parts.astype(jnp.bfloat16)

    shape = jax.ShapeDtypeStruct((size + EXTRA_ROWS, width), jnp.bfloat16)
    operands = [(images, VMEM), (labels, VMEM)]
    return call(kernel, "labelled", operands, [shape], [], 2**21, size, after)[0]


def bundled(arrays, cost):
    width = arrays[0].shape[1]

    def kernel(ins, outs):
        first = 0
        for ref in ins:
            outs[0][pl.ds(first, ref.shape[0]), :] = ref[...]
            first += ref.shape[0]

    shape = jax.ShapeDtypeStruct((sum(a.shape[0] for a in arrays), width), jnp.bfloat16)
    operands = [(a, VMEM) for a in arrays]
    return call(kernel, "bundled", operands, [shape], [], 2**21, cost)[0]


def first_row(mask, size):
    owner = (lax.axis_index("blk") ^ mask[0]) * lax.axis_size("grp") + (lax.axis_index("grp") ^ mask[1])
    return owner * size


def keys_of(block, size, mask, is_image):
    if not is_image:
        ids = lax.broadcasted_iota(jnp.int32, (1, size), 1) + first_row(mask, size)
        return ids.astype(jnp.float32)
    parts = piece(block, (size, EXTRA_ROWS), (0, 0, 0, size))[...].astype(jnp.float32)
    return parts[0:1] * LABEL_BASE + parts[1:2]


def gradient_sums(name, size, scalars, x_blocks, y_blocks, masks, x_images, jobs, before, emits, sequence, after=()):
    width = x_blocks[0][0][0].shape[1]
    x_masks, y_masks = masks
    per_tile = TILE // size
    widths = part_widths(width)
    shapes, where = [], {}

    def result(extra, w, dtype):
        shapes.append(jax.ShapeDtypeStruct((size + extra, w), dtype))
        return len(shapes) - 1

    for r, kind in enumerate(emits):
        if kind == "float":
            where[r] = [(result(0, width, jnp.float32), 0, 0)]
        else:
            cut = widths if kind == "parts" else (width,)
            where[r] = [(result(EXTRA_ROWS, w, jnp.int16), 0, 0) for w in cut]
    operands = Operands()
    slope_at, shift_at = [operands.add(s, SMEM) for s in scalars]
    for b in sequence:
        operands.block(b)
    x_views = [operands.block(b) for b in x_blocks]
    y_views = [operands.block(b) for b in y_blocks]
    before_at = {r: operands.add(b, VMEM) for r, b in before.items()}

    def kernel(ins, refs):
        outs, weights = refs[:-1], refs[-1]
        slope, shift = ins[slope_at][0] * LOG2E, ins[shift_at][0] * LOG2E
        x_refs, y_refs = [v(ins) for v in x_views], [v(ins) for v in y_views]

        def stacked(chosen):
            return jnp.concatenate(
                [ref[pl.ds(row, size), pl.ds(column, width)] for ((ref, row, column),) in chosen],
                axis=0,
            )

        for rows, columns in jobs:
            x_all = stacked([x_refs[r] for r in rows])
            keys = [
                jnp.broadcast_to(keys_of(x_refs[r], size, x_masks[r], x_images), (size, size)).T
                for r in rows
            ]
            for n in range(0, len(columns), per_tile):
                chosen = columns[n : n + per_tile]
                other = jnp.concatenate(
                    [keys_of(y_refs[c], size, y_masks[c], not x_images) for c in chosen], axis=1
                )
                scores = lax.dot_general(
                    x_all,
                    stacked([y_refs[c] for c in chosen]),
                    (((1,), (1,)), ((), ())),
                    preferred_element_type=jnp.float32,
                )
                for i in range(len(rows)):
                    z = scores[i * size : (i + 1) * size] * slope + shift
                    sig = 1.0 / (1.0 + jnp.exp2(-z))
                    w = jnp.where(jnp.tile(keys[i], (1, len(chosen))) == other, sig - 1.0, sig)
                    there = pl.ds(n * size, len(chosen) * size)
                    weights[pl.ds(i * size, size), there] = w.astype(jnp.bfloat16)
            for tile in column_tiles(width):
                sums = jnp.dot(
                    weights[pl.ds(0, len(rows) * size), pl.ds(0, len(columns) * size)],
                    jnp.concatenate([piece(y_refs[c], (0, size), tile)[...] for c in columns], axis=0),
                    preferred_element_type=jnp.float32,
                )
                for i, r in enumerate(rows):
                    block = sums[i * size : (i + 1) * size]
                    if r in before_at:
                        block = block + piece(whole(ins[before_at[r]]), (0, size), tile)[...]
                    out = tuple((outs[o], row, column) for o, row, column in where[r])
                    if emits[r] == "float":
                        piece(out, (0, size), tile)[...] = block
                    else:
                        encode(block, out, tile)

    pairs = sum(len(rows) * len(columns) for rows, columns in jobs)
    scratch = [pltpu.VMEM((len(x_blocks) * size, len(y_blocks) * size), jnp.bfloat16)]
    room = len(x_blocks) * len(y_blocks) * size * size * 2 + 8 * 2**20
    results = call(kernel, name, operands.pairs, shapes, scratch, room, pairs * size, after)
    return [tuple(results[o] for o, _, _ in where[r]) for r in range(len(emits))]


def passed_sum(kept, received, part, held_back=(), after=()):
    size, width = kept.shape
    operands = Operands()
    kept_at = operands.add(kept, VMEM)
    views = [operands.block(b if part is None or len(b) == 1 else (b[part],) * 2) for b in received]

    def kernel(ins, outs):
        for tile in column_tiles(width):
            p, inner, _, span = tile
            if part is None or p == part:
                total = piece(whole(ins[kept_at]), (0, size), tile)[...]
                for view in views:
                    total = total + decoded(view(ins), size, tile)
                encode(total, whole(outs[0]), tile if part is None else (0, 0, inner, span))

    cut = width if part is None else part_widths(width)[part]
    shape = jax.ShapeDtypeStruct((size + EXTRA_ROWS, cut), jnp.int16)
    return call(kernel, "passed_sum", operands.pairs, [shape], [], 2**21, size, after, held_back)


def output_sums(sharpness, sums):
    size, width = sums[0][0].shape
    operands = Operands()
    sharpness_at = operands.add(sharpness, SMEM)
    views = [(operands.add(kept, VMEM), [operands.block(b) for b in blocks]) for kept, blocks in sums]

    def kernel(ins, outs):
        for out, (kept_at, received) in zip(outs, views):
            for tile in column_tiles(width):
                total = piece(whole(ins[kept_at]), (0, size), tile)[...]
                for view in received:
                    total = total + decoded(view(ins), size, tile)
                piece(whole(out), (0, size), tile)[...] = total * ins[sharpness_at][0]

    shapes = [jax.ShapeDtypeStruct((size, width), jnp.float32)] * len(sums)
    return call(kernel, "output_sums", operands.pairs, shapes, [], 2**21, size)


def swapped(array, step):
    axis, bit = step
    return lax.ppermute(array, axis, [(i, i ^ bit) for i in range(lax.axis_size(axis))])


def scattered(kept, coded, steps, after):
    def sent(array, step):
        return (swapped(array, step), 0, 0)

    half = len(kept)
    received = [[]] + [[(sent(c[0], steps[-1]),)] for c in coded[1:]]
    waiting, last = [c[1] for c in coded[1:]], [coded[0][0]]
    for s in reversed(range(len(steps) - 1)):
        for m in reversed(range(1 << s)):
            n = m | 1 << s
            first, *begun = passed_sum(kept[n], received[n], 0, waiting + last)
            if waiting:
                begun_with = [first]
            for r, c in zip(received[1:], begun):
                r[0] = r[0] + (sent(c, steps[-1]),)
            received[0] += [(sent(c, steps[-1]),) for c in begun[len(waiting) :]]
            first = sent(first, steps[s])
            (second,) = passed_sum(kept[n], received[n], 1, (), [first[0], *after])
            received[m].append((first, sent(second, steps[s])))
            waiting, last, after = [], [], [second]
    return kept[0], received[0], after, begun_with


def in_order(arrays, after=(), cost=HELD_COST):
    return call(lambda *refs: None, "held", [], [], [], 2**21, cost, after, arrays)


def bit_steps(axis):
    return [(axis, 1 << k) for k in range(int(math.log2(lax.axis_size(axis))))]


def owner_masks(steps):
    masks = [(0, 0)]
    for axis, bit in steps:
        masks = masks + [(b ^ bit, g) if axis == "blk" else (b, g ^ bit) for b, g in masks]
    return masks


def per_device(
    picture_vectors, caption_vectors, matching_caption, sharpness_parameter, additive_intercept
):
    scalars = (sharpness_parameter, additive_intercept)
    size = picture_vectors.shape[0]
    core, *grp_steps = bit_steps("grp")
    every = grp_steps + bit_steps("blk")
    steps = [every[0::2], every[1::2]]
    assert len(steps[0]) == len(steps[1]) >= 2
    masks = [owner_masks(s + [core]) for s in steps]
    count = 1 << len(steps[0])
    half = count // 2
    early, late = list(range(half + 1)), list(range(half + 1, count))
    labels = matching_caption[None, :]
    (first_texts,) = in_order([swapped(caption_vectors, steps[1][0])], (), 1)
    first_images = [swapped(a, steps[0][0]) for a in (picture_vectors, labels)]
    arrays = [{0: labelled(picture_vectors, labels), 1: labelled(*first_images, [first_texts])}, {0: caption_vectors, 1: first_texts}]
    for i in range(1, len(steps[0])):
        for k in (1, 0):
            for m in range(1 << i):
                arrays[k][m | 1 << i] = swapped(arrays[k][m], steps[k][i])
    blocks = [[whole(a[m]) for m in range(count)] for a in arrays]
    others = [{}, {}]
    both = bundled([arrays[1][1], arrays[0][1]], BUNDLE_COST)
    rest = [m for m in early if m != 1]
    both = swapped(bundled([both] + [arrays[k][m] for m in rest for k in (1, 0)], size), core)
    for i, m in enumerate([1] + rest):
        row = i * (2 * size + EXTRA_ROWS)
        others[1][m], others[0][m] = ((both, row, 0),), ((both, row + size, 0),)

    def sums(name, kind, rows, columns, jobs, before, emits, after=()):
        other = 1 - kind
        x_blocks = [blocks[kind][m] for m in rows]
        y_blocks = [(blocks, others)[c][other][m] for c, m in columns]
        x_masks = [masks[kind][m] for m in rows]
        y_masks = [masks[other][m + c * count] for c, m in columns]
        return gradient_sums(
            name,
            size,
            scalars,
            x_blocks,
            y_blocks,
            (x_masks, y_masks),
            kind == 0,
            jobs,
            before,
            emits,
            [blocks[k][m] for m in rows[1:] + rows[:1] for k in (1, 0)],
            after,
        )

    def both_cores(chosen):
        return [(c, m) for c in range(2) for m in chosen]

    def every_pair(rows, columns):
        return [(list(range(len(rows))), list(range(len(columns))))]

    before = []
    for k in range(2):
        columns = both_cores(early)
        jobs, emits = every_pair(early, columns), ["float"] * len(early)
        results = sums("early_sums", k, early, columns, jobs, {}, emits)
        before.append({m: s for m, (s,) in zip(early, results)})
    arrays = [[b[m][0][0] for m in late] for b in blocks[::-1]]
    arrays, before = lax.optimization_barrier((arrays, before))
    for k in (1, 0):
        for m, a in zip(late, arrays[1 - k]):
            blocks[k][m] = whole(a)
            others[k][m] = whole(swapped(a, core))
    after = ()
    coded = [[None] * half, [None] * half]
    for k in (1, 0):
        columns = both_cores(early)
        jobs, emits = every_pair(late, columns), ["float"] * len(late)
        results = sums("late_rows_begun", k, late, columns, jobs, {}, emits, after)
        begun = {i: s for i, (s,) in enumerate(results)}
        columns = both_cores(late)
        jobs, emits = every_pair(late, columns), ["parts"] * len(late)
        coded[k][1:] = sums("late_rows", k, late, columns, jobs, begun, emits)
        after = coded[k][1]
    sums_in = [None, None]
    ordering = ()
    for k in (1, 0):
        columns = both_cores(late)
        jobs, emits = every_pair(early, columns), ["float"] * half + ["whole"]
        *whole_sums, coded[k][0] = sums("late_columns", k, early, columns, jobs, before[k], emits, after)
        kept = [s for (s,) in whole_sums]
        *sums_in[k], ordering, after = scattered(kept, coded[k], steps[k], ordering)
    (kept_images, image_blocks), (kept_texts, text_blocks) = sums_in
    ends = ()
    for blocks_in in (text_blocks, image_blocks):
        ends = in_order([part[0] for b in blocks_in if len(b) > 1 for part in b], ends)
        parts = iter(ends)
        blocks_in[:] = [tuple((next(parts), 0, 0) for _ in b) if len(b) > 1 else b for b in blocks_in]
    return tuple(output_sums(scalars[0], [(kept_images, image_blocks), (kept_texts, text_blocks)]))


def solution(mesh):
    placed = (P(("blk", "grp"), None), P(("blk", "grp"), None), P(("blk", "grp")), P(), P())
    return jax.shard_map(
        per_device,
        mesh=mesh,
        in_specs=placed,
        out_specs=(P(("blk", "grp"), None), P(("blk", "grp"), None)),
        check_vma=False,
    )
```

```python
import math

import jax
import jax.numpy as jnp
from jax import lax
from jax.experimental import pallas as pl
from jax.experimental.pallas import tpu as pltpu
from jax.sharding import PartitionSpec as P

LOG2E = 1.4426950408889634
CODE_TOP = 32000.0
CODE_STEPS = 32.0
EXTRA_ROWS = 8
LABEL_BASE = 128
TILE = 256
LANES = 128
BUNDLE_COST = 6 * 10**8
SMEM = pl.BlockSpec(memory_space=pltpu.SMEM)
VMEM = pl.BlockSpec(memory_space=pltpu.VMEM)
ANY = pl.BlockSpec(memory_space=pl.ANY)


def whole(array):
    return ((array, 0, 0),)


def part_widths(width):
    first = min(3 * TILE, width - LANES)
    return (first, width - first)


def column_tiles(width):
    tiles, begin = [], 0
    for p, w in enumerate(part_widths(width)):
        tiles += [(p, k, begin + k, min(TILE, w - k)) for k in range(0, w, TILE)]
        begin += w
    return tiles


def piece(block, rows, tile):
    p, inner, start, span = tile
    ref, row, column = block[0 if len(block) == 1 else p]
    first = start if len(block) == 1 else inner
    return ref.at[pl.ds(row + rows[0], rows[1]), pl.ds(column + first, span)]


class Operands:
    def __init__(self):
        self.pairs = []

    def add(self, array, spec):
        for i, (a, s) in enumerate(self.pairs):
            if a is array and s is spec:
                return i
        self.pairs.append((array, spec))
        return len(self.pairs) - 1

    def block(self, block):
        at = [(self.add(a, VMEM), row, column) for a, row, column in block]
        return lambda refs: tuple((refs[i], row, column) for i, row, column in at)


def scale_code(top):
    return jnp.ceil(jnp.log(jnp.maximum(top, 1e-30)) * (CODE_STEPS * LOG2E))


def encode(value, block, tile):
    size, span = value.shape
    code = scale_code(jnp.max(jnp.abs(value), axis=0, keepdims=True))
    gain = CODE_TOP * jnp.exp(code * (-1.0 / (CODE_STEPS * LOG2E)))
    piece(block, (0, size), tile)[...] = (
        jnp.round(value * gain).astype(jnp.int32).astype(jnp.int16)
    )
    scales = jnp.broadcast_to(code.astype(jnp.int32), (EXTRA_ROWS, span)).astype(jnp.int16)
    piece(block, (size, EXTRA_ROWS), tile)[...] = scales


def decoded(block, size, tile):
    code = piece(block, (size, EXTRA_ROWS), tile)[...].astype(jnp.int32).astype(jnp.float32)
    gain = jnp.exp(code[:1] * (1.0 / (CODE_STEPS * LOG2E))) * (1.0 / CODE_TOP)
    return piece(block, (0, size), tile)[...].astype(jnp.int32).astype(jnp.float32) * gain


def call(kernel, name, operands, out_shape, scratch, room, cost, after=(), held_back=()):
    arrays = [a for a, _ in operands]
    held = sum(math.prod(a.shape) * a.dtype.itemsize for a in [*arrays, *out_shape])

    def body(*refs):
        results = refs[len(arrays) + len(after) + len(held_back) :]
        kernel(refs[: len(arrays)], results[: len(out_shape)] + results[len(out_shape) + len(held_back) :])

    return pl.pallas_call(
        body,
        out_shape=[*out_shape, *(jax.ShapeDtypeStruct(a.shape, a.dtype) for a in held_back)],
        in_specs=[s for _, s in operands] + [ANY] * (len(after) + len(held_back)),
        out_specs=[VMEM] * len(out_shape) + [ANY] * len(held_back),
        input_output_aliases={
            len(arrays) + len(after) + i: len(out_shape) + i for i in range(len(held_back))
        },
        scratch_shapes=scratch,
        compiler_params=pltpu.CompilerParams(vmem_limit_bytes=held + room),
        cost_estimate=pl.CostEstimate(flops=cost, bytes_accessed=cost, transcendentals=0),
        name=name,
    )(*arrays, *after, *held_back)


def labelled(images, labels, after=()):
    size, width = images.shape

    def kernel(ins, outs):
        outs[0][pl.ds(0, size), :] = ins[0][...]
        outs[0][pl.ds(size, EXTRA_ROWS), :] = jnp.zeros((EXTRA_ROWS, width), jnp.bfloat16)
        row = ins[1][...]
        low, high = lax.rem(row, LABEL_BASE), lax.div(row, LABEL_BASE)
        at = lax.broadcasted_iota(jnp.int32, (EXTRA_ROWS, size), 0)
        parts = jnp.where(at == 0, high, jnp.where(at == 1, low, 0)).astype(jnp.float32)
        outs[0][pl.ds(size, EXTRA_ROWS), pl.ds(0, size)] = parts.astype(jnp.bfloat16)

    shape = jax.ShapeDtypeStruct((size + EXTRA_ROWS, width), jnp.bfloat16)
    operands = [(images, VMEM), (labels, VMEM)]
    return call(kernel, "labelled", operands, [shape], [], 2**21, size, after)[0]


def bundled(arrays, cost):
    width = arrays[0].shape[1]

    def kernel(ins, outs):
        first = 0
        for ref in ins:
            outs[0][pl.ds(first, ref.shape[0]), :] = ref[...]
            first += ref.shape[0]

    shape = jax.ShapeDtypeStruct((sum(a.shape[0] for a in arrays), width), jnp.bfloat16)
    operands = [(a, VMEM) for a in arrays]
    return call(kernel, "bundled", operands, [shape], [], 2**21, cost)[0]


def first_row(mask, size):
    owner = (lax.axis_index("blk") ^ mask[0]) * lax.axis_size("grp") + (lax.axis_index("grp") ^ mask[1])
    return owner * size


def keys_of(block, size, mask, is_image):
    if not is_image:
        ids = lax.broadcasted_iota(jnp.int32, (1, size), 1) + first_row(mask, size)
        return ids.astype(jnp.float32)
    parts = piece(block, (size, EXTRA_ROWS), (0, 0, 0, size))[...].astype(jnp.float32)
    return parts[0:1] * LABEL_BASE + parts[1:2]


def core_number():
    return lax.rem(lax.axis_index("grp"), 2)


def gradient_sums(name, size, scalars, variants, emits, after=()):
    width = variants[0][0][0][0][0].shape[1]
    per_tile = TILE // size
    shapes = [
        jax.ShapeDtypeStruct((size, width), jnp.float32)
        if kind == "float"
        else jax.ShapeDtypeStruct((size + EXTRA_ROWS, width), jnp.int16)
        for kind in emits
    ]
    operands = Operands()
    slope_at, shift_at = [operands.add(s, SMEM) for s in scalars]
    views = []
    for x_blocks, y_blocks, masks, x_images, jobs, before, sequence in variants:
        for b in sequence:
            operands.block(b)
        x_views = [operands.block(b) for b in x_blocks]
        y_views = [operands.block(b) for b in y_blocks]
        before_at = {r: operands.add(b, VMEM) for r, b in before.items()}
        views.append((x_views, y_views, masks, x_images, jobs, before_at))

    def summed(ins, outs, weights, view):
        x_views, y_views, (x_masks, y_masks), x_images, jobs, before_at = view
        slope, shift = ins[slope_at][0] * LOG2E, ins[shift_at][0] * LOG2E
        x_refs, y_refs = [v(ins) for v in x_views], [v(ins) for v in y_views]

        def stacked(chosen):
            return jnp.concatenate(
                [ref[pl.ds(row, size), pl.ds(column, width)] for ((ref, row, column),) in chosen],
                axis=0,
            )

        for rows, columns in jobs:
            x_all = stacked([x_refs[r] for r in rows])
            keys = [
                jnp.broadcast_to(keys_of(x_refs[r], size, x_masks[r], x_images), (size, size)).T
                for r in rows
            ]
            for n in range(0, len(columns), per_tile):
                chosen = columns[n : n + per_tile]
                other = jnp.concatenate(
                    [keys_of(y_refs[c], size, y_masks[c], not x_images) for c in chosen], axis=1
                )
                scores = lax.dot_general(
                    x_all,
                    stacked([y_refs[c] for c in chosen]),
                    (((1,), (1,)), ((), ())),
                    preferred_element_type=jnp.float32,
                )
                for i in range(len(rows)):
                    z = scores[i * size : (i + 1) * size] * slope + shift
                    sig = 1.0 / (1.0 + jnp.exp2(-z))
                    w = jnp.where(jnp.tile(keys[i], (1, len(chosen))) == other, sig - 1.0, sig)
                    there = pl.ds(n * size, len(chosen) * size)
                    weights[pl.ds(i * size, size), there] = w.astype(jnp.bfloat16)
            for tile in column_tiles(width):
                sums = jnp.dot(
                    weights[pl.ds(0, len(rows) * size), pl.ds(0, len(columns) * size)],
                    jnp.concatenate([piece(y_refs[c], (0, size), tile)[...] for c in columns], axis=0),
                    preferred_element_type=jnp.float32,
                )
                for i, r in enumerate(rows):
                    block = sums[i * size : (i + 1) * size]
                    if r in before_at:
                        block = block + piece(whole(ins[before_at[r]]), (0, size), tile)[...]
                    if emits[r] == "float":
                        piece(whole(outs[r]), (0, size), tile)[...] = block
                    else:
                        encode(block, whole(outs[r]), tile)

    def kernel(ins, refs):
        outs, weights = refs[:-1], refs[-1]
        if len(views) == 1:
            summed(ins, outs, weights, views[0])
            return
        for core, view in enumerate(views):
            pl.when(core_number() == core)(lambda view=view: summed(ins, outs, weights, view))

    x_blocks, y_blocks, jobs = variants[0][0], variants[0][1], variants[0][4]
    pairs = sum(len(rows) * len(columns) for rows, columns in jobs)
    scratch = [pltpu.VMEM((len(x_blocks) * size, len(y_blocks) * size), jnp.bfloat16)]
    room = len(x_blocks) * len(y_blocks) * size * size * 2 + 8 * 2**20
    return call(kernel, name, operands.pairs, shapes, scratch, room, pairs * size, after)


def passed_sum(kept, received, held_back=(), after=()):
    size, width = kept.shape
    operands = Operands()
    kept_at = operands.add(kept, VMEM)
    views = [operands.block(b) for b in received]

    def kernel(ins, outs):
        for tile in column_tiles(width):
            total = piece(whole(ins[kept_at]), (0, size), tile)[...]
            for view in views:
                total = total + decoded(view(ins), size, tile)
            encode(total, whole(outs[0]), tile)

    shape = jax.ShapeDtypeStruct((size + EXTRA_ROWS, width), jnp.int16)
    return call(kernel, "passed_sum", operands.pairs, [shape], [], 2**21, size, after, held_back)


def output_sums(sharpness, sums):
    size, width = sums[0][0].shape
    operands = Operands()
    sharpness_at = operands.add(sharpness, SMEM)
    views = [(operands.add(kept, VMEM), [operands.block(b) for b in blocks]) for kept, blocks in sums]

    def write(ins, outs):
        for out, (kept_at, received) in zip(outs, views):
            for tile in column_tiles(width):
                total = piece(whole(ins[kept_at]), (0, size), tile)[...]
                for view in received:
                    total = total + decoded(view(ins), size, tile)
                piece(whole(out), (0, size), tile)[...] = total * ins[sharpness_at][0]

    def kernel(ins, outs):
        for core, order in enumerate((outs[::-1], outs)):
            pl.when(core_number() == core)(lambda order=order: write(ins, order))

    shapes = [jax.ShapeDtypeStruct((size, width), jnp.float32)] * len(sums)
    return call(kernel, "output_sums", operands.pairs, shapes, [], 2**21, size)


def swapped(array, step):
    axis, bit = step
    return lax.ppermute(array, axis, [(i, i ^ bit) for i in range(lax.axis_size(axis))])


def swapped_by_core(array, steps):
    grp_count = lax.axis_size("grp")
    route = []
    for i in range(lax.axis_size("blk") * grp_count):
        axis, bit = steps[i % 2]
        route.append((i, i ^ (bit * grp_count if axis == "blk" else bit)))
    return lax.ppermute(array, ("blk", "grp"), route)


def scattered(kept, coded, steps, after):
    steps = list(zip(*steps))

    def sent(array, step):
        return whole(swapped_by_core(array, step))

    half, waiting = len(kept), coded[:1]
    received = [[]] + [[sent(c, steps[-1])] for c in coded[1:]]
    for s in reversed(range(len(steps) - 1)):
        for m in reversed(range(1 << s)):
            n = m | 1 << s
            block, *held = passed_sum(kept[n], received[n], waiting, after)
            received[0] += [sent(c, steps[-1]) for c in held]
            received[m].append(sent(block, steps[s]))
            waiting, after = (), [block]
    return kept[0], received[0][::-1], after


def in_order(arrays, after=()):
    return call(lambda *refs: None, "held", [], [], [], 2**21, 1, after, arrays)


def bit_steps(axis):
    return [(axis, 1 << k) for k in range(int(math.log2(lax.axis_size(axis))))]


def owner_masks(steps):
    masks = [(0, 0)]
    for axis, bit in steps:
        masks = masks + [(b ^ bit, g) if axis == "blk" else (b, g ^ bit) for b, g in masks]
    return masks


def per_device(
    picture_vectors, caption_vectors, matching_caption, sharpness_parameter, additive_intercept
):
    scalars = (sharpness_parameter, additive_intercept)
    size = picture_vectors.shape[0]
    core, *grp_steps = bit_steps("grp")
    every = grp_steps + bit_steps("blk")
    steps = [every[0::2], every[1::2]]
    assert len(steps[0]) == len(steps[1]) >= 2
    masks = [owner_masks(s + [core]) for s in steps]
    count = 1 << len(steps[0])
    half = count // 2
    early, late = list(range(half + 1)), list(range(half + 1, count))
    labels = matching_caption[None, :]
    (first_texts,) = in_order([swapped(caption_vectors, steps[1][0])])
    first_images = [swapped(a, steps[0][0]) for a in (picture_vectors, labels)]
    arrays = [{0: labelled(picture_vectors, labels), 1: labelled(*first_images, [first_texts])}, {0: caption_vectors, 1: first_texts}]
    for i in range(1, len(steps[0])):
        for k in (1, 0):
            for m in range(1 << i):
                arrays[k][m | 1 << i] = swapped(arrays[k][m], steps[k][i])
    blocks = [[whole(a[m]) for m in range(count)] for a in arrays]
    others = [{}, {}]
    both = bundled([arrays[1][1], arrays[0][1]], BUNDLE_COST)
    rest = [m for m in early if m != 1]
    both = swapped(bundled([both] + [arrays[k][m] for m in rest for k in (1, 0)], size), core)
    for i, m in enumerate([1] + rest):
        row = i * (2 * size + EXTRA_ROWS)
        others[1][m], others[0][m] = ((both, row, 0),), ((both, row + size, 0),)

    def sums(name, kinds, rows, columns, jobs, befores, emits, after=()):
        variants = []
        for kind, before in zip(kinds, befores):
            other = 1 - kind
            x_blocks = [blocks[kind][m] for m in rows]
            y_blocks = [(blocks, others)[c][other][m] for c, m in columns]
            x_masks = [masks[kind][m] for m in rows]
            y_masks = [masks[other][m + c * count] for c, m in columns]
            sequence = [blocks[k][m] for m in rows[1:] + rows[:1] for k in (1, 0)]
            variants.append(
                (x_blocks, y_blocks, (x_masks, y_masks), kind == 0, jobs, before, sequence)
            )
        return gradient_sums(name, size, scalars, variants, emits, after)

    def both_cores(chosen):
        return [(c, m) for c in range(2) for m in chosen]

    def every_pair(rows, columns):
        return [(list(range(len(rows))), list(range(len(columns))))]

    before = []
    for k in range(2):
        columns = both_cores(early)
        jobs, emits = every_pair(early, columns), ["float"] * len(early)
        results = sums("early_sums", [k], early, columns, jobs, [{}], emits)
        before.append(dict(zip(early, results)))
    arrays = [[b[m][0][0] for m in late] for b in blocks[::-1]]
    arrays, before = lax.optimization_barrier((arrays, before))
    for k in (1, 0):
        for m, a in zip(late, arrays[1 - k]):
            blocks[k][m] = whole(a)
            others[k][m] = whole(swapped(a, core))
    turns, after = ((1, 0), (0, 1)), ()
    coded, kept, received = [[None] * half, [None] * half], [None, None], [None, None]
    for t, kinds in enumerate(turns):
        columns = [(0, m) for m in range(count)] + [(1, m) for m in early]
        jobs, emits = every_pair(late, columns), ["float"] * len(late)
        results = sums("late_rows_begun", kinds, late, columns, jobs, [{}, {}], emits, after)
        begun = dict(enumerate(results))
        columns = [(1, m) for m in late]
        jobs, emits = every_pair(late, columns), ["codes"] * len(late)
        coded[t][1:] = sums("late_rows", kinds, late, columns, jobs, [begun, begun], emits)
        after = coded[t][1:2]
    for t, kinds in enumerate(turns):
        columns = both_cores(late)
        jobs, emits = every_pair(early, columns), ["float"] * half + ["codes"]
        *kept[t], coded[t][0] = sums(
            "late_columns", kinds, early, columns, jobs, [before[k] for k in kinds], emits, after
        )
        after = coded[t][:1]
    after, ends = (), ()
    for t, kinds in enumerate(turns):
        kept[t], received[t], after = scattered(kept[t], coded[t], [steps[k] for k in kinds], after)
    for t in range(2):
        ends = in_order([b[0][0] for b in received[t][:-1]], ends)
        received[t] = [whole(a) for a in ends] + received[t][-1:]
    return tuple(output_sums(scalars[0], list(zip(kept, received))))


def solution(mesh):
    placed = (P(("blk", "grp"), None), P(("blk", "grp"), None), P(("blk", "grp")), P(), P())
    return jax.shard_map(
        per_device,
        mesh=mesh,
        in_specs=placed,
        out_specs=(P(("blk", "grp"), None), P(("blk", "grp"), None)),
        check_vma=False,
    )
```

```python
import math

import jax
import jax.numpy as jnp
from jax import lax
from jax.experimental import pallas as pl
from jax.experimental.pallas import tpu as pltpu
from jax.sharding import PartitionSpec as P

LOG2E = 1.4426950408889634
CODE_TOP = 32000.0
CODE_STEPS = 32.0
EXTRA_ROWS = 8
LABEL_BASE = 128
TILE = 256
LANES = 128
BUNDLE_COST = 6 * 10**8
HELD_COST = 85 * 10**7
SMEM = pl.BlockSpec(memory_space=pltpu.SMEM)
VMEM = pl.BlockSpec(memory_space=pltpu.VMEM)
ANY = pl.BlockSpec(memory_space=pl.ANY)


def whole(array):
    return ((array, 0, 0),)


def part_widths(width):
    first = (width // LANES + 1) // 2 * LANES
    return (first, width - first)


def column_tiles(width):
    tiles, begin = [], 0
    for p, w in enumerate(part_widths(width)):
        tiles += [(p, k, begin + k, min(TILE, w - k)) for k in range(0, w, TILE)]
        begin += w
    return tiles


def piece(block, rows, tile):
    p, inner, start, span = tile
    ref, row, column = block[0 if len(block) == 1 else p]
    first = start if len(block) == 1 else inner
    return ref.at[pl.ds(row + rows[0], rows[1]), pl.ds(column + first, span)]


class Operands:
    def __init__(self):
        self.pairs = []

    def add(self, array, spec):
        for i, (a, s) in enumerate(self.pairs):
            if a is array and s is spec:
                return i
        self.pairs.append((array, spec))
        return len(self.pairs) - 1

    def block(self, block):
        at = [(self.add(a, VMEM), row, column) for a, row, column in block]
        return lambda refs: tuple((refs[i], row, column) for i, row, column in at)


def scale_code(top):
    return jnp.ceil(jnp.log(jnp.maximum(top, 1e-30)) * (CODE_STEPS * LOG2E))


def encode(value, block, tile):
    size, span = value.shape
    code = scale_code(jnp.max(jnp.abs(value), axis=0, keepdims=True))
    gain = CODE_TOP * jnp.exp(code * (-1.0 / (CODE_STEPS * LOG2E)))
    piece(block, (0, size), tile)[...] = (
        jnp.round(value * gain).astype(jnp.int32).astype(jnp.int16)
    )
    scales = jnp.broadcast_to(code.astype(jnp.int32), (EXTRA_ROWS, span)).astype(jnp.int16)
    piece(block, (size, EXTRA_ROWS), tile)[...] = scales


def decoded(block, size, tile):
    code = piece(block, (size, EXTRA_ROWS), tile)[...].astype(jnp.int32).astype(jnp.float32)
    gain = jnp.exp(code[:1] * (1.0 / (CODE_STEPS * LOG2E))) * (1.0 / CODE_TOP)
    return piece(block, (0, size), tile)[...].astype(jnp.int32).astype(jnp.float32) * gain


def call(kernel, name, operands, out_shape, scratch, room, cost, after=(), held_back=()):
    arrays = [a for a, _ in operands]
    held = sum(math.prod(a.shape) * a.dtype.itemsize for a in [*arrays, *out_shape])

    def body(*refs):
        results = refs[len(arrays) + len(after) + len(held_back) :]
        kernel(refs[: len(arrays)], results[: len(out_shape)] + results[len(out_shape) + len(held_back) :])

    return pl.pallas_call(
        body,
        out_shape=[*out_shape, *(jax.ShapeDtypeStruct(a.shape, a.dtype) for a in held_back)],
        in_specs=[s for _, s in operands] + [ANY] * (len(after) + len(held_back)),
        out_specs=[VMEM] * len(out_shape) + [ANY] * len(held_back),
        input_output_aliases={
            len(arrays) + len(after) + i: len(out_shape) + i for i in range(len(held_back))
        },
        scratch_shapes=scratch,
        compiler_params=pltpu.CompilerParams(vmem_limit_bytes=held + room),
        cost_estimate=pl.CostEstimate(flops=cost, bytes_accessed=cost, transcendentals=0),
        name=name,
    )(*arrays, *after, *held_back)


def labelled(images, labels, after=()):
    size, width = images.shape

    def kernel(ins, outs):
        outs[0][pl.ds(0, size), :] = ins[0][...]
        outs[0][pl.ds(size, EXTRA_ROWS), :] = jnp.zeros((EXTRA_ROWS, width), jnp.bfloat16)
        row = ins[1][...]
        low, high = lax.rem(row, LABEL_BASE), lax.div(row, LABEL_BASE)
        at = lax.broadcasted_iota(jnp.int32, (EXTRA_ROWS, size), 0)
        parts = jnp.where(at == 0, high, jnp.where(at == 1, low, 0)).astype(jnp.float32)
        outs[0][pl.ds(size, EXTRA_ROWS), pl.ds(0, size)] = parts.astype(jnp.bfloat16)

    shape = jax.ShapeDtypeStruct((size + EXTRA_ROWS, width), jnp.bfloat16)
    operands = [(images, VMEM), (labels, VMEM)]
    return call(kernel, "labelled", operands, [shape], [], 2**21, size, after)[0]


def bundled(arrays, cost):
    width = arrays[0].shape[1]

    def kernel(ins, outs):
        first = 0
        for ref in ins:
            outs[0][pl.ds(first, ref.shape[0]), :] = ref[...]
            first += ref.shape[0]

    shape = jax.ShapeDtypeStruct((sum(a.shape[0] for a in arrays), width), jnp.bfloat16)
    operands = [(a, VMEM) for a in arrays]
    return call(kernel, "bundled", operands, [shape], [], 2**21, cost)[0]


def first_row(mask, size):
    owner = (lax.axis_index("blk") ^ mask[0]) * lax.axis_size("grp") + (lax.axis_index("grp") ^ mask[1])
    return owner * size


def keys_of(block, size, mask, is_image):
    if not is_image:
        ids = lax.broadcasted_iota(jnp.int32, (1, size), 1) + first_row(mask, size)
        return ids.astype(jnp.float32)
    parts = piece(block, (size, EXTRA_ROWS), (0, 0, 0, size))[...].astype(jnp.float32)
    return parts[0:1] * LABEL_BASE + parts[1:2]


def gradient_sums(name, size, scalars, x_blocks, y_blocks, masks, x_images, jobs, before, emits, sequence, after=()):
    width = x_blocks[0][0][0].shape[1]
    x_masks, y_masks = masks
    per_tile = TILE // size
    widths = part_widths(width)
    shapes, where = [], {}

    def result(extra, w, dtype):
        shapes.append(jax.ShapeDtypeStruct((size + extra, w), dtype))
        return len(shapes) - 1

    for r, kind in enumerate(emits):
        if kind == "float":
            where[r] = [(result(0, width, jnp.float32), 0, 0)]
        else:
            cut = widths if kind == "parts" else (width,)
            where[r] = [(result(EXTRA_ROWS, w, jnp.int16), 0, 0) for w in cut]
    operands = Operands()
    slope_at, shift_at = [operands.add(s, SMEM) for s in scalars]
    for b in sequence:
        operands.block(b)
    x_views = [operands.block(b) for b in x_blocks]
    y_views = [operands.block(b) for b in y_blocks]
    before_at = {r: operands.add(b, VMEM) for r, b in before.items()}

    def kernel(ins, refs):
        outs, weights = refs[:-1], refs[-1]
        slope, shift = ins[slope_at][0] * LOG2E, ins[shift_at][0] * LOG2E
        x_refs, y_refs = [v(ins) for v in x_views], [v(ins) for v in y_views]

        def stacked(chosen):
            return jnp.concatenate(
                [ref[pl.ds(row, size), pl.ds(column, width)] for ((ref, row, column),) in chosen],
                axis=0,
            )

        for rows, columns in jobs:
            x_all = stacked([x_refs[r] for r in rows])
            keys = [
                jnp.broadcast_to(keys_of(x_refs[r], size, x_masks[r], x_images), (size, size)).T
                for r in rows
            ]
            for n in range(0, len(columns), per_tile):
                chosen = columns[n : n + per_tile]
                other = jnp.concatenate(
                    [keys_of(y_refs[c], size, y_masks[c], not x_images) for c in chosen], axis=1
                )
                scores = lax.dot_general(
                    x_all,
                    stacked([y_refs[c] for c in chosen]),
                    (((1,), (1,)), ((), ())),
                    preferred_element_type=jnp.float32,
                )
                for i in range(len(rows)):
                    z = scores[i * size : (i + 1) * size] * slope + shift
                    sig = 1.0 / (1.0 + jnp.exp2(-z))
                    w = jnp.where(jnp.tile(keys[i], (1, len(chosen))) == other, sig - 1.0, sig)
                    there = pl.ds(n * size, len(chosen) * size)
                    weights[pl.ds(i * size, size), there] = w.astype(jnp.bfloat16)
            for tile in column_tiles(width):
                sums = jnp.dot(
                    weights[pl.ds(0, len(rows) * size), pl.ds(0, len(columns) * size)],
                    jnp.concatenate([piece(y_refs[c], (0, size), tile)[...] for c in columns], axis=0),
                    preferred_element_type=jnp.float32,
                )
                for i, r in enumerate(rows):
                    block = sums[i * size : (i + 1) * size]
                    if r in before_at:
                        block = block + piece(whole(ins[before_at[r]]), (0, size), tile)[...]
                    out = tuple((outs[o], row, column) for o, row, column in where[r])
                    if emits[r] == "float":
                        piece(out, (0, size), tile)[...] = block
                    else:
                        encode(block, out, tile)

    pairs = sum(len(rows) * len(columns) for rows, columns in jobs)
    scratch = [pltpu.VMEM((len(x_blocks) * size, len(y_blocks) * size), jnp.bfloat16)]
    room = len(x_blocks) * len(y_blocks) * size * size * 2 + 8 * 2**20
    results = call(kernel, name, operands.pairs, shapes, scratch, room, pairs * size, after)
    return [tuple(results[o] for o, _, _ in where[r]) for r in range(len(emits))]


def passed_sum(kept, received, part, held_back=(), after=()):
    size, width = kept.shape
    operands = Operands()
    kept_at = operands.add(kept, VMEM)
    views = [operands.block(b if part is None or len(b) == 1 else (b[part],) * 2) for b in received]

    def kernel(ins, outs):
        for tile in column_tiles(width):
            p, inner, _, span = tile
            if part is None or p == part:
                total = piece(whole(ins[kept_at]), (0, size), tile)[...]
                for view in views:
                    total = total + decoded(view(ins), size, tile)
                encode(total, whole(outs[0]), tile if part is None else (0, 0, inner, span))

    cut = width if part is None else part_widths(width)[part]
    shape = jax.ShapeDtypeStruct((size + EXTRA_ROWS, cut), jnp.int16)
    return call(kernel, "passed_sum", operands.pairs, [shape], [], 2**21, size, after, held_back)


def output_sums(sharpness, sums):
    size, width = sums[0][0].shape
    operands = Operands()
    sharpness_at = operands.add(sharpness, SMEM)
    views = [(operands.add(kept, VMEM), [operands.block(b) for b in blocks]) for kept, blocks in sums]

    def kernel(ins, outs):
        for out, (kept_at, received) in zip(outs, views):
            for tile in column_tiles(width):
                total = piece(whole(ins[kept_at]), (0, size), tile)[...]
                for view in received:
                    total = total + decoded(view(ins), size, tile)
                piece(whole(out), (0, size), tile)[...] = total * ins[sharpness_at][0]

    shapes = [jax.ShapeDtypeStruct((size, width), jnp.float32)] * len(sums)
    return call(kernel, "output_sums", operands.pairs, shapes, [], 2**21, size)


def swapped(array, step):
    axis, bit = step
    return lax.ppermute(array, axis, [(i, i ^ bit) for i in range(lax.axis_size(axis))])


def scattered(kept, coded, steps, after):
    def sent(array, step):
        return (swapped(array, step), 0, 0)

    half = len(kept)
    received = [[]] + [[(sent(c[0], steps[-1]),)] for c in coded[1:]]
    waiting, last = [c[1] for c in coded[1:]], [coded[0][0]]
    for s in reversed(range(len(steps) - 1)):
        for m in reversed(range(1 << s)):
            n = m | 1 << s
            first, *begun = passed_sum(kept[n], received[n], 0, waiting + last)
            for r, c in zip(received[1:], begun):
                r[0] = r[0] + (sent(c, steps[-1]),)
            received[0] += [(sent(c, steps[-1]),) for c in begun[len(waiting) :]]
            first = sent(first, steps[s])
            (second,) = passed_sum(kept[n], received[n], 1, (), [first[0], *after])
            received[m].append((first, sent(second, steps[s])))
            waiting, last, after = [], [], [second]
    return kept[0], received[0], after


def in_order(arrays, after=(), cost=HELD_COST):
    return call(lambda *refs: None, "held", [], [], [], 2**21, cost, after, arrays)


def bit_steps(axis):
    return [(axis, 1 << k) for k in range(int(math.log2(lax.axis_size(axis))))]


def owner_masks(steps):
    masks = [(0, 0)]
    for axis, bit in steps:
        masks = masks + [(b ^ bit, g) if axis == "blk" else (b, g ^ bit) for b, g in masks]
    return masks


def per_device(
    picture_vectors, caption_vectors, matching_caption, sharpness_parameter, additive_intercept
):
    scalars = (sharpness_parameter, additive_intercept)
    size = picture_vectors.shape[0]
    core, *grp_steps = bit_steps("grp")
    every = grp_steps + bit_steps("blk")
    steps = [every[0::2], every[1::2]]
    assert len(steps[0]) == len(steps[1]) >= 2
    masks = [owner_masks(s + [core]) for s in steps]
    count = 1 << len(steps[0])
    half = count // 2
    early, late = list(range(half + 1)), list(range(half + 1, count))
    labels = matching_caption[None, :]
    (first_texts,) = in_order([swapped(caption_vectors, steps[1][0])], (), 1)
    first_images = [swapped(a, steps[0][0]) for a in (picture_vectors, labels)]
    arrays = [{0: labelled(picture_vectors, labels), 1: labelled(*first_images, [first_texts])}, {0: caption_vectors, 1: first_texts}]
    for i in range(1, len(steps[0])):
        for k in (1, 0):
            for m in range(1 << i):
                arrays[k][m | 1 << i] = swapped(arrays[k][m], steps[k][i])
    blocks = [[whole(a[m]) for m in range(count)] for a in arrays]
    others = [{}, {}]
    both = bundled([arrays[1][1], arrays[0][1]], BUNDLE_COST)
    rest = [m for m in early if m != 1]
    both = swapped(bundled([both] + [arrays[k][m] for m in rest for k in (1, 0)], size), core)
    for i, m in enumerate([1] + rest):
        row = i * (2 * size + EXTRA_ROWS)
        others[1][m], others[0][m] = ((both, row, 0),), ((both, row + size, 0),)

    def sums(name, kind, rows, columns, jobs, before, emits, after=()):
        other = 1 - kind
        x_blocks = [blocks[kind][m] for m in rows]
        y_blocks = [(blocks, others)[c][other][m] for c, m in columns]
        x_masks = [masks[kind][m] for m in rows]
        y_masks = [masks[other][m + c * count] for c, m in columns]
        return gradient_sums(
            name,
            size,
            scalars,
            x_blocks,
            y_blocks,
            (x_masks, y_masks),
            kind == 0,
            jobs,
            before,
            emits,
            [blocks[k][m] for m in rows[1:] + rows[:1] for k in (1, 0)],
            after,
        )

    def both_cores(chosen):
        return [(c, m) for c in range(2) for m in chosen]

    def every_pair(rows, columns):
        return [(list(range(len(rows))), list(range(len(columns))))]

    before = []
    for k in range(2):
        columns = both_cores(early)
        jobs, emits = every_pair(early, columns), ["float"] * len(early)
        results = sums("early_sums", k, early, columns, jobs, {}, emits)
        before.append({m: s for m, (s,) in zip(early, results)})
    after = [s for k in range(2) for s in before[k].values()]
    for k in range(2):
        held = in_order([blocks[k][m][0][0] for m in late], after if k == 0 else (), (1, BUNDLE_COST)[k])
        after = [swapped(a, core) for a in held]
        for m, mine, other in zip(late, held, after):
            blocks[k][m], others[k][m] = whole(mine), whole(other)
    after = ()
    coded, kept = [[None] * half, [None] * half], [None, None]
    for k in (1, 0):
        columns = both_cores(range(count))
        jobs, emits = every_pair(late, columns), ["parts"] * len(late)
        coded[k][1:] = sums("late_rows", k, late, columns, jobs, {}, emits, after)
        after = coded[k][1]
    for k in (1, 0):
        columns = both_cores(late)
        jobs, emits = every_pair(early, columns), ["float"] * half + ["whole"]
        *whole_sums, coded[k][0] = sums("late_columns", k, early, columns, jobs, before[k], emits, after)
        kept[k], after = [s for (s,) in whole_sums], coded[k][0]
    kept_texts, text_blocks, after = scattered(kept[1], coded[1], steps[1], ())
    kept_images, image_blocks, _ = scattered(kept[0], coded[0], steps[0], after)
    ends = ()
    for blocks_in in (text_blocks, image_blocks):
        ends = in_order([part[0] for b in blocks_in if len(b) > 1 for part in b], ends)
        parts = iter(ends)
        blocks_in[:] = [tuple((next(parts), 0, 0) for _ in b) if len(b) > 1 else b for b in blocks_in]
    return tuple(output_sums(scalars[0], [(kept_images, image_blocks), (kept_texts, text_blocks)]))


def solution(mesh):
    placed = (P(("blk", "grp"), None), P(("blk", "grp"), None), P(("blk", "grp")), P(), P())
    return jax.shard_map(
        per_device,
        mesh=mesh,
        in_specs=placed,
        out_specs=(P(("blk", "grp"), None), P(("blk", "grp"), None)),
        check_vma=False,
    )
```

```python
import math

import jax
import jax.numpy as jnp
from jax import lax
from jax.experimental import pallas as pl
from jax.experimental.pallas import tpu as pltpu
from jax.sharding import PartitionSpec as P

LOG2E = 1.4426950408889634
CODE_TOP = 32000.0
CODE_STEPS = 32.0
EXTRA_ROWS = 8
LABEL_BASE = 128
TILE = 256
LANES = 128
BUNDLE_COST = 6 * 10**8
HELD_COST = 85 * 10**7
SMEM = pl.BlockSpec(memory_space=pltpu.SMEM)
VMEM = pl.BlockSpec(memory_space=pltpu.VMEM)
ANY = pl.BlockSpec(memory_space=pl.ANY)


def whole(array):
    return ((array, 0, 0),)


def part_widths(width):
    first = (width // LANES + 1) // 2 * LANES
    return (first, width - first)


def column_tiles(width):
    tiles, begin = [], 0
    for p, w in enumerate(part_widths(width)):
        tiles += [(p, k, begin + k, min(TILE, w - k)) for k in range(0, w, TILE)]
        begin += w
    return tiles


def piece(block, rows, tile):
    p, inner, start, span = tile
    ref, row, column = block[0 if len(block) == 1 else p]
    first = start if len(block) == 1 else inner
    return ref.at[pl.ds(row + rows[0], rows[1]), pl.ds(column + first, span)]


class Operands:
    def __init__(self):
        self.pairs = []

    def add(self, array, spec):
        for i, (a, s) in enumerate(self.pairs):
            if a is array and s is spec:
                return i
        self.pairs.append((array, spec))
        return len(self.pairs) - 1

    def block(self, block):
        at = [(self.add(a, VMEM), row, column) for a, row, column in block]
        return lambda refs: tuple((refs[i], row, column) for i, row, column in at)


def scale_code(top):
    return jnp.ceil(jnp.log(jnp.maximum(top, 1e-30)) * (CODE_STEPS * LOG2E))


def encode(value, block, tile):
    size, span = value.shape
    code = scale_code(jnp.max(jnp.abs(value), axis=0, keepdims=True))
    gain = CODE_TOP * jnp.exp(code * (-1.0 / (CODE_STEPS * LOG2E)))
    piece(block, (0, size), tile)[...] = (
        jnp.round(value * gain).astype(jnp.int32).astype(jnp.int16)
    )
    scales = jnp.broadcast_to(code.astype(jnp.int32), (EXTRA_ROWS, span)).astype(jnp.int16)
    piece(block, (size, EXTRA_ROWS), tile)[...] = scales


def decoded(block, size, tile):
    code = piece(block, (size, EXTRA_ROWS), tile)[...].astype(jnp.int32).astype(jnp.float32)
    gain = jnp.exp(code[:1] * (1.0 / (CODE_STEPS * LOG2E))) * (1.0 / CODE_TOP)
    return piece(block, (0, size), tile)[...].astype(jnp.int32).astype(jnp.float32) * gain


def call(kernel, name, operands, out_shape, scratch, room, cost, after=(), held_back=(), out_spec=VMEM):
    arrays = [a for a, _ in operands]
    held = sum(math.prod(a.shape) * a.dtype.itemsize for a in [*arrays, *out_shape])

    def body(*refs):
        results = refs[len(arrays) + len(after) + len(held_back) :]
        kernel(refs[: len(arrays)], results[: len(out_shape)] + results[len(out_shape) + len(held_back) :])

    return pl.pallas_call(
        body,
        out_shape=[*out_shape, *(jax.ShapeDtypeStruct(a.shape, a.dtype) for a in held_back)],
        in_specs=[s for _, s in operands] + [ANY] * (len(after) + len(held_back)),
        out_specs=[out_spec] * len(out_shape) + [ANY] * len(held_back),
        input_output_aliases={
            len(arrays) + len(after) + i: len(out_shape) + i for i in range(len(held_back))
        },
        scratch_shapes=scratch,
        compiler_params=pltpu.CompilerParams(vmem_limit_bytes=held + room),
        cost_estimate=pl.CostEstimate(flops=cost, bytes_accessed=cost, transcendentals=0),
        name=name,
    )(*arrays, *after, *held_back)


def labelled(images, labels, after=()):
    size, width = images.shape

    def kernel(ins, outs):
        outs[0][pl.ds(0, size), :] = ins[0][...]
        outs[0][pl.ds(size, EXTRA_ROWS), :] = jnp.zeros((EXTRA_ROWS, width), jnp.bfloat16)
        row = ins[1][...]
        low, high = lax.rem(row, LABEL_BASE), lax.div(row, LABEL_BASE)
        at = lax.broadcasted_iota(jnp.int32, (EXTRA_ROWS, size), 0)
        parts = jnp.where(at == 0, high, jnp.where(at == 1, low, 0)).astype(jnp.float32)
        outs[0][pl.ds(size, EXTRA_ROWS), pl.ds(0, size)] = parts.astype(jnp.bfloat16)

    shape = jax.ShapeDtypeStruct((size + EXTRA_ROWS, width), jnp.bfloat16)
    operands = [(images, VMEM), (labels, VMEM)]
    return call(kernel, "labelled", operands, [shape], [], 2**21, size, after)[0]


def bundled(arrays, cost):
    width = arrays[0].shape[1]

    def kernel(ins, outs):
        first = 0
        for ref in ins:
            outs[0][pl.ds(first, ref.shape[0]), :] = ref[...]
            first += ref.shape[0]

    shape = jax.ShapeDtypeStruct((sum(a.shape[0] for a in arrays), width), jnp.bfloat16)
    operands = [(a, VMEM) for a in arrays]
    return call(kernel, "bundled", operands, [shape], [], 2**21, cost)[0]


def first_row(mask, size):
    owner = (lax.axis_index("blk") ^ mask[0]) * lax.axis_size("grp") + (lax.axis_index("grp") ^ mask[1])
    return owner * size


def keys_of(block, size, mask, is_image):
    if not is_image:
        ids = lax.broadcasted_iota(jnp.int32, (1, size), 1) + first_row(mask, size)
        return ids.astype(jnp.float32)
    parts = piece(block, (size, EXTRA_ROWS), (0, 0, 0, size))[...].astype(jnp.float32)
    return parts[0:1] * LABEL_BASE + parts[1:2]


def gradient_sums(name, size, scalars, x_blocks, y_blocks, masks, x_images, jobs, before, emits, sequence, after=()):
    width = x_blocks[0][0][0].shape[1]
    x_masks, y_masks = masks
    per_tile = TILE // size
    widths = part_widths(width)
    shapes, where = [], {}

    def result(extra, w, dtype):
        shapes.append(jax.ShapeDtypeStruct((size + extra, w), dtype))
        return len(shapes) - 1

    for r, kind in enumerate(emits):
        if kind == "float":
            where[r] = [(result(0, width, jnp.float32), 0, 0)]
        else:
            cut = widths if kind == "parts" else (width,)
            where[r] = [(result(EXTRA_ROWS, w, jnp.int16), 0, 0) for w in cut]
    operands = Operands()
    slope_at, shift_at = [operands.add(s, SMEM) for s in scalars]
    for b in sequence:
        operands.block(b)
    x_views = [operands.block(b) for b in x_blocks]
    y_views = [operands.block(b) for b in y_blocks]
    before_at = {r: operands.add(b, VMEM) for r, b in before.items()}

    def kernel(ins, refs):
        outs, weights = refs[:-1], refs[-1]
        slope, shift = ins[slope_at][0] * LOG2E, ins[shift_at][0] * LOG2E
        x_refs, y_refs = [v(ins) for v in x_views], [v(ins) for v in y_views]

        def stacked(chosen):
            return jnp.concatenate(
                [ref[pl.ds(row, size), pl.ds(column, width)] for ((ref, row, column),) in chosen],
                axis=0,
            )

        for rows, columns in jobs:
            x_all = stacked([x_refs[r] for r in rows])
            keys = [
                jnp.broadcast_to(keys_of(x_refs[r], size, x_masks[r], x_images), (size, size)).T
                for r in rows
            ]
            for n in range(0, len(columns), per_tile):
                chosen = columns[n : n + per_tile]
                other = jnp.concatenate(
                    [keys_of(y_refs[c], size, y_masks[c], not x_images) for c in chosen], axis=1
                )
                scores = lax.dot_general(
                    x_all,
                    stacked([y_refs[c] for c in chosen]),
                    (((1,), (1,)), ((), ())),
                    preferred_element_type=jnp.float32,
                )
                for i in range(len(rows)):
                    z = scores[i * size : (i + 1) * size] * slope + shift
                    sig = 1.0 / (1.0 + jnp.exp2(-z))
                    w = jnp.where(jnp.tile(keys[i], (1, len(chosen))) == other, sig - 1.0, sig)
                    there = pl.ds(n * size, len(chosen) * size)
                    weights[pl.ds(i * size, size), there] = w.astype(jnp.bfloat16)
            for tile in column_tiles(width):
                sums = jnp.dot(
                    weights[pl.ds(0, len(rows) * size), pl.ds(0, len(columns) * size)],
                    jnp.concatenate([piece(y_refs[c], (0, size), tile)[...] for c in columns], axis=0),
                    preferred_element_type=jnp.float32,
                )
                for i, r in enumerate(rows):
                    block = sums[i * size : (i + 1) * size]
                    if r in before_at:
                        block = block + piece(whole(ins[before_at[r]]), (0, size), tile)[...]
                    out = tuple((outs[o], row, column) for o, row, column in where[r])
                    if emits[r] == "float":
                        piece(out, (0, size), tile)[...] = block
                    else:
                        encode(block, out, tile)

    pairs = sum(len(rows) * len(columns) for rows, columns in jobs)
    scratch = [pltpu.VMEM((len(x_blocks) * size, len(y_blocks) * size), jnp.bfloat16)]
    room = len(x_blocks) * len(y_blocks) * size * size * 2 + 8 * 2**20
    results = call(kernel, name, operands.pairs, shapes, scratch, room, pairs * size, after)
    return [tuple(results[o] for o, _, _ in where[r]) for r in range(len(emits))]


def passed_sum(kept, received, part, held_back=(), after=()):
    size, width = kept.shape
    operands = Operands()
    kept_at = operands.add(kept, VMEM)
    views = [operands.block(b if part is None or len(b) == 1 else (b[part],) * 2) for b in received]

    def kernel(ins, outs):
        for tile in column_tiles(width):
            p, inner, _, span = tile
            if part is None or p == part:
                total = piece(whole(ins[kept_at]), (0, size), tile)[...]
                for view in views:
                    total = total + decoded(view(ins), size, tile)
                encode(total, whole(outs[0]), tile if part is None else (0, 0, inner, span))

    cut = width if part is None else part_widths(width)[part]
    shape = jax.ShapeDtypeStruct((size + EXTRA_ROWS, cut), jnp.int16)
    return call(kernel, "passed_sum", operands.pairs, [shape], [], 2**21, size, after, held_back)


def output_sums(sharpness, sums):
    size, width = sums[0][0].shape
    operands = Operands()
    sharpness_at = operands.add(sharpness, SMEM)
    views = [(operands.add(kept, VMEM), [operands.block(b) for b in blocks]) for kept, blocks in sums]
    tiles = column_tiles(width)

    def kernel(ins, refs):
        outs, held, sems = refs[: len(sums)], refs[len(sums) : -1], refs[-1]
        copies = []
        for k, (kept_at, received) in enumerate(views):
            for n, tile in enumerate(tiles):
                total = piece(whole(ins[kept_at]), (0, size), tile)[...]
                for view in received:
                    total = total + decoded(view(ins), size, tile)
                source = piece(whole(held[k]), (0, size), tile)
                source[...] = total * ins[sharpness_at][0]
                target = piece(whole(outs[k]), (0, size), tile)
                copies.append(pltpu.make_async_copy(source, target, sems.at[k, n]))
                copies[-1].start()
        for c in copies:
            c.wait()

    shapes = [jax.ShapeDtypeStruct((size, width), jnp.float32)] * len(sums)
    scratch = [pltpu.VMEM((size, width), jnp.float32) for _ in sums]
    scratch += [pltpu.SemaphoreType.DMA((len(sums), len(tiles)))]
    return call(kernel, "output_sums", operands.pairs, shapes, scratch, 2**22, size, out_spec=ANY)


def swapped(array, step):
    axis, bit = step
    return lax.ppermute(array, axis, [(i, i ^ bit) for i in range(lax.axis_size(axis))])


def scattered(kept, coded, steps, after):
    def sent(array, step):
        return (swapped(array, step), 0, 0)

    half = len(kept)
    received = [[]] + [[(sent(c[0], steps[-1]),)] for c in coded[1:]]
    waiting, last = [c[1] for c in coded[1:]], [coded[0][0]]
    for s in reversed(range(len(steps) - 1)):
        for m in reversed(range(1 << s)):
            n = m | 1 << s
            first, *begun = passed_sum(kept[n], received[n], 0, waiting + last)
            for r, c in zip(received[1:], begun):
                r[0] = r[0] + (sent(c, steps[-1]),)
            received[0] += [(sent(c, steps[-1]),) for c in begun[len(waiting) :]]
            first = sent(first, steps[s])
            (second,) = passed_sum(kept[n], received[n], 1, (), [first[0], *after])
            received[m].append((first, sent(second, steps[s])))
            waiting, last, after = [], [], [second]
    return kept[0], received[0], after


def in_order(arrays, after=(), cost=HELD_COST):
    return call(lambda *refs: None, "held", [], [], [], 2**21, cost, after, arrays)


def bit_steps(axis):
    return [(axis, 1 << k) for k in range(int(math.log2(lax.axis_size(axis))))]


def owner_masks(steps):
    masks = [(0, 0)]
    for axis, bit in steps:
        masks = masks + [(b ^ bit, g) if axis == "blk" else (b, g ^ bit) for b, g in masks]
    return masks


def per_device(
    picture_vectors, caption_vectors, matching_caption, sharpness_parameter, additive_intercept
):
    scalars = (sharpness_parameter, additive_intercept)
    size = picture_vectors.shape[0]
    core, *grp_steps = bit_steps("grp")
    every = grp_steps + bit_steps("blk")
    steps = [every[0::2], every[1::2]]
    assert len(steps[0]) == len(steps[1]) >= 2
    masks = [owner_masks(s + [core]) for s in steps]
    count = 1 << len(steps[0])
    half = count // 2
    early, late = list(range(half + 1)), list(range(half + 1, count))
    labels = matching_caption[None, :]
    (first_texts,) = in_order([swapped(caption_vectors, steps[1][0])], (), 1)
    first_images = [swapped(a, steps[0][0]) for a in (picture_vectors, labels)]
    arrays = [{0: labelled(picture_vectors, labels), 1: labelled(*first_images, [first_texts])}, {0: caption_vectors, 1: first_texts}]
    for i in range(1, len(steps[0])):
        for k in (1, 0):
            for m in range(1 << i):
                arrays[k][m | 1 << i] = swapped(arrays[k][m], steps[k][i])
    blocks = [[whole(a[m]) for m in range(count)] for a in arrays]
    others = [{}, {}]
    both = bundled([arrays[1][1], arrays[0][1]], BUNDLE_COST)
    rest = [m for m in early if m != 1]
    both = swapped(bundled([both] + [arrays[k][m] for m in rest for k in (1, 0)], size), core)
    for i, m in enumerate([1] + rest):
        row = i * (2 * size + EXTRA_ROWS)
        others[1][m], others[0][m] = ((both, row, 0),), ((both, row + size, 0),)

    def sums(name, kind, rows, columns, jobs, before, emits, after=()):
        other = 1 - kind
        x_blocks = [blocks[kind][m] for m in rows]
        y_blocks = [(blocks, others)[c][other][m] for c, m in columns]
        x_masks = [masks[kind][m] for m in rows]
        y_masks = [masks[other][m + c * count] for c, m in columns]
        return gradient_sums(
            name,
            size,
            scalars,
            x_blocks,
            y_blocks,
            (x_masks, y_masks),
            kind == 0,
            jobs,
            before,
            emits,
            [blocks[k][m] for m in rows[1:] + rows[:1] for k in (1, 0)],
            after,
        )

    def both_cores(chosen):
        return [(c, m) for c in range(2) for m in chosen]

    def every_pair(rows, columns):
        return [(list(range(len(rows))), list(range(len(columns))))]

    before = []
    for k in range(2):
        columns = both_cores(early)
        jobs, emits = every_pair(early, columns), ["float"] * len(early)
        results = sums("early_sums", k, early, columns, jobs, {}, emits)
        before.append({m: s for m, (s,) in zip(early, results)})
    arrays = [[b[m][0][0] for m in late] for b in blocks[::-1]]
    arrays, before = lax.optimization_barrier((arrays, before))
    for k in (1, 0):
        for m, a in zip(late, arrays[1 - k]):
            blocks[k][m] = whole(a)
            others[k][m] = whole(swapped(a, core))
    after = ()
    coded, kept = [[None] * half, [None] * half], [None, None]
    for k in (1, 0):
        columns = [(0, m) for m in range(count)] + [(1, m) for m in early]
        jobs, emits = every_pair(late, columns), ["float"] * len(late)
        results = sums("late_rows_begun", k, late, columns, jobs, {}, emits, after)
        begun = {i: s for i, (s,) in enumerate(results)}
        columns = [(1, m) for m in late]
        jobs, emits = every_pair(late, columns), ["parts"] * len(late)
        coded[k][1:] = sums("late_rows", k, late, columns, jobs, begun, emits)
        after = coded[k][1]
    for k in (1, 0):
        columns = both_cores(late)
        jobs, emits = every_pair(early, columns), ["float"] * half + ["whole"]
        *whole_sums, coded[k][0] = sums("late_columns", k, early, columns, jobs, before[k], emits, after)
        kept[k], after = [s for (s,) in whole_sums], coded[k][0]
    kept_texts, text_blocks, after = scattered(kept[1], coded[1], steps[1], ())
    kept_images, image_blocks, _ = scattered(kept[0], coded[0], steps[0], after)
    ends = ()
    for blocks_in in (text_blocks, image_blocks):
        ends = in_order([part[0] for b in blocks_in if len(b) > 1 for part in b], ends)
        parts = iter(ends)
        blocks_in[:] = [tuple((next(parts), 0, 0) for _ in b) if len(b) > 1 else b for b in blocks_in]
    return tuple(output_sums(scalars[0], [(kept_images, image_blocks), (kept_texts, text_blocks)]))


def solution(mesh):
    placed = (P(("blk", "grp"), None), P(("blk", "grp"), None), P(("blk", "grp")), P(), P())
    return jax.shard_map(
        per_device,
        mesh=mesh,
        in_specs=placed,
        out_specs=(P(("blk", "grp"), None), P(("blk", "grp"), None)),
        check_vma=False,
    )
```

```python
import math

import jax
import jax.numpy as jnp
from jax import lax
from jax.experimental import pallas as pl
from jax.experimental.pallas import tpu as pltpu
from jax.sharding import PartitionSpec as P

LOG2E = 1.4426950408889634
CODE_TOP = 32000.0
CODE_STEPS = 32.0
EXTRA_ROWS = 8
LABEL_BASE = 128
TILE = 256
LANES = 128
BUNDLE_COST = 6 * 10**8
SMEM = pl.BlockSpec(memory_space=pltpu.SMEM)
VMEM = pl.BlockSpec(memory_space=pltpu.VMEM)
ANY = pl.BlockSpec(memory_space=pl.ANY)


def whole(array):
    return ((array, 0, 0),)


def part_widths(width):
    first = min(3 * TILE, width - LANES)
    return (first, width - first)


def column_tiles(width):
    tiles, begin = [], 0
    for p, w in enumerate(part_widths(width)):
        tiles += [(p, k, begin + k, min(TILE, w - k)) for k in range(0, w, TILE)]
        begin += w
    return tiles


def piece(block, rows, tile):
    p, inner, start, span = tile
    ref, row, column = block[0 if len(block) == 1 else p]
    first = start if len(block) == 1 else inner
    return ref.at[pl.ds(row + rows[0], rows[1]), pl.ds(column + first, span)]


class Operands:
    def __init__(self):
        self.pairs = []

    def add(self, array, spec):
        for i, (a, s) in enumerate(self.pairs):
            if a is array and s is spec:
                return i
        self.pairs.append((array, spec))
        return len(self.pairs) - 1

    def block(self, block):
        at = [(self.add(a, VMEM), row, column) for a, row, column in block]
        return lambda refs: tuple((refs[i], row, column) for i, row, column in at)


def scale_code(top):
    return jnp.ceil(jnp.log(jnp.maximum(top, 1e-30)) * (CODE_STEPS * LOG2E))


def encode(value, block, tile):
    size, span = value.shape
    code = scale_code(jnp.max(jnp.abs(value), axis=0, keepdims=True))
    gain = CODE_TOP * jnp.exp(code * (-1.0 / (CODE_STEPS * LOG2E)))
    piece(block, (0, size), tile)[...] = (
        jnp.round(value * gain).astype(jnp.int32).astype(jnp.int16)
    )
    scales = jnp.broadcast_to(code.astype(jnp.int32), (EXTRA_ROWS, span)).astype(jnp.int16)
    piece(block, (size, EXTRA_ROWS), tile)[...] = scales


def decoded(block, size, tile):
    code = piece(block, (size, EXTRA_ROWS), tile)[...].astype(jnp.int32).astype(jnp.float32)
    gain = jnp.exp(code[:1] * (1.0 / (CODE_STEPS * LOG2E))) * (1.0 / CODE_TOP)
    return piece(block, (0, size), tile)[...].astype(jnp.int32).astype(jnp.float32) * gain


def call(kernel, name, operands, out_shape, scratch, room, cost, after=(), held_back=()):
    arrays = [a for a, _ in operands]
    held = sum(math.prod(a.shape) * a.dtype.itemsize for a in [*arrays, *out_shape])

    def body(*refs):
        results = refs[len(arrays) + len(after) + len(held_back) :]
        kernel(refs[: len(arrays)], results[: len(out_shape)] + results[len(out_shape) + len(held_back) :])

    return pl.pallas_call(
        body,
        out_shape=[*out_shape, *(jax.ShapeDtypeStruct(a.shape, a.dtype) for a in held_back)],
        in_specs=[s for _, s in operands] + [ANY] * (len(after) + len(held_back)),
        out_specs=[VMEM] * len(out_shape) + [ANY] * len(held_back),
        input_output_aliases={
            len(arrays) + len(after) + i: len(out_shape) + i for i in range(len(held_back))
        },
        scratch_shapes=scratch,
        compiler_params=pltpu.CompilerParams(vmem_limit_bytes=held + room),
        cost_estimate=pl.CostEstimate(flops=cost, bytes_accessed=cost, transcendentals=0),
        name=name,
    )(*arrays, *after, *held_back)


def labelled(images, labels, after=()):
    size, width = images.shape

    def kernel(ins, outs):
        outs[0][pl.ds(0, size), :] = ins[0][...]
        outs[0][pl.ds(size, EXTRA_ROWS), :] = jnp.zeros((EXTRA_ROWS, width), jnp.bfloat16)
        row = ins[1][...]
        low, high = lax.rem(row, LABEL_BASE), lax.div(row, LABEL_BASE)
        at = lax.broadcasted_iota(jnp.int32, (EXTRA_ROWS, size), 0)
        parts = jnp.where(at == 0, high, jnp.where(at == 1, low, 0)).astype(jnp.float32)
        outs[0][pl.ds(size, EXTRA_ROWS), pl.ds(0, size)] = parts.astype(jnp.bfloat16)

    shape = jax.ShapeDtypeStruct((size + EXTRA_ROWS, width), jnp.bfloat16)
    operands = [(images, VMEM), (labels, VMEM)]
    return call(kernel, "labelled", operands, [shape], [], 2**21, size, after)[0]


def crossed(texts, images):
    size = texts.shape[0]

    def kernel(ins, outs):
        def write(texts_out, images_out):
            texts_out[pl.ds(0, size), :] = ins[0][...]
            texts_out[pl.ds(size, EXTRA_ROWS), :] = jnp.zeros((EXTRA_ROWS, texts.shape[1]), jnp.bfloat16)
            images_out[...] = ins[1][...]

        for core, order in enumerate((outs, outs[::-1])):
            pl.when(core_number() == core)(lambda order=order: write(*order))

    shapes = [jax.ShapeDtypeStruct(images.shape, jnp.bfloat16)] * 2
    return call(kernel, "crossed", [(texts, VMEM), (images, VMEM)], shapes, [], 2**21, size)


def bundled(arrays, cost):
    width = arrays[0].shape[1]

    def kernel(ins, outs):
        first = 0
        for ref in ins:
            outs[0][pl.ds(first, ref.shape[0]), :] = ref[...]
            first += ref.shape[0]

    shape = jax.ShapeDtypeStruct((sum(a.shape[0] for a in arrays), width), jnp.bfloat16)
    operands = [(a, VMEM) for a in arrays]
    return call(kernel, "bundled", operands, [shape], [], 2**21, cost)[0]


def first_row(mask, size):
    owner = (lax.axis_index("blk") ^ mask[0]) * lax.axis_size("grp") + (lax.axis_index("grp") ^ mask[1])
    return owner * size


def keys_of(block, size, mask, is_image):
    if not is_image:
        ids = lax.broadcasted_iota(jnp.int32, (1, size), 1) + first_row(mask, size)
        return ids.astype(jnp.float32)
    parts = piece(block, (size, EXTRA_ROWS), (0, 0, 0, size))[...].astype(jnp.float32)
    return parts[0:1] * LABEL_BASE + parts[1:2]


def core_number():
    return lax.rem(lax.axis_index("grp"), 2)


def gradient_sums(name, size, scalars, variants, emits, after=()):
    width = variants[0][0][0][0][0].shape[1]
    per_tile = TILE // size
    shapes = [
        jax.ShapeDtypeStruct((size, width), jnp.float32)
        if kind == "float"
        else jax.ShapeDtypeStruct((size + EXTRA_ROWS, width), jnp.int16)
        for kind in emits
    ]
    operands = Operands()
    slope_at, shift_at = [operands.add(s, SMEM) for s in scalars]
    views = []
    for x_blocks, y_blocks, masks, x_images, jobs, before, sequence in variants:
        for b in sequence:
            operands.block(b)
        x_views = [operands.block(b) for b in x_blocks]
        y_views = [operands.block(b) for b in y_blocks]
        before_at = {r: operands.add(b, VMEM) for r, b in before.items()}
        views.append((x_views, y_views, masks, x_images, jobs, before_at))

    def summed(ins, outs, weights, view):
        x_views, y_views, (x_masks, y_masks), x_images, jobs, before_at = view
        slope, shift = ins[slope_at][0] * LOG2E, ins[shift_at][0] * LOG2E
        x_refs, y_refs = [v(ins) for v in x_views], [v(ins) for v in y_views]

        def stacked(chosen):
            return jnp.concatenate(
                [ref[pl.ds(row, size), pl.ds(column, width)] for ((ref, row, column),) in chosen],
                axis=0,
            )

        for rows, columns in jobs:
            x_all = stacked([x_refs[r] for r in rows])
            keys = [
                jnp.broadcast_to(keys_of(x_refs[r], size, x_masks[r], x_images), (size, size)).T
                for r in rows
            ]
            for n in range(0, len(columns), per_tile):
                chosen = columns[n : n + per_tile]
                other = jnp.concatenate(
                    [keys_of(y_refs[c], size, y_masks[c], not x_images) for c in chosen], axis=1
                )
                scores = lax.dot_general(
                    x_all,
                    stacked([y_refs[c] for c in chosen]),
                    (((1,), (1,)), ((), ())),
                    preferred_element_type=jnp.float32,
                )
                for i in range(len(rows)):
                    z = scores[i * size : (i + 1) * size] * slope + shift
                    sig = 1.0 / (1.0 + jnp.exp2(-z))
                    w = jnp.where(jnp.tile(keys[i], (1, len(chosen))) == other, sig - 1.0, sig)
                    there = pl.ds(n * size, len(chosen) * size)
                    weights[pl.ds(i * size, size), there] = w.astype(jnp.bfloat16)
            for tile in column_tiles(width):
                sums = jnp.dot(
                    weights[pl.ds(0, len(rows) * size), pl.ds(0, len(columns) * size)],
                    jnp.concatenate([piece(y_refs[c], (0, size), tile)[...] for c in columns], axis=0),
                    preferred_element_type=jnp.float32,
                )
                for i, r in enumerate(rows):
                    block = sums[i * size : (i + 1) * size]
                    if r in before_at:
                        block = block + piece(whole(ins[before_at[r]]), (0, size), tile)[...]
                    if emits[r] == "float":
                        piece(whole(outs[r]), (0, size), tile)[...] = block
                    else:
                        encode(block, whole(outs[r]), tile)

    def kernel(ins, refs):
        outs, weights = refs[:-1], refs[-1]
        if len(views) == 1:
            summed(ins, outs, weights, views[0])
            return
        for core, view in enumerate(views):
            pl.when(core_number() == core)(lambda view=view: summed(ins, outs, weights, view))

    x_blocks, y_blocks, jobs = variants[0][0], variants[0][1], variants[0][4]
    pairs = sum(len(rows) * len(columns) for rows, columns in jobs)
    scratch = [pltpu.VMEM((len(x_blocks) * size, len(y_blocks) * size), jnp.bfloat16)]
    room = len(x_blocks) * len(y_blocks) * size * size * 2 + 8 * 2**20
    return call(kernel, name, operands.pairs, shapes, scratch, room, pairs * size, after)


def passed_sum(kept, received, held_back=(), after=()):
    size, width = kept.shape
    operands = Operands()
    kept_at = operands.add(kept, VMEM)
    views = [operands.block(b) for b in received]

    def kernel(ins, outs):
        for tile in column_tiles(width):
            total = piece(whole(ins[kept_at]), (0, size), tile)[...]
            for view in views:
                total = total + decoded(view(ins), size, tile)
            encode(total, whole(outs[0]), tile)

    shape = jax.ShapeDtypeStruct((size + EXTRA_ROWS, width), jnp.int16)
    return call(kernel, "passed_sum", operands.pairs, [shape], [], 2**21, size, after, held_back)


def output_sums(sharpness, sums):
    size, width = sums[0][0].shape
    operands = Operands()
    sharpness_at = operands.add(sharpness, SMEM)
    views = [(operands.add(kept, VMEM), [operands.block(b) for b in blocks]) for kept, blocks in sums]

    def kernel(ins, outs):
        for out, (kept_at, received) in zip(outs, views):
            for tile in column_tiles(width):
                total = piece(whole(ins[kept_at]), (0, size), tile)[...]
                for view in received:
                    total = total + decoded(view(ins), size, tile)
                piece(whole(out), (0, size), tile)[...] = total * ins[sharpness_at][0]

    shapes = [jax.ShapeDtypeStruct((size, width), jnp.float32)] * len(sums)
    return call(kernel, "output_sums", operands.pairs, shapes, [], 2**21, size)


def swapped(array, step):
    axis, bit = step
    return lax.ppermute(array, axis, [(i, i ^ bit) for i in range(lax.axis_size(axis))])


def swapped_by_core(array, steps):
    grp_count = lax.axis_size("grp")
    route = []
    for i in range(lax.axis_size("blk") * grp_count):
        axis, bit = steps[i % 2]
        route.append((i, i ^ (bit * grp_count if axis == "blk" else bit)))
    return lax.ppermute(array, ("blk", "grp"), route)


def scattered(kept, coded, steps, after):
    def sent(array, step):
        return whole(swapped(array, step))

    half, waiting = len(kept), coded[:1]
    received = [[]] + [[sent(c, steps[-1])] for c in coded[1:]]
    for s in reversed(range(len(steps) - 1)):
        for m in reversed(range(1 << s)):
            n = m | 1 << s
            block, *held = passed_sum(kept[n], received[n], waiting, after)
            received[0] += [sent(c, steps[-1]) for c in held]
            received[m].append(sent(block, steps[s]))
            waiting, after = (), [block]
    return kept[0], received[0][::-1], after


def in_order(arrays, after=()):
    return call(lambda *refs: None, "held", [], [], [], 2**21, 1, after, arrays)


def bit_steps(axis):
    return [(axis, 1 << k) for k in range(int(math.log2(lax.axis_size(axis))))]


def owner_masks(steps):
    masks = [(0, 0)]
    for axis, bit in steps:
        masks = masks + [(b ^ bit, g) if axis == "blk" else (b, g ^ bit) for b, g in masks]
    return masks


def per_device(
    picture_vectors, caption_vectors, matching_caption, sharpness_parameter, additive_intercept
):
    scalars = (sharpness_parameter, additive_intercept)
    size = picture_vectors.shape[0]
    core, *grp_steps = bit_steps("grp")
    every = grp_steps + bit_steps("blk")
    steps = [every[0::2], every[1::2]]
    assert len(steps[0]) == len(steps[1]) >= 2
    masks = [owner_masks(s + [core]) for s in steps]
    count = 1 << len(steps[0])
    half = count // 2
    early, late = list(range(half + 1)), list(range(half + 1, count))
    labels = matching_caption[None, :]
    (first_texts,) = in_order([swapped(caption_vectors, steps[1][0])])
    first_images = [swapped(a, steps[0][0]) for a in (picture_vectors, labels)]
    arrays = [{0: labelled(picture_vectors, labels), 1: labelled(*first_images, [first_texts])}, {0: caption_vectors, 1: first_texts}]
    for i in range(1, len(steps[0])):
        for m in range(1 << i):
            if (m | 1 << i) not in late:
                for k in (1, 0):
                    arrays[k][m | 1 << i] = swapped(arrays[k][m], steps[k][i])
    lasts = [steps[1][-1], steps[0][-1]]
    relayed = {}
    for m in late:
        pair = crossed(arrays[1][m - half], arrays[0][m - half])
        relayed[m] = [swapped_by_core(p, o) for p, o in zip(pair, (lasts, lasts[::-1]))]
    blocks = [{m: whole(a[m]) for m in early} for a in arrays]
    others = [{}, {}]
    both = bundled([arrays[1][1], arrays[0][1]], BUNDLE_COST)
    rest = [m for m in early if m != 1]
    both = swapped(bundled([both] + [arrays[k][m] for m in rest for k in (1, 0)], size), core)
    for i, m in enumerate([1] + rest):
        row = i * (2 * size + EXTRA_ROWS)
        others[1][m], others[0][m] = ((both, row, 0),), ((both, row + size, 0),)

    tables = [(blocks, others)]

    def sums(name, kind, rows, columns, jobs, before, emits, after=()):
        other, variants = 1 - kind, []
        for table in tables:
            x_blocks = [table[0][kind][m] for m in rows]
            y_blocks = [table[c][other][m] for c, m in columns]
            x_masks = [masks[kind][m] for m in rows]
            y_masks = [masks[other][m + c * count] for c, m in columns]
            sequence = [blocks[k][m] for m in early[1:] + early[:1] for k in (1, 0)]
            variants.append(
                (x_blocks, y_blocks, (x_masks, y_masks), kind == 0, jobs, before, sequence if rows == early else [])
            )
        return gradient_sums(name, size, scalars, variants, emits, after)

    def both_cores(chosen):
        return [(c, m) for c in range(2) for m in chosen]

    def every_pair(rows, columns):
        return [(list(range(len(rows))), list(range(len(columns))))]

    before = []
    for k in range(2):
        columns = both_cores(early)
        jobs, emits = every_pair(early, columns), ["float"] * len(early)
        results = sums("early_sums", k, early, columns, jobs, {}, emits)
        before.append(dict(zip(early, results)))
    relayed, before = lax.optimization_barrier((relayed, before))
    swaps = {m: [swapped(a, core) for a in relayed[m]] for m in late}
    tables = []
    for c in range(2):
        own, other = [dict(b) for b in blocks], [dict(o) for o in others]
        for m in late:
            own[1 - c][m], own[c][m] = [whole(a) for a in relayed[m]]
            other[c][m], other[1 - c][m] = [whole(a) for a in swaps[m]]
        tables.append((own, other))
    after = ()
    coded, kept, received = [[None] * half, [None] * half], [None, None], [None, None]
    for k in (1, 0):
        columns = [(0, m) for m in range(count)] + [(1, m) for m in early]
        jobs, emits = every_pair(late, columns), ["float"] * len(late)
        begun = dict(enumerate(sums("late_rows_begun", k, late, columns, jobs, {}, emits, after)))
        columns = [(1, m) for m in late]
        jobs, emits = every_pair(late, columns), ["codes"] * len(late)
        coded[k][1:] = sums("late_rows", k, late, columns, jobs, begun, emits)
        after = coded[k][1:2]
    for k in (1, 0):
        columns = both_cores(late)
        jobs, emits = every_pair(early, columns), ["float"] * half + ["codes"]
        *kept[k], coded[k][0] = sums("late_columns", k, early, columns, jobs, before[k], emits, after)
        after = coded[k][:1]
    after, ends = (), ()
    for k in (1, 0):
        kept[k], received[k], after = scattered(kept[k], coded[k], steps[k], after)
    for k in (1, 0):
        ends = in_order([b[0][0] for b in received[k][:-1]], ends)
        received[k] = [whole(a) for a in ends] + received[k][-1:]
    return tuple(output_sums(scalars[0], list(zip(kept, received))))


def solution(mesh):
    placed = (P(("blk", "grp"), None), P(("blk", "grp"), None), P(("blk", "grp")), P(), P())
    return jax.shard_map(
        per_device,
        mesh=mesh,
        in_specs=placed,
        out_specs=(P(("blk", "grp"), None), P(("blk", "grp"), None)),
        check_vma=False,
    )
```

```python
import math

import jax
import jax.numpy as jnp
from jax import lax
from jax.experimental import pallas as pl
from jax.experimental.pallas import tpu as pltpu
from jax.sharding import PartitionSpec as P

LOG2E = 1.4426950408889634
CODE_TOP = 32000.0
CODE_STEPS = 32.0
EXTRA_ROWS = 8
LABEL_BASE = 128
TILE = 256
LANES = 128
BUNDLE_COST = 6 * 10**8
HELD_COST = 85 * 10**7
SMEM = pl.BlockSpec(memory_space=pltpu.SMEM)
VMEM = pl.BlockSpec(memory_space=pltpu.VMEM)
ANY = pl.BlockSpec(memory_space=pl.ANY)


def whole(array):
    return ((array, 0, 0),)


def part_widths(width):
    first = (width // LANES + 1) // 2 * LANES
    return (first, width - first)


def column_tiles(width):
    tiles, begin = [], 0
    for p, w in enumerate(part_widths(width)):
        tiles += [(p, k, begin + k, min(TILE, w - k)) for k in range(0, w, TILE)]
        begin += w
    return tiles


def piece(block, rows, tile):
    p, inner, start, span = tile
    ref, row, column = block[0 if len(block) == 1 else p]
    first = start if len(block) == 1 else inner
    return ref.at[pl.ds(row + rows[0], rows[1]), pl.ds(column + first, span)]


class Operands:
    def __init__(self):
        self.pairs = []

    def add(self, array, spec):
        for i, (a, s) in enumerate(self.pairs):
            if a is array and s is spec:
                return i
        self.pairs.append((array, spec))
        return len(self.pairs) - 1

    def block(self, block):
        at = [(self.add(a, VMEM), row, column) for a, row, column in block]
        return lambda refs: tuple((refs[i], row, column) for i, row, column in at)


def scale_code(top):
    return jnp.ceil(jnp.log(jnp.maximum(top, 1e-30)) * (CODE_STEPS * LOG2E))


def encode(value, block, tile):
    size, span = value.shape
    code = scale_code(jnp.max(jnp.abs(value), axis=0, keepdims=True))
    gain = CODE_TOP * jnp.exp(code * (-1.0 / (CODE_STEPS * LOG2E)))
    piece(block, (0, size), tile)[...] = (
        jnp.round(value * gain).astype(jnp.int32).astype(jnp.int16)
    )
    scales = jnp.broadcast_to(code.astype(jnp.int32), (EXTRA_ROWS, span)).astype(jnp.int16)
    piece(block, (size, EXTRA_ROWS), tile)[...] = scales


def decoded(block, size, tile):
    code = piece(block, (size, EXTRA_ROWS), tile)[...].astype(jnp.int32).astype(jnp.float32)
    gain = jnp.exp(code[:1] * (1.0 / (CODE_STEPS * LOG2E))) * (1.0 / CODE_TOP)
    return piece(block, (0, size), tile)[...].astype(jnp.int32).astype(jnp.float32) * gain


def call(kernel, name, operands, out_shape, scratch, room, cost, after=(), held_back=()):
    arrays = [a for a, _ in operands]
    held = sum(math.prod(a.shape) * a.dtype.itemsize for a in [*arrays, *out_shape])

    def body(*refs):
        results = refs[len(arrays) + len(after) + len(held_back) :]
        kernel(refs[: len(arrays)], results[: len(out_shape)] + results[len(out_shape) + len(held_back) :])

    return pl.pallas_call(
        body,
        out_shape=[*out_shape, *(jax.ShapeDtypeStruct(a.shape, a.dtype) for a in held_back)],
        in_specs=[s for _, s in operands] + [ANY] * (len(after) + len(held_back)),
        out_specs=[VMEM] * len(out_shape) + [ANY] * len(held_back),
        input_output_aliases={
            len(arrays) + len(after) + i: len(out_shape) + i for i in range(len(held_back))
        },
        scratch_shapes=scratch,
        compiler_params=pltpu.CompilerParams(vmem_limit_bytes=held + room),
        cost_estimate=pl.CostEstimate(flops=cost, bytes_accessed=cost, transcendentals=0),
        name=name,
    )(*arrays, *after, *held_back)


def labelled(images, labels, after=()):
    size, width = images.shape

    def kernel(ins, outs):
        outs[0][pl.ds(0, size), :] = ins[0][...]
        outs[0][pl.ds(size, EXTRA_ROWS), :] = jnp.zeros((EXTRA_ROWS, width), jnp.bfloat16)
        row = ins[1][...]
        low, high = lax.rem(row, LABEL_BASE), lax.div(row, LABEL_BASE)
        at = lax.broadcasted_iota(jnp.int32, (EXTRA_ROWS, size), 0)
        parts = jnp.where(at == 0, high, jnp.where(at == 1, low, 0)).astype(jnp.float32)
        outs[0][pl.ds(size, EXTRA_ROWS), pl.ds(0, size)] = parts.astype(jnp.bfloat16)

    shape = jax.ShapeDtypeStruct((size + EXTRA_ROWS, width), jnp.bfloat16)
    operands = [(images, VMEM), (labels, VMEM)]
    return call(kernel, "labelled", operands, [shape], [], 2**21, size, after)[0]


def crossed(texts, images):
    size = texts.shape[0]

    def kernel(ins, outs):
        def write(texts_out, images_out):
            texts_out[pl.ds(0, size), :] = ins[0][...]
            texts_out[pl.ds(size, EXTRA_ROWS), :] = jnp.zeros((EXTRA_ROWS, texts.shape[1]), jnp.bfloat16)
            images_out[...] = ins[1][...]

        for core, order in enumerate((outs, outs[::-1])):
            pl.when(core_number() == core)(lambda order=order: write(*order))

    shapes = [jax.ShapeDtypeStruct(images.shape, jnp.bfloat16)] * 2
    return call(kernel, "crossed", [(texts, VMEM), (images, VMEM)], shapes, [], 2**21, size)


def bundled(arrays, cost):
    width = arrays[0].shape[1]

    def kernel(ins, outs):
        first = 0
        for ref in ins:
            outs[0][pl.ds(first, ref.shape[0]), :] = ref[...]
            first += ref.shape[0]

    shape = jax.ShapeDtypeStruct((sum(a.shape[0] for a in arrays), width), jnp.bfloat16)
    operands = [(a, VMEM) for a in arrays]
    return call(kernel, "bundled", operands, [shape], [], 2**21, cost)[0]


def first_row(mask, size):
    owner = (lax.axis_index("blk") ^ mask[0]) * lax.axis_size("grp") + (lax.axis_index("grp") ^ mask[1])
    return owner * size


def keys_of(block, size, mask, is_image):
    if not is_image:
        ids = lax.broadcasted_iota(jnp.int32, (1, size), 1) + first_row(mask, size)
        return ids.astype(jnp.float32)
    parts = piece(block, (size, EXTRA_ROWS), (0, 0, 0, size))[...].astype(jnp.float32)
    return parts[0:1] * LABEL_BASE + parts[1:2]


def core_number():
    return lax.rem(lax.axis_index("grp"), 2)


def gradient_sums(name, size, scalars, variants, emits, after=()):
    width = variants[0][0][0][0][0].shape[1]
    per_tile = TILE // size
    shapes, where = [], []
    for kind in emits:
        cut = part_widths(width) if kind == "parts" else (width,)
        where.append((len(shapes), len(shapes) + len(cut)))
        for w in cut:
            if kind == "float":
                shapes.append(jax.ShapeDtypeStruct((size, w), jnp.float32))
            else:
                shapes.append(jax.ShapeDtypeStruct((size + EXTRA_ROWS, w), jnp.int16))
    operands = Operands()
    slope_at, shift_at = [operands.add(s, SMEM) for s in scalars]
    views = []
    for x_blocks, y_blocks, masks, x_images, jobs, before, sequence in variants:
        for b in sequence:
            operands.block(b)
        x_views = [operands.block(b) for b in x_blocks]
        y_views = [operands.block(b) for b in y_blocks]
        before_at = {r: operands.add(b, VMEM) for r, b in before.items()}
        views.append((x_views, y_views, masks, x_images, jobs, before_at))

    def summed(ins, outs, weights, view):
        x_views, y_views, (x_masks, y_masks), x_images, jobs, before_at = view
        slope, shift = ins[slope_at][0] * LOG2E, ins[shift_at][0] * LOG2E
        x_refs, y_refs = [v(ins) for v in x_views], [v(ins) for v in y_views]

        def stacked(chosen):
            return jnp.concatenate(
                [ref[pl.ds(row, size), pl.ds(column, width)] for ((ref, row, column),) in chosen],
                axis=0,
            )

        for rows, columns in jobs:
            x_all = stacked([x_refs[r] for r in rows])
            keys = [
                jnp.broadcast_to(keys_of(x_refs[r], size, x_masks[r], x_images), (size, size)).T
                for r in rows
            ]
            for n in range(0, len(columns), per_tile):
                chosen = columns[n : n + per_tile]
                other = jnp.concatenate(
                    [keys_of(y_refs[c], size, y_masks[c], not x_images) for c in chosen], axis=1
                )
                scores = lax.dot_general(
                    x_all,
                    stacked([y_refs[c] for c in chosen]),
                    (((1,), (1,)), ((), ())),
                    preferred_element_type=jnp.float32,
                )
                for i in range(len(rows)):
                    z = scores[i * size : (i + 1) * size] * slope + shift
                    sig = 1.0 / (1.0 + jnp.exp2(-z))
                    w = jnp.where(jnp.tile(keys[i], (1, len(chosen))) == other, sig - 1.0, sig)
                    there = pl.ds(n * size, len(chosen) * size)
                    weights[pl.ds(i * size, size), there] = w.astype(jnp.bfloat16)
            for tile in column_tiles(width):
                sums = jnp.dot(
                    weights[pl.ds(0, len(rows) * size), pl.ds(0, len(columns) * size)],
                    jnp.concatenate([piece(y_refs[c], (0, size), tile)[...] for c in columns], axis=0),
                    preferred_element_type=jnp.float32,
                )
                for i, r in enumerate(rows):
                    block = sums[i * size : (i + 1) * size]
                    if r in before_at:
                        block = block + piece(whole(ins[before_at[r]]), (0, size), tile)[...]
                    out = tuple((o, 0, 0) for o in outs[where[r][0] : where[r][1]])
                    if emits[r] == "float":
                        piece(out, (0, size), tile)[...] = block
                    else:
                        encode(block, out, tile)

    def kernel(ins, refs):
        outs, weights = refs[:-1], refs[-1]
        if len(views) == 1:
            summed(ins, outs, weights, views[0])
            return
        for core, view in enumerate(views):
            pl.when(core_number() == core)(lambda view=view: summed(ins, outs, weights, view))

    x_blocks, y_blocks, jobs = variants[0][0], variants[0][1], variants[0][4]
    pairs = sum(len(rows) * len(columns) for rows, columns in jobs)
    scratch = [pltpu.VMEM((len(x_blocks) * size, len(y_blocks) * size), jnp.bfloat16)]
    room = len(x_blocks) * len(y_blocks) * size * size * 2 + 8 * 2**20
    results = call(kernel, name, operands.pairs, shapes, scratch, room, pairs * size, after)
    return [tuple(results[a:b]) for a, b in where]


def passed_sum(kept, received, part, held_back=(), after=()):
    size, width = kept.shape
    operands = Operands()
    kept_at = operands.add(kept, VMEM)
    views = [operands.block(b if part is None or len(b) == 1 else (b[part],) * 2) for b in received]

    def kernel(ins, outs):
        for tile in column_tiles(width):
            p, inner, _, span = tile
            if part is None or p == part:
                total = piece(whole(ins[kept_at]), (0, size), tile)[...]
                for view in views:
                    total = total + decoded(view(ins), size, tile)
                encode(total, whole(outs[0]), tile if part is None else (0, 0, inner, span))

    cut = width if part is None else part_widths(width)[part]
    shape = jax.ShapeDtypeStruct((size + EXTRA_ROWS, cut), jnp.int16)
    return call(kernel, "passed_sum", operands.pairs, [shape], [], 2**21, size, after, held_back)


def output_sums(sharpness, sums):
    size, width = sums[0][0].shape
    operands = Operands()
    sharpness_at = operands.add(sharpness, SMEM)
    views = [(operands.add(kept, VMEM), [operands.block(b) for b in blocks]) for kept, blocks in sums]

    def kernel(ins, outs):
        for out, (kept_at, received) in zip(outs, views):
            for tile in column_tiles(width):
                total = piece(whole(ins[kept_at]), (0, size), tile)[...]
                for view in received:
                    total = total + decoded(view(ins), size, tile)
                piece(whole(out), (0, size), tile)[...] = total * ins[sharpness_at][0]

    shapes = [jax.ShapeDtypeStruct((size, width), jnp.float32)] * len(sums)
    return call(kernel, "output_sums", operands.pairs, shapes, [], 2**21, size)


def swapped(array, step):
    axis, bit = step
    return lax.ppermute(array, axis, [(i, i ^ bit) for i in range(lax.axis_size(axis))])


def swapped_by_core(array, steps):
    grp_count = lax.axis_size("grp")
    route = []
    for i in range(lax.axis_size("blk") * grp_count):
        axis, bit = steps[i % 2]
        route.append((i, i ^ (bit * grp_count if axis == "blk" else bit)))
    return lax.ppermute(array, ("blk", "grp"), route)


def scattered(kept, coded, steps, after):
    def sent(array, step):
        return (swapped(array, step), 0, 0)

    half = len(kept)
    received = [[]] + [[(sent(c[0], steps[-1]),)] for c in coded[1:]]
    waiting, last = [c[1] for c in coded[1:]], [coded[0][0]]
    for s in reversed(range(len(steps) - 1)):
        for m in reversed(range(1 << s)):
            n = m | 1 << s
            first, *begun = passed_sum(kept[n], received[n], 0, waiting + last)
            for r, c in zip(received[1:], begun):
                r[0] = r[0] + (sent(c, steps[-1]),)
            received[0] += [(sent(c, steps[-1]),) for c in begun[len(waiting) :]]
            first = sent(first, steps[s])
            (second,) = passed_sum(kept[n], received[n], 1, (), [first[0], *after])
            received[m].append((first, sent(second, steps[s])))
            waiting, last, after = [], [], [second]
    return kept[0], received[0], after


def in_order(arrays, after=(), cost=HELD_COST):
    return call(lambda *refs: None, "held", [], [], [], 2**21, cost, after, arrays)


def bit_steps(axis):
    return [(axis, 1 << k) for k in range(int(math.log2(lax.axis_size(axis))))]


def owner_masks(steps):
    masks = [(0, 0)]
    for axis, bit in steps:
        masks = masks + [(b ^ bit, g) if axis == "blk" else (b, g ^ bit) for b, g in masks]
    return masks


def per_device(
    picture_vectors, caption_vectors, matching_caption, sharpness_parameter, additive_intercept
):
    scalars = (sharpness_parameter, additive_intercept)
    size = picture_vectors.shape[0]
    core, *grp_steps = bit_steps("grp")
    every = grp_steps + bit_steps("blk")
    steps = [every[0::2], every[1::2]]
    assert len(steps[0]) == len(steps[1]) >= 2
    masks = [owner_masks(s + [core]) for s in steps]
    count = 1 << len(steps[0])
    half = count // 2
    early, late = list(range(half + 1)), list(range(half + 1, count))
    labels = matching_caption[None, :]
    (first_texts,) = in_order([swapped(caption_vectors, steps[1][0])], (), 1)
    first_images = [swapped(a, steps[0][0]) for a in (picture_vectors, labels)]
    arrays = [{0: labelled(picture_vectors, labels), 1: labelled(*first_images, [first_texts])}, {0: caption_vectors, 1: first_texts}]
    for i in range(1, len(steps[0])):
        for m in range(1 << i):
            if (m | 1 << i) not in late:
                for k in (1, 0):
                    arrays[k][m | 1 << i] = swapped(arrays[k][m], steps[k][i])
    lasts = [steps[1][-1], steps[0][-1]]
    relayed = {}
    for m in late:
        pair = crossed(arrays[1][m - half], arrays[0][m - half])
        relayed[m] = [swapped_by_core(p, o) for p, o in zip(pair, (lasts, lasts[::-1]))]
    blocks = [{m: whole(a[m]) for m in early} for a in arrays]
    others = [{}, {}]
    both = bundled([arrays[1][1], arrays[0][1]], BUNDLE_COST)
    rest = [m for m in early if m != 1]
    both = swapped(bundled([both] + [arrays[k][m] for m in rest for k in (1, 0)], size), core)
    for i, m in enumerate([1] + rest):
        row = i * (2 * size + EXTRA_ROWS)
        others[1][m], others[0][m] = ((both, row, 0),), ((both, row + size, 0),)

    tables = [(blocks, others)]

    def sums(name, kind, rows, columns, jobs, before, emits, after=()):
        other, variants = 1 - kind, []
        for table in tables:
            x_blocks = [table[0][kind][m] for m in rows]
            y_blocks = [table[c][other][m] for c, m in columns]
            x_masks = [masks[kind][m] for m in rows]
            y_masks = [masks[other][m + c * count] for c, m in columns]
            sequence = [blocks[k][m] for m in early[1:] + early[:1] for k in (1, 0)]
            variants.append(
                (x_blocks, y_blocks, (x_masks, y_masks), kind == 0, jobs, before, sequence if rows == early else [])
            )
        return gradient_sums(name, size, scalars, variants, emits, after)

    def both_cores(chosen):
        return [(c, m) for c in range(2) for m in chosen]

    def every_pair(rows, columns):
        return [(list(range(len(rows))), list(range(len(columns))))]

    before = []
    for k in range(2):
        columns = both_cores(early)
        jobs, emits = every_pair(early, columns), ["float"] * len(early)
        results = sums("early_sums", k, early, columns, jobs, {}, emits)
        before.append({m: s for m, (s,) in zip(early, results)})
    relayed, before = lax.optimization_barrier((relayed, before))
    swaps = {m: [swapped(a, core) for a in relayed[m]] for m in late}
    tables = []
    for c in range(2):
        own, other = [dict(b) for b in blocks], [dict(o) for o in others]
        for m in late:
            own[1 - c][m], own[c][m] = [whole(a) for a in relayed[m]]
            other[c][m], other[1 - c][m] = [whole(a) for a in swaps[m]]
        tables.append((own, other))
    after = ()
    coded, kept = [[None] * half, [None] * half], [None, None]
    for k in (1, 0):
        columns = [(0, m) for m in range(count)] + [(1, m) for m in early]
        jobs, emits = every_pair(late, columns), ["float"] * len(late)
        results = sums("late_rows_begun", k, late, columns, jobs, {}, emits, after)
        begun = {i: s for i, (s,) in enumerate(results)}
        columns = [(1, m) for m in late]
        jobs, emits = every_pair(late, columns), ["parts"] * len(late)
        coded[k][1:] = sums("late_rows", k, late, columns, jobs, begun, emits)
        after = coded[k][1]
    for k in (1, 0):
        columns = both_cores(late)
        jobs, emits = every_pair(early, columns), ["float"] * half + ["whole"]
        *whole_sums, coded[k][0] = sums("late_columns", k, early, columns, jobs, before[k], emits, after)
        kept[k], after = [s for (s,) in whole_sums], coded[k][0]
    kept_texts, text_blocks, after = scattered(kept[1], coded[1], steps[1], ())
    kept_images, image_blocks, _ = scattered(kept[0], coded[0], steps[0], after)
    ends = ()
    for blocks_in in (text_blocks, image_blocks):
        ends = in_order([part[0] for b in blocks_in if len(b) > 1 for part in b], ends)
        parts = iter(ends)
        blocks_in[:] = [tuple((next(parts), 0, 0) for _ in b) if len(b) > 1 else b for b in blocks_in]
    return tuple(output_sums(scalars[0], [(kept_images, image_blocks), (kept_texts, text_blocks)]))


def solution(mesh):
    placed = (P(("blk", "grp"), None), P(("blk", "grp"), None), P(("blk", "grp")), P(), P())
    return jax.shard_map(
        per_device,
        mesh=mesh,
        in_specs=placed,
        out_specs=(P(("blk", "grp"), None), P(("blk", "grp"), None)),
        check_vma=False,
    )
```

```python
import math

import jax
import jax.numpy as jnp
from jax import lax
from jax.experimental import pallas as pl
from jax.experimental.pallas import tpu as pltpu
from jax.sharding import PartitionSpec as P

LOG2E = 1.4426950408889634
CODE_TOP = 32000.0
CODE_STEPS = 32.0
EXTRA_ROWS = 8
LABEL_BASE = 128
TILE = 256
LANES = 128
BUNDLE_COST = 6 * 10**8
HELD_COST = 85 * 10**7
SMEM = pl.BlockSpec(memory_space=pltpu.SMEM)
VMEM = pl.BlockSpec(memory_space=pltpu.VMEM)
ANY = pl.BlockSpec(memory_space=pl.ANY)


def whole(array):
    return ((array, 0, 0),)


def part_widths(width):
    first = (width // LANES + 1) // 2 * LANES
    return (first, width - first)


def column_tiles(width):
    tiles, begin = [], 0
    for p, w in enumerate(part_widths(width)):
        tiles += [(p, k, begin + k, min(TILE, w - k)) for k in range(0, w, TILE)]
        begin += w
    return tiles


def piece(block, rows, tile):
    p, inner, start, span = tile
    ref, row, column = block[0 if len(block) == 1 else p]
    first = start if len(block) == 1 else inner
    return ref.at[pl.ds(row + rows[0], rows[1]), pl.ds(column + first, span)]


class Operands:
    def __init__(self):
        self.pairs = []

    def add(self, array, spec):
        for i, (a, s) in enumerate(self.pairs):
            if a is array and s is spec:
                return i
        self.pairs.append((array, spec))
        return len(self.pairs) - 1

    def block(self, block):
        at = [(self.add(a, VMEM), row, column) for a, row, column in block]
        return lambda refs: tuple((refs[i], row, column) for i, row, column in at)


def scale_code(top):
    return jnp.ceil(jnp.log(jnp.maximum(top, 1e-30)) * (CODE_STEPS * LOG2E))


def encode(value, block, tile):
    size, span = value.shape
    code = scale_code(jnp.max(jnp.abs(value), axis=0, keepdims=True))
    gain = CODE_TOP * jnp.exp(code * (-1.0 / (CODE_STEPS * LOG2E)))
    piece(block, (0, size), tile)[...] = (
        jnp.round(value * gain).astype(jnp.int32).astype(jnp.int16)
    )
    scales = jnp.broadcast_to(code.astype(jnp.int32), (EXTRA_ROWS, span)).astype(jnp.int16)
    piece(block, (size, EXTRA_ROWS), tile)[...] = scales


def decoded(block, size, tile):
    code = piece(block, (size, EXTRA_ROWS), tile)[...].astype(jnp.int32).astype(jnp.float32)
    gain = jnp.exp(code[:1] * (1.0 / (CODE_STEPS * LOG2E))) * (1.0 / CODE_TOP)
    return piece(block, (0, size), tile)[...].astype(jnp.int32).astype(jnp.float32) * gain


def call(kernel, name, operands, out_shape, scratch, room, cost, after=(), held_back=()):
    arrays = [a for a, _ in operands]
    held = sum(math.prod(a.shape) * a.dtype.itemsize for a in [*arrays, *out_shape])

    def body(*refs):
        results = refs[len(arrays) + len(after) + len(held_back) :]
        kernel(refs[: len(arrays)], results[: len(out_shape)] + results[len(out_shape) + len(held_back) :])

    return pl.pallas_call(
        body,
        out_shape=[*out_shape, *(jax.ShapeDtypeStruct(a.shape, a.dtype) for a in held_back)],
        in_specs=[s for _, s in operands] + [ANY] * (len(after) + len(held_back)),
        out_specs=[VMEM] * len(out_shape) + [ANY] * len(held_back),
        input_output_aliases={
            len(arrays) + len(after) + i: len(out_shape) + i for i in range(len(held_back))
        },
        scratch_shapes=scratch,
        compiler_params=pltpu.CompilerParams(vmem_limit_bytes=held + room),
        cost_estimate=pl.CostEstimate(flops=cost, bytes_accessed=cost, transcendentals=0),
        name=name,
    )(*arrays, *after, *held_back)


def labelled(images, labels, after=()):
    size, width = images.shape

    def kernel(ins, outs):
        outs[0][pl.ds(0, size), :] = ins[0][...]
        outs[0][pl.ds(size, EXTRA_ROWS), :] = jnp.zeros((EXTRA_ROWS, width), jnp.bfloat16)
        row = ins[1][...]
        low, high = lax.rem(row, LABEL_BASE), lax.div(row, LABEL_BASE)
        at = lax.broadcasted_iota(jnp.int32, (EXTRA_ROWS, size), 0)
        parts = jnp.where(at == 0, high, jnp.where(at == 1, low, 0)).astype(jnp.float32)
        outs[0][pl.ds(size, EXTRA_ROWS), pl.ds(0, size)] = parts.astype(jnp.bfloat16)

    shape = jax.ShapeDtypeStruct((size + EXTRA_ROWS, width), jnp.bfloat16)
    operands = [(images, VMEM), (labels, VMEM)]
    return call(kernel, "labelled", operands, [shape], [], 2**21, size, after)[0]


def crossed(texts, images):
    size = texts.shape[0]

    def kernel(ins, outs):
        def write(texts_out, images_out):
            texts_out[pl.ds(0, size), :] = ins[0][...]
            texts_out[pl.ds(size, EXTRA_ROWS), :] = jnp.zeros((EXTRA_ROWS, texts.shape[1]), jnp.bfloat16)
            images_out[...] = ins[1][...]

        for core, order in enumerate((outs, outs[::-1])):
            pl.when(core_number() == core)(lambda order=order: write(*order))

    shapes = [jax.ShapeDtypeStruct(images.shape, jnp.bfloat16)] * 2
    return call(kernel, "crossed", [(texts, VMEM), (images, VMEM)], shapes, [], 2**21, size)


def bundled(arrays, cost):
    width = arrays[0].shape[1]

    def kernel(ins, outs):
        first = 0
        for ref in ins:
            outs[0][pl.ds(first, ref.shape[0]), :] = ref[...]
            first += ref.shape[0]

    shape = jax.ShapeDtypeStruct((sum(a.shape[0] for a in arrays), width), jnp.bfloat16)
    operands = [(a, VMEM) for a in arrays]
    return call(kernel, "bundled", operands, [shape], [], 2**21, cost)[0]


def first_row(mask, size):
    owner = (lax.axis_index("blk") ^ mask[0]) * lax.axis_size("grp") + (lax.axis_index("grp") ^ mask[1])
    return owner * size


def keys_of(block, size, mask, is_image):
    if not is_image:
        ids = lax.broadcasted_iota(jnp.int32, (1, size), 1) + first_row(mask, size)
        return ids.astype(jnp.float32)
    parts = piece(block, (size, EXTRA_ROWS), (0, 0, 0, size))[...].astype(jnp.float32)
    return parts[0:1] * LABEL_BASE + parts[1:2]


def core_number():
    return lax.rem(lax.axis_index("grp"), 2)


def gradient_sums(name, size, scalars, variants, emits, after=()):
    width = variants[0][0][0][0][0].shape[1]
    per_tile = TILE // size
    shapes, where = [], []
    for kind in emits:
        cut = part_widths(width) if kind == "parts" else (width,)
        where.append((len(shapes), len(shapes) + len(cut)))
        for w in cut:
            if kind == "float":
                shapes.append(jax.ShapeDtypeStruct((size, w), jnp.float32))
            else:
                shapes.append(jax.ShapeDtypeStruct((size + EXTRA_ROWS, w), jnp.int16))
    operands = Operands()
    slope_at, shift_at = [operands.add(s, SMEM) for s in scalars]
    views = []
    for x_blocks, y_blocks, masks, x_images, jobs, before, sequence in variants:
        for b in sequence:
            operands.block(b)
        x_views = [operands.block(b) for b in x_blocks]
        y_views = [operands.block(b) for b in y_blocks]
        before_at = {r: operands.add(b, VMEM) for r, b in before.items()}
        views.append((x_views, y_views, masks, x_images, jobs, before_at))

    def summed(ins, outs, weights, view):
        x_views, y_views, (x_masks, y_masks), x_images, jobs, before_at = view
        slope, shift = ins[slope_at][0] * LOG2E, ins[shift_at][0] * LOG2E
        x_refs, y_refs = [v(ins) for v in x_views], [v(ins) for v in y_views]

        def stacked(chosen):
            return jnp.concatenate(
                [ref[pl.ds(row, size), pl.ds(column, width)] for ((ref, row, column),) in chosen],
                axis=0,
            )

        for rows, columns in jobs:
            x_all = stacked([x_refs[r] for r in rows])
            keys = [
                jnp.broadcast_to(keys_of(x_refs[r], size, x_masks[r], x_images), (size, size)).T
                for r in rows
            ]
            for n in range(0, len(columns), per_tile):
                chosen = columns[n : n + per_tile]
                other = jnp.concatenate(
                    [keys_of(y_refs[c], size, y_masks[c], not x_images) for c in chosen], axis=1
                )
                scores = lax.dot_general(
                    x_all,
                    stacked([y_refs[c] for c in chosen]),
                    (((1,), (1,)), ((), ())),
                    preferred_element_type=jnp.float32,
                )
                for i in range(len(rows)):
                    z = scores[i * size : (i + 1) * size] * slope + shift
                    sig = 1.0 / (1.0 + jnp.exp2(-z))
                    w = jnp.where(jnp.tile(keys[i], (1, len(chosen))) == other, sig - 1.0, sig)
                    there = pl.ds(n * size, len(chosen) * size)
                    weights[pl.ds(i * size, size), there] = w.astype(jnp.bfloat16)
            for tile in column_tiles(width):
                sums = jnp.dot(
                    weights[pl.ds(0, len(rows) * size), pl.ds(0, len(columns) * size)],
                    jnp.concatenate([piece(y_refs[c], (0, size), tile)[...] for c in columns], axis=0),
                    preferred_element_type=jnp.float32,
                )
                for i, r in enumerate(rows):
                    block = sums[i * size : (i + 1) * size]
                    if r in before_at:
                        block = block + piece(whole(ins[before_at[r]]), (0, size), tile)[...]
                    out = tuple((o, 0, 0) for o in outs[where[r][0] : where[r][1]])
                    if emits[r] == "float":
                        piece(out, (0, size), tile)[...] = block
                    else:
                        encode(block, out, tile)

    def kernel(ins, refs):
        outs, weights = refs[:-1], refs[-1]
        if len(views) == 1:
            summed(ins, outs, weights, views[0])
            return
        for core, view in enumerate(views):
            pl.when(core_number() == core)(lambda view=view: summed(ins, outs, weights, view))

    x_blocks, y_blocks, jobs = variants[0][0], variants[0][1], variants[0][4]
    pairs = sum(len(rows) * len(columns) for rows, columns in jobs)
    scratch = [pltpu.VMEM((len(x_blocks) * size, len(y_blocks) * size), jnp.bfloat16)]
    room = len(x_blocks) * len(y_blocks) * size * size * 2 + 8 * 2**20
    results = call(kernel, name, operands.pairs, shapes, scratch, room, pairs * size, after)
    return [tuple(results[a:b]) for a, b in where]


def passed_sum(kept, received, part, held_back=(), after=()):
    size, width = kept.shape
    operands = Operands()
    kept_at = operands.add(kept, VMEM)
    views = [operands.block(b if part is None or len(b) == 1 else (b[part],) * 2) for b in received]

    def kernel(ins, outs):
        for tile in column_tiles(width):
            p, inner, _, span = tile
            if part is None or p == part:
                total = piece(whole(ins[kept_at]), (0, size), tile)[...]
                for view in views:
                    total = total + decoded(view(ins), size, tile)
                encode(total, whole(outs[0]), tile if part is None else (0, 0, inner, span))

    cut = width if part is None else part_widths(width)[part]
    shape = jax.ShapeDtypeStruct((size + EXTRA_ROWS, cut), jnp.int16)
    return call(kernel, "passed_sum", operands.pairs, [shape], [], 2**21, size, after, held_back)


def output_sums(sharpness, sums):
    size, width = sums[0][0].shape
    operands = Operands()
    sharpness_at = operands.add(sharpness, SMEM)
    views = [(operands.add(kept, VMEM), [operands.block(b) for b in blocks]) for kept, blocks in sums]

    def kernel(ins, outs):
        for out, (kept_at, received) in zip(outs, views):
            for tile in column_tiles(width):
                total = piece(whole(ins[kept_at]), (0, size), tile)[...]
                for view in received:
                    total = total + decoded(view(ins), size, tile)
                piece(whole(out), (0, size), tile)[...] = total * ins[sharpness_at][0]

    shapes = [jax.ShapeDtypeStruct((size, width), jnp.float32)] * len(sums)
    return call(kernel, "output_sums", operands.pairs, shapes, [], 2**21, size)


def swapped(array, step):
    axis, bit = step
    return lax.ppermute(array, axis, [(i, i ^ bit) for i in range(lax.axis_size(axis))])


def swapped_by_core(array, steps):
    grp_count = lax.axis_size("grp")
    route = []
    for i in range(lax.axis_size("blk") * grp_count):
        axis, bit = steps[i % 2]
        route.append((i, i ^ (bit * grp_count if axis == "blk" else bit)))
    return lax.ppermute(array, ("blk", "grp"), route)


def scattered(kept, coded, steps, after):
    def sent(array, step):
        return (swapped(array, step), 0, 0)

    half = len(kept)
    received = [[]] + [[(sent(c[0], steps[-1]),)] for c in coded[1:]]
    waiting, last = [c[1] for c in coded[1:]], [coded[0][0]]
    for s in reversed(range(len(steps) - 1)):
        for m in reversed(range(1 << s)):
            n = m | 1 << s
            first, *begun = passed_sum(kept[n], received[n], 0, waiting + last)
            if waiting:
                begun_with = [first]
            for r, c in zip(received[1:], begun):
                r[0] = r[0] + (sent(c, steps[-1]),)
            received[0] += [(sent(c, steps[-1]),) for c in begun[len(waiting) :]]
            first = sent(first, steps[s])
            (second,) = passed_sum(kept[n], received[n], 1, (), [first[0], *after])
            received[m].append((first, sent(second, steps[s])))
            waiting, last, after = [], [], [second]
    return kept[0], received[0], after, begun_with


def in_order(arrays, after=(), cost=HELD_COST):
    return call(lambda *refs: None, "held", [], [], [], 2**21, cost, after, arrays)


def bit_steps(axis):
    return [(axis, 1 << k) for k in range(int(math.log2(lax.axis_size(axis))))]


def owner_masks(steps):
    masks = [(0, 0)]
    for axis, bit in steps:
        masks = masks + [(b ^ bit, g) if axis == "blk" else (b, g ^ bit) for b, g in masks]
    return masks


def per_device(
    picture_vectors, caption_vectors, matching_caption, sharpness_parameter, additive_intercept
):
    scalars = (sharpness_parameter, additive_intercept)
    size = picture_vectors.shape[0]
    core, *grp_steps = bit_steps("grp")
    every = grp_steps + bit_steps("blk")
    steps = [every[0::2], every[1::2]]
    assert len(steps[0]) == len(steps[1]) >= 2
    masks = [owner_masks(s + [core]) for s in steps]
    count = 1 << len(steps[0])
    half = count // 2
    early, late = list(range(half + 1)), list(range(half + 1, count))
    labels = matching_caption[None, :]
    (first_texts,) = in_order([swapped(caption_vectors, steps[1][0])], (), 1)
    first_images = [swapped(a, steps[0][0]) for a in (picture_vectors, labels)]
    arrays = [{0: labelled(picture_vectors, labels), 1: labelled(*first_images, [first_texts])}, {0: caption_vectors, 1: first_texts}]
    for i in range(1, len(steps[0])):
        for m in range(1 << i):
            if (m | 1 << i) not in late:
                for k in (1, 0):
                    arrays[k][m | 1 << i] = swapped(arrays[k][m], steps[k][i])
    lasts = [steps[1][-1], steps[0][-1]]
    relayed = {}
    for m in late:
        pair = crossed(arrays[1][m - half], arrays[0][m - half])
        relayed[m] = [swapped_by_core(p, o) for p, o in zip(pair, (lasts, lasts[::-1]))]
    blocks = [{m: whole(a[m]) for m in early} for a in arrays]
    others = [{}, {}]
    both = bundled([arrays[1][1], arrays[0][1]], BUNDLE_COST)
    rest = [m for m in early if m != 1]
    both = swapped(bundled([both] + [arrays[k][m] for m in rest for k in (1, 0)], size), core)
    for i, m in enumerate([1] + rest):
        row = i * (2 * size + EXTRA_ROWS)
        others[1][m], others[0][m] = ((both, row, 0),), ((both, row + size, 0),)

    tables = [(blocks, others)]

    def sums(name, kind, rows, columns, jobs, before, emits, after=()):
        other, variants = 1 - kind, []
        for table in tables:
            x_blocks = [table[0][kind][m] for m in rows]
            y_blocks = [table[c][other][m] for c, m in columns]
            x_masks = [masks[kind][m] for m in rows]
            y_masks = [masks[other][m + c * count] for c, m in columns]
            sequence = [blocks[k][m] for m in early[1:] + early[:1] for k in (1, 0)]
            variants.append(
                (x_blocks, y_blocks, (x_masks, y_masks), kind == 0, jobs, before, sequence if rows == early else [])
            )
        return gradient_sums(name, size, scalars, variants, emits, after)

    def both_cores(chosen):
        return [(c, m) for c in range(2) for m in chosen]

    def every_pair(rows, columns):
        return [(list(range(len(rows))), list(range(len(columns))))]

    before = []
    for k in range(2):
        columns = both_cores(early)
        jobs, emits = every_pair(early, columns), ["float"] * len(early)
        results = sums("early_sums", k, early, columns, jobs, {}, emits)
        before.append({m: s for m, (s,) in zip(early, results)})
    relayed, before = lax.optimization_barrier((relayed, before))
    swaps = {m: [swapped(a, core) for a in relayed[m]] for m in late}
    tables = []
    for c in range(2):
        own, other = [dict(b) for b in blocks], [dict(o) for o in others]
        for m in late:
            own[1 - c][m], own[c][m] = [whole(a) for a in relayed[m]]
            other[c][m], other[1 - c][m] = [whole(a) for a in swaps[m]]
        tables.append((own, other))
    after = ()
    coded = [[None] * half, [None] * half]
    for k in (1, 0):
        columns = [(0, m) for m in range(count)] + [(1, m) for m in early]
        jobs, emits = every_pair(late, columns), ["float"] * len(late)
        results = sums("late_rows_begun", k, late, columns, jobs, {}, emits, after)
        begun = {i: s for i, (s,) in enumerate(results)}
        columns = [(1, m) for m in late]
        jobs, emits = every_pair(late, columns), ["parts"] * len(late)
        coded[k][1:] = sums("late_rows", k, late, columns, jobs, begun, emits)
        after = coded[k][1]
    sums_in = [None, None]
    ordering = ()
    for k in (1, 0):
        columns = both_cores(late)
        jobs, emits = every_pair(early, columns), ["float"] * half + ["whole"]
        *whole_sums, coded[k][0] = sums("late_columns", k, early, columns, jobs, before[k], emits, after)
        kept = [s for (s,) in whole_sums]
        *sums_in[k], ordering, after = scattered(kept, coded[k], steps[k], ordering)
    (kept_images, image_blocks), (kept_texts, text_blocks) = sums_in
    ends = ()
    for blocks_in in (text_blocks, image_blocks):
        ends = in_order([part[0] for b in blocks_in if len(b) > 1 for part in b], ends)
        parts = iter(ends)
        blocks_in[:] = [tuple((next(parts), 0, 0) for _ in b) if len(b) > 1 else b for b in blocks_in]
    return tuple(output_sums(scalars[0], [(kept_images, image_blocks), (kept_texts, text_blocks)]))


def solution(mesh):
    placed = (P(("blk", "grp"), None), P(("blk", "grp"), None), P(("blk", "grp")), P(), P())
    return jax.shard_map(
        per_device,
        mesh=mesh,
        in_specs=placed,
        out_specs=(P(("blk", "grp"), None), P(("blk", "grp"), None)),
        check_vma=False,
    )
```

```python
import math

import jax
import jax.numpy as jnp
from jax import lax
from jax.experimental import pallas as pl
from jax.experimental.pallas import tpu as pltpu
from jax.sharding import PartitionSpec as P

LOG2E = 1.4426950408889634
CODE_TOP = 32000.0
CODE_STEPS = 32.0
EXTRA_ROWS = 8
LABEL_BASE = 128
TILE = 256
LANES = 128
BUNDLE_COST = 6 * 10**8
HELD_COST = 85 * 10**7
SMEM = pl.BlockSpec(memory_space=pltpu.SMEM)
VMEM = pl.BlockSpec(memory_space=pltpu.VMEM)
ANY = pl.BlockSpec(memory_space=pl.ANY)


def whole(array):
    return ((array, 0, 0),)


def part_widths(width):
    first = (width // LANES + 1) // 2 * LANES
    return (first, width - first)


def column_tiles(width):
    tiles, begin = [], 0
    for p, w in enumerate(part_widths(width)):
        tiles += [(p, k, begin + k, min(TILE, w - k)) for k in range(0, w, TILE)]
        begin += w
    return tiles


def piece(block, rows, tile):
    p, inner, start, span = tile
    ref, row, column = block[0 if len(block) == 1 else p]
    first = start if len(block) == 1 else inner
    return ref.at[pl.ds(row + rows[0], rows[1]), pl.ds(column + first, span)]


class Operands:
    def __init__(self):
        self.pairs = []

    def add(self, array, spec):
        for i, (a, s) in enumerate(self.pairs):
            if a is array and s is spec:
                return i
        self.pairs.append((array, spec))
        return len(self.pairs) - 1

    def block(self, block):
        at = [(self.add(a, VMEM), row, column) for a, row, column in block]
        return lambda refs: tuple((refs[i], row, column) for i, row, column in at)


def scale_code(top):
    return jnp.ceil(jnp.log(jnp.maximum(top, 1e-30)) * (CODE_STEPS * LOG2E))


def encode(value, block, tile):
    size, span = value.shape
    code = scale_code(jnp.max(jnp.abs(value), axis=0, keepdims=True))
    gain = CODE_TOP * jnp.exp(code * (-1.0 / (CODE_STEPS * LOG2E)))
    piece(block, (0, size), tile)[...] = (
        jnp.round(value * gain).astype(jnp.int32).astype(jnp.int16)
    )
    scales = jnp.broadcast_to(code.astype(jnp.int32), (EXTRA_ROWS, span)).astype(jnp.int16)
    piece(block, (size, EXTRA_ROWS), tile)[...] = scales


def decoded(block, size, tile):
    code = piece(block, (size, EXTRA_ROWS), tile)[...].astype(jnp.int32).astype(jnp.float32)
    gain = jnp.exp(code[:1] * (1.0 / (CODE_STEPS * LOG2E))) * (1.0 / CODE_TOP)
    return piece(block, (0, size), tile)[...].astype(jnp.int32).astype(jnp.float32) * gain


def call(kernel, name, operands, out_shape, scratch, room, cost, after=(), held_back=()):
    arrays = [a for a, _ in operands]
    held = sum(math.prod(a.shape) * a.dtype.itemsize for a in [*arrays, *out_shape])

    def body(*refs):
        results = refs[len(arrays) + len(after) + len(held_back) :]
        kernel(refs[: len(arrays)], results[: len(out_shape)] + results[len(out_shape) + len(held_back) :])

    return pl.pallas_call(
        body,
        out_shape=[*out_shape, *(jax.ShapeDtypeStruct(a.shape, a.dtype) for a in held_back)],
        in_specs=[s for _, s in operands] + [ANY] * (len(after) + len(held_back)),
        out_specs=[VMEM] * len(out_shape) + [ANY] * len(held_back),
        input_output_aliases={
            len(arrays) + len(after) + i: len(out_shape) + i for i in range(len(held_back))
        },
        scratch_shapes=scratch,
        compiler_params=pltpu.CompilerParams(vmem_limit_bytes=held + room),
        cost_estimate=pl.CostEstimate(flops=cost, bytes_accessed=cost, transcendentals=0),
        name=name,
    )(*arrays, *after, *held_back)


def labelled(images, labels, after=()):
    size, width = images.shape

    def kernel(ins, outs):
        outs[0][pl.ds(0, size), :] = ins[0][...]
        outs[0][pl.ds(size, EXTRA_ROWS), :] = jnp.zeros((EXTRA_ROWS, width), jnp.bfloat16)
        row = ins[1][...]
        low, high = lax.rem(row, LABEL_BASE), lax.div(row, LABEL_BASE)
        at = lax.broadcasted_iota(jnp.int32, (EXTRA_ROWS, size), 0)
        parts = jnp.where(at == 0, high, jnp.where(at == 1, low, 0)).astype(jnp.float32)
        outs[0][pl.ds(size, EXTRA_ROWS), pl.ds(0, size)] = parts.astype(jnp.bfloat16)

    shape = jax.ShapeDtypeStruct((size + EXTRA_ROWS, width), jnp.bfloat16)
    operands = [(images, VMEM), (labels, VMEM)]
    return call(kernel, "labelled", operands, [shape], [], 2**21, size, after)[0]


def bundled(arrays, cost):
    width = arrays[0].shape[1]

    def kernel(ins, outs):
        first = 0
        for ref in ins:
            outs[0][pl.ds(first, ref.shape[0]), :] = ref[...]
            first += ref.shape[0]

    shape = jax.ShapeDtypeStruct((sum(a.shape[0] for a in arrays), width), jnp.bfloat16)
    operands = [(a, VMEM) for a in arrays]
    return call(kernel, "bundled", operands, [shape], [], 2**21, cost)[0]


def first_row(mask, size):
    owner = (lax.axis_index("blk") ^ mask[0]) * lax.axis_size("grp") + (lax.axis_index("grp") ^ mask[1])
    return owner * size


def keys_of(block, size, mask, is_image):
    if not is_image:
        ids = lax.broadcasted_iota(jnp.int32, (1, size), 1) + first_row(mask, size)
        return ids.astype(jnp.float32)
    parts = piece(block, (size, EXTRA_ROWS), (0, 0, 0, size))[...].astype(jnp.float32)
    return parts[0:1] * LABEL_BASE + parts[1:2]


def reciprocal(value):
    near = pl.reciprocal(value, approx=True)
    return near * (2.0 - value * near)


def gradient_sums(name, size, scalars, x_blocks, y_blocks, masks, x_images, jobs, before, emits, sequence, after=()):
    width = x_blocks[0][0][0].shape[1]
    x_masks, y_masks = masks
    per_tile = TILE // size
    widths = part_widths(width)
    shapes, where = [], {}

    def result(extra, w, dtype):
        shapes.append(jax.ShapeDtypeStruct((size + extra, w), dtype))
        return len(shapes) - 1

    for r, kind in enumerate(emits):
        if kind == "float":
            where[r] = [(result(0, width, jnp.float32), 0, 0)]
        else:
            cut = widths if kind == "parts" else (width,)
            where[r] = [(result(EXTRA_ROWS, w, jnp.int16), 0, 0) for w in cut]
    operands = Operands()
    slope_at, shift_at = [operands.add(s, SMEM) for s in scalars]
    for b in sequence:
        operands.block(b)
    x_views = [operands.block(b) for b in x_blocks]
    y_views = [operands.block(b) for b in y_blocks]
    before_at = {r: operands.add(b, VMEM) for r, b in before.items()}

    def kernel(ins, refs):
        outs, weights = refs[:-1], refs[-1]
        slope, shift = ins[slope_at][0] * -LOG2E, ins[shift_at][0] * -LOG2E
        x_refs, y_refs = [v(ins) for v in x_views], [v(ins) for v in y_views]

        def stacked(chosen):
            return jnp.concatenate(
                [ref[pl.ds(row, size), pl.ds(column, width)] for ((ref, row, column),) in chosen],
                axis=0,
            )

        for rows, columns in jobs:
            x_all = stacked([x_refs[r] for r in rows])
            keys = [
                jnp.broadcast_to(keys_of(x_refs[r], size, x_masks[r], x_images), (size, size)).T
                for r in rows
            ]
            for n in range(0, len(columns), per_tile):
                chosen = columns[n : n + per_tile]
                other = jnp.concatenate(
                    [keys_of(y_refs[c], size, y_masks[c], not x_images) for c in chosen], axis=1
                )
                scores = lax.dot_general(
                    x_all,
                    stacked([y_refs[c] for c in chosen]),
                    (((1,), (1,)), ((), ())),
                    preferred_element_type=jnp.float32,
                )
                for i in range(len(rows)):
                    z = scores[i * size : (i + 1) * size] * slope + shift
                    sig = reciprocal(1.0 + jnp.exp2(jnp.minimum(z, 126.0)))
                    w = jnp.where(jnp.tile(keys[i], (1, len(chosen))) == other, sig - 1.0, sig)
                    there = pl.ds(n * size, len(chosen) * size)
                    weights[pl.ds(i * size, size), there] = w.astype(jnp.bfloat16)
            for tile in column_tiles(width):
                sums = jnp.dot(
                    weights[pl.ds(0, len(rows) * size), pl.ds(0, len(columns) * size)],
                    jnp.concatenate([piece(y_refs[c], (0, size), tile)[...] for c in columns], axis=0),
                    preferred_element_type=jnp.float32,
                )
                for i, r in enumerate(rows):
                    block = sums[i * size : (i + 1) * size]
                    if r in before_at:
                        block = block + piece(whole(ins[before_at[r]]), (0, size), tile)[...]
                    out = tuple((outs[o], row, column) for o, row, column in where[r])
                    if emits[r] == "float":
                        piece(out, (0, size), tile)[...] = block
                    else:
                        encode(block, out, tile)

    pairs = sum(len(rows) * len(columns) for rows, columns in jobs)
    scratch = [pltpu.VMEM((len(x_blocks) * size, len(y_blocks) * size), jnp.bfloat16)]
    room = len(x_blocks) * len(y_blocks) * size * size * 2 + 8 * 2**20
    results = call(kernel, name, operands.pairs, shapes, scratch, room, pairs * size, after)
    return [tuple(results[o] for o, _, _ in where[r]) for r in range(len(emits))]


def passed_sum(kept, received, part, held_back=(), after=()):
    size, width = kept.shape
    operands = Operands()
    kept_at = operands.add(kept, VMEM)
    views = [operands.block(b if part is None or len(b) == 1 else (b[part],) * 2) for b in received]

    def kernel(ins, outs):
        for tile in column_tiles(width):
            p, inner, _, span = tile
            if part is None or p == part:
                total = piece(whole(ins[kept_at]), (0, size), tile)[...]
                for view in views:
                    total = total + decoded(view(ins), size, tile)
                encode(total, whole(outs[0]), tile if part is None else (0, 0, inner, span))

    cut = width if part is None else part_widths(width)[part]
    shape = jax.ShapeDtypeStruct((size + EXTRA_ROWS, cut), jnp.int16)
    return call(kernel, "passed_sum", operands.pairs, [shape], [], 2**21, size, after, held_back)


def output_sums(sharpness, sums):
    size, width = sums[0][0].shape
    operands = Operands()
    sharpness_at = operands.add(sharpness, SMEM)
    views = [(operands.add(kept, VMEM), [operands.block(b) for b in blocks]) for kept, blocks in sums]

    def kernel(ins, outs):
        for out, (kept_at, received) in zip(outs, views):
            for tile in column_tiles(width):
                total = piece(whole(ins[kept_at]), (0, size), tile)[...]
                for view in received:
                    total = total + decoded(view(ins), size, tile)
                piece(whole(out), (0, size), tile)[...] = total * ins[sharpness_at][0]

    shapes = [jax.ShapeDtypeStruct((size, width), jnp.float32)] * len(sums)
    return call(kernel, "output_sums", operands.pairs, shapes, [], 2**21, size)


def swapped(array, step):
    axis, bit = step
    return lax.ppermute(array, axis, [(i, i ^ bit) for i in range(lax.axis_size(axis))])


def scattered(kept, coded, steps, after):
    def sent(array, step):
        return (swapped(array, step), 0, 0)

    half = len(kept)
    received = [[]] + [[(sent(c[0], steps[-1]),)] for c in coded[1:]]
    waiting, last = [c[1] for c in coded[1:]], [coded[0][0]]
    for s in reversed(range(len(steps) - 1)):
        for m in reversed(range(1 << s)):
            n = m | 1 << s
            first, *begun = passed_sum(kept[n], received[n], 0, waiting + last)
            for r, c in zip(received[1:], begun):
                r[0] = r[0] + (sent(c, steps[-1]),)
            received[0] += [(sent(c, steps[-1]),) for c in begun[len(waiting) :]]
            first = sent(first, steps[s])
            (second,) = passed_sum(kept[n], received[n], 1, (), [first[0], *after])
            received[m].append((first, sent(second, steps[s])))
            waiting, last, after = [], [], [second]
    return kept[0], received[0], after


def in_order(arrays, after=(), cost=HELD_COST):
    return call(lambda *refs: None, "held", [], [], [], 2**21, cost, after, arrays)


def bit_steps(axis):
    return [(axis, 1 << k) for k in range(int(math.log2(lax.axis_size(axis))))]


def owner_masks(steps):
    masks = [(0, 0)]
    for axis, bit in steps:
        masks = masks + [(b ^ bit, g) if axis == "blk" else (b, g ^ bit) for b, g in masks]
    return masks


def per_device(
    picture_vectors, caption_vectors, matching_caption, sharpness_parameter, additive_intercept
):
    scalars = (sharpness_parameter, additive_intercept)
    size = picture_vectors.shape[0]
    core, *grp_steps = bit_steps("grp")
    every = grp_steps + bit_steps("blk")
    steps = [every[0::2], every[1::2]]
    assert len(steps[0]) == len(steps[1]) >= 2
    masks = [owner_masks(s + [core]) for s in steps]
    count = 1 << len(steps[0])
    half = count // 2
    early, late = list(range(half + 1)), list(range(half + 1, count))
    labels = matching_caption[None, :]
    (first_texts,) = in_order([swapped(caption_vectors, steps[1][0])], (), 1)
    first_images = [swapped(a, steps[0][0]) for a in (picture_vectors, labels)]
    arrays = [{0: labelled(picture_vectors, labels), 1: labelled(*first_images, [first_texts])}, {0: caption_vectors, 1: first_texts}]
    for i in range(1, len(steps[0])):
        for k in (1, 0):
            for m in range(1 << i):
                arrays[k][m | 1 << i] = swapped(arrays[k][m], steps[k][i])
    blocks = [[whole(a[m]) for m in range(count)] for a in arrays]
    others = [{}, {}]
    both = bundled([arrays[1][1], arrays[0][1]], BUNDLE_COST)
    rest = [m for m in early if m != 1]
    both = swapped(bundled([both] + [arrays[k][m] for m in rest for k in (1, 0)], size), core)
    for i, m in enumerate([1] + rest):
        row = i * (2 * size + EXTRA_ROWS)
        others[1][m], others[0][m] = ((both, row, 0),), ((both, row + size, 0),)

    def sums(name, kind, rows, columns, jobs, before, emits, after=()):
        other = 1 - kind
        x_blocks = [blocks[kind][m] for m in rows]
        y_blocks = [(blocks, others)[c][other][m] for c, m in columns]
        x_masks = [masks[kind][m] for m in rows]
        y_masks = [masks[other][m + c * count] for c, m in columns]
        return gradient_sums(
            name,
            size,
            scalars,
            x_blocks,
            y_blocks,
            (x_masks, y_masks),
            kind == 0,
            jobs,
            before,
            emits,
            [blocks[k][m] for m in rows[1:] + rows[:1] for k in (1, 0)],
            after,
        )

    def both_cores(chosen):
        return [(c, m) for c in range(2) for m in chosen]

    def every_pair(rows, columns):
        return [(list(range(len(rows))), list(range(len(columns))))]

    before = []
    for k in range(2):
        columns = both_cores(early)
        jobs, emits = every_pair(early, columns), ["float"] * len(early)
        results = sums("early_sums", k, early, columns, jobs, {}, emits)
        before.append({m: s for m, (s,) in zip(early, results)})
    arrays = [[b[m][0][0] for m in late] for b in blocks[::-1]]
    arrays, before = lax.optimization_barrier((arrays, before))
    for k in (1, 0):
        for m, a in zip(late, arrays[1 - k]):
            blocks[k][m] = whole(a)
            others[k][m] = whole(swapped(a, core))
    after = ()
    coded, kept = [[None] * half, [None] * half], [None, None]
    for k in (1, 0):
        columns = [(0, m) for m in range(count)] + [(1, m) for m in early]
        jobs, emits = every_pair(late, columns), ["float"] * len(late)
        results = sums("late_rows_begun", k, late, columns, jobs, {}, emits, after)
        begun = {i: s for i, (s,) in enumerate(results)}
        columns = [(1, m) for m in late]
        jobs, emits = every_pair(late, columns), ["parts"] * len(late)
        coded[k][1:] = sums("late_rows", k, late, columns, jobs, begun, emits)
        after = coded[k][1]
    for k in (1, 0):
        columns = both_cores(late)
        jobs, emits = every_pair(early, columns), ["float"] * half + ["whole"]
        *whole_sums, coded[k][0] = sums("late_columns", k, early, columns, jobs, before[k], emits, after)
        kept[k], after = [s for (s,) in whole_sums], coded[k][0]
    kept_texts, text_blocks, after = scattered(kept[1], coded[1], steps[1], ())
    kept_images, image_blocks, _ = scattered(kept[0], coded[0], steps[0], after)
    ends = ()
    for blocks_in in (text_blocks, image_blocks):
        ends = in_order([part[0] for b in blocks_in if len(b) > 1 for part in b], ends)
        parts = iter(ends)
        blocks_in[:] = [tuple((next(parts), 0, 0) for _ in b) if len(b) > 1 else b for b in blocks_in]
    return tuple(output_sums(scalars[0], [(kept_images, image_blocks), (kept_texts, text_blocks)]))


def solution(mesh):
    placed = (P(("blk", "grp"), None), P(("blk", "grp"), None), P(("blk", "grp")), P(), P())
    return jax.shard_map(
        per_device,
        mesh=mesh,
        in_specs=placed,
        out_specs=(P(("blk", "grp"), None), P(("blk", "grp"), None)),
        check_vma=False,
    )
```

```python
import math

import jax
import jax.numpy as jnp
from jax import lax
from jax.experimental import pallas as pl
from jax.experimental.pallas import tpu as pltpu
from jax.sharding import PartitionSpec as P

LOG2E = 1.4426950408889634
CODE_TOP = 32000.0
CODE_STEPS = 32.0
EXTRA_ROWS = 8
LABEL_BASE = 128
TILE = 256
LANES = 128
BUNDLE_COST = 6 * 10**8
HELD_COST = 3 * 10**8
SMEM = pl.BlockSpec(memory_space=pltpu.SMEM)
VMEM = pl.BlockSpec(memory_space=pltpu.VMEM)
ANY = pl.BlockSpec(memory_space=pl.ANY)


def whole(array):
    return ((array, 0, 0),)


def part_widths(width):
    first = width // (2 * LANES) * LANES
    return (first, width - first)


def column_tiles(width):
    tiles, begin = [], 0
    for p, w in enumerate(part_widths(width)):
        tiles += [(p, k, begin + k, min(TILE, w - k)) for k in range(0, w, TILE)]
        begin += w
    return tiles


def piece(block, rows, tile):
    p, inner, start, span = tile
    ref, row, column = block[0 if len(block) == 1 else p]
    first = start if len(block) == 1 else inner
    return ref.at[pl.ds(row + rows[0], rows[1]), pl.ds(column + first, span)]


class Operands:
    def __init__(self):
        self.pairs = []

    def add(self, array, spec):
        for i, (a, s) in enumerate(self.pairs):
            if a is array and s is spec:
                return i
        self.pairs.append((array, spec))
        return len(self.pairs) - 1

    def block(self, block):
        at = [(self.add(a, VMEM), row, column) for a, row, column in block]
        return lambda refs: tuple((refs[i], row, column) for i, row, column in at)


def scale_code(top):
    return jnp.ceil(jnp.log(jnp.maximum(top, 1e-30)) * (CODE_STEPS * LOG2E))


def encode(value, block, tile):
    size, span = value.shape
    code = scale_code(jnp.max(jnp.abs(value), axis=0, keepdims=True))
    gain = CODE_TOP * jnp.exp(code * (-1.0 / (CODE_STEPS * LOG2E)))
    piece(block, (0, size), tile)[...] = (
        jnp.round(value * gain).astype(jnp.int32).astype(jnp.int16)
    )
    scales = jnp.broadcast_to(code.astype(jnp.int32), (EXTRA_ROWS, span)).astype(jnp.int16)
    piece(block, (size, EXTRA_ROWS), tile)[...] = scales


def decoded(block, size, tile):
    code = piece(block, (size, EXTRA_ROWS), tile)[...].astype(jnp.int32).astype(jnp.float32)
    gain = jnp.exp(code[:1] * (1.0 / (CODE_STEPS * LOG2E))) * (1.0 / CODE_TOP)
    return piece(block, (0, size), tile)[...].astype(jnp.int32).astype(jnp.float32) * gain


def call(kernel, name, operands, out_shape, scratch, room, cost, after=(), held_back=()):
    arrays = [a for a, _ in operands]
    held = sum(math.prod(a.shape) * a.dtype.itemsize for a in [*arrays, *out_shape])

    def body(*refs):
        results = refs[len(arrays) + len(after) + len(held_back) :]
        kernel(refs[: len(arrays)], results[: len(out_shape)] + results[len(out_shape) + len(held_back) :])

    return pl.pallas_call(
        body,
        out_shape=[*out_shape, *(jax.ShapeDtypeStruct(a.shape, a.dtype) for a in held_back)],
        in_specs=[s for _, s in operands] + [ANY] * (len(after) + len(held_back)),
        out_specs=[VMEM] * len(out_shape) + [ANY] * len(held_back),
        input_output_aliases={
            len(arrays) + len(after) + i: len(out_shape) + i for i in range(len(held_back))
        },
        scratch_shapes=scratch,
        compiler_params=pltpu.CompilerParams(vmem_limit_bytes=held + room),
        cost_estimate=pl.CostEstimate(flops=cost, bytes_accessed=cost, transcendentals=0),
        name=name,
    )(*arrays, *after, *held_back)


def labelled(images, labels, after=()):
    size, width = images.shape

    def kernel(ins, outs):
        outs[0][pl.ds(0, size), :] = ins[0][...]
        outs[0][pl.ds(size, EXTRA_ROWS), :] = jnp.zeros((EXTRA_ROWS, width), jnp.bfloat16)
        row = ins[1][...]
        low, high = lax.rem(row, LABEL_BASE), lax.div(row, LABEL_BASE)
        at = lax.broadcasted_iota(jnp.int32, (EXTRA_ROWS, size), 0)
        parts = jnp.where(at == 0, high, jnp.where(at == 1, low, 0)).astype(jnp.float32)
        outs[0][pl.ds(size, EXTRA_ROWS), pl.ds(0, size)] = parts.astype(jnp.bfloat16)

    shape = jax.ShapeDtypeStruct((size + EXTRA_ROWS, width), jnp.bfloat16)
    operands = [(images, VMEM), (labels, VMEM)]
    return call(kernel, "labelled", operands, [shape], [], 2**21, size, after)[0]


def bundled(arrays, cost):
    width = arrays[0].shape[1]

    def kernel(ins, outs):
        first = 0
        for ref in ins:
            outs[0][pl.ds(first, ref.shape[0]), :] = ref[...]
            first += ref.shape[0]

    shape = jax.ShapeDtypeStruct((sum(a.shape[0] for a in arrays), width), jnp.bfloat16)
    operands = [(a, VMEM) for a in arrays]
    return call(kernel, "bundled", operands, [shape], [], 2**21, cost)[0]


def first_row(mask, size):
    owner = (lax.axis_index("blk") ^ mask[0]) * lax.axis_size("grp") + (lax.axis_index("grp") ^ mask[1])
    return owner * size


def keys_of(block, size, mask, is_image):
    if not is_image:
        ids = lax.broadcasted_iota(jnp.int32, (1, size), 1) + first_row(mask, size)
        return ids.astype(jnp.float32)
    parts = piece(block, (size, EXTRA_ROWS), (0, 0, 0, size))[...].astype(jnp.float32)
    return parts[0:1] * LABEL_BASE + parts[1:2]


def gradient_sums(name, size, scalars, x_blocks, y_blocks, masks, x_images, jobs, before, emits, sequence, after=()):
    width = x_blocks[0][0][0].shape[1]
    x_masks, y_masks = masks
    per_tile = TILE // size
    widths = part_widths(width)
    shapes, where = [], {}

    def result(extra, w, dtype):
        shapes.append(jax.ShapeDtypeStruct((size + extra, w), dtype))
        return len(shapes) - 1

    for r, kind in enumerate(emits):
        if kind == "float":
            where[r] = [(result(0, width, jnp.float32), 0, 0)]
        else:
            cut = widths if kind == "parts" else (width,)
            where[r] = [(result(EXTRA_ROWS, w, jnp.int16), 0, 0) for w in cut]
    operands = Operands()
    slope_at, shift_at = [operands.add(s, SMEM) for s in scalars]
    for b in sequence:
        operands.block(b)
    x_views = [operands.block(b) for b in x_blocks]
    y_views = [operands.block(b) for b in y_blocks]
    before_at = {r: operands.add(b, VMEM) for r, b in before.items()}

    def kernel(ins, refs):
        outs, weights = refs[:-1], refs[-1]
        slope, shift = ins[slope_at][0] * LOG2E, ins[shift_at][0] * LOG2E
        x_refs, y_refs = [v(ins) for v in x_views], [v(ins) for v in y_views]

        def stacked(chosen):
            return jnp.concatenate(
                [ref[pl.ds(row, size), pl.ds(column, width)] for ((ref, row, column),) in chosen],
                axis=0,
            )

        for rows, columns in jobs:
            x_all = stacked([x_refs[r] for r in rows])
            keys = [
                jnp.broadcast_to(keys_of(x_refs[r], size, x_masks[r], x_images), (size, size)).T
                for r in rows
            ]
            for n in range(0, len(columns), per_tile):
                chosen = columns[n : n + per_tile]
                other = jnp.concatenate(
                    [keys_of(y_refs[c], size, y_masks[c], not x_images) for c in chosen], axis=1
                )
                scores = lax.dot_general(
                    x_all,
                    stacked([y_refs[c] for c in chosen]),
                    (((1,), (1,)), ((), ())),
                    preferred_element_type=jnp.float32,
                )
                for i in range(len(rows)):
                    z = scores[i * size : (i + 1) * size] * slope + shift
                    sig = 1.0 / (1.0 + jnp.exp2(-z))
                    w = jnp.where(jnp.tile(keys[i], (1, len(chosen))) == other, sig - 1.0, sig)
                    there = pl.ds(n * size, len(chosen) * size)
                    weights[pl.ds(i * size, size), there] = w.astype(jnp.bfloat16)
            for tile in column_tiles(width):
                sums = jnp.dot(
                    weights[pl.ds(0, len(rows) * size), pl.ds(0, len(columns) * size)],
                    jnp.concatenate([piece(y_refs[c], (0, size), tile)[...] for c in columns], axis=0),
                    preferred_element_type=jnp.float32,
                )
                for i, r in enumerate(rows):
                    block = sums[i * size : (i + 1) * size]
                    if r in before_at:
                        block = block + piece(whole(ins[before_at[r]]), (0, size), tile)[...]
                    out = tuple((outs[o], row, column) for o, row, column in where[r])
                    if emits[r] == "float":
                        piece(out, (0, size), tile)[...] = block
                    else:
                        encode(block, out, tile)

    pairs = sum(len(rows) * len(columns) for rows, columns in jobs)
    scratch = [pltpu.VMEM((len(x_blocks) * size, len(y_blocks) * size), jnp.bfloat16)]
    room = len(x_blocks) * len(y_blocks) * size * size * 2 + 8 * 2**20
    results = call(kernel, name, operands.pairs, shapes, scratch, room, pairs * size, after)
    return [tuple(results[o] for o, _, _ in where[r]) for r in range(len(emits))]


def passed_sum(kept, received, part, held_back=(), after=()):
    size, width = kept.shape
    operands = Operands()
    kept_at = operands.add(kept, VMEM)
    views = [operands.block(b if part is None or len(b) == 1 else (b[part],) * 2) for b in received]

    def kernel(ins, outs):
        for tile in column_tiles(width):
            p, inner, _, span = tile
            if part is None or p == part:
                total = piece(whole(ins[kept_at]), (0, size), tile)[...]
                for view in views:
                    total = total + decoded(view(ins), size, tile)
                encode(total, whole(outs[0]), tile if part is None else (0, 0, inner, span))

    cut = width if part is None else part_widths(width)[part]
    shape = jax.ShapeDtypeStruct((size + EXTRA_ROWS, cut), jnp.int16)
    return call(kernel, "passed_sum", operands.pairs, [shape], [], 2**21, size, after, held_back)


def output_sums(sharpness, sums):
    size, width = sums[0][0].shape
    operands = Operands()
    sharpness_at = operands.add(sharpness, SMEM)
    views = [(operands.add(kept, VMEM), [operands.block(b) for b in blocks]) for kept, blocks in sums]

    def kernel(ins, outs):
        for out, (kept_at, received) in zip(outs, views):
            for tile in column_tiles(width):
                total = piece(whole(ins[kept_at]), (0, size), tile)[...]
                for view in received:
                    total = total + decoded(view(ins), size, tile)
                piece(whole(out), (0, size), tile)[...] = total * ins[sharpness_at][0]

    shapes = [jax.ShapeDtypeStruct((size, width), jnp.float32)] * len(sums)
    return call(kernel, "output_sums", operands.pairs, shapes, [], 2**21, size)


def swapped(array, step):
    axis, bit = step
    return lax.ppermute(array, axis, [(i, i ^ bit) for i in range(lax.axis_size(axis))])


def scattered(kept, coded, steps, after):
    def sent(array, step):
        return (swapped(array, step), 0, 0)

    half = len(kept)
    received = [[]] + [[(sent(c[0], steps[-1]),)] for c in coded[1:]]
    waiting, last = [c[1] for c in coded[1:]], []
    for s in reversed(range(len(steps) - 1)):
        for m in reversed(range(1 << s)):
            n = m | 1 << s
            first, *begun = passed_sum(kept[n], received[n], 0, waiting + last)
            if waiting:
                begun_with = [first]
            for r, c in zip(received[1:], begun):
                r[0] = r[0] + (sent(c, steps[-1]),)
            received[0] += [(sent(c, steps[-1]),) for c in begun[len(waiting) :]]
            first = sent(first, steps[s])
            (second,) = passed_sum(kept[n], received[n], 1, (), [first[0], *after])
            received[m].append((first, sent(second, steps[s])))
            waiting, last, after = [], [], [second]
    return received[0], after, begun_with


def in_order(arrays, after=(), cost=HELD_COST):
    return call(lambda *refs: None, "held", [], [], [], 2**21, cost, after, arrays)


def bit_steps(axis):
    return [(axis, 1 << k) for k in range(int(math.log2(lax.axis_size(axis))))]


def owner_masks(steps):
    masks = [(0, 0)]
    for axis, bit in steps:
        masks = masks + [(b ^ bit, g) if axis == "blk" else (b, g ^ bit) for b, g in masks]
    return masks


def per_device(
    picture_vectors, caption_vectors, matching_caption, sharpness_parameter, additive_intercept
):
    scalars = (sharpness_parameter, additive_intercept)
    size = picture_vectors.shape[0]
    core, *grp_steps = bit_steps("grp")
    every = grp_steps + bit_steps("blk")
    steps = [every[0::2], every[1::2]]
    assert len(steps[0]) == len(steps[1]) >= 2
    masks = [owner_masks(s + [core]) for s in steps]
    count = 1 << len(steps[0])
    half = count // 2
    early, late = list(range(half + 1)), list(range(half + 1, count))
    labels = matching_caption[None, :]
    (first_texts,) = in_order([swapped(caption_vectors, steps[1][0])], (), 1)
    first_images = [swapped(a, steps[0][0]) for a in (picture_vectors, labels)]
    arrays = [{0: labelled(picture_vectors, labels), 1: labelled(*first_images, [first_texts])}, {0: caption_vectors, 1: first_texts}]
    for i in range(1, len(steps[0])):
        for k in (1, 0):
            for m in range(1 << i):
                arrays[k][m | 1 << i] = swapped(arrays[k][m], steps[k][i])
    blocks = [[whole(a[m]) for m in range(count)] for a in arrays]
    others = [{}, {}]
    both = bundled([arrays[1][1], arrays[0][1]], BUNDLE_COST)
    rest = [m for m in early if m != 1]
    both = swapped(bundled([both] + [arrays[k][m] for m in rest for k in (1, 0)], size), core)
    for i, m in enumerate([1] + rest):
        row = i * (2 * size + EXTRA_ROWS)
        others[1][m], others[0][m] = ((both, row, 0),), ((both, row + size, 0),)

    def sums(name, kind, rows, columns, jobs, before, emits, after=()):
        other = 1 - kind
        x_blocks = [blocks[kind][m] for m in rows]
        y_blocks = [(blocks, others)[c][other][m] for c, m in columns]
        x_masks = [masks[kind][m] for m in rows]
        y_masks = [masks[other][m + c * count] for c, m in columns]
        return gradient_sums(
            name,
            size,
            scalars,
            x_blocks,
            y_blocks,
            (x_masks, y_masks),
            kind == 0,
            jobs,
            before,
            emits,
            [blocks[k][m] for m in rows[1:] + rows[:1] for k in (1, 0)],
            after,
        )

    def both_cores(chosen):
        return [(c, m) for c in range(2) for m in chosen]

    def every_pair(rows, columns):
        return [(list(range(len(rows))), list(range(len(columns))))]

    before = []
    for k in range(2):
        columns = both_cores(early)
        jobs, emits = every_pair(early, columns), ["float"] * len(early)
        results = sums("early_sums", k, early, columns, jobs, {}, emits)
        before.append({m: s for m, (s,) in zip(early, results)})
    arrays = [[b[m][0][0] for m in late] for b in blocks[::-1]]
    arrays, before = lax.optimization_barrier((arrays, before))
    for k in (1, 0):
        for m, a in zip(late, arrays[1 - k]):
            blocks[k][m] = whole(a)
            others[k][m] = whole(swapped(a, core))
    after = ()
    coded, kept = [[None] * half, [None] * half], [None, None]
    for k in (1, 0):
        columns = [(0, m) for m in range(count)] + [(1, m) for m in early]
        jobs, emits = every_pair(late, columns), ["float"] * len(late)
        results = sums("late_rows_begun", k, late, columns, jobs, {}, emits, after)
        begun = {i: s for i, (s,) in enumerate(results)}
        columns = [(1, m) for m in late]
        jobs, emits = every_pair(late, columns), ["parts"] * len(late)
        coded[k][1:] = sums("late_rows", k, late, columns, jobs, begun, emits)
        after = coded[k][1]
    def last_columns(k, rows, emits, after):
        columns = both_cores(late)
        begun = {i: before[k][m] for i, m in enumerate(rows)}
        return [r[0] for r in sums("late_columns", k, rows, columns, every_pair(rows, columns), begun, emits, after)]

    middle = list(range(1, half))
    for k in (1, 0):
        kept[k] = [None] + last_columns(k, middle, ["float"] * len(middle), after)
        after = kept[k][-1:]
    text_blocks, after, _ = scattered(kept[1], coded[1], steps[1], ())
    image_blocks, _, after = scattered(kept[0], coded[0], steps[0], after)
    ends_at = [image_blocks, text_blocks]
    for k in (1, 0):
        kept[k][0], code = last_columns(k, [0, half], ["float", "whole"], after)
        ends_at[k].append(whole(swapped(code, steps[k][-1])))
        after = [code]
    kept_images, kept_texts = kept[0][0], kept[1][0]
    ends = ()
    for blocks_in in (text_blocks, image_blocks):
        ends = in_order([part[0] for b in blocks_in if len(b) > 1 for part in b], ends)
        parts = iter(ends)
        blocks_in[:] = [tuple((next(parts), 0, 0) for _ in b) if len(b) > 1 else b for b in blocks_in]
    return tuple(output_sums(scalars[0], [(kept_images, image_blocks), (kept_texts, text_blocks)]))


def solution(mesh):
    placed = (P(("blk", "grp"), None), P(("blk", "grp"), None), P(("blk", "grp")), P(), P())
    return jax.shard_map(
        per_device,
        mesh=mesh,
        in_specs=placed,
        out_specs=(P(("blk", "grp"), None), P(("blk", "grp"), None)),
        check_vma=False,
    )
```

```python
import math

import jax
import jax.numpy as jnp
from jax import lax
from jax.experimental import pallas as pl
from jax.experimental.pallas import tpu as pltpu
from jax.sharding import PartitionSpec as P

LOG2E = 1.4426950408889634
CODE_TOP = 32000.0
CODE_STEPS = 32.0
EXTRA_ROWS = 8
LABEL_BASE = 128
TILE = 256
LANES = 128
BUNDLE_COST = 6 * 10**8
HELD_COST = 3 * 10**8
SMEM = pl.BlockSpec(memory_space=pltpu.SMEM)
VMEM = pl.BlockSpec(memory_space=pltpu.VMEM)
ANY = pl.BlockSpec(memory_space=pl.ANY)


def whole(array):
    return ((array, 0, 0),)


def part_widths(width):
    first = (width // LANES + 1) // 2 * LANES
    return (first, width - first)


def column_tiles(width):
    tiles, begin = [], 0
    for p, w in enumerate(part_widths(width)):
        tiles += [(p, k, begin + k, min(TILE, w - k)) for k in range(0, w, TILE)]
        begin += w
    return tiles


def piece(block, rows, tile):
    p, inner, start, span = tile
    ref, row, column = block[0 if len(block) == 1 else p]
    first = start if len(block) == 1 else inner
    return ref.at[pl.ds(row + rows[0], rows[1]), pl.ds(column + first, span)]


class Operands:
    def __init__(self):
        self.pairs = []

    def add(self, array, spec):
        for i, (a, s) in enumerate(self.pairs):
            if a is array and s is spec:
                return i
        self.pairs.append((array, spec))
        return len(self.pairs) - 1

    def block(self, block):
        at = [(self.add(a, VMEM), row, column) for a, row, column in block]
        return lambda refs: tuple((refs[i], row, column) for i, row, column in at)


def scale_code(top):
    return jnp.ceil(jnp.log(jnp.maximum(top, 1e-30)) * (CODE_STEPS * LOG2E))


def encode(value, block, tile):
    size, span = value.shape
    code = scale_code(jnp.max(jnp.abs(value), axis=0, keepdims=True))
    gain = CODE_TOP * jnp.exp(code * (-1.0 / (CODE_STEPS * LOG2E)))
    piece(block, (0, size), tile)[...] = (
        jnp.round(value * gain).astype(jnp.int32).astype(jnp.int16)
    )
    scales = jnp.broadcast_to(code.astype(jnp.int32), (EXTRA_ROWS, span)).astype(jnp.int16)
    piece(block, (size, EXTRA_ROWS), tile)[...] = scales


def decoded(block, size, tile):
    code = piece(block, (size, EXTRA_ROWS), tile)[...].astype(jnp.int32).astype(jnp.float32)
    gain = jnp.exp(code[:1] * (1.0 / (CODE_STEPS * LOG2E))) * (1.0 / CODE_TOP)
    return piece(block, (0, size), tile)[...].astype(jnp.int32).astype(jnp.float32) * gain


def call(kernel, name, operands, out_shape, scratch, room, cost, after=(), held_back=()):
    arrays = [a for a, _ in operands]
    held = sum(math.prod(a.shape) * a.dtype.itemsize for a in [*arrays, *out_shape])

    def body(*refs):
        results = refs[len(arrays) + len(after) + len(held_back) :]
        kernel(refs[: len(arrays)], results[: len(out_shape)] + results[len(out_shape) + len(held_back) :])

    return pl.pallas_call(
        body,
        out_shape=[*out_shape, *(jax.ShapeDtypeStruct(a.shape, a.dtype) for a in held_back)],
        in_specs=[s for _, s in operands] + [ANY] * (len(after) + len(held_back)),
        out_specs=[VMEM] * len(out_shape) + [ANY] * len(held_back),
        input_output_aliases={
            len(arrays) + len(after) + i: len(out_shape) + i for i in range(len(held_back))
        },
        scratch_shapes=scratch,
        compiler_params=pltpu.CompilerParams(vmem_limit_bytes=held + room),
        cost_estimate=pl.CostEstimate(flops=cost, bytes_accessed=cost, transcendentals=0),
        name=name,
    )(*arrays, *after, *held_back)


def labelled(images, labels, after=()):
    size, width = images.shape

    def kernel(ins, outs):
        outs[0][pl.ds(0, size), :] = ins[0][...]
        outs[0][pl.ds(size, EXTRA_ROWS), :] = jnp.zeros((EXTRA_ROWS, width), jnp.bfloat16)
        row = ins[1][...]
        low, high = lax.rem(row, LABEL_BASE), lax.div(row, LABEL_BASE)
        at = lax.broadcasted_iota(jnp.int32, (EXTRA_ROWS, size), 0)
        parts = jnp.where(at == 0, high, jnp.where(at == 1, low, 0)).astype(jnp.float32)
        outs[0][pl.ds(size, EXTRA_ROWS), pl.ds(0, size)] = parts.astype(jnp.bfloat16)

    shape = jax.ShapeDtypeStruct((size + EXTRA_ROWS, width), jnp.bfloat16)
    operands = [(images, VMEM), (labels, VMEM)]
    return call(kernel, "labelled", operands, [shape], [], 2**21, size, after)[0]


def bundled(arrays, cost):
    width = arrays[0].shape[1]

    def kernel(ins, outs):
        first = 0
        for ref in ins:
            outs[0][pl.ds(first, ref.shape[0]), :] = ref[...]
            first += ref.shape[0]

    shape = jax.ShapeDtypeStruct((sum(a.shape[0] for a in arrays), width), jnp.bfloat16)
    operands = [(a, VMEM) for a in arrays]
    return call(kernel, "bundled", operands, [shape], [], 2**21, cost)[0]


def first_row(mask, size):
    owner = (lax.axis_index("blk") ^ mask[0]) * lax.axis_size("grp") + (lax.axis_index("grp") ^ mask[1])
    return owner * size


def keys_of(block, size, mask, is_image):
    if not is_image:
        ids = lax.broadcasted_iota(jnp.int32, (1, size), 1) + first_row(mask, size)
        return ids.astype(jnp.float32)
    parts = piece(block, (size, EXTRA_ROWS), (0, 0, 0, size))[...].astype(jnp.float32)
    return parts[0:1] * LABEL_BASE + parts[1:2]


def gradient_sums(name, size, scalars, x_blocks, y_blocks, masks, x_images, jobs, before, emits, sequence, after=()):
    width = x_blocks[0][0][0].shape[1]
    x_masks, y_masks = masks
    per_tile = TILE // size
    widths = part_widths(width)
    shapes, where = [], {}

    def result(extra, w, dtype):
        shapes.append(jax.ShapeDtypeStruct((size + extra, w), dtype))
        return len(shapes) - 1

    for r, kind in enumerate(emits):
        if kind == "float":
            where[r] = [(result(0, width, jnp.float32), 0, 0)]
        else:
            cut = widths if kind == "parts" else (width,)
            where[r] = [(result(EXTRA_ROWS, w, jnp.int16), 0, 0) for w in cut]
    operands = Operands()
    slope_at, shift_at = [operands.add(s, SMEM) for s in scalars]
    for b in sequence:
        operands.block(b)
    x_views = [operands.block(b) for b in x_blocks]
    y_views = [operands.block(b) for b in y_blocks]
    before_at = {r: operands.add(b, VMEM) for r, b in before.items()}

    def kernel(ins, refs):
        outs, weights = refs[:-1], refs[-1]
        slope, shift = ins[slope_at][0] * LOG2E, ins[shift_at][0] * LOG2E
        x_refs, y_refs = [v(ins) for v in x_views], [v(ins) for v in y_views]

        def stacked(chosen):
            return jnp.concatenate(
                [ref[pl.ds(row, size), pl.ds(column, width)] for ((ref, row, column),) in chosen],
                axis=0,
            )

        for rows, columns in jobs:
            x_all = stacked([x_refs[r] for r in rows])
            keys = [
                jnp.broadcast_to(keys_of(x_refs[r], size, x_masks[r], x_images), (size, size)).T
                for r in rows
            ]
            for n in range(0, len(columns), per_tile):
                chosen = columns[n : n + per_tile]
                other = jnp.concatenate(
                    [keys_of(y_refs[c], size, y_masks[c], not x_images) for c in chosen], axis=1
                )
                scores = lax.dot_general(
                    x_all,
                    stacked([y_refs[c] for c in chosen]),
                    (((1,), (1,)), ((), ())),
                    preferred_element_type=jnp.float32,
                )
                for i in range(len(rows)):
                    z = scores[i * size : (i + 1) * size] * slope + shift
                    sig = 1.0 / (1.0 + jnp.exp2(-z))
                    w = jnp.where(jnp.tile(keys[i], (1, len(chosen))) == other, sig - 1.0, sig)
                    there = pl.ds(n * size, len(chosen) * size)
                    weights[pl.ds(i * size, size), there] = w.astype(jnp.bfloat16)
            for tile in column_tiles(width):
                sums = jnp.dot(
                    weights[pl.ds(0, len(rows) * size), pl.ds(0, len(columns) * size)],
                    jnp.concatenate([piece(y_refs[c], (0, size), tile)[...] for c in columns], axis=0),
                    preferred_element_type=jnp.float32,
                )
                for i, r in enumerate(rows):
                    block = sums[i * size : (i + 1) * size]
                    if r in before_at:
                        block = block + piece(whole(ins[before_at[r]]), (0, size), tile)[...]
                    out = tuple((outs[o], row, column) for o, row, column in where[r])
                    if emits[r] == "float":
                        piece(out, (0, size), tile)[...] = block
                    else:
                        encode(block, out, tile)

    pairs = sum(len(rows) * len(columns) for rows, columns in jobs)
    scratch = [pltpu.VMEM((len(x_blocks) * size, len(y_blocks) * size), jnp.bfloat16)]
    room = len(x_blocks) * len(y_blocks) * size * size * 2 + 8 * 2**20
    results = call(kernel, name, operands.pairs, shapes, scratch, room, pairs * size, after)
    return [tuple(results[o] for o, _, _ in where[r]) for r in range(len(emits))]


def passed_sum(kept, received, part, held_back=(), after=()):
    size, width = kept.shape
    operands = Operands()
    kept_at = operands.add(kept, VMEM)
    views = [operands.block(b if part is None or len(b) == 1 else (b[part],) * 2) for b in received]

    def kernel(ins, outs):
        for tile in column_tiles(width):
            p, inner, _, span = tile
            if part is None or p == part:
                total = piece(whole(ins[kept_at]), (0, size), tile)[...]
                for view in views:
                    total = total + decoded(view(ins), size, tile)
                encode(total, whole(outs[0]), tile if part is None else (0, 0, inner, span))

    cut = width if part is None else part_widths(width)[part]
    shape = jax.ShapeDtypeStruct((size + EXTRA_ROWS, cut), jnp.int16)
    return call(kernel, "passed_sum", operands.pairs, [shape], [], 2**21, size, after, held_back)


def output_sums(sharpness, sums):
    size, width = sums[0][0].shape
    operands = Operands()
    sharpness_at = operands.add(sharpness, SMEM)
    views = [(operands.add(kept, VMEM), [operands.block(b) for b in blocks]) for kept, blocks in sums]

    def kernel(ins, outs):
        for out, (kept_at, received) in zip(outs, views):
            for tile in column_tiles(width):
                total = piece(whole(ins[kept_at]), (0, size), tile)[...]
                for view in received:
                    total = total + decoded(view(ins), size, tile)
                piece(whole(out), (0, size), tile)[...] = total * ins[sharpness_at][0]

    shapes = [jax.ShapeDtypeStruct((size, width), jnp.float32)] * len(sums)
    return call(kernel, "output_sums", operands.pairs, shapes, [], 2**21, size)


def swapped(array, step):
    axis, bit = step
    return lax.ppermute(array, axis, [(i, i ^ bit) for i in range(lax.axis_size(axis))])


def scattered(kept, coded, steps, after):
    def sent(array, step):
        return (swapped(array, step), 0, 0)

    half = len(kept)
    received = [[]] + [[(sent(c[0], steps[-1]),)] for c in coded[1:]]
    waiting, last = [c[1] for c in coded[1:]], []
    for s in reversed(range(len(steps) - 1)):
        for m in reversed(range(1 << s)):
            n = m | 1 << s
            first, *begun = passed_sum(kept[n], received[n], 0, waiting + last)
            if waiting:
                begun_with = [first]
            for r, c in zip(received[1:], begun):
                r[0] = r[0] + (sent(c, steps[-1]),)
            received[0] += [(sent(c, steps[-1]),) for c in begun[len(waiting) :]]
            first = sent(first, steps[s])
            (second,) = passed_sum(kept[n], received[n], 1, (), [first[0], *after])
            received[m].append((first, sent(second, steps[s])))
            waiting, last, after = [], [], [second]
    return received[0], after, begun_with


def in_order(arrays, after=(), cost=HELD_COST):
    return call(lambda *refs: None, "held", [], [], [], 2**21, cost, after, arrays)


def bit_steps(axis):
    return [(axis, 1 << k) for k in range(int(math.log2(lax.axis_size(axis))))]


def owner_masks(steps):
    masks = [(0, 0)]
    for axis, bit in steps:
        masks = masks + [(b ^ bit, g) if axis == "blk" else (b, g ^ bit) for b, g in masks]
    return masks


def per_device(
    picture_vectors, caption_vectors, matching_caption, sharpness_parameter, additive_intercept
):
    scalars = (sharpness_parameter, additive_intercept)
    size = picture_vectors.shape[0]
    core, *grp_steps = bit_steps("grp")
    every = grp_steps + bit_steps("blk")
    steps = [every[0::2], every[1::2]]
    assert len(steps[0]) == len(steps[1]) >= 2
    masks = [owner_masks(s + [core]) for s in steps]
    count = 1 << len(steps[0])
    half = count // 2
    early, late = list(range(half + 1)), list(range(half + 1, count))
    labels = matching_caption[None, :]
    (first_texts,) = in_order([swapped(caption_vectors, steps[1][0])], (), 1)
    first_images = [swapped(a, steps[0][0]) for a in (picture_vectors, labels)]
    arrays = [{0: labelled(picture_vectors, labels), 1: labelled(*first_images, [first_texts])}, {0: caption_vectors, 1: first_texts}]
    for i in range(1, len(steps[0])):
        for k in (1, 0):
            for m in range(1 << i):
                arrays[k][m | 1 << i] = swapped(arrays[k][m], steps[k][i])
    blocks = [[whole(a[m]) for m in range(count)] for a in arrays]
    others = [{}, {}]
    both = bundled([arrays[1][1], arrays[0][1]], BUNDLE_COST)
    rest = [m for m in early if m != 1]
    both = swapped(bundled([both] + [arrays[k][m] for m in rest for k in (1, 0)], size), core)
    for i, m in enumerate([1] + rest):
        row = i * (2 * size + EXTRA_ROWS)
        others[1][m], others[0][m] = ((both, row, 0),), ((both, row + size, 0),)

    def sums(name, kind, rows, columns, jobs, before, emits, after=()):
        other = 1 - kind
        x_blocks = [blocks[kind][m] for m in rows]
        y_blocks = [(blocks, others)[c][other][m] for c, m in columns]
        x_masks = [masks[kind][m] for m in rows]
        y_masks = [masks[other][m + c * count] for c, m in columns]
        return gradient_sums(
            name,
            size,
            scalars,
            x_blocks,
            y_blocks,
            (x_masks, y_masks),
            kind == 0,
            jobs,
            before,
            emits,
            [blocks[k][m] for m in rows[1:] + rows[:1] for k in (1, 0)],
            after,
        )

    def both_cores(chosen):
        return [(c, m) for c in range(2) for m in chosen]

    def every_pair(rows, columns):
        return [(list(range(len(rows))), list(range(len(columns))))]

    before = []
    for k in range(2):
        columns = both_cores(early)
        jobs, emits = every_pair(early, columns), ["float"] * len(early)
        results = sums("early_sums", k, early, columns, jobs, {}, emits)
        before.append({m: s for m, (s,) in zip(early, results)})
    arrays = [[b[m][0][0] for m in late] for b in blocks[::-1]]
    arrays, before = lax.optimization_barrier((arrays, before))
    for k in (1, 0):
        for m, a in zip(late, arrays[1 - k]):
            blocks[k][m] = whole(a)
            others[k][m] = whole(swapped(a, core))
    after = ()
    coded, kept = [[None] * half, [None] * half], [None, None]
    for k in (1, 0):
        columns = [(0, m) for m in range(count)] + [(1, m) for m in early]
        jobs, emits = every_pair(late, columns), ["float"] * len(late)
        results = sums("late_rows_begun", k, late, columns, jobs, {}, emits, after)
        begun = {i: s for i, (s,) in enumerate(results)}
        columns = [(1, m) for m in late]
        jobs, emits = every_pair(late, columns), ["parts"] * len(late)
        coded[k][1:] = sums("late_rows", k, late, columns, jobs, begun, emits)
        after = coded[k][1]
    def last_columns(k, rows, emits, after):
        columns = both_cores(late)
        begun = {i: before[k][m] for i, m in enumerate(rows)}
        return [r[0] for r in sums("late_columns", k, rows, columns, every_pair(rows, columns), begun, emits, after)]

    middle = list(range(1, half))
    for k in (1, 0):
        kept[k] = [None] + last_columns(k, middle, ["float"] * len(middle), after)
        after = kept[k][-1:]
    text_blocks, after, _ = scattered(kept[1], coded[1], steps[1], ())
    image_blocks, _, after = scattered(kept[0], coded[0], steps[0], after)
    ends_at = [image_blocks, text_blocks]
    for k in (1, 0):
        kept[k][0], code = last_columns(k, [0, half], ["float", "whole"], after)
        ends_at[k].append(whole(swapped(code, steps[k][-1])))
        after = [code]
    kept_images, kept_texts = kept[0][0], kept[1][0]
    ends = ()
    for blocks_in in (text_blocks, image_blocks):
        ends = in_order([part[0] for b in blocks_in if len(b) > 1 for part in b], ends)
        parts = iter(ends)
        blocks_in[:] = [tuple((next(parts), 0, 0) for _ in b) if len(b) > 1 else b for b in blocks_in]
    return tuple(output_sums(scalars[0], [(kept_images, image_blocks), (kept_texts, text_blocks)]))


def solution(mesh):
    placed = (P(("blk", "grp"), None), P(("blk", "grp"), None), P(("blk", "grp")), P(), P())
    return jax.shard_map(
        per_device,
        mesh=mesh,
        in_specs=placed,
        out_specs=(P(("blk", "grp"), None), P(("blk", "grp"), None)),
        check_vma=False,
    )
```

```python
import math

import jax
import jax.numpy as jnp
from jax import lax
from jax.experimental import pallas as pl
from jax.experimental.pallas import tpu as pltpu
from jax.sharding import PartitionSpec as P

LOG2E = 1.4426950408889634
CODE_TOP = 32000.0
CODE_STEPS = 32.0
EXTRA_ROWS = 8
LABEL_BASE = 128
TILE = 256
LANES = 128
BUNDLE_COST = 6 * 10**8
HELD_COST = 85 * 10**7
SMEM = pl.BlockSpec(memory_space=pltpu.SMEM)
VMEM = pl.BlockSpec(memory_space=pltpu.VMEM)
ANY = pl.BlockSpec(memory_space=pl.ANY)


def whole(array):
    return ((array, 0, 0),)


def part_widths(width):
    first = width // (2 * LANES) * LANES
    return (first, width - first)


def column_tiles(width):
    tiles, begin = [], 0
    for p, w in enumerate(part_widths(width)):
        tiles += [(p, k, begin + k, min(TILE, w - k)) for k in range(0, w, TILE)]
        begin += w
    return tiles


def piece(block, rows, tile):
    p, inner, start, span = tile
    ref, row, column = block[0 if len(block) == 1 else p]
    first = start if len(block) == 1 else inner
    return ref.at[pl.ds(row + rows[0], rows[1]), pl.ds(column + first, span)]


class Operands:
    def __init__(self):
        self.pairs = []

    def add(self, array, spec):
        for i, (a, s) in enumerate(self.pairs):
            if a is array and s is spec:
                return i
        self.pairs.append((array, spec))
        return len(self.pairs) - 1

    def block(self, block):
        at = [(self.add(a, VMEM), row, column) for a, row, column in block]
        return lambda refs: tuple((refs[i], row, column) for i, row, column in at)


def scale_code(top):
    return jnp.ceil(jnp.log(jnp.maximum(top, 1e-30)) * (CODE_STEPS * LOG2E))


def encode(value, block, tile):
    size, span = value.shape
    code = scale_code(jnp.max(jnp.abs(value), axis=0, keepdims=True))
    gain = CODE_TOP * jnp.exp(code * (-1.0 / (CODE_STEPS * LOG2E)))
    piece(block, (0, size), tile)[...] = (
        jnp.round(value * gain).astype(jnp.int32).astype(jnp.int16)
    )
    scales = jnp.broadcast_to(code.astype(jnp.int32), (EXTRA_ROWS, span)).astype(jnp.int16)
    piece(block, (size, EXTRA_ROWS), tile)[...] = scales


def decoded(block, size, tile):
    code = piece(block, (size, EXTRA_ROWS), tile)[...].astype(jnp.int32).astype(jnp.float32)
    gain = jnp.exp(code[:1] * (1.0 / (CODE_STEPS * LOG2E))) * (1.0 / CODE_TOP)
    return piece(block, (0, size), tile)[...].astype(jnp.int32).astype(jnp.float32) * gain


def call(kernel, name, operands, out_shape, scratch, room, cost, after=(), held_back=()):
    arrays = [a for a, _ in operands]
    held = sum(math.prod(a.shape) * a.dtype.itemsize for a in [*arrays, *out_shape])

    def body(*refs):
        results = refs[len(arrays) + len(after) + len(held_back) :]
        kernel(refs[: len(arrays)], results[: len(out_shape)] + results[len(out_shape) + len(held_back) :])

    return pl.pallas_call(
        body,
        out_shape=[*out_shape, *(jax.ShapeDtypeStruct(a.shape, a.dtype) for a in held_back)],
        in_specs=[s for _, s in operands] + [ANY] * (len(after) + len(held_back)),
        out_specs=[VMEM] * len(out_shape) + [ANY] * len(held_back),
        input_output_aliases={
            len(arrays) + len(after) + i: len(out_shape) + i for i in range(len(held_back))
        },
        scratch_shapes=scratch,
        compiler_params=pltpu.CompilerParams(vmem_limit_bytes=held + room),
        cost_estimate=pl.CostEstimate(flops=cost, bytes_accessed=cost, transcendentals=0),
        name=name,
    )(*arrays, *after, *held_back)


def labelled(images, labels, after=()):
    size, width = images.shape

    def kernel(ins, outs):
        outs[0][pl.ds(0, size), :] = ins[0][...]
        outs[0][pl.ds(size, EXTRA_ROWS), :] = jnp.zeros((EXTRA_ROWS, width), jnp.bfloat16)
        row = ins[1][...]
        low, high = lax.rem(row, LABEL_BASE), lax.div(row, LABEL_BASE)
        at = lax.broadcasted_iota(jnp.int32, (EXTRA_ROWS, size), 0)
        parts = jnp.where(at == 0, high, jnp.where(at == 1, low, 0)).astype(jnp.float32)
        outs[0][pl.ds(size, EXTRA_ROWS), pl.ds(0, size)] = parts.astype(jnp.bfloat16)

    shape = jax.ShapeDtypeStruct((size + EXTRA_ROWS, width), jnp.bfloat16)
    operands = [(images, VMEM), (labels, VMEM)]
    return call(kernel, "labelled", operands, [shape], [], 2**21, size, after)[0]


def bundled(arrays, cost):
    width = arrays[0].shape[1]

    def kernel(ins, outs):
        first = 0
        for ref in ins:
            outs[0][pl.ds(first, ref.shape[0]), :] = ref[...]
            first += ref.shape[0]

    shape = jax.ShapeDtypeStruct((sum(a.shape[0] for a in arrays), width), jnp.bfloat16)
    operands = [(a, VMEM) for a in arrays]
    return call(kernel, "bundled", operands, [shape], [], 2**21, cost)[0]


def first_row(mask, size):
    owner = (lax.axis_index("blk") ^ mask[0]) * lax.axis_size("grp") + (lax.axis_index("grp") ^ mask[1])
    return owner * size


def keys_of(block, size, mask, is_image):
    if not is_image:
        ids = lax.broadcasted_iota(jnp.int32, (1, size), 1) + first_row(mask, size)
        return ids.astype(jnp.float32)
    parts = piece(block, (size, EXTRA_ROWS), (0, 0, 0, size))[...].astype(jnp.float32)
    return parts[0:1] * LABEL_BASE + parts[1:2]


def gradient_sums(name, size, scalars, x_blocks, y_blocks, masks, x_images, jobs, before, emits, sequence, after=()):
    width = x_blocks[0][0][0].shape[1]
    x_masks, y_masks = masks
    per_tile = TILE // size
    widths = part_widths(width)
    shapes, where = [], {}

    def result(extra, w, dtype):
        shapes.append(jax.ShapeDtypeStruct((size + extra, w), dtype))
        return len(shapes) - 1

    for r, kind in enumerate(emits):
        if kind == "float":
            where[r] = [(result(0, width, jnp.float32), 0, 0)]
        else:
            cut = widths if kind == "parts" else (width,)
            where[r] = [(result(EXTRA_ROWS, w, jnp.int16), 0, 0) for w in cut]
    operands = Operands()
    slope_at, shift_at = [operands.add(s, SMEM) for s in scalars]
    for b in sequence:
        operands.block(b)
    x_views = [operands.block(b) for b in x_blocks]
    y_views = [operands.block(b) for b in y_blocks]
    before_at = {r: operands.add(b, VMEM) for r, b in before.items()}

    def kernel(ins, refs):
        outs, weights = refs[:-1], refs[-1]
        slope, shift = ins[slope_at][0] * LOG2E, ins[shift_at][0] * LOG2E
        x_refs, y_refs = [v(ins) for v in x_views], [v(ins) for v in y_views]

        def stacked(chosen):
            return jnp.concatenate(
                [ref[pl.ds(row, size), pl.ds(column, width)] for ((ref, row, column),) in chosen],
                axis=0,
            )

        for rows, columns in jobs:
            x_all = stacked([x_refs[r] for r in rows])
            keys = [
                jnp.broadcast_to(keys_of(x_refs[r], size, x_masks[r], x_images), (size, size)).T
                for r in rows
            ]
            for n in range(0, len(columns), per_tile):
                chosen = columns[n : n + per_tile]
                other = jnp.concatenate(
                    [keys_of(y_refs[c], size, y_masks[c], not x_images) for c in chosen], axis=1
                )
                scores = lax.dot_general(
                    x_all,
                    stacked([y_refs[c] for c in chosen]),
                    (((1,), (1,)), ((), ())),
                    preferred_element_type=jnp.float32,
                )
                for i in range(len(rows)):
                    z = scores[i * size : (i + 1) * size] * slope + shift
                    sig = 1.0 / (1.0 + jnp.exp2(-z))
                    w = jnp.where(jnp.tile(keys[i], (1, len(chosen))) == other, sig - 1.0, sig)
                    there = pl.ds(n * size, len(chosen) * size)
                    weights[pl.ds(i * size, size), there] = w.astype(jnp.bfloat16)
            for tile in column_tiles(width):
                sums = jnp.dot(
                    weights[pl.ds(0, len(rows) * size), pl.ds(0, len(columns) * size)],
                    jnp.concatenate([piece(y_refs[c], (0, size), tile)[...] for c in columns], axis=0),
                    preferred_element_type=jnp.float32,
                )
                for i, r in enumerate(rows):
                    block = sums[i * size : (i + 1) * size]
                    if r in before_at:
                        block = block + piece(whole(ins[before_at[r]]), (0, size), tile)[...]
                    out = tuple((outs[o], row, column) for o, row, column in where[r])
                    if emits[r] == "float":
                        piece(out, (0, size), tile)[...] = block
                    else:
                        encode(block, out, tile)

    pairs = sum(len(rows) * len(columns) for rows, columns in jobs)
    scratch = [pltpu.VMEM((len(x_blocks) * size, len(y_blocks) * size), jnp.bfloat16)]
    room = len(x_blocks) * len(y_blocks) * size * size * 2 + 8 * 2**20
    results = call(kernel, name, operands.pairs, shapes, scratch, room, pairs * size, after)
    return [tuple(results[o] for o, _, _ in where[r]) for r in range(len(emits))]


def passed_sum(kept, received, part, held_back=(), after=()):
    size, width = kept.shape
    operands = Operands()
    kept_at = operands.add(kept, VMEM)
    views = [operands.block(b if part is None or len(b) == 1 else (b[part],) * 2) for b in received]

    def kernel(ins, outs):
        for tile in column_tiles(width):
            p, inner, _, span = tile
            if part is None or p == part:
                total = piece(whole(ins[kept_at]), (0, size), tile)[...]
                for view in views:
                    total = total + decoded(view(ins), size, tile)
                encode(total, whole(outs[0]), tile if part is None else (0, 0, inner, span))

    cut = width if part is None else part_widths(width)[part]
    shape = jax.ShapeDtypeStruct((size + EXTRA_ROWS, cut), jnp.int16)
    return call(kernel, "passed_sum", operands.pairs, [shape], [], 2**21, size, after, held_back)


def output_sums(sharpness, sums):
    size, width = sums[0][0].shape
    operands = Operands()
    sharpness_at = operands.add(sharpness, SMEM)
    views = [(operands.add(kept, VMEM), [operands.block(b) for b in blocks]) for kept, blocks in sums]

    def kernel(ins, outs):
        for out, (kept_at, received) in zip(outs, views):
            for tile in column_tiles(width):
                total = piece(whole(ins[kept_at]), (0, size), tile)[...]
                for view in received:
                    total = total + decoded(view(ins), size, tile)
                piece(whole(out), (0, size), tile)[...] = total * ins[sharpness_at][0]

    shapes = [jax.ShapeDtypeStruct((size, width), jnp.float32)] * len(sums)
    return call(kernel, "output_sums", operands.pairs, shapes, [], 2**21, size)


def swapped(array, step):
    axis, bit = step
    return lax.ppermute(array, axis, [(i, i ^ bit) for i in range(lax.axis_size(axis))])


def scattered(kept, coded, steps, after):
    def sent(array, step):
        return (swapped(array, step), 0, 0)

    half = len(kept)
    received = [[]] + [[(sent(c[0], steps[-1]),)] for c in coded[1:]]
    waiting, last = [c[1] for c in coded[1:]], []
    for s in reversed(range(len(steps) - 1)):
        for m in reversed(range(1 << s)):
            n = m | 1 << s
            first, *begun = passed_sum(kept[n], received[n], 0, waiting + last)
            if waiting:
                begun_with = [first]
            for r, c in zip(received[1:], begun):
                r[0] = r[0] + (sent(c, steps[-1]),)
            received[0] += [(sent(c, steps[-1]),) for c in begun[len(waiting) :]]
            first = sent(first, steps[s])
            (second,) = passed_sum(kept[n], received[n], 1, (), [first[0], *after])
            received[m].append((first, sent(second, steps[s])))
            waiting, last, after = [], [], [second]
    return received[0], after, begun_with


def in_order(arrays, after=(), cost=HELD_COST):
    return call(lambda *refs: None, "held", [], [], [], 2**21, cost, after, arrays)


def bit_steps(axis):
    return [(axis, 1 << k) for k in range(int(math.log2(lax.axis_size(axis))))]


def owner_masks(steps):
    masks = [(0, 0)]
    for axis, bit in steps:
        masks = masks + [(b ^ bit, g) if axis == "blk" else (b, g ^ bit) for b, g in masks]
    return masks


def per_device(
    picture_vectors, caption_vectors, matching_caption, sharpness_parameter, additive_intercept
):
    scalars = (sharpness_parameter, additive_intercept)
    size = picture_vectors.shape[0]
    core, *grp_steps = bit_steps("grp")
    every = grp_steps + bit_steps("blk")
    steps = [every[0::2], every[1::2]]
    assert len(steps[0]) == len(steps[1]) >= 2
    masks = [owner_masks(s + [core]) for s in steps]
    count = 1 << len(steps[0])
    half = count // 2
    early, late = list(range(half + 1)), list(range(half + 1, count))
    labels = matching_caption[None, :]
    (first_texts,) = in_order([swapped(caption_vectors, steps[1][0])], (), 1)
    first_images = [swapped(a, steps[0][0]) for a in (picture_vectors, labels)]
    arrays = [{0: labelled(picture_vectors, labels), 1: labelled(*first_images, [first_texts])}, {0: caption_vectors, 1: first_texts}]
    for i in range(1, len(steps[0])):
        for k in (1, 0):
            for m in range(1 << i):
                arrays[k][m | 1 << i] = swapped(arrays[k][m], steps[k][i])
    blocks = [[whole(a[m]) for m in range(count)] for a in arrays]
    others = [{}, {}]
    both = bundled([arrays[1][1], arrays[0][1]], BUNDLE_COST)
    rest = [m for m in early if m != 1]
    both = swapped(bundled([both] + [arrays[k][m] for m in rest for k in (1, 0)], size), core)
    for i, m in enumerate([1] + rest):
        row = i * (2 * size + EXTRA_ROWS)
        others[1][m], others[0][m] = ((both, row, 0),), ((both, row + size, 0),)

    def sums(name, kind, rows, columns, jobs, before, emits, after=()):
        other = 1 - kind
        x_blocks = [blocks[kind][m] for m in rows]
        y_blocks = [(blocks, others)[c][other][m] for c, m in columns]
        x_masks = [masks[kind][m] for m in rows]
        y_masks = [masks[other][m + c * count] for c, m in columns]
        return gradient_sums(
            name,
            size,
            scalars,
            x_blocks,
            y_blocks,
            (x_masks, y_masks),
            kind == 0,
            jobs,
            before,
            emits,
            [blocks[k][m] for m in rows[1:] + rows[:1] for k in (1, 0)],
            after,
        )

    def both_cores(chosen):
        return [(c, m) for c in range(2) for m in chosen]

    def every_pair(rows, columns):
        return [(list(range(len(rows))), list(range(len(columns))))]

    before = []
    for k in range(2):
        columns = both_cores(early)
        jobs, emits = every_pair(early, columns), ["float"] * len(early)
        results = sums("early_sums", k, early, columns, jobs, {}, emits)
        before.append({m: s for m, (s,) in zip(early, results)})
    arrays = [[b[m][0][0] for m in late] for b in blocks[::-1]]
    arrays, before = lax.optimization_barrier((arrays, before))
    for k in (1, 0):
        for m, a in zip(late, arrays[1 - k]):
            blocks[k][m] = whole(a)
            others[k][m] = whole(swapped(a, core))
    after = ()
    coded, kept = [[None] * half, [None] * half], [None, None]
    for k in (1, 0):
        columns = [(0, m) for m in range(count)] + [(1, m) for m in early]
        jobs, emits = every_pair(late, columns), ["float"] * len(late)
        results = sums("late_rows_begun", k, late, columns, jobs, {}, emits, after)
        begun = {i: s for i, (s,) in enumerate(results)}
        columns = [(1, m) for m in late]
        jobs, emits = every_pair(late, columns), ["parts"] * len(late)
        coded[k][1:] = sums("late_rows", k, late, columns, jobs, begun, emits)
        after = coded[k][1]
    def last_columns(k, rows, emits, after):
        columns = both_cores(late)
        begun = {i: before[k][m] for i, m in enumerate(rows)}
        return [r[0] for r in sums("late_columns", k, rows, columns, every_pair(rows, columns), begun, emits, after)]

    middle = list(range(1, half))
    for k in (1, 0):
        kept[k] = [None] + last_columns(k, middle, ["float"] * len(middle), after)
        after = kept[k][-1:]
    text_blocks, after, _ = scattered(kept[1], coded[1], steps[1], ())
    image_blocks, _, after = scattered(kept[0], coded[0], steps[0], after)
    ends_at = [image_blocks, text_blocks]
    for k in (1, 0):
        kept[k][0], code = last_columns(k, [0, half], ["float", "whole"], after)
        ends_at[k].append(whole(swapped(code, steps[k][-1])))
        after = [code]
    kept_images, kept_texts = kept[0][0], kept[1][0]
    ends = ()
    for blocks_in in (text_blocks, image_blocks):
        ends = in_order([part[0] for b in blocks_in if len(b) > 1 for part in b], ends)
        parts = iter(ends)
        blocks_in[:] = [tuple((next(parts), 0, 0) for _ in b) if len(b) > 1 else b for b in blocks_in]
    return tuple(output_sums(scalars[0], [(kept_images, image_blocks), (kept_texts, text_blocks)]))


def solution(mesh):
    placed = (P(("blk", "grp"), None), P(("blk", "grp"), None), P(("blk", "grp")), P(), P())
    return jax.shard_map(
        per_device,
        mesh=mesh,
        in_specs=placed,
        out_specs=(P(("blk", "grp"), None), P(("blk", "grp"), None)),
        check_vma=False,
    )
```
